32 devices in a mesh: ctx: 8 (over z, core), ch: 4 (over y, x).
Axes of the slice: x: 2, y: 2, z: 4, core: 2. Of those that a mesh axis runs over, the one named last changes fastest.
Arguments:
- features: bfloat16 [4096, 3, 4096], P('ctx', None, 'ch'), may hold values from -6 to 6
- residual_in: bfloat16 [4096, 4096], P('ctx', 'ch'), may hold values from -6 to 6
- short_filter: float32 [3, 7, 256], P(None, None, 'ch'), may hold values from -2 to 2
- medium_filter: float32 [128, 256], P(None, 'ch'), may hold values from -0.5 to 0.5
- skip_gain: float32 [4096], P('ch'), may hold values from -4 to 4
- out_weight: bfloat16 [4096, 4096], P('ch'), may hold values from -0.125 to 0.125
- norm_gain: float32 [4096], replicated, may hold values from 0.1 to 1.9
- attn_weight: bfloat16 [4096, 6144], P(None, 'ch'), may hold values from -2 to 2, as said below
- attn_out: bfloat16 [2048, 4096], P('ch'), may hold values from -0.1875 to 0.1875
Outputs:
- result: bfloat16 [4096, 4096], P('ctx', 'ch')
The draws below stay inside these ranges and needn't reach their ends.
Inputs may be any that keep to these rules, and one draw needn't show every extreme that they name: `attn_weight`: entries of order 4096 ** -0.5 times a few.
All inputs are finite; a program needn't handle non-finite values.
Results may differ from the reference program's by a relative error of at most 0.03.
Values may be sent and summed in bfloat16 or wider, within the bound.
No kernel may reach another device: no remote copies, remote signals or barrier semaphores. Data moves between devices by JAX's collectives and lax.ppermute only.
A program may use at most 128 MiB of HBM per device.

```python
import jax
import jax.numpy as jnp
from jax import lax

D = 4096
HEAD = 128
GROUP_SIZE = 16
SHORT = 7
MED = 128
HEADS = 16
GROUPS = 256
TOKENS = 4096
N_CH = 4


def draw_attn_weight(key, part):
    first_key = jax.random.fold_in(jax.random.fold_in(key, 17), 0)
    drawn = jnp.clip(jax.random.normal(first_key, (D, HEADS, 3, HEAD), jnp.float32), -5.0, 5.0)
    boosted = jnp.ones((1, HEADS, 1, 1), jnp.float32)
    kind_scale = jnp.array([1.4, 1.4, 4.0], jnp.float32)[None, None, :, None]
    kind_boost = jnp.where(jnp.arange(3)[None, None, :, None] < 2, boosted, 1.0)
    weights = drawn * kind_scale * kind_boost / D ** 0.5
    return weights.reshape(D, HEADS * 3 * HEAD).astype(jnp.bfloat16)


def with_spikes(result, stream_key, source, target, parts, factor):
    def block_of(position):
        return (jnp.arange(result.shape[position]) // (result.shape[position] // parts)).reshape((-1,) + (1,) * (result.ndim - 1 - position))

    one_side = jax.random.permutation(stream_key, parts)[block_of(target)]
    other_side = (block_of(target) + parts // 2) % parts
    return jnp.where((block_of(source) == one_side) | (block_of(source) == other_side), factor * result, result)


def shard_levels(rng, extent, cuts, smallest, top_value):
    gain = 1.0
    for dim, parts in cuts:
        draws = jax.random.uniform(jax.random.fold_in(jax.random.fold_in(rng, 6), dim), (parts,), jnp.float32, smallest / len(cuts), top_value / len(cuts))
        gain = gain * jnp.repeat(jnp.exp(draws), extent[dim] // parts).reshape((-1,) + (1,) * (len(extent) - 1 - dim))
    return gain


def gaussian(stream_key, shape, scale, bound, shards=(), held_as=jnp.bfloat16):
    entries = jax.random.normal(stream_key, shape, jnp.float32) * scale
    if len(shards) > 0:
        entries = shard_levels(stream_key, shape, shards, -0.22, 0.18) * entries
    return jnp.clip(entries, min=-bound, max=bound).astype(held_as)


def heavy_noise(own_key, shape, width, limit, shards, heavy, kind=jnp.bfloat16):
    values = width * jax.random.normal(own_key, shape, jnp.float32)
    if shards:
        values = values * shard_levels(own_key, shape, shards, -0.22, 0.18)
    return jnp.clip(with_spikes(values, jax.random.fold_in(own_key, 3), *heavy), -limit, limit).astype(kind)


def setup_inputs(seed: int = 0) -> dict:
    keys = jax.random.split(jax.random.key(seed), 10)
    return {
        "features": gaussian(keys[0], (TOKENS, 3, D), 1.0, 6.0, ((0, 8), (2, 4))),
        "residual_in": gaussian(keys[1], (TOKENS, D), 1.0, 6.0, ((0, 8), (1, 4))),
        "short_filter": gaussian(keys[2], (3, SHORT, GROUPS), SHORT ** -0.5, 2.0, ((2, 4),), jnp.float32),
        "medium_filter": gaussian(keys[3], (MED, GROUPS), MED ** -0.5, 0.5, ((1, 4),), jnp.float32),
        "skip_gain": gaussian(keys[4], (D,), 1.0, 4.0, ((0, 4),), jnp.float32),
        "out_weight": heavy_noise(keys[5], (D, D), D ** -0.5, 0.125, ((0, 4),), (0, 1, 4, 2.0)),
        "norm_gain": jnp.clip(1.0 + 0.18 * jax.random.normal(keys[6], (D,), jnp.float32), 0.1, 1.9),
        "attn_weight": draw_attn_weight(jax.random.fold_in(keys[9], 71), 0),
        "attn_out": heavy_noise(keys[8], (HEADS * HEAD, D), (HEADS * HEAD) ** -0.5, 0.1875, ((0, 4),), (0, 1, 4, 2.0)),
    }


def rotate_rows(block, positions):
    half_size = block.shape[-1] // 2
    frequency = 10000.0 ** (-jnp.arange(half_size, dtype=jnp.float32) * 2.0 / block.shape[-1])
    angles = positions.astype(jnp.float32)[:, None] * frequency[None, :]
    cosine = jnp.cos(angles)[:, None, :]
    sine_part = jnp.sin(angles)[:, None, :]
    first_half = block[..., :half_size]
    second_half = block[..., half_size:]
    return jnp.concatenate([first_half * cosine - second_half * sine_part, second_half * cosine + first_half * sine_part], axis=-1)

def blockwise_sum(left, right, block_count):
    width_block = left.shape[1] // block_count
    summed = jnp.zeros((left.shape[0], right.shape[1]), jnp.float32)
    for block_index in range(block_count):
        lower = block_index * width_block
        partial_term = jnp.dot(left[:, lower:lower + width_block], right[lower:lower + width_block], preferred_element_type=jnp.float32).astype(jnp.bfloat16)
        summed = summed + lax.optimization_barrier(partial_term).astype(jnp.float32)
    return summed

def reference(features, residual_in, short_filter, medium_filter, skip_gain, out_weight, norm_gain, attn_weight, attn_out):
    widened = features.astype(jnp.float32)
    short_taps = jnp.repeat(short_filter, GROUP_SIZE, axis=2)
    padded = jnp.pad(widened, ((SHORT - 1, 0), (0, 0), (0, 0)))
    featured = jnp.zeros(widened.shape, jnp.float32)
    for tap_index in range(SHORT):
        begin_row = SHORT - 1 - tap_index
        featured = featured + short_taps[:, tap_index, :][None] * padded[begin_row:begin_row + TOKENS]
    product = (featured[:, 1, :] * featured[:, 2, :]).astype(jnp.bfloat16)
    medium_taps = jnp.repeat(medium_filter, GROUP_SIZE, axis=1)
    product_pad = jnp.pad(product.astype(jnp.float32), ((MED - 1, 0), (0, 0)))

    def add_tap(tap_index, accum):
        begin_row = (MED - 1 - tap_index).astype(jnp.int32)
        window = lax.dynamic_slice_in_dim(product_pad, begin_row, TOKENS, 0)
        tap_row = lax.dynamic_index_in_dim(medium_taps, tap_index.astype(jnp.int32), 0, keepdims=False)
        return accum + tap_row[None, :] * window
    mixed = lax.fori_loop(0, MED, add_tap, jnp.zeros((TOKENS, D), jnp.float32))
    mixed = mixed + skip_gain[None, :] * product.astype(jnp.float32)
    gated = (featured[:, 0, :] * mixed).astype(jnp.bfloat16)
    hyena_out = blockwise_sum(gated, out_weight, N_CH)
    stream = (residual_in.astype(jnp.float32) + hyena_out).astype(jnp.bfloat16)
    stream_wide = stream.astype(jnp.float32)
    inverse = lax.rsqrt(lax.optimization_barrier(jnp.mean(stream_wide * stream_wide, axis=1)) + 1e-05)
    normed = (stream_wide * inverse[:, None] * norm_gain[None, :]).astype(jnp.bfloat16)
    projected = jnp.dot(normed, attn_weight, preferred_element_type=jnp.float32).reshape(TOKENS, HEADS, 3, HEAD)
    positions = jnp.arange(TOKENS, dtype=jnp.int32)
    queries = rotate_rows(projected[:, :, 0, :], positions).astype(jnp.bfloat16)
    key_rows = rotate_rows(projected[:, :, 1, :], positions).astype(jnp.bfloat16)
    value_rows = projected[:, :, 2, :].astype(jnp.bfloat16)
    causal = positions[None, :] <= positions[:, None]
    scale_factor = 1.0 / HEAD ** 0.5

    def one_head(operands):
        query_head, key_head, value_head = operands
        scores = jnp.dot(query_head, key_head.T, preferred_element_type=jnp.float32) * scale_factor
        scores = jnp.where(causal, scores, -1e+30)
        row_max = lax.optimization_barrier(jnp.max(scores, axis=1, keepdims=True))
        weights = jnp.where(causal, jnp.exp(scores - row_max), 0.0)
        row_total = lax.optimization_barrier(jnp.sum(weights, axis=1, keepdims=True))
        output = jnp.dot(weights.astype(jnp.bfloat16), value_head, preferred_element_type=jnp.float32) / row_total
        return output.astype(jnp.bfloat16)
    attended = lax.map(one_head, (jnp.transpose(queries, (1, 0, 2)), jnp.transpose(key_rows, (1, 0, 2)), jnp.transpose(value_rows, (1, 0, 2))))
    attended = jnp.transpose(attended, (1, 0, 2)).reshape(TOKENS, HEADS * HEAD)
    attn_mix = blockwise_sum(attended, attn_out, N_CH)
    return (stream_wide + attn_mix).astype(jnp.bfloat16)
```

```python
import functools

import jax
import jax.numpy as jnp
from jax import lax
from jax.experimental import pallas as pl
from jax.experimental.pallas import tpu as pltpu
from jax.sharding import PartitionSpec as P

HEAD = 128
GROUP_SIZE = 16
LANES = 128
LEAD = 16
norm_eps = 1e-05
MIB = 1024 * 1024
F32 = jnp.float32
BF16 = jnp.bfloat16


def swap_ch(value, mask):
    count = lax.axis_size("ch")
    return lax.ppermute(value, "ch", [(i, i ^ mask) for i in range(count)])


def swap_core(value):
    count = lax.axis_size("ctx")
    return lax.ppermute(value, "ctx", [(i, i ^ 1) for i in range(count)])


def rotate_chips(value, distance):
    count = lax.axis_size("ctx")
    return lax.ppermute(value, "ctx", [(i, (i + 2 * distance) % count) for i in range(count)])


def conv_kernel(first_row, halo_rows, taps_ref, base_ref, skip_ref, *rest):
    if first_row == 0:
        halo_ref, rows_ref, out_ref, wide, product, table = rest
    else:
        rows_ref, out_ref, wide, product, table = rest
    count = out_ref.shape[0]
    length = base_ref.shape[1] // 2
    taps = taps_ref.shape[0] // 3

    if first_row == 0:
        wide[0, halo_rows - LEAD : halo_rows] = halo_ref[2 * halo_rows : 2 * halo_rows + LEAD].astype(F32)
        wide[1, :halo_rows] = halo_ref[:halo_rows].astype(F32)
        wide[2, :halo_rows] = halo_ref[halo_rows : 2 * halo_rows].astype(F32)
        for kind in range(3):
            wide[kind, halo_rows:] = rows_ref[kind].astype(F32)
    else:
        for kind in range(3):
            wide[kind] = rows_ref[kind, first_row - halo_rows : first_row + count].astype(F32)

    groups = base_ref.shape[0]
    for group in range(groups):
        spread = jnp.broadcast_to(base_ref[group : group + 1, :], (length, 2 * length))
        rolled = pltpu.roll(spread, 0, 1, stride=1, stride_axis=0)
        table[group * length : (group + 1) * length, :] = rolled.astype(BF16)

    def featured(kind, start):
        total = taps_ref[kind * taps : kind * taps + 1, :] * wide[kind, start : start + length, :]
        for tap in range(1, taps):
            weight = taps_ref[kind * taps + tap : kind * taps + tap + 1, :]
            total = total + weight * wide[kind, start - tap : start - tap + length, :]
        return total

    for block in range(count // length + 1):
        start = LEAD + block * length
        product[block * length : (block + 1) * length, :] = (
            featured(1, start) * featured(2, start)
        ).astype(BF16)

    group_of = lax.broadcasted_iota(jnp.int32, (length, 2 * LANES), 1) % LANES // GROUP_SIZE
    for pair in range(count // (2 * length)):
        begin = pair * 2 * length
        window = jnp.concatenate(
            [
                product[begin : begin + 2 * length, :],
                product[begin + length : begin + 3 * length, :],
            ],
            axis=1,
        )
        spread = jnp.dot(table[...], window, preferred_element_type=F32)
        mixed = spread[:length]
        for group in range(1, groups):
            mixed = jnp.where(group_of == group, spread[group * length : (group + 1) * length], mixed)
        for part in range(2):
            row = begin + part * length
            direct = skip_ref[...] * product[row + length : row + 2 * length, :].astype(F32)
            gate = featured(0, halo_rows + row)
            out_ref[row : row + length, :] = (
                gate * (mixed[:, part * LANES : (part + 1) * LANES] + direct)
            ).astype(BF16)


def conv_chunk(features, halo, first_row, count, taps, base, skip):
    kinds, rows, channels = features.shape
    length = base.shape[1] // 2
    halo_rows = length + LEAD
    groups = LANES // GROUP_SIZE
    specs = [
        pl.BlockSpec((taps.shape[0], LANES), lambda i: (0, i)),
        pl.BlockSpec((groups, 2 * length), lambda i: (i, 0)),
        pl.BlockSpec((1, LANES), lambda i: (0, i)),
    ]
    operands = [taps, base, skip]
    if first_row == 0:
        specs.append(pl.BlockSpec((halo.shape[0], LANES), lambda i: (0, i)))
        operands.append(halo)
        specs.append(pl.BlockSpec((kinds, count, LANES), lambda i: (0, 0, i)))
    else:
        specs.append(pl.BlockSpec((kinds, rows, LANES), lambda i: (0, 0, i)))
    operands.append(features)
    return pl.pallas_call(
        functools.partial(conv_kernel, first_row, halo_rows),
        grid=(channels // LANES,),
        in_specs=specs,
        out_specs=pl.BlockSpec((count, LANES), lambda i: (0, i)),
        out_shape=jax.ShapeDtypeStruct((count, channels), BF16),
        scratch_shapes=[
            pltpu.VMEM((kinds, halo_rows + count, LANES), F32),
            pltpu.VMEM((length + count, LANES), BF16),
            pltpu.VMEM((groups * length, 2 * length), BF16),
        ],
        compiler_params=pltpu.CompilerParams(vmem_limit_bytes=24 * MIB),
        name="hyena_filters",
    )(*operands)


def columns_kernel(steps_of, order_ref, left_ref, right_ref, *outs):
    step = pl.program_id(0)
    value = jnp.dot(left_ref[...], right_ref[...], preferred_element_type=F32).astype(BF16)
    begin = 0
    for out, steps in zip(outs, steps_of):

        @pl.when((step >= begin) & (step < begin + steps))
        def _():
            out[...] = value

        begin += steps


def column_products(left, right, order, steps_of, width):
    rows, depth = left.shape
    specs, shapes, begin = [], [], 0
    for steps in steps_of:
        specs.append(
            pl.BlockSpec(
                (rows, width),
                functools.partial(lambda b, s, i, order: (0, jnp.clip(i - b, 0, s - 1)), begin, steps),
            )
        )
        shapes.append(jax.ShapeDtypeStruct((rows, steps * width), BF16))
        begin += steps
    return pl.pallas_call(
        functools.partial(columns_kernel, steps_of),
        grid_spec=pltpu.PrefetchScalarGridSpec(
            num_scalar_prefetch=1,
            grid=(sum(steps_of),),
            in_specs=[
                pl.BlockSpec((rows, depth), lambda i, order: (0, 0)),
                pl.BlockSpec((depth, width), lambda i, order: (0, order[i])),
            ],
            out_specs=specs,
        ),
        out_shape=shapes,
        compiler_params=pltpu.CompilerParams(vmem_limit_bytes=24 * MIB),
        name="hyena_projection",
    )(order, left, right)


def qkv_kernel(chips, meta_ref, own, from_x, from_y, diag_a, diag_b, gain, cosine, sine, weight, *rest):
    outs, (normed, total) = rest[:chips], rest[chips:]
    step = pl.program_id(0)
    steps = pl.num_programs(0)
    depth = weight.shape[0]
    rows, channels = own.shape
    per_block = channels // depth

    @pl.when(step == 0)
    def _():
        half = rows // 2
        blocks = [own[...], from_x[...], from_y[...], None]
        blocks[3] = jnp.concatenate([diag_a[...], diag_b[...]], axis=0)
        square = jnp.zeros((rows, 1), F32)
        for block in blocks:
            wide = block.astype(F32)
            square = square + jnp.sum(wide * wide, axis=1, keepdims=True)
        inverse = lax.rsqrt(square / (4 * channels) + norm_eps)
        for index, block in enumerate(blocks):
            scaled = block.astype(F32) * inverse * gain[pl.ds(meta_ref[index], 1), :]
            for part in range(per_block):
                normed[index * per_block + part] = scaled[:, part * depth : (part + 1) * depth].astype(BF16)

    term = jnp.dot(normed[step], weight[...], preferred_element_type=F32)

    @pl.when(step == 0)
    def _():
        total[...] = term

    @pl.when(step > 0)
    def _():
        total[...] += term

    @pl.when(step == steps - 1)
    def _():
        for distance, out in enumerate(outs):
            head = lax.rem(meta_ref[4] + distance, chips)
            for kind in range(3):
                column = pl.multiple_of((head * 3 + kind) * HEAD, HEAD)
                part = total[:, pl.ds(column, HEAD)]
                if kind < 2:
                    part = part * cosine[...] + pltpu.roll(part, HEAD // 2, 1) * sine[...]
                out[kind] = part.astype(BF16)


def project(meta, own, from_x, from_y, diag_a, diag_b, gain, cosine, sine, weight, chips):
    rows, channels = own.shape
    width = weight.shape[1]
    depth = 512
    per_block = channels // depth
    full = lambda shape: pl.BlockSpec(shape, lambda i, meta: (0,) * len(shape))
    return pl.pallas_call(
        functools.partial(qkv_kernel, chips),
        grid_spec=pltpu.PrefetchScalarGridSpec(
            num_scalar_prefetch=1,
            grid=(4 * per_block,),
            in_specs=[
                full(own.shape),
                full(from_x.shape),
                full(from_y.shape),
                full(diag_a.shape),
                full(diag_b.shape),
                full(gain.shape),
                full(cosine.shape),
                full(sine.shape),
                pl.BlockSpec(
                    (depth, width),
                    lambda i, meta: (meta[i // per_block] * per_block + i % per_block, 0),
                ),
            ],
            out_specs=[full((3, rows, HEAD))] * chips,
            scratch_shapes=[
                pltpu.VMEM((4 * per_block, rows, depth), BF16),
                pltpu.VMEM((rows, width), F32),
            ],
        ),
        out_shape=[jax.ShapeDtypeStruct((3, rows, HEAD), BF16)] * chips,
        compiler_params=pltpu.CompilerParams(vmem_limit_bytes=40 * MIB),
        name="norm_qkv",
    )(meta, own, from_x, from_y, diag_a, diag_b, gain, cosine, sine, weight)


def attention_kernel(chips, chunks, meta_ref, *refs):
    own, other, outs = refs[:chunks], refs[chunks : 2 * chunks], refs[2 * chunks :]
    chip, core = meta_ref[4], meta_ref[5]
    scale = 1.0 / HEAD**0.5 * 1.4426950408889634

    def rows(refs_in, distance, kind):
        return jnp.concatenate([ref[distance, kind] for ref in refs_in], axis=0)

    def scores_of(queries, keys):
        return lax.dot_general(queries, keys, (((1,), (1,)), ((), ())), preferred_element_type=F32) * scale

    def update(state, scores, values):
        top, total, acc = state
        new_top = jnp.maximum(top, jnp.max(scores, axis=1, keepdims=True))
        weights = jnp.exp2(scores - new_top)
        shrink = jnp.exp2(top - new_top)
        total = total * shrink + jnp.sum(weights, axis=1, keepdims=True)
        acc = acc * shrink + jnp.dot(weights.astype(BF16), values, preferred_element_type=F32)
        return new_top, total, acc

    for distance, out in enumerate(outs):
        place = lax.rem(chip + distance, chips)
        here = lax.rem(chip - place + chips, chips)
        queries = rows(own, here, 0)
        count = queries.shape[0]
        scores = scores_of(queries, rows(own, here, 1))
        row = lax.broadcasted_iota(jnp.int32, scores.shape, 0)
        column = lax.broadcasted_iota(jnp.int32, scores.shape, 1)
        scores = jnp.where(column <= row, scores, -1e30)
        state = (
            jnp.full((count, 1), -1e30, F32),
            jnp.zeros((count, 1), F32),
            jnp.zeros((count, HEAD), F32),
        )
        state = update(state, scores, rows(own, here, 2))

        def own_block(index, state):
            there = lax.rem(chip - index + chips, chips)
            return update(state, scores_of(queries, rows(own, there, 1)), rows(own, there, 2))

        def other_block(index, state):
            there = lax.rem(chip - index + chips, chips)
            return update(state, scores_of(queries, rows(other, there, 0)), rows(other, there, 1))

        state = lax.fori_loop(0, place, own_block, state)
        state = lax.fori_loop(0, place + core, other_block, state)
        out[...] = (state[2] / state[1]).astype(BF16)


def attend(meta, own, other, chips):
    chunks = len(own)
    count = sum(piece.shape[2] for piece in own)
    whole = lambda shape: pl.BlockSpec(shape, lambda i, meta: (0,) * len(shape))
    return pl.pallas_call(
        functools.partial(attention_kernel, chips, chunks),
        grid_spec=pltpu.PrefetchScalarGridSpec(
            num_scalar_prefetch=1,
            grid=(1,),
            in_specs=[whole(piece.shape) for piece in own + other],
            out_specs=[whole((count, HEAD))] * chips,
        ),
        out_shape=[jax.ShapeDtypeStruct((count, HEAD), BF16)] * chips,
        compiler_params=pltpu.CompilerParams(vmem_limit_bytes=40 * MIB),
        name="attention",
    )(meta, *own, *other)


def mix_kernel(chips, meta_ref, own, from_x, from_y, diag_a, diag_b, stream, own_w, near_w, far_w, out, ordered):
    chip, core = meta_ref[4], meta_ref[5]
    rows = stream.shape[0]
    half_rows = near_w.shape[1]

    @pl.when(pl.program_id(0) == 0)
    def _():
        for distance in range(chips):
            head = lax.rem(chip - distance + chips, chips)
            column = pl.ds(pl.multiple_of(head * HEAD, HEAD), HEAD)
            ordered[0, :, column] = own[distance]
            ordered[1, :, column] = from_x[distance]
            ordered[2, :, column] = from_y[distance]
            ordered[3, : rows // 2, column] = diag_a[distance]
            ordered[3, rows // 2 :, column] = diag_b[distance]

    total = stream[...].astype(F32)
    total = total + jnp.dot(ordered[0], own_w[...], preferred_element_type=F32)
    near = pl.ds(pl.multiple_of(core * half_rows, half_rows), half_rows)
    far = pl.ds(pl.multiple_of((1 - core) * half_rows, half_rows), half_rows)
    for index in range(3):
        total = total + jnp.dot(ordered[index + 1, :, near], near_w[index], preferred_element_type=F32)
        total = total + jnp.dot(ordered[index + 1, :, far], far_w[index], preferred_element_type=F32)
    out[...] = total.astype(BF16)


def mix(meta, own, from_x, from_y, diag_a, diag_b, stream, own_w, near_w, far_w, chips):
    rows, channels = stream.shape
    width = 256
    full = lambda shape: pl.BlockSpec(shape, lambda i, meta: (0,) * len(shape))
    return pl.pallas_call(
        functools.partial(mix_kernel, chips),
        grid_spec=pltpu.PrefetchScalarGridSpec(
            num_scalar_prefetch=1,
            grid=(channels // width,),
            in_specs=[
                full(own.shape),
                full(from_x.shape),
                full(from_y.shape),
                full(diag_a.shape),
                full(diag_b.shape),
                pl.BlockSpec((rows, width), lambda i, meta: (0, i)),
                pl.BlockSpec((own_w.shape[0], width), lambda i, meta: (0, i)),
                pl.BlockSpec((3, near_w.shape[1], width), lambda i, meta: (0, 0, i)),
                pl.BlockSpec((3, far_w.shape[1], width), lambda i, meta: (0, 0, i)),
            ],
            out_specs=pl.BlockSpec((rows, width), lambda i, meta: (0, i)),
            scratch_shapes=[pltpu.VMEM((4, rows, chips * HEAD), BF16)],
        ),
        out_shape=jax.ShapeDtypeStruct((rows, channels), BF16),
        compiler_params=pltpu.CompilerParams(vmem_limit_bytes=40 * MIB),
        name="attention_mix",
    )(meta, own, from_x, from_y, diag_a, diag_b, stream, own_w, near_w, far_w)


def rotate_rows(block, positions):
    half_size = block.shape[-1] // 2
    frequency = 10000.0 ** (-jnp.arange(half_size, dtype=jnp.float32) * 2.0 / block.shape[-1])
    angles = positions.astype(jnp.float32)[:, None] * frequency[None, :]
    cosine = jnp.cos(angles)[:, None, :]
    sine_part = jnp.sin(angles)[:, None, :]
    first_half = block[..., :half_size]
    second_half = block[..., half_size:]
    return jnp.concatenate(
        [
            first_half * cosine - second_half * sine_part,
            second_half * cosine + first_half * sine_part,
        ],
        axis=-1,
    )


def run_attention(queries, query_pos, key_rows, value_rows, position_of):
    head_count = queries.shape[1]
    row_count = queries.shape[0]
    head_size = queries.shape[2]
    scale_factor = 1.0 / head_size**0.5
    last_query = jnp.max(query_pos)
    initial = (
        jnp.zeros((head_count, row_count, head_size), jnp.float32),
        jnp.full((head_count, row_count), -1e30, jnp.float32),
        jnp.zeros((head_count, row_count), jnp.float32),
    )
    piece_keys = lax.all_gather(key_rows, "ctx", axis=0, tiled=True)
    piece_values = lax.all_gather(value_rows, "ctx", axis=0, tiled=True)
    piece_rows = piece_keys.shape[0]
    block_rows = 512

    def one_block(state_in, block_index):
        first_block = block_index * block_rows
        key_block = lax.dynamic_slice_in_dim(piece_keys, first_block, block_rows, 0)
        value_block = lax.dynamic_slice_in_dim(piece_values, first_block, block_rows, 0)
        key_pos = position_of(first_block + jnp.arange(block_rows))

        def update(state_old):
            acc_sum, run_max, run_total = state_old
            scores = (
                jnp.einsum("thd,khd->htk", queries, key_block, preferred_element_type=jnp.float32)
                * scale_factor
            )
            causal = (key_pos[None, :] <= query_pos[:, None])[None]
            block_max = jnp.max(jnp.where(causal, scores, -1e30), axis=-1)
            new_max = jnp.maximum(run_max, block_max)
            weights = jnp.where(causal, jnp.exp(scores - new_max[..., None]), 0.0)
            correction = jnp.exp(run_max - new_max)
            new_total = run_total * correction + jnp.sum(weights, axis=-1)
            update_sum = jnp.einsum(
                "htk,khd->htd",
                weights.astype(jnp.bfloat16),
                value_block,
                preferred_element_type=jnp.float32,
            )
            return (acc_sum * correction[..., None] + update_sum, new_max, new_total)

        def unchanged(state_old):
            return state_old

        state_out = lax.cond(jnp.min(key_pos) > last_query, unchanged, update, state_in)
        return (state_out, None)

    state_end, unused = lax.scan(one_block, initial, jnp.arange(piece_rows // block_rows))
    acc_sum, run_max, run_total = state_end
    output = acc_sum / run_total[..., None]
    return jnp.transpose(output, (1, 0, 2)).astype(jnp.bfloat16)


def after_gating(gated, residual_in, out_weight, norm_gain, attn_weight, attn_out):
    tok_rows, chan_count = gated.shape
    hyena_terms = jnp.dot(gated, out_weight, preferred_element_type=jnp.float32)
    hyena_out = lax.psum_scatter(
        hyena_terms.astype(jnp.bfloat16), "ch", scatter_dimension=1, tiled=True
    ).astype(jnp.float32)
    stream = (residual_in.astype(jnp.float32) + hyena_out).astype(jnp.bfloat16)
    stream_wide = stream.astype(jnp.float32)
    full_width = chan_count * lax.axis_size("ch")
    head_cols = attn_weight.shape[1]
    square_total = lax.psum(jnp.sum(stream_wide * stream_wide, axis=1), "ch")
    inverse = lax.rsqrt(square_total / full_width + norm_eps)
    gain_part = lax.dynamic_slice_in_dim(norm_gain, lax.axis_index("ch") * chan_count, chan_count)
    normed = (stream_wide * inverse[:, None] * gain_part[None, :]).astype(jnp.bfloat16)
    projected = jnp.dot(
        lax.all_gather(normed, "ch", axis=1, tiled=True),
        attn_weight,
        preferred_element_type=jnp.float32,
    )
    head_count = head_cols // (3 * HEAD)
    projected = projected.reshape(tok_rows, head_count, 3, HEAD)
    ctx_index = lax.axis_index("ctx")
    positions = ctx_index * tok_rows + jnp.arange(tok_rows, dtype=jnp.int32)
    queries = rotate_rows(projected[:, :, 0, :], positions).astype(jnp.bfloat16)
    key_rows = rotate_rows(projected[:, :, 1, :], positions).astype(jnp.bfloat16)
    value_rows = projected[:, :, 2, :].astype(jnp.bfloat16)

    def position_of(global_row):
        return global_row

    attended = run_attention(queries, positions, key_rows, value_rows, position_of)
    head_terms = jnp.dot(
        attended.reshape(tok_rows, head_count * HEAD), attn_out, preferred_element_type=jnp.float32
    )
    attn_mix = lax.psum_scatter(
        head_terms.astype(jnp.bfloat16), "ch", scatter_dimension=1, tiled=True
    ).astype(jnp.float32)
    return (stream_wide + attn_mix).astype(jnp.bfloat16)


def rotation_tables(positions):
    half_size = HEAD // 2
    frequency = 10000.0 ** (-jnp.arange(half_size, dtype=F32) * 2.0 / HEAD)
    angles = positions.astype(F32)[:, None] * frequency[None, :]
    cosine, sine = jnp.cos(angles), jnp.sin(angles)
    return jnp.concatenate([cosine, cosine], axis=1), jnp.concatenate([-sine, sine], axis=1)


def shards(
    features,
    residual_in,
    short_filter,
    medium_filter,
    skip_gain,
    out_weight,
    norm_gain,
    attn_weight,
    attn_out,
):
    rows, _, channels = features.shape
    chips = lax.axis_size("ctx") // 2
    length = medium_filter.shape[0]
    chunk = rows // 2
    half = channels // 2
    ctx, ch = lax.axis_index("ctx"), lax.axis_index("ch")
    meta = jnp.stack([ch, ch ^ 1, ch ^ 2, ch ^ 3, ctx // 2, ctx % 2]).astype(jnp.int32)

    by_kind = jnp.transpose(features, (1, 0, 2))
    halo_rows = length + LEAD
    edge = jnp.concatenate(
        [by_kind[1, rows - halo_rows :], by_kind[2, rows - halo_rows :], by_kind[0, rows - LEAD :]], axis=0
    )
    count = lax.axis_size("ctx")
    halo = lax.ppermute(edge, "ctx", [(i, i + 1) for i in range(count - 1)])

    taps = jnp.repeat(short_filter, GROUP_SIZE, axis=2).reshape(-1, channels)
    base = jnp.pad(medium_filter.T[:, ::-1], ((0, 0), (1, length - 1)))
    skip = skip_gain.reshape(1, channels)
    starts = [rows - chunk, 0]
    if lax.axis_size("ch") != 4 or attn_weight.shape[1] != 3 * HEAD * chips:
        gated = [conv_chunk(by_kind, halo, start, chunk, taps, base, skip) for start in starts]
        return after_gating(
            jnp.concatenate(gated[::-1], axis=0), residual_in, out_weight, norm_gain, attn_weight, attn_out
        )

    gain = norm_gain.reshape(4, channels)
    cosine, sine = rotation_tables(ctx * rows + jnp.arange(rows, dtype=jnp.int32))

    first = jnp.stack([2 * (ch ^ 3), 2 * (ch ^ 1), 2 * (ch ^ 3) + 1, 2 * (ch ^ 2) + 1]).astype(jnp.int32)
    second = jnp.stack([2 * (ch ^ 1) + 1, 2 * (ch ^ 2), 2 * ch, 2 * ch + 1]).astype(jnp.int32)

    stream = {}
    for start in starts:
        gated = conv_chunk(by_kind, halo, start, chunk, taps, base, skip)
        to_x, to_y = column_products(gated, out_weight, first, (2, 2), half)
        from_x, from_y = swap_ch(to_x, 1), swap_ch(to_y, 2)
        along_x, along_y, kept = column_products(gated, out_weight, second, (1, 1, 2), half)
        along_x = (along_x.astype(F32) + from_y[:, :half].astype(F32)).astype(BF16)
        along_y = (along_y.astype(F32) + from_x[:, :half].astype(F32)).astype(BF16)
        late_x, late_y = swap_ch(along_x, 1), swap_ch(along_y, 2)
        hyena = kept.astype(F32) + jnp.concatenate(
            [
                from_x[:, half:].astype(F32) + late_y.astype(F32),
                from_y[:, half:].astype(F32) + late_x.astype(F32),
            ],
            axis=1,
        )
        stream[start] = (residual_in[start : start + chunk].astype(F32) + hyena).astype(BF16)

    own, other = {}, {}
    for start in starts:
        part = stream[start]
        near_x, near_y = swap_ch(part, 1), swap_ch(part, 2)
        diag_a = swap_ch(near_x[: chunk // 2], 2)
        diag_b = swap_ch(near_y[chunk // 2 :], 1)
        outs = project(
            meta,
            part,
            near_x,
            near_y,
            diag_a,
            diag_b,
            gain,
            cosine[start : start + chunk],
            sine[start : start + chunk],
            attn_weight,
            chips,
        )
        pieces = [outs[0]] + [rotate_chips(outs[d], d) for d in range(1, chips)]
        own[start] = jnp.stack(pieces)
        other[start] = swap_core(jnp.stack([piece[1:] for piece in pieces]))

    later, _ = lax.optimization_barrier((attn_out, stream[0]))
    half_rows = later.shape[0] // 2
    mine = lax.dynamic_slice_in_dim(later, (ctx % 2) * half_rows, half_rows, 0)
    near_w = jnp.stack(
        [
            swap_ch(lax.dynamic_slice_in_dim(mine, (ch ^ mask) * channels, channels, 1), mask)
            for mask in (1, 2, 3)
        ]
    )
    far_w = swap_core(near_w)
    own_w = lax.dynamic_slice_in_dim(attn_out, ch * channels, channels, 1)

    outs = attend(meta, [own[0], own[chunk]], [other[0], other[chunk]], chips)
    heads = jnp.stack([outs[0]] + [rotate_chips(outs[d], d) for d in range(1, chips)])
    near_x, near_y = swap_ch(heads, 1), swap_ch(heads, 2)
    diag_a = swap_ch(near_x[:, : rows // 2], 2)
    diag_b = swap_ch(near_y[:, rows // 2 :], 1)
    whole_stream = jnp.concatenate([stream[0], stream[chunk]], axis=0)
    return mix(meta, heads, near_x, near_y, diag_a, diag_b, whole_stream, own_w, near_w, far_w, chips)


def solution(mesh):
    in_specs = (
        P("ctx", None, "ch"),
        P("ctx", "ch"),
        P(None, None, "ch"),
        P(None, "ch"),
        P("ch"),
        P("ch", None),
        P(),
        P(None, "ch"),
        P("ch", None),
    )
    out_specs = P("ctx", "ch")
    return jax.shard_map(shards, mesh=mesh, in_specs=in_specs, out_specs=out_specs, check_vma=False)
```

```python
import functools

import jax
import jax.numpy as jnp
from jax import lax
from jax.experimental import pallas as pl
from jax.experimental.pallas import tpu as pltpu
from jax.sharding import PartitionSpec as P

HEAD = 128
GROUP_SIZE = 16
LANES = 128
LEAD = 16
norm_eps = 1e-05
MIB = 1024 * 1024
F32 = jnp.float32
BF16 = jnp.bfloat16


def swap_ch(value, mask):
    count = lax.axis_size("ch")
    return lax.ppermute(value, "ch", [(i, i ^ mask) for i in range(count)])


def swap_core(value):
    count = lax.axis_size("ctx")
    return lax.ppermute(value, "ctx", [(i, i ^ 1) for i in range(count)])


def rotate_chips(value, distance):
    count = lax.axis_size("ctx")
    return lax.ppermute(value, "ctx", [(i, (i + 2 * distance) % count) for i in range(count)])


def filter_tile(first_row, tile, short_ref, medium_ref, skip_ref, halo_ref, rows_ref, wide, product, table, store):
    taps, groups_all = short_ref.shape[1:]
    groups, length = medium_ref.shape
    span = wide.shape[1]
    halo_rows = length + LEAD
    count = span - halo_rows

    for kind in range(3):
        if first_row == 0:
            wide[kind, :halo_rows] = halo_ref[kind].astype(F32)
            wide[kind, halo_rows:] = rows_ref[kind].astype(F32)
        else:
            wide[kind] = rows_ref[kind, first_row - halo_rows : first_row + count].astype(F32)

    group_row = lax.broadcasted_iota(jnp.int32, (groups_all, LANES), 0)
    group_col = lax.broadcasted_iota(jnp.int32, (groups_all, LANES), 1) // GROUP_SIZE + tile * groups
    chosen = jnp.where(group_row == group_col, 1.0, 0.0).astype(F32)
    weights = [
        jnp.dot(short_ref[kind], chosen, precision=lax.Precision.HIGHEST, preferred_element_type=F32)
        for kind in range(3)
    ]

    tap_row = lax.broadcasted_iota(jnp.int32, (length, 2 * length), 0)
    place = lax.broadcasted_iota(jnp.int32, (length, 2 * length), 1)
    turned = jnp.where(tap_row + place == length, 1.0, 0.0).astype(BF16)
    base = jnp.dot(medium_ref[...].astype(BF16), turned, preferred_element_type=F32)
    for group in range(groups):
        spread = jnp.broadcast_to(base[group : group + 1, :], (length, 2 * length))
        rolled = pltpu.roll(spread, 0, 1, stride=1, stride_axis=0)
        table[group * length : (group + 1) * length, :] = rolled.astype(BF16)

    def featured(kind, start):
        total = weights[kind][0:1, :] * wide[kind, start : start + length, :]
        for tap in range(1, taps):
            total = total + weights[kind][tap : tap + 1, :] * wide[kind, start - tap : start - tap + length, :]
        return total

    for block in range(count // length + 1):
        start = LEAD + block * length
        product[block * length : (block + 1) * length, :] = (
            featured(1, start) * featured(2, start)
        ).astype(BF16)

    group_of = lax.broadcasted_iota(jnp.int32, (length, 2 * LANES), 1) % LANES // GROUP_SIZE
    for pair in range(count // (2 * length)):
        begin = pair * 2 * length
        window = jnp.concatenate(
            [
                product[begin : begin + 2 * length, :],
                product[begin + length : begin + 3 * length, :],
            ],
            axis=1,
        )
        spread = jnp.dot(table[...], window, preferred_element_type=F32)
        mixed = spread[:length]
        for group in range(1, groups):
            mixed = jnp.where(group_of == group, spread[group * length : (group + 1) * length], mixed)
        for part in range(2):
            row = begin + part * length
            direct = skip_ref[...] * product[row + length : row + 2 * length, :].astype(F32)
            gate = featured(0, halo_rows + row)
            store(row, (gate * (mixed[:, part * LANES : (part + 1) * LANES] + direct)).astype(BF16))


def filter_call(body, features, halo, first_row, count, short_filter, medium_rows, skip, more, scalars):
    kinds, rows, channels = features.shape
    length = medium_rows.shape[1]
    groups = LANES // GROUP_SIZE
    extra, out_specs, out_shape, scratch, limit, name = more
    specs = [
        pl.BlockSpec(short_filter.shape, lambda i, *_: (0, 0, 0)),
        pl.BlockSpec((groups, length), lambda i, *_: (i, 0)),
        pl.BlockSpec((1, LANES), lambda i, *_: (0, i)),
    ]
    operands = [short_filter, medium_rows, skip]
    if first_row == 0:
        specs.append(pl.BlockSpec((kinds, length + LEAD, LANES), lambda i, *_: (0, 0, i)))
        operands.append(halo)
        specs.append(pl.BlockSpec((kinds, count, LANES), lambda i, *_: (0, 0, i)))
    else:
        specs.append(pl.BlockSpec((kinds, rows, LANES), lambda i, *_: (0, 0, i)))
    operands.append(features)
    return pl.pallas_call(
        functools.partial(body, first_row),
        grid_spec=pltpu.PrefetchScalarGridSpec(
            num_scalar_prefetch=1,
            grid=(channels // LANES,),
            in_specs=specs + [pl.BlockSpec(memory_space=pltpu.HBM)] * len(extra),
            out_specs=out_specs,
            scratch_shapes=[
                pltpu.VMEM((kinds, length + LEAD + count, LANES), F32),
                pltpu.VMEM((length + count, LANES), BF16),
                pltpu.VMEM((groups * length, 2 * length), BF16),
            ]
            + scratch,
        ),
        out_shape=out_shape,
        compiler_params=pltpu.CompilerParams(vmem_limit_bytes=limit * MIB),
        name=name,
    )(scalars, *operands, *extra)


def split_refs(first_row, refs):
    head, rest = refs[:3], refs[3:]
    halo_ref, rest = (rest[0], rest[1:]) if first_row == 0 else (None, rest)
    return head, halo_ref, rest[0], rest[1:]


def gated_kernel(first_row, scalars, *refs):
    head, halo_ref, rows_ref, (out_ref, wide, product, table) = split_refs(first_row, refs)

    def store(row, value):
        out_ref[row : row + value.shape[0], :] = value

    filter_tile(first_row, pl.program_id(0), *head, halo_ref, rows_ref, wide, product, table, store)


def gated_chunk(features, halo, first_row, count, short_filter, medium_rows, skip, scalars):
    channels = features.shape[2]
    more = (
        [],
        pl.BlockSpec((count, LANES), lambda i, *_: (0, i)),
        jax.ShapeDtypeStruct((count, channels), BF16),
        [],
        24,
        "hyena_filters",
    )
    return filter_call(
        gated_kernel, features, halo, first_row, count, short_filter, medium_rows, skip, more, scalars
    )


def terms_kernel(first_row, order_ref, *refs):
    head, halo_ref, rows_ref, rest = split_refs(first_row, refs)
    weight, to_x, to_y, along_x, along_y, kept, wide, product, table, gated, held, sems = rest
    tile = pl.program_id(0)
    pieces, _, width = held.shape

    def fetch(piece):
        columns = pl.ds(pl.multiple_of(order_ref[piece] * width, width), width)
        return pltpu.make_async_copy(weight.at[:, columns], held.at[piece], sems.at[piece])

    @pl.when(tile == 0)
    def _():
        for piece in range(pieces):
            fetch(piece).start()

    lanes = pl.ds(pl.multiple_of(tile * LANES, LANES), LANES)

    def store(row, value):
        gated[row : row + value.shape[0], lanes] = value

    filter_tile(first_row, tile, *head, halo_ref, rows_ref, wide, product, table, store)

    @pl.when(tile == pl.num_programs(0) - 1)
    def _():
        places = [(to_x, 0), (to_x, 1), (to_y, 0), (to_y, 1), (along_x, 0), (along_y, 0), (kept, 0), (kept, 1)]
        for piece, (out, part) in enumerate(places):
            fetch(piece).wait()
            term = jnp.dot(gated[...], held[piece], preferred_element_type=F32)
            out[:, part * width : (part + 1) * width] = term.astype(BF16)


def terms_chunk(features, halo, first_row, count, short_filter, medium_rows, skip, order, out_weight):
    depth, columns = out_weight.shape
    width = columns // 8
    widths = [2 * width, 2 * width, width, width, 2 * width]
    more = (
        [out_weight],
        [pl.BlockSpec((count, w), lambda i, *_: (0, 0)) for w in widths],
        [jax.ShapeDtypeStruct((count, w), BF16) for w in widths],
        [
            pltpu.VMEM((count, depth), BF16),
            pltpu.VMEM((8, depth, width), BF16),
            pltpu.SemaphoreType.DMA((8,)),
        ],
        32,
        "hyena_terms",
    )
    return filter_call(
        terms_kernel, features, halo, first_row, count, short_filter, medium_rows, skip, more, order
    )


def forward_kernel(along_x, along_y, from_x, from_y, out_x, out_y):
    out_x[...] = (along_x[...].astype(F32) + from_y[...].astype(F32)).astype(BF16)
    out_y[...] = (along_y[...].astype(F32) + from_x[...].astype(F32)).astype(BF16)


def add_forwarded(along_x, along_y, from_x, from_y):
    shape = along_x.shape
    spec = pl.BlockSpec(shape, lambda i: (0, 0))
    return pl.pallas_call(
        forward_kernel,
        grid=(1,),
        in_specs=[spec] * 4,
        out_specs=[spec] * 2,
        out_shape=[jax.ShapeDtypeStruct(shape, BF16)] * 2,
        name="add_forwarded",
    )(along_x, along_y, from_x, from_y)


def stream_kernel(kept, from_x, from_y, late_x, late_y, residual, out):
    half = late_x.shape[1]
    wide = lambda ref: ref[...].astype(F32)
    left = kept[:, :half].astype(F32) + wide(from_x) + wide(late_y)
    right = kept[:, half:].astype(F32) + wide(from_y) + wide(late_x)
    out[:, :half] = (residual[:, :half].astype(F32) + left).astype(BF16)
    out[:, half:] = (residual[:, half:].astype(F32) + right).astype(BF16)


def add_stream(kept, from_x, from_y, late_x, late_y, residual, start):
    rows, channels = kept.shape
    half = channels // 2
    full = pl.BlockSpec((rows, channels), lambda i: (0, 0))
    second = pl.BlockSpec((rows, half), lambda i: (0, 1))
    late = pl.BlockSpec((rows, half), lambda i: (0, 0))
    return pl.pallas_call(
        stream_kernel,
        grid=(1,),
        in_specs=[full, second, second, late, late, pl.BlockSpec((rows, channels), lambda i: (start // rows, 0))],
        out_specs=full,
        out_shape=jax.ShapeDtypeStruct((rows, channels), BF16),
        name="add_stream",
    )(kept, from_x, from_y, late_x, late_y, residual)


def fetch_rows(meta_ref, weight, held, sems, first, blocks):
    depth = held.shape[1]
    copies = []
    for index in range(blocks):
        for part in range(2):
            row = pl.multiple_of(meta_ref[first + index] * 2 * depth + part * depth, depth)
            slot = 2 * index + part
            copies.append(pltpu.make_async_copy(weight.at[pl.ds(row, depth), :], held.at[slot], sems.at[slot]))
    return copies


def near_kernel(meta_ref, own, from_x, from_y, gain, weight, total, square, held, sems):
    depth = held.shape[1]
    copies = fetch_rows(meta_ref, weight, held, sems, 0, 3)
    for copy in copies:
        copy.start()
    squares = jnp.zeros(square.shape, F32)
    for index, block in enumerate([own, from_x, from_y]):
        for part in range(2):
            wide = block[:, part * depth : (part + 1) * depth].astype(F32)
            squares = squares + jnp.sum(wide * wide, axis=1, keepdims=True)
            factor = gain[pl.ds(meta_ref[index], 1), part * depth : (part + 1) * depth]
            copies[2 * index + part].wait()
            term = jnp.dot((wide * factor).astype(BF16), held[2 * index + part], preferred_element_type=F32)
            if index + part == 0:
                total[...] = term
            else:
                total[...] += term
    square[...] = squares


def project_near(meta, own, from_x, from_y, gain, weight):
    rows, channels = own.shape
    width = weight.shape[1]
    full = lambda shape: pl.BlockSpec(shape, lambda i, meta: (0,) * len(shape))
    return pl.pallas_call(
        near_kernel,
        grid_spec=pltpu.PrefetchScalarGridSpec(
            num_scalar_prefetch=1,
            grid=(1,),
            in_specs=[full(own.shape)] * 3 + [full(gain.shape), pl.BlockSpec(memory_space=pltpu.HBM)],
            out_specs=[full((rows, width)), full((rows, LANES))],
            scratch_shapes=[
                pltpu.VMEM((6, channels // 2, width), BF16),
                pltpu.SemaphoreType.DMA((6,)),
            ],
        ),
        out_shape=[jax.ShapeDtypeStruct((rows, width), F32), jax.ShapeDtypeStruct((rows, LANES), F32)],
        compiler_params=pltpu.CompilerParams(vmem_limit_bytes=32 * MIB),
        name="qkv_near",
    )(meta, own, from_x, from_y, gain, weight)


def far_kernel(chips, channels, meta_ref, diag_a, diag_b, near, square, gain, cosine, sine, weight, *rest):
    outs, (total, held, sems) = rest[:chips], rest[chips:]
    depth = held.shape[1]
    copies = fetch_rows(meta_ref, weight, held, sems, 3, 1)
    for copy in copies:
        copy.start()
    squares = square[...]
    for part in range(2):
        columns = slice(part * depth, (part + 1) * depth)
        wide = jnp.concatenate([diag_a[:, columns], diag_b[:, columns]], axis=0).astype(F32)
        squares = squares + jnp.sum(wide * wide, axis=1, keepdims=True)
        factor = gain[pl.ds(meta_ref[3], 1), columns]
        copies[part].wait()
        term = jnp.dot((wide * factor).astype(BF16), held[part], preferred_element_type=F32)
        if part == 0:
            total[...] = near[...] + term
        else:
            total[...] += term
    inverse = lax.rsqrt(squares / (4 * channels) + norm_eps)
    for distance, out in enumerate(outs):
        head = lax.rem(meta_ref[4] + distance, chips)
        for kind in range(3):
            column = pl.multiple_of((head * 3 + kind) * HEAD, HEAD)
            part = total[:, pl.ds(column, HEAD)] * inverse
            if kind < 2:
                part = part * cosine[...] + pltpu.roll(part, HEAD // 2, 1) * sine[...]
            out[kind] = part.astype(BF16)


def project_far(meta, diag_a, diag_b, near, square, gain, cosine, sine, weight, chips):
    rows, width = near.shape
    channels = diag_a.shape[1]
    full = lambda shape: pl.BlockSpec(shape, lambda i, meta: (0,) * len(shape))
    return pl.pallas_call(
        functools.partial(far_kernel, chips, channels),
        grid_spec=pltpu.PrefetchScalarGridSpec(
            num_scalar_prefetch=1,
            grid=(1,),
            in_specs=[full(x.shape) for x in (diag_a, diag_b, near, square, gain, cosine, sine)]
            + [pl.BlockSpec(memory_space=pltpu.HBM)],
            out_specs=[full((3, rows, HEAD))] * chips,
            scratch_shapes=[
                pltpu.VMEM((rows, width), F32),
                pltpu.VMEM((2, channels // 2, width), BF16),
                pltpu.SemaphoreType.DMA((2,)),
            ],
        ),
        out_shape=[jax.ShapeDtypeStruct((3, rows, HEAD), BF16)] * chips,
        compiler_params=pltpu.CompilerParams(vmem_limit_bytes=32 * MIB),
        name="qkv_far",
    )(meta, diag_a, diag_b, near, square, gain, cosine, sine, weight)


def attention_kernel(chips, chunks, meta_ref, *refs):
    own, other, outs = refs[:chunks], refs[chunks : 2 * chunks], refs[2 * chunks :]
    chip, core = meta_ref[4], meta_ref[5]
    scale = 1.0 / HEAD**0.5 * 1.4426950408889634

    def rows(refs_in, distance, kind):
        return jnp.concatenate([ref[distance, kind] for ref in refs_in], axis=0)

    def scores_of(queries, keys):
        return lax.dot_general(queries, keys, (((1,), (1,)), ((), ())), preferred_element_type=F32) * scale

    def update(state, scores, values):
        top, total, acc = state
        new_top = jnp.maximum(top, jnp.max(scores, axis=1, keepdims=True))
        weights = jnp.exp2(scores - new_top)
        shrink = jnp.exp2(top - new_top)
        total = total * shrink + jnp.sum(weights, axis=1, keepdims=True)
        acc = acc * shrink + jnp.dot(weights.astype(BF16), values, preferred_element_type=F32)
        return new_top, total, acc

    for distance, out in enumerate(outs):
        place = lax.rem(chip + distance, chips)
        here = lax.rem(chip - place + chips, chips)
        queries = rows(own, here, 0)
        count = queries.shape[0]
        scores = scores_of(queries, rows(own, here, 1))
        row = lax.broadcasted_iota(jnp.int32, scores.shape, 0)
        column = lax.broadcasted_iota(jnp.int32, scores.shape, 1)
        scores = jnp.where(column <= row, scores, -1e30)
        state = (
            jnp.full((count, 1), -1e30, F32),
            jnp.zeros((count, 1), F32),
            jnp.zeros((count, HEAD), F32),
        )
        state = update(state, scores, rows(own, here, 2))

        def own_block(index, state):
            there = lax.rem(chip - index + chips, chips)
            return update(state, scores_of(queries, rows(own, there, 1)), rows(own, there, 2))

        def other_block(index, state):
            there = lax.rem(chip - index + chips, chips)
            return update(state, scores_of(queries, rows(other, there, 0)), rows(other, there, 1))

        state = lax.fori_loop(0, place, own_block, state)
        state = lax.fori_loop(0, place + core, other_block, state)
        out[...] = (state[2] / state[1]).astype(BF16)


def attend(meta, own, other, chips):
    chunks = len(own)
    count = sum(piece.shape[2] for piece in own)
    whole = lambda shape: pl.BlockSpec(shape, lambda i, meta: (0,) * len(shape))
    return pl.pallas_call(
        functools.partial(attention_kernel, chips, chunks),
        grid_spec=pltpu.PrefetchScalarGridSpec(
            num_scalar_prefetch=1,
            grid=(1,),
            in_specs=[whole(piece.shape) for piece in own + other],
            out_specs=[whole((count, HEAD))] * chips,
        ),
        out_shape=[jax.ShapeDtypeStruct((count, HEAD), BF16)] * chips,
        compiler_params=pltpu.CompilerParams(vmem_limit_bytes=40 * MIB),
        name="attention",
    )(meta, *own, *other)


def mix_kernel(chips, meta_ref, own, from_x, from_y, diag_a, diag_b, stream, own_w, near_w, far_w, out, ordered):
    chip, core = meta_ref[4], meta_ref[5]
    rows = stream.shape[0]
    half_rows = near_w.shape[1]

    @pl.when(pl.program_id(0) == 0)
    def _():
        for distance in range(chips):
            head = lax.rem(chip - distance + chips, chips)
            column = pl.ds(pl.multiple_of(head * HEAD, HEAD), HEAD)
            ordered[0, :, column] = own[distance]
            ordered[1, :, column] = from_x[distance]
            ordered[2, :, column] = from_y[distance]
            ordered[3, : rows // 2, column] = diag_a[distance]
            ordered[3, rows // 2 :, column] = diag_b[distance]

    total = stream[...].astype(F32)
    total = total + jnp.dot(ordered[0], own_w[...], preferred_element_type=F32)
    near = pl.ds(pl.multiple_of(core * half_rows, half_rows), half_rows)
    far = pl.ds(pl.multiple_of((1 - core) * half_rows, half_rows), half_rows)
    for index in range(3):
        total = total + jnp.dot(ordered[index + 1, :, near], near_w[index], preferred_element_type=F32)
        total = total + jnp.dot(ordered[index + 1, :, far], far_w[index], preferred_element_type=F32)
    out[...] = total.astype(BF16)


def mix(meta, own, from_x, from_y, diag_a, diag_b, stream, own_w, near_w, far_w, chips):
    rows, channels = stream.shape
    width = 256
    full = lambda shape: pl.BlockSpec(shape, lambda i, meta: (0,) * len(shape))
    return pl.pallas_call(
        functools.partial(mix_kernel, chips),
        grid_spec=pltpu.PrefetchScalarGridSpec(
            num_scalar_prefetch=1,
            grid=(channels // width,),
            in_specs=[
                full(own.shape),
                full(from_x.shape),
                full(from_y.shape),
                full(diag_a.shape),
                full(diag_b.shape),
                pl.BlockSpec((rows, width), lambda i, meta: (0, i)),
                pl.BlockSpec((own_w.shape[0], width), lambda i, meta: (0, i)),
                pl.BlockSpec((3, near_w.shape[1], width), lambda i, meta: (0, 0, i)),
                pl.BlockSpec((3, far_w.shape[1], width), lambda i, meta: (0, 0, i)),
            ],
            out_specs=pl.BlockSpec((rows, width), lambda i, meta: (0, i)),
            scratch_shapes=[pltpu.VMEM((4, rows, chips * HEAD), BF16)],
        ),
        out_shape=jax.ShapeDtypeStruct((rows, channels), BF16),
        compiler_params=pltpu.CompilerParams(vmem_limit_bytes=40 * MIB),
        name="attention_mix",
    )(meta, own, from_x, from_y, diag_a, diag_b, stream, own_w, near_w, far_w)


def rotate_rows(block, positions):
    half_size = block.shape[-1] // 2
    frequency = 10000.0 ** (-jnp.arange(half_size, dtype=jnp.float32) * 2.0 / block.shape[-1])
    angles = positions.astype(jnp.float32)[:, None] * frequency[None, :]
    cosine = jnp.cos(angles)[:, None, :]
    sine_part = jnp.sin(angles)[:, None, :]
    first_half = block[..., :half_size]
    second_half = block[..., half_size:]
    return jnp.concatenate(
        [
            first_half * cosine - second_half * sine_part,
            second_half * cosine + first_half * sine_part,
        ],
        axis=-1,
    )


def run_attention(queries, query_pos, key_rows, value_rows, position_of):
    head_count = queries.shape[1]
    row_count = queries.shape[0]
    head_size = queries.shape[2]
    scale_factor = 1.0 / head_size**0.5
    last_query = jnp.max(query_pos)
    initial = (
        jnp.zeros((head_count, row_count, head_size), jnp.float32),
        jnp.full((head_count, row_count), -1e30, jnp.float32),
        jnp.zeros((head_count, row_count), jnp.float32),
    )
    piece_keys = lax.all_gather(key_rows, "ctx", axis=0, tiled=True)
    piece_values = lax.all_gather(value_rows, "ctx", axis=0, tiled=True)
    piece_rows = piece_keys.shape[0]
    block_rows = 512

    def one_block(state_in, block_index):
        first_block = block_index * block_rows
        key_block = lax.dynamic_slice_in_dim(piece_keys, first_block, block_rows, 0)
        value_block = lax.dynamic_slice_in_dim(piece_values, first_block, block_rows, 0)
        key_pos = position_of(first_block + jnp.arange(block_rows))

        def update(state_old):
            acc_sum, run_max, run_total = state_old
            scores = (
                jnp.einsum("thd,khd->htk", queries, key_block, preferred_element_type=jnp.float32)
                * scale_factor
            )
            causal = (key_pos[None, :] <= query_pos[:, None])[None]
            block_max = jnp.max(jnp.where(causal, scores, -1e30), axis=-1)
            new_max = jnp.maximum(run_max, block_max)
            weights = jnp.where(causal, jnp.exp(scores - new_max[..., None]), 0.0)
            correction = jnp.exp(run_max - new_max)
            new_total = run_total * correction + jnp.sum(weights, axis=-1)
            update_sum = jnp.einsum(
                "htk,khd->htd",
                weights.astype(jnp.bfloat16),
                value_block,
                preferred_element_type=jnp.float32,
            )
            return (acc_sum * correction[..., None] + update_sum, new_max, new_total)

        def unchanged(state_old):
            return state_old

        state_out = lax.cond(jnp.min(key_pos) > last_query, unchanged, update, state_in)
        return (state_out, None)

    state_end, unused = lax.scan(one_block, initial, jnp.arange(piece_rows // block_rows))
    acc_sum, run_max, run_total = state_end
    output = acc_sum / run_total[..., None]
    return jnp.transpose(output, (1, 0, 2)).astype(jnp.bfloat16)


def after_gating(gated, residual_in, out_weight, norm_gain, attn_weight, attn_out):
    tok_rows, chan_count = gated.shape
    hyena_terms = jnp.dot(gated, out_weight, preferred_element_type=jnp.float32)
    hyena_out = lax.psum_scatter(
        hyena_terms.astype(jnp.bfloat16), "ch", scatter_dimension=1, tiled=True
    ).astype(jnp.float32)
    stream = (residual_in.astype(jnp.float32) + hyena_out).astype(jnp.bfloat16)
    stream_wide = stream.astype(jnp.float32)
    full_width = chan_count * lax.axis_size("ch")
    head_cols = attn_weight.shape[1]
    square_total = lax.psum(jnp.sum(stream_wide * stream_wide, axis=1), "ch")
    inverse = lax.rsqrt(square_total / full_width + norm_eps)
    gain_part = lax.dynamic_slice_in_dim(norm_gain, lax.axis_index("ch") * chan_count, chan_count)
    normed = (stream_wide * inverse[:, None] * gain_part[None, :]).astype(jnp.bfloat16)
    projected = jnp.dot(
        lax.all_gather(normed, "ch", axis=1, tiled=True),
        attn_weight,
        preferred_element_type=jnp.float32,
    )
    head_count = head_cols // (3 * HEAD)
    projected = projected.reshape(tok_rows, head_count, 3, HEAD)
    ctx_index = lax.axis_index("ctx")
    positions = ctx_index * tok_rows + jnp.arange(tok_rows, dtype=jnp.int32)
    queries = rotate_rows(projected[:, :, 0, :], positions).astype(jnp.bfloat16)
    key_rows = rotate_rows(projected[:, :, 1, :], positions).astype(jnp.bfloat16)
    value_rows = projected[:, :, 2, :].astype(jnp.bfloat16)

    def position_of(global_row):
        return global_row

    attended = run_attention(queries, positions, key_rows, value_rows, position_of)
    head_terms = jnp.dot(
        attended.reshape(tok_rows, head_count * HEAD), attn_out, preferred_element_type=jnp.float32
    )
    attn_mix = lax.psum_scatter(
        head_terms.astype(jnp.bfloat16), "ch", scatter_dimension=1, tiled=True
    ).astype(jnp.float32)
    return (stream_wide + attn_mix).astype(jnp.bfloat16)


def rotation_tables(positions):
    half_size = HEAD // 2
    frequency = 10000.0 ** (-jnp.arange(half_size, dtype=F32) * 2.0 / HEAD)
    angles = positions.astype(F32)[:, None] * frequency[None, :]
    cosine, sine = jnp.cos(angles), jnp.sin(angles)
    return jnp.concatenate([cosine, cosine], axis=1), jnp.concatenate([-sine, sine], axis=1)


def shards(
    features,
    residual_in,
    short_filter,
    medium_filter,
    skip_gain,
    out_weight,
    norm_gain,
    attn_weight,
    attn_out,
):
    rows, _, channels = features.shape
    chips = lax.axis_size("ctx") // 2
    length = medium_filter.shape[0]
    chunk = rows // 2
    ctx, ch = lax.axis_index("ctx"), lax.axis_index("ch")
    meta = jnp.stack([ch, ch ^ 1, ch ^ 2, ch ^ 3, ctx // 2, ctx % 2]).astype(jnp.int32)

    by_kind = jnp.transpose(features, (1, 0, 2))
    count = lax.axis_size("ctx")
    halo = lax.ppermute(by_kind[:, rows - length - LEAD :], "ctx", [(i, i + 1) for i in range(count - 1)])
    medium_rows = medium_filter.T
    skip = skip_gain.reshape(1, channels)

    starts = [rows - chunk, 0]
    if lax.axis_size("ch") != 4 or attn_weight.shape[1] != 3 * HEAD * chips:
        gated = [
            gated_chunk(by_kind, halo, start, chunk, short_filter, medium_rows, skip, meta) for start in starts
        ]
        return after_gating(
            jnp.concatenate(gated[::-1], axis=0), residual_in, out_weight, norm_gain, attn_weight, attn_out
        )

    gain = norm_gain.reshape(4, channels)
    cosine, sine = rotation_tables(ctx * rows + jnp.arange(rows, dtype=jnp.int32))
    near_x, near_y, across = ch ^ 1, ch ^ 2, ch ^ 3
    order = [2 * across, 2 * near_x, 2 * across + 1, 2 * near_y + 1, 2 * near_x + 1, 2 * near_y, 2 * ch, 2 * ch + 1]
    order = jnp.stack(order).astype(jnp.int32)

    stream = {}
    for start in starts:
        to_x, to_y, along_x, along_y, kept = terms_chunk(
            by_kind, halo, start, chunk, short_filter, medium_rows, skip, order, out_weight
        )
        from_x, from_y = swap_ch(to_x, 1), swap_ch(to_y, 2)
        along_x, along_y = add_forwarded(along_x, along_y, from_x, from_y)
        late_x, late_y = swap_ch(along_x, 1), swap_ch(along_y, 2)
        stream[start] = add_stream(kept, from_x, from_y, late_x, late_y, residual_in, start)

    own, other = {}, {}
    for start in starts:
        part = stream[start]
        near_x, near_y = swap_ch(part, 1), swap_ch(part, 2)
        diag_a = swap_ch(near_x[: chunk // 2], 2)
        diag_b = swap_ch(near_y[chunk // 2 :], 1)
        near, square = project_near(meta, part, near_x, near_y, gain, attn_weight)
        turn = slice(start, start + chunk)
        outs = project_far(meta, diag_a, diag_b, near, square, gain, cosine[turn], sine[turn], attn_weight, chips)
        pieces = [outs[0]] + [rotate_chips(outs[d], d) for d in range(1, chips)]
        own[start] = jnp.stack(pieces)
        other[start] = swap_core(jnp.stack([piece[1:] for piece in pieces]))

    later, _ = lax.optimization_barrier((attn_out, stream[0]))
    half_rows = later.shape[0] // 2
    mine = lax.dynamic_slice_in_dim(later, (ctx % 2) * half_rows, half_rows, 0)
    near_w = jnp.stack(
        [
            swap_ch(lax.dynamic_slice_in_dim(mine, (ch ^ mask) * channels, channels, 1), mask)
            for mask in (1, 2, 3)
        ]
    )
    far_w = swap_core(near_w)
    own_w = lax.dynamic_slice_in_dim(attn_out, ch * channels, channels, 1)

    outs = attend(meta, [own[0], own[chunk]], [other[0], other[chunk]], chips)
    heads = jnp.stack([outs[0]] + [rotate_chips(outs[d], d) for d in range(1, chips)])
    near_x, near_y = swap_ch(heads, 1), swap_ch(heads, 2)
    diag_a = swap_ch(near_x[:, : rows // 2], 2)
    diag_b = swap_ch(near_y[:, rows // 2 :], 1)
    whole_stream = jnp.concatenate([stream[0], stream[chunk]], axis=0)
    return mix(meta, heads, near_x, near_y, diag_a, diag_b, whole_stream, own_w, near_w, far_w, chips)


def solution(mesh):
    in_specs = (
        P("ctx", None, "ch"),
        P("ctx", "ch"),
        P(None, None, "ch"),
        P(None, "ch"),
        P("ch"),
        P("ch", None),
        P(),
        P(None, "ch"),
        P("ch", None),
    )
    out_specs = P("ctx", "ch")
    return jax.shard_map(shards, mesh=mesh, in_specs=in_specs, out_specs=out_specs, check_vma=False)
```

```python
import functools

import jax
import jax.numpy as jnp
from jax import lax
from jax.experimental import pallas as pl
from jax.experimental.pallas import tpu as pltpu
from jax.sharding import PartitionSpec as P

HEAD = 128
GROUP_SIZE = 16
LANES = 128
LEAD = 16
norm_eps = 1e-05
SCORE_SCALE = 1.4426950408889634 / HEAD**0.5
MIB = 1024 * 1024
MOST_VMEM = 60 * MIB
F32 = jnp.float32
BF16 = jnp.bfloat16


def swap_ch(value, mask):
    count = lax.axis_size("ch")
    return lax.ppermute(value, "ch", [(i, i ^ mask) for i in range(count)])


def swap_core(value):
    count = lax.axis_size("ctx")
    return lax.ppermute(value, "ctx", [(i, i ^ 1) for i in range(count)])


def rotate_chips(value, distance):
    count = lax.axis_size("ctx")
    return lax.ppermute(value, "ctx", [(i, (i + 2 * distance) % count) for i in range(count)])


def filter_tile(first_row, tile, short_ref, medium_ref, skip_ref, halo_ref, rows_ref, wide, product, table, store):
    taps, groups_all = short_ref.shape[1:]
    groups, length = medium_ref.shape
    span = wide.shape[1]
    halo_rows = length + LEAD
    count = span - halo_rows

    for kind in range(3):
        if first_row == 0:
            wide[kind, :halo_rows] = halo_ref[kind].astype(F32)
            wide[kind, halo_rows:] = rows_ref[kind].astype(F32)
        else:
            wide[kind] = rows_ref[kind, first_row - halo_rows : first_row + count].astype(F32)

    group_row = lax.broadcasted_iota(jnp.int32, (groups_all, LANES), 0)
    group_col = lax.broadcasted_iota(jnp.int32, (groups_all, LANES), 1) // GROUP_SIZE + tile * groups
    chosen = jnp.where(group_row == group_col, 1.0, 0.0).astype(F32)
    weights = [
        jnp.dot(short_ref[kind], chosen, precision=lax.Precision.HIGHEST, preferred_element_type=F32)
        for kind in range(3)
    ]

    tap_row = lax.broadcasted_iota(jnp.int32, (length, 2 * length), 0)
    place = lax.broadcasted_iota(jnp.int32, (length, 2 * length), 1)
    turned = jnp.where(tap_row + place == length, 1.0, 0.0).astype(BF16)
    base = jnp.dot(medium_ref[...].astype(BF16), turned, preferred_element_type=F32)
    for group in range(groups):
        spread = jnp.broadcast_to(base[group : group + 1, :], (length, 2 * length))
        rolled = pltpu.roll(spread, 0, 1, stride=1, stride_axis=0)
        table[group * length : (group + 1) * length, :] = rolled.astype(BF16)

    def featured(kind, start):
        total = weights[kind][0:1, :] * wide[kind, start : start + length, :]
        for tap in range(1, taps):
            total = total + weights[kind][tap : tap + 1, :] * wide[kind, start - tap : start - tap + length, :]
        return total

    for block in range(count // length + 1):
        start = LEAD + block * length
        product[block * length : (block + 1) * length, :] = (
            featured(1, start) * featured(2, start)
        ).astype(BF16)

    group_of = lax.broadcasted_iota(jnp.int32, (length, 2 * LANES), 1) % LANES // GROUP_SIZE
    for pair in range(count // (2 * length)):
        begin = pair * 2 * length
        window = jnp.concatenate(
            [
                product[begin : begin + 2 * length, :],
                product[begin + length : begin + 3 * length, :],
            ],
            axis=1,
        )
        spread = jnp.dot(table[...], window, preferred_element_type=F32)
        mixed = spread[:length]
        for group in range(1, groups):
            mixed = jnp.where(group_of == group, spread[group * length : (group + 1) * length], mixed)
        for part in range(2):
            row = begin + part * length
            direct = skip_ref[...] * product[row + length : row + 2 * length, :].astype(F32)
            gate = featured(0, halo_rows + row)
            store(row, (gate * (mixed[:, part * LANES : (part + 1) * LANES] + direct)).astype(BF16))


def filter_call(body, features, halo, first_row, count, short_filter, medium_rows, skip, more, scalars):
    kinds, rows, channels = features.shape
    length = medium_rows.shape[1]
    groups = LANES // GROUP_SIZE
    extra, out_specs, out_shape, scratch, name = more
    specs = [
        pl.BlockSpec(short_filter.shape, lambda i, *_: (0, 0, 0)),
        pl.BlockSpec((groups, length), lambda i, *_: (i, 0)),
        pl.BlockSpec((1, LANES), lambda i, *_: (0, i)),
    ]
    operands = [short_filter, medium_rows, skip]
    if first_row == 0:
        specs.append(pl.BlockSpec((kinds, length + LEAD, LANES), lambda i, *_: (0, 0, i)))
        operands.append(halo)
        specs.append(pl.BlockSpec((kinds, count, LANES), lambda i, *_: (0, 0, i)))
    else:
        specs.append(pl.BlockSpec((kinds, rows, LANES), lambda i, *_: (0, 0, i)))
    operands.append(features)
    return pl.pallas_call(
        functools.partial(body, first_row),
        grid_spec=pltpu.PrefetchScalarGridSpec(
            num_scalar_prefetch=1,
            grid=(channels // LANES,),
            in_specs=specs + [pl.BlockSpec(memory_space=pltpu.HBM)] * len(extra),
            out_specs=out_specs,
            scratch_shapes=[
                pltpu.VMEM((kinds, length + LEAD + count, LANES), F32),
                pltpu.VMEM((length + count, LANES), BF16),
                pltpu.VMEM((groups * length, 2 * length), BF16),
            ]
            + scratch,
        ),
        out_shape=out_shape,
        compiler_params=pltpu.CompilerParams(vmem_limit_bytes=MOST_VMEM),
        name=name,
    )(scalars, *operands, *extra)


def split_refs(first_row, refs):
    head, rest = refs[:3], refs[3:]
    halo_ref, rest = (rest[0], rest[1:]) if first_row == 0 else (None, rest)
    return head, halo_ref, rest[0], rest[1:]


def gated_kernel(first_row, scalars, *refs):
    head, halo_ref, rows_ref, (out_ref, wide, product, table) = split_refs(first_row, refs)

    def store(row, value):
        out_ref[row : row + value.shape[0], :] = value

    filter_tile(first_row, pl.program_id(0), *head, halo_ref, rows_ref, wide, product, table, store)


def gated_chunk(features, halo, first_row, count, short_filter, medium_rows, skip, scalars):
    channels = features.shape[2]
    more = (
        [],
        pl.BlockSpec((count, LANES), lambda i, *_: (0, i)),
        jax.ShapeDtypeStruct((count, channels), BF16),
        [],
        "hyena_filters",
    )
    return filter_call(
        gated_kernel, features, halo, first_row, count, short_filter, medium_rows, skip, more, scalars
    )


def terms_kernel(first_row, order_ref, *refs):
    head, halo_ref, rows_ref, rest = split_refs(first_row, refs)
    weight, _, to_x, to_y, gated, wide, product, table, held, sems = rest
    tile = pl.program_id(0)
    pieces, _, width = held.shape

    def fetch(piece):
        columns = pl.ds(pl.multiple_of(order_ref[piece] * width, width), width)
        return pltpu.make_async_copy(weight.at[:, columns], held.at[piece], sems.at[piece])

    @pl.when(tile == 0)
    def _():
        for piece in range(pieces):
            fetch(piece).start()

    lanes = pl.ds(pl.multiple_of(tile * LANES, LANES), LANES)

    def store(row, value):
        gated[row : row + value.shape[0], lanes] = value

    filter_tile(first_row, tile, *head, halo_ref, rows_ref, wide, product, table, store)

    @pl.when(tile == pl.num_programs(0) - 1)
    def _():
        for piece, (out, part) in enumerate([(to_x, 0), (to_x, 1), (to_y, 0), (to_y, 1)]):
            fetch(piece).wait()
            term = jnp.dot(gated[...], held[piece], preferred_element_type=F32)
            out[:, part * width : (part + 1) * width] = term.astype(BF16)


def terms_chunk(features, halo, first_row, count, short_filter, medium_rows, skip, order, out_weight, after):
    depth, columns = out_weight.shape
    width = columns // 8
    widths = [2 * width, 2 * width, depth]
    more = (
        [out_weight, after],
        [pl.BlockSpec((count, w), lambda i, *_: (0, 0)) for w in widths],
        [jax.ShapeDtypeStruct((count, w), BF16) for w in widths],
        [
            pltpu.VMEM((4, depth, width), BF16),
            pltpu.SemaphoreType.DMA((4,)),
        ],
        "hyena_terms",
    )
    return filter_call(
        terms_kernel, features, halo, first_row, count, short_filter, medium_rows, skip, more, order
    )


def rest_kernel(order_ref, gated, weight, along_x, along_y, kept, held, sems):
    pieces, _, width = held.shape

    def fetch(piece):
        columns = pl.ds(pl.multiple_of(order_ref[4 + piece] * width, width), width)
        return pltpu.make_async_copy(weight.at[:, columns], held.at[piece], sems.at[piece])

    for piece in range(pieces):
        fetch(piece).start()
    for piece, (out, part) in enumerate([(along_x, 0), (along_y, 0), (kept, 0), (kept, 1)]):
        fetch(piece).wait()
        term = jnp.dot(gated[...], held[piece], preferred_element_type=F32)
        out[:, part * width : (part + 1) * width] = term.astype(BF16)


def rest_terms(order, gated, out_weight):
    count, depth = gated.shape
    width = out_weight.shape[1] // 8
    widths = [width, width, 2 * width]
    return pl.pallas_call(
        rest_kernel,
        grid_spec=pltpu.PrefetchScalarGridSpec(
            num_scalar_prefetch=1,
            grid=(1,),
            in_specs=[pl.BlockSpec(gated.shape, lambda i, *_: (0, 0)), pl.BlockSpec(memory_space=pltpu.HBM)],
            out_specs=[pl.BlockSpec((count, w), lambda i, *_: (0, 0)) for w in widths],
            scratch_shapes=[pltpu.VMEM((4, depth, width), BF16), pltpu.SemaphoreType.DMA((4,))],
        ),
        out_shape=[jax.ShapeDtypeStruct((count, w), BF16) for w in widths],
        compiler_params=pltpu.CompilerParams(vmem_limit_bytes=MOST_VMEM),
        name="hyena_rest",
    )(order, gated, out_weight)


def forward_kernel(along_x, along_y, from_x, from_y, after, out_x, out_y):
    out_x[...] = (along_x[...].astype(F32) + from_y[...].astype(F32)).astype(BF16)
    out_y[...] = (along_y[...].astype(F32) + from_x[...].astype(F32)).astype(BF16)


def add_forwarded(along_x, along_y, from_x, from_y, after):
    rows, width = along_x.shape
    spec = pl.BlockSpec((rows // 2, width), lambda i: (i, 0))
    return pl.pallas_call(
        forward_kernel,
        grid=(2,),
        in_specs=[spec] * 4 + [pl.BlockSpec(memory_space=pltpu.HBM)],
        out_specs=[spec] * 2,
        out_shape=[jax.ShapeDtypeStruct((rows, width), BF16)] * 2,
        compiler_params=pltpu.CompilerParams(vmem_limit_bytes=MOST_VMEM),
        name="add_forwarded",
    )(along_x, along_y, from_x, from_y, after)


def stream_kernel(kept, from_x, from_y, late_x, late_y, residual, after, top, bottom):
    half = late_x.shape[1]
    wide = lambda ref: ref[...].astype(F32)
    left = kept[:, :half].astype(F32) + wide(from_x) + wide(late_y)
    right = kept[:, half:].astype(F32) + wide(from_y) + wide(late_x)
    left = (residual[:, :half].astype(F32) + left).astype(BF16)
    right = (residual[:, half:].astype(F32) + right).astype(BF16)
    for index, out in enumerate([top, bottom]):

        @pl.when(pl.program_id(0) == index)
        def _():
            out[:, :half] = left
            out[:, half:] = right


def add_stream(kept, from_x, from_y, late_x, late_y, residual, start, after):
    rows, channels = kept.shape
    half = channels // 2
    count = rows // 2
    full = pl.BlockSpec((count, channels), lambda i: (i, 0))
    second = pl.BlockSpec((count, half), lambda i: (i, 1))
    late = pl.BlockSpec((count, half), lambda i: (i, 0))
    held = pl.BlockSpec((count, channels), lambda i: (start // count + i, 0))
    return pl.pallas_call(
        stream_kernel,
        grid=(2,),
        in_specs=[full, second, second, late, late, held, pl.BlockSpec(memory_space=pltpu.HBM)],
        out_specs=[pl.BlockSpec((count, channels), lambda i: (0, 0))] * 2,
        out_shape=[jax.ShapeDtypeStruct((count, channels), BF16)] * 2,
        compiler_params=pltpu.CompilerParams(vmem_limit_bytes=MOST_VMEM),
        name="add_stream",
    )(kept, from_x, from_y, late_x, late_y, residual, after)


def fetch_rows(meta_ref, weight, held, sems, first, blocks):
    depth = held.shape[1]
    copies = []
    for index in range(blocks):
        for part in range(2):
            row = pl.multiple_of(meta_ref[first + index] * 2 * depth + part * depth, depth)
            slot = 2 * index + part
            copies.append(pltpu.make_async_copy(weight.at[pl.ds(row, depth), :], held.at[slot], sems.at[slot]))
    return copies


def near_kernel(meta_ref, *refs):
    halves, (gain, weight, _, total, square, held, sems) = refs[:6], refs[6:]
    depth = held.shape[1]
    copies = fetch_rows(meta_ref, weight, held, sems, 0, 3)
    for copy in copies:
        copy.start()
    squares = jnp.zeros(square.shape, F32)
    for index in range(3):
        for part in range(2):
            columns = slice(part * depth, (part + 1) * depth)
            wide = jnp.concatenate([half[:, columns] for half in halves[2 * index : 2 * index + 2]], axis=0)
            wide = wide.astype(F32)
            squares = squares + jnp.sum(wide * wide, axis=1, keepdims=True)
            factor = gain[pl.ds(meta_ref[index], 1), columns]
            copies[2 * index + part].wait()
            term = jnp.dot((wide * factor).astype(BF16), held[2 * index + part], preferred_element_type=F32)
            if index + part == 0:
                total[...] = term
            else:
                total[...] += term
    square[...] = squares


def project_near(meta, halves, gain, weight, after):
    count, channels = halves[0].shape
    rows = 2 * count
    width = weight.shape[1]
    full = lambda shape: pl.BlockSpec(shape, lambda i, meta: (0,) * len(shape))
    return pl.pallas_call(
        near_kernel,
        grid_spec=pltpu.PrefetchScalarGridSpec(
            num_scalar_prefetch=1,
            grid=(1,),
            in_specs=[full(half.shape) for half in halves]
            + [full(gain.shape)]
            + [pl.BlockSpec(memory_space=pltpu.HBM)] * 2,
            out_specs=[full((rows, width)), full((rows, LANES))],
            scratch_shapes=[
                pltpu.VMEM((6, channels // 2, width), BF16),
                pltpu.SemaphoreType.DMA((6,)),
            ],
        ),
        out_shape=[jax.ShapeDtypeStruct((rows, width), F32), jax.ShapeDtypeStruct((rows, LANES), F32)],
        compiler_params=pltpu.CompilerParams(vmem_limit_bytes=MOST_VMEM),
        name="qkv_near",
    )(meta, *halves, gain, weight, after)


def far_kernel(chips, channels, meta_ref, diag_a, diag_b, near, square, gain, cosine, sine, weight, _, *rest):
    outs, (total, held, sems) = rest[:chips], rest[chips:]
    depth = held.shape[1]
    copies = fetch_rows(meta_ref, weight, held, sems, 3, 1)
    for copy in copies:
        copy.start()
    squares = square[...]
    for part in range(2):
        columns = slice(part * depth, (part + 1) * depth)
        wide = jnp.concatenate([diag_a[:, columns], diag_b[:, columns]], axis=0).astype(F32)
        squares = squares + jnp.sum(wide * wide, axis=1, keepdims=True)
        factor = gain[pl.ds(meta_ref[3], 1), columns]
        copies[part].wait()
        term = jnp.dot((wide * factor).astype(BF16), held[part], preferred_element_type=F32)
        if part == 0:
            total[...] = near[...] + term
        else:
            total[...] += term
    inverse = lax.rsqrt(squares / (4 * channels) + norm_eps)
    for distance, out in enumerate(outs):
        head = lax.rem(meta_ref[4] + distance, chips)
        for kind in range(3):
            column = pl.multiple_of((head * 3 + kind) * HEAD, HEAD)
            part = total[:, pl.ds(column, HEAD)] * inverse
            if kind < 2:
                part = part * cosine[...] + pltpu.roll(part, HEAD // 2, 1) * sine[...]
            if kind == 0:
                part = part * SCORE_SCALE
            if kind == 2:
                tiles = [part[row : row + HEAD].T for row in range(0, part.shape[0], HEAD)]
                part = jnp.concatenate(tiles, axis=0)
            out[kind] = part.astype(BF16)


def project_far(meta, diag_a, diag_b, near, square, gain, cosine, sine, weight, after, chips):
    rows, width = near.shape
    channels = diag_a.shape[1]
    full = lambda shape: pl.BlockSpec(shape, lambda i, meta: (0,) * len(shape))
    return pl.pallas_call(
        functools.partial(far_kernel, chips, channels),
        grid_spec=pltpu.PrefetchScalarGridSpec(
            num_scalar_prefetch=1,
            grid=(1,),
            in_specs=[full(x.shape) for x in (diag_a, diag_b, near, square, gain, cosine, sine)]
            + [pl.BlockSpec(memory_space=pltpu.HBM)] * 2,
            out_specs=[full((3, rows, HEAD))] * chips,
            scratch_shapes=[
                pltpu.VMEM((rows, width), F32),
                pltpu.VMEM((2, channels // 2, width), BF16),
                pltpu.SemaphoreType.DMA((2,)),
            ],
        ),
        out_shape=[jax.ShapeDtypeStruct((3, rows, HEAD), BF16)] * chips,
        compiler_params=pltpu.CompilerParams(vmem_limit_bytes=MOST_VMEM),
        name="qkv_far",
    )(meta, diag_a, diag_b, near, square, gain, cosine, sine, weight, after)


def attention_kernel(chips, chunks, distances, meta_ref, *refs):
    pieces = chunks * chips
    own, other = refs[:pieces], refs[pieces : 2 * pieces]
    outs, (keys, values) = refs[2 * pieces : -2], refs[-2:]
    chip, core = meta_ref[4], meta_ref[5]
    rows = own[0].shape[1]
    count = rows * chunks

    for side, source in enumerate([own, other]):
        for distance in range(chips):
            place = lax.rem(chip - distance + chips, chips)
            for chunk in range(chunks):
                piece = source[chunk * chips + distance]
                keys[side, place, chunk * rows : (chunk + 1) * rows, :] = piece[1]
                for tile in range(rows // HEAD):
                    first = chunk * rows + tile * HEAD
                    values[side, place, :, first : first + HEAD] = piece[2, tile * HEAD : (tile + 1) * HEAD, :]

    def scores_of(side, place, queries):
        return lax.dot_general(
            keys[side, place], queries, (((1,), (1,)), ((), ())), preferred_element_type=F32
        )

    def update(state, mine, others, place):
        top, total, acc = state
        new_top = jnp.maximum(jnp.max(mine, axis=0, keepdims=True), jnp.max(others, axis=0, keepdims=True))
        if top is not None:
            new_top = jnp.maximum(new_top, top)
        mine = jnp.exp2(mine - new_top)
        others = jnp.exp2(others - new_top)
        gained = jnp.sum(mine, axis=0, keepdims=True) + jnp.sum(others, axis=0, keepdims=True)
        added = jnp.dot(values[0, place], mine.astype(BF16), preferred_element_type=F32)
        added = added + jnp.dot(values[1, place], others.astype(BF16), preferred_element_type=F32)
        if top is None:
            return new_top, gained, added
        shrink = jnp.exp2(top - new_top)
        return new_top, total * shrink + gained, acc * shrink + added

    key_row = lax.broadcasted_iota(jnp.int32, (count, count), 0)
    query_column = lax.broadcasted_iota(jnp.int32, (count, count), 1)
    for distance, out in zip(distances, outs):
        back = (chips - distance) % chips
        place = lax.rem(chip + distance, chips)
        queries = jnp.concatenate([own[chunk * chips + back][0] for chunk in range(chunks)], axis=0)
        mine = jnp.where(key_row <= query_column, scores_of(0, place, queries), -1e30)
        others = jnp.where(core == 1, scores_of(1, place, queries), -1e30)
        state = update((None, None, None), mine, others, place)

        def earlier(index, state):
            return update(state, scores_of(0, index, queries), scores_of(1, index, queries), index)

        state = lax.fori_loop(0, place, earlier, state)
        out[...] = (state[2] / state[1]).T.astype(BF16)


def attend(meta, own, other, distances, chips, chunks):
    count = own[0].shape[1] * chunks
    whole = lambda shape: pl.BlockSpec(shape, lambda i, meta: (0,) * len(shape))
    return pl.pallas_call(
        functools.partial(attention_kernel, chips, chunks, distances),
        grid_spec=pltpu.PrefetchScalarGridSpec(
            num_scalar_prefetch=1,
            grid=(1,),
            in_specs=[whole(piece.shape) for piece in own + other],
            out_specs=[whole((count, HEAD))] * len(distances),
            scratch_shapes=[
                pltpu.VMEM((2, chips, count, HEAD), BF16),
                pltpu.VMEM((2, chips, HEAD, count), BF16),
            ],
        ),
        out_shape=[jax.ShapeDtypeStruct((count, HEAD), BF16)] * len(distances),
        compiler_params=pltpu.CompilerParams(vmem_limit_bytes=MOST_VMEM),
        name="attention",
    )(meta, *own, *other)


def mix_kernel(chips, distances, streams, meta_ref, *refs):
    heads, refs = refs[: 4 * len(distances)], refs[4 * len(distances) :]
    before, (own_w, *others_w), (out, ordered) = refs[:streams], refs[streams:-2], refs[-2:]
    near_w, far_w = others_w[:3], others_w[3:]
    chip, core = meta_ref[4], meta_ref[5]
    parity = lax.rem(chip + distances[0], 2)
    for index, distance in enumerate(distances):
        head = lax.rem(chip - distance + chips, chips)
        column = pl.ds(pl.multiple_of(head // 2 * HEAD, HEAD), HEAD)
        for source in range(4):
            ordered[source, :, column] = heads[index * 4 + source][...]
    mine = jnp.concatenate(
        [own_w[pl.ds(pl.multiple_of((2 * j + parity) * HEAD, HEAD), HEAD), :] for j in range(chips // 2)], axis=0
    )
    total = jnp.dot(ordered[0], mine, preferred_element_type=F32)
    if streams == 1:
        total = total + before[0][...]
    else:
        total = total + jnp.concatenate([part[...] for part in before], axis=0).astype(F32)

    def finish(weights):
        result = total
        for source in range(3):
            result = result + jnp.dot(ordered[source + 1], weights[source][...], preferred_element_type=F32)
        out[...] = result.astype(out.dtype)

    @pl.when(core == parity)
    def _():
        finish(near_w)

    @pl.when(core != parity)
    def _():
        finish(far_w)


def mix(meta, heads, distances, before, own_w, near_w, far_w, kind, chips):
    rows = heads[0].shape[0]
    channels = own_w.shape[1]
    full = lambda shape: pl.BlockSpec(shape, lambda i, meta: (0,) * len(shape))
    operands = [*heads, *before, own_w, *near_w, *far_w]
    return pl.pallas_call(
        functools.partial(mix_kernel, chips, distances, len(before)),
        grid_spec=pltpu.PrefetchScalarGridSpec(
            num_scalar_prefetch=1,
            grid=(1,),
            in_specs=[full(x.shape) for x in operands],
            out_specs=full((rows, channels)),
            scratch_shapes=[pltpu.VMEM((4, rows, chips // 2 * HEAD), BF16)],
        ),
        out_shape=jax.ShapeDtypeStruct((rows, channels), kind),
        compiler_params=pltpu.CompilerParams(vmem_limit_bytes=MOST_VMEM),
        name="attention_mix",
    )(meta, *operands)


def rotate_rows(block, positions):
    half_size = block.shape[-1] // 2
    frequency = 10000.0 ** (-jnp.arange(half_size, dtype=jnp.float32) * 2.0 / block.shape[-1])
    angles = positions.astype(jnp.float32)[:, None] * frequency[None, :]
    cosine = jnp.cos(angles)[:, None, :]
    sine_part = jnp.sin(angles)[:, None, :]
    first_half = block[..., :half_size]
    second_half = block[..., half_size:]
    return jnp.concatenate(
        [
            first_half * cosine - second_half * sine_part,
            second_half * cosine + first_half * sine_part,
        ],
        axis=-1,
    )


def run_attention(queries, query_pos, key_rows, value_rows, position_of):
    head_count = queries.shape[1]
    row_count = queries.shape[0]
    head_size = queries.shape[2]
    scale_factor = 1.0 / head_size**0.5
    last_query = jnp.max(query_pos)
    initial = (
        jnp.zeros((head_count, row_count, head_size), jnp.float32),
        jnp.full((head_count, row_count), -1e30, jnp.float32),
        jnp.zeros((head_count, row_count), jnp.float32),
    )
    piece_keys = lax.all_gather(key_rows, "ctx", axis=0, tiled=True)
    piece_values = lax.all_gather(value_rows, "ctx", axis=0, tiled=True)
    piece_rows = piece_keys.shape[0]
    block_rows = 512

    def one_block(state_in, block_index):
        first_block = block_index * block_rows
        key_block = lax.dynamic_slice_in_dim(piece_keys, first_block, block_rows, 0)
        value_block = lax.dynamic_slice_in_dim(piece_values, first_block, block_rows, 0)
        key_pos = position_of(first_block + jnp.arange(block_rows))

        def update(state_old):
            acc_sum, run_max, run_total = state_old
            scores = (
                jnp.einsum("thd,khd->htk", queries, key_block, preferred_element_type=jnp.float32)
                * scale_factor
            )
            causal = (key_pos[None, :] <= query_pos[:, None])[None]
            block_max = jnp.max(jnp.where(causal, scores, -1e30), axis=-1)
            new_max = jnp.maximum(run_max, block_max)
            weights = jnp.where(causal, jnp.exp(scores - new_max[..., None]), 0.0)
            correction = jnp.exp(run_max - new_max)
            new_total = run_total * correction + jnp.sum(weights, axis=-1)
            update_sum = jnp.einsum(
                "htk,khd->htd",
                weights.astype(jnp.bfloat16),
                value_block,
                preferred_element_type=jnp.float32,
            )
            return (acc_sum * correction[..., None] + update_sum, new_max, new_total)

        def unchanged(state_old):
            return state_old

        state_out = lax.cond(jnp.min(key_pos) > last_query, unchanged, update, state_in)
        return (state_out, None)

    state_end, unused = lax.scan(one_block, initial, jnp.arange(piece_rows // block_rows))
    acc_sum, run_max, run_total = state_end
    output = acc_sum / run_total[..., None]
    return jnp.transpose(output, (1, 0, 2)).astype(jnp.bfloat16)


def after_gating(gated, residual_in, out_weight, norm_gain, attn_weight, attn_out):
    tok_rows, chan_count = gated.shape
    hyena_terms = jnp.dot(gated, out_weight, preferred_element_type=jnp.float32)
    hyena_out = lax.psum_scatter(
        hyena_terms.astype(jnp.bfloat16), "ch", scatter_dimension=1, tiled=True
    ).astype(jnp.float32)
    stream = (residual_in.astype(jnp.float32) + hyena_out).astype(jnp.bfloat16)
    stream_wide = stream.astype(jnp.float32)
    full_width = chan_count * lax.axis_size("ch")
    head_cols = attn_weight.shape[1]
    square_total = lax.psum(jnp.sum(stream_wide * stream_wide, axis=1), "ch")
    inverse = lax.rsqrt(square_total / full_width + norm_eps)
    gain_part = lax.dynamic_slice_in_dim(norm_gain, lax.axis_index("ch") * chan_count, chan_count)
    normed = (stream_wide * inverse[:, None] * gain_part[None, :]).astype(jnp.bfloat16)
    projected = jnp.dot(
        lax.all_gather(normed, "ch", axis=1, tiled=True),
        attn_weight,
        preferred_element_type=jnp.float32,
    )
    head_count = head_cols // (3 * HEAD)
    projected = projected.reshape(tok_rows, head_count, 3, HEAD)
    ctx_index = lax.axis_index("ctx")
    positions = ctx_index * tok_rows + jnp.arange(tok_rows, dtype=jnp.int32)
    queries = rotate_rows(projected[:, :, 0, :], positions).astype(jnp.bfloat16)
    key_rows = rotate_rows(projected[:, :, 1, :], positions).astype(jnp.bfloat16)
    value_rows = projected[:, :, 2, :].astype(jnp.bfloat16)

    def position_of(global_row):
        return global_row

    attended = run_attention(queries, positions, key_rows, value_rows, position_of)
    head_terms = jnp.dot(
        attended.reshape(tok_rows, head_count * HEAD), attn_out, preferred_element_type=jnp.float32
    )
    attn_mix = lax.psum_scatter(
        head_terms.astype(jnp.bfloat16), "ch", scatter_dimension=1, tiled=True
    ).astype(jnp.float32)
    return (stream_wide + attn_mix).astype(jnp.bfloat16)


def rotation_tables(positions):
    half_size = HEAD // 2
    frequency = 10000.0 ** (-jnp.arange(half_size, dtype=F32) * 2.0 / HEAD)
    angles = positions.astype(F32)[:, None] * frequency[None, :]
    cosine, sine = jnp.cos(angles), jnp.sin(angles)
    return jnp.concatenate([cosine, cosine], axis=1), jnp.concatenate([-sine, sine], axis=1)


def shards(
    features,
    residual_in,
    short_filter,
    medium_filter,
    skip_gain,
    out_weight,
    norm_gain,
    attn_weight,
    attn_out,
):
    rows, _, channels = features.shape
    chips = lax.axis_size("ctx") // 2
    length = medium_filter.shape[0]
    chunk = rows // 2
    ctx, ch = lax.axis_index("ctx"), lax.axis_index("ch")
    meta = jnp.stack([ch, ch ^ 1, ch ^ 2, ch ^ 3, ctx // 2, ctx % 2]).astype(jnp.int32)

    by_kind = jnp.transpose(features, (1, 0, 2))
    count = lax.axis_size("ctx")
    halo = lax.ppermute(by_kind[:, rows - length - LEAD :], "ctx", [(i, i + 1) for i in range(count - 1)])
    medium_rows = medium_filter.T
    skip = skip_gain.reshape(1, channels)

    starts = [rows - chunk, 0]
    if lax.axis_size("ch") != 4 or attn_weight.shape[1] != 3 * HEAD * chips or chips % 2:
        gated = [
            gated_chunk(by_kind, halo, start, chunk, short_filter, medium_rows, skip, meta) for start in starts
        ]
        return after_gating(
            jnp.concatenate(gated[::-1], axis=0), residual_in, out_weight, norm_gain, attn_weight, attn_out
        )

    gain = norm_gain.reshape(4, channels)
    cosine, sine = rotation_tables(ctx * rows + jnp.arange(rows, dtype=jnp.int32))
    near_x, near_y, across = ch ^ 1, ch ^ 2, ch ^ 3
    order = [2 * across, 2 * near_x, 2 * across + 1, 2 * near_y + 1, 2 * near_x + 1, 2 * near_y, 2 * ch, 2 * ch + 1]
    order = jnp.stack(order).astype(jnp.int32)

    sent, after = {}, order
    for start in starts:
        to_x, to_y, gated = terms_chunk(
            by_kind, halo, start, chunk, short_filter, medium_rows, skip, order, out_weight, after
        )
        sent[start] = [swap_ch(to_x, 1), swap_ch(to_y, 2), *rest_terms(order, gated, out_weight)]
        after = sent[start][-1]
    stream, late, after = {}, {}, sent[0][-1]
    for start in starts:
        from_x, from_y, along_x, along_y, kept = sent[start]
        along_x, along_y = add_forwarded(along_x, along_y, from_x, from_y, after)
        late_x, late_y = swap_ch(along_x, 1), swap_ch(along_y, 2)
        stream[start] = add_stream(kept, from_x, from_y, late_x, late_y, residual_in, start, along_x)
        late[start] = along_x
        after = stream[start][0]

    own, other, after = [], [], [late[0], stream[0][0]]
    for step, start in enumerate(starts):
        top, bottom = stream[start]
        x_top, y_bottom, y_top, x_bottom = swap_ch(top, 1), swap_ch(bottom, 2), swap_ch(top, 2), swap_ch(bottom, 1)
        diag_a, diag_b = swap_ch(x_top, 2), swap_ch(y_bottom, 1)
        near, square = project_near(
            meta, [top, bottom, x_top, x_bottom, y_top, y_bottom], gain, attn_weight, after[0]
        )
        turn = slice(start, start + chunk)
        outs = project_far(
            meta, diag_a, diag_b, near, square, gain, cosine[turn], sine[turn], attn_weight, after[1], chips
        )
        after = [outs[0], outs[0]]
        pieces = [outs[0]] + [rotate_chips(outs[d], d) for d in range(1, chips)]
        own = pieces + own
        other = [swap_core(piece) for piece in pieces] + other

    later, _ = lax.optimization_barrier((attn_out, after[0]))
    by_parity = later.reshape(chips // 2, 2, HEAD, later.shape[1])
    mine = lax.dynamic_slice_in_dim(by_parity, ctx % 2, 1, 1).reshape(chips // 2 * HEAD, later.shape[1])
    near_w = [
        swap_ch(lax.dynamic_slice_in_dim(mine, (ch ^ mask) * channels, channels, 1), mask) for mask in (1, 2, 3)
    ]
    own_w = lax.dynamic_slice_in_dim(later, ch * channels, channels, 1)

    groups = [tuple(range(0, chips, 2)), tuple(range(1, chips, 2))]
    attended = [attend(meta, own, other, distances, chips, 2) for distances in groups]
    near_w, _ = lax.optimization_barrier((near_w, attended[1]))
    far_w = [swap_core(weight) for weight in near_w]
    before, kinds = [*stream[0], *stream[chunk]], [F32, BF16]
    for group, distances in enumerate(groups):
        heads = []
        for index, (distance, piece) in enumerate(zip(distances, attended[group])):
            back = rotate_chips(piece, distance) if distance else piece
            by_x, by_y = swap_ch(back, 1), swap_ch(back, 2)
            across = swap_ch(by_x, 2) if index % 2 == 0 else swap_ch(by_y, 1)
            heads += [back, by_x, by_y, across]
        before = [mix(meta, heads, distances, before, own_w, near_w, far_w, kinds[group], chips)]
    return before[0]


def solution(mesh):
    in_specs = (
        P("ctx", None, "ch"),
        P("ctx", "ch"),
        P(None, None, "ch"),
        P(None, "ch"),
        P("ch"),
        P("ch", None),
        P(),
        P(None, "ch"),
        P("ch", None),
    )
    out_specs = P("ctx", "ch")
    return jax.shard_map(shards, mesh=mesh, in_specs=in_specs, out_specs=out_specs, check_vma=False)
```

```python
import functools

import jax
import jax.numpy as jnp
from jax import lax
from jax.experimental import pallas as pl
from jax.experimental.pallas import tpu as pltpu
from jax.sharding import PartitionSpec as P

HEAD = 128
GROUP_SIZE = 16
LANES = 128
LEAD = 16
norm_eps = 1e-05
SCORE_SCALE = 1.4426950408889634 / HEAD**0.5
MIB = 1024 * 1024
F32 = jnp.float32
BF16 = jnp.bfloat16


def swap_ch(value, mask):
    count = lax.axis_size("ch")
    return lax.ppermute(value, "ch", [(i, i ^ mask) for i in range(count)])


def swap_core(value):
    count = lax.axis_size("ctx")
    return lax.ppermute(value, "ctx", [(i, i ^ 1) for i in range(count)])


def rotate_chips(value, distance):
    count = lax.axis_size("ctx")
    return lax.ppermute(value, "ctx", [(i, (i + 2 * distance) % count) for i in range(count)])


def filter_tile(first_row, tile, short_ref, medium_ref, skip_ref, halo_ref, rows_ref, wide, product, table, store):
    taps, groups_all = short_ref.shape[1:]
    groups, length = medium_ref.shape
    span = wide.shape[1]
    halo_rows = length + LEAD
    count = span - halo_rows

    for kind in range(3):
        if first_row == 0:
            wide[kind, :halo_rows] = halo_ref[kind].astype(F32)
            wide[kind, halo_rows:] = rows_ref[kind].astype(F32)
        else:
            wide[kind] = rows_ref[kind, first_row - halo_rows : first_row + count].astype(F32)

    group_row = lax.broadcasted_iota(jnp.int32, (groups_all, LANES), 0)
    group_col = lax.broadcasted_iota(jnp.int32, (groups_all, LANES), 1) // GROUP_SIZE + tile * groups
    chosen = jnp.where(group_row == group_col, 1.0, 0.0).astype(F32)
    weights = [
        jnp.dot(short_ref[kind], chosen, precision=lax.Precision.HIGHEST, preferred_element_type=F32)
        for kind in range(3)
    ]

    tap_row = lax.broadcasted_iota(jnp.int32, (length, 2 * length), 0)
    place = lax.broadcasted_iota(jnp.int32, (length, 2 * length), 1)
    turned = jnp.where(tap_row + place == length, 1.0, 0.0).astype(BF16)
    base = jnp.dot(medium_ref[...].astype(BF16), turned, preferred_element_type=F32)
    for group in range(groups):
        spread = jnp.broadcast_to(base[group : group + 1, :], (length, 2 * length))
        rolled = pltpu.roll(spread, 0, 1, stride=1, stride_axis=0)
        table[group * length : (group + 1) * length, :] = rolled.astype(BF16)

    def featured(kind, start):
        total = weights[kind][0:1, :] * wide[kind, start : start + length, :]
        for tap in range(1, taps):
            total = total + weights[kind][tap : tap + 1, :] * wide[kind, start - tap : start - tap + length, :]
        return total

    for block in range(count // length + 1):
        start = LEAD + block * length
        product[block * length : (block + 1) * length, :] = (
            featured(1, start) * featured(2, start)
        ).astype(BF16)

    group_of = lax.broadcasted_iota(jnp.int32, (length, 2 * LANES), 1) % LANES // GROUP_SIZE
    for pair in range(count // (2 * length)):
        begin = pair * 2 * length
        window = jnp.concatenate(
            [
                product[begin : begin + 2 * length, :],
                product[begin + length : begin + 3 * length, :],
            ],
            axis=1,
        )
        spread = jnp.dot(table[...], window, preferred_element_type=F32)
        mixed = spread[:length]
        for group in range(1, groups):
            mixed = jnp.where(group_of == group, spread[group * length : (group + 1) * length], mixed)
        for part in range(2):
            row = begin + part * length
            direct = skip_ref[...] * product[row + length : row + 2 * length, :].astype(F32)
            gate = featured(0, halo_rows + row)
            store(row, (gate * (mixed[:, part * LANES : (part + 1) * LANES] + direct)).astype(BF16))


def gated_kernel(first_row, loads, *refs):
    head, rest = refs[:3], refs[3:]
    halo_ref, rest = (rest[0], rest[1:]) if first_row == 0 else (None, rest)
    rows_ref, rest = rest[0], rest[1:]
    if loads:
        weight, out_ref, held, wide, product, table, sem = rest
        copy = pltpu.make_async_copy(weight, held, sem)
        pl.when(pl.program_id(0) == 0)(copy.start)
    else:
        out_ref, wide, product, table = rest

    def store(row, value):
        out_ref[row : row + value.shape[0], :] = value

    filter_tile(first_row, pl.program_id(0), *head, halo_ref, rows_ref, wide, product, table, store)
    if loads:
        pl.when(pl.program_id(0) == pl.num_programs(0) - 1)(copy.wait)


def gated_chunk(features, halo, first_row, count, short_filter, medium_rows, skip, weight=None):
    kinds, rows, channels = features.shape
    length = medium_rows.shape[1]
    groups = LANES // GROUP_SIZE
    loads = weight is not None
    in_specs = [
        pl.BlockSpec(short_filter.shape, lambda i: (0, 0, 0)),
        pl.BlockSpec((groups, length), lambda i: (i, 0)),
        pl.BlockSpec((1, LANES), lambda i: (0, i)),
    ]
    operands = [short_filter, medium_rows, skip]
    if first_row == 0:
        in_specs.append(pl.BlockSpec((kinds, length + LEAD, LANES), lambda i: (0, 0, i)))
        operands.append(halo)
        in_specs.append(pl.BlockSpec((kinds, count, LANES), lambda i: (0, 0, i)))
    else:
        in_specs.append(pl.BlockSpec((kinds, rows, LANES), lambda i: (0, 0, i)))
    operands.append(features)
    out_specs = [pl.BlockSpec((count, LANES), lambda i: (0, i))]
    out_shape = [jax.ShapeDtypeStruct((count, channels), BF16)]
    scratch = [
        pltpu.VMEM((kinds, length + LEAD + count, LANES), F32),
        pltpu.VMEM((length + count, LANES), BF16),
        pltpu.VMEM((groups * length, 2 * length), BF16),
    ]
    if loads:
        in_specs.append(pl.BlockSpec(memory_space=pltpu.HBM))
        operands.append(pltpu.with_memory_space_constraint(weight, pltpu.HBM))
        out_specs.append(pl.BlockSpec(memory_space=pltpu.VMEM))
        out_shape.append(pltpu.VMEM(weight.shape, weight.dtype))
        scratch.append(pltpu.SemaphoreType.DMA)
    outs = pl.pallas_call(
        functools.partial(gated_kernel, first_row, loads),
        grid=(channels // LANES,),
        in_specs=in_specs,
        out_specs=out_specs,
        out_shape=out_shape,
        scratch_shapes=scratch,
        compiler_params=pltpu.CompilerParams(vmem_limit_bytes=16 * MIB),
        name="hyena_filters",
    )(*operands)
    return outs if loads else outs[0]


def vmem_call(body, name, scalars, operands, outs, scratch=()):
    return pl.pallas_call(
        body,
        in_specs=[pl.BlockSpec(memory_space=pltpu.SMEM)] + [pl.BlockSpec(memory_space=pltpu.VMEM)] * len(operands),
        out_specs=[pl.BlockSpec(memory_space=pltpu.VMEM)] * len(outs),
        out_shape=[jax.ShapeDtypeStruct(shape, kind) for shape, kind in outs],
        scratch_shapes=list(scratch),
        compiler_params=pltpu.CompilerParams(vmem_limit_bytes=20 * MIB),
        name=name,
    )(scalars, *operands)


def columns_kernel(first, places, order_ref, upper, lower, weight, *outs):
    gated = jnp.concatenate([upper[...], lower[...]], axis=0)
    width = weight.shape[1] // 8
    for piece, (out, part) in enumerate(places):
        columns = pl.ds(pl.multiple_of(order_ref[first + piece] * width, width), width)
        term = jnp.dot(gated, weight[:, columns], preferred_element_type=F32)
        outs[out][:, part * width : (part + 1) * width] = term.astype(BF16)


def column_terms(order, upper, lower, weight, first, places):
    rows, width = 2 * upper.shape[0], weight.shape[1] // 8
    outs = [((rows, width * sum(p[0] == out for p in places)), BF16) for out in range(places[-1][0] + 1)]
    body = functools.partial(columns_kernel, first, places)
    return vmem_call(body, "hyena_terms", order, [upper, lower, weight], outs)


def stream_kernel(_, kept, direct_x, direct_y, late_x, late_y, residual, *parts):
    half = late_x.shape[1]
    rows = parts[0].shape[0]
    for index, out in enumerate(parts):
        span = slice(index * rows, (index + 1) * rows)
        wide = lambda ref: ref[span].astype(F32)
        left = wide(residual)[:, :half] + (wide(kept)[:, :half] + wide(direct_x) + wide(late_y))
        right = wide(residual)[:, half:] + (wide(kept)[:, half:] + wide(direct_y) + wide(late_x))
        out[...] = jnp.concatenate([left, right], axis=1).astype(BF16)


def near_kernel(meta_ref, *refs):
    halves, (gain, weight, total, square) = refs[:6], refs[6:]
    channels = halves[0].shape[1]
    squares = jnp.zeros(square.shape, F32)
    result = None
    for index in range(3):
        wide = jnp.concatenate([half[...] for half in halves[2 * index : 2 * index + 2]], axis=0).astype(F32)
        squares = squares + jnp.sum(wide * wide, axis=1, keepdims=True)
        factor = gain[pl.ds(meta_ref[index], 1), :]
        block = weight[pl.ds(pl.multiple_of(meta_ref[index] * channels, channels), channels), :]
        term = jnp.dot((wide * factor).astype(BF16), block, preferred_element_type=F32)
        result = term if result is None else result + term
    total[...] = result
    square[...] = squares


def far_kernel(chips, meta_ref, diag_a, diag_b, near, square, gain, cosine, sine, weight, *rest):
    outs, total = rest[:chips], rest[chips]
    channels = diag_a.shape[1]
    wide = jnp.concatenate([diag_a[...], diag_b[...]], axis=0).astype(F32)
    squares = square[...] + jnp.sum(wide * wide, axis=1, keepdims=True)
    factor = gain[pl.ds(meta_ref[3], 1), :]
    block = weight[pl.ds(pl.multiple_of(meta_ref[3] * channels, channels), channels), :]
    total[...] = near[...] + jnp.dot((wide * factor).astype(BF16), block, preferred_element_type=F32)
    inverse = lax.rsqrt(squares / (4 * channels) + norm_eps)
    for distance, out in enumerate(outs):
        head = lax.rem(meta_ref[4] + distance, chips)
        for kind in range(3):
            column = pl.multiple_of((head * 3 + kind) * HEAD, HEAD)
            part = total[:, pl.ds(column, HEAD)] * inverse
            if kind < 2:
                part = part * cosine[...] + pltpu.roll(part, HEAD // 2, 1) * sine[...]
            if kind == 0:
                part = part * SCORE_SCALE
            if kind == 2:
                tiles = [part[row : row + HEAD].T for row in range(0, part.shape[0], HEAD)]
                part = jnp.concatenate(tiles, axis=0)
            out[kind] = part.astype(BF16)


def gather_keys(chips, chunks, meta_ref, refs, keys, values):
    pieces = chunks * chips
    rows = refs[0].shape[1]
    for side in range(2):
        for distance in range(chips):
            place = lax.rem(meta_ref[4] - distance + chips, chips)
            for chunk in range(chunks):
                piece = refs[side * pieces + chunk * chips + distance]
                keys[side, place, chunk * rows : (chunk + 1) * rows, :] = piece[1]
                for tile in range(rows // HEAD):
                    first = chunk * rows + tile * HEAD
                    values[side, place, :, first : first + HEAD] = piece[2, tile * HEAD : (tile + 1) * HEAD, :]


def attention_kernel(chips, chunks, distances, leading, meta_ref, *refs):
    if leading:
        pieces, rest = refs[: 2 * chunks * chips], refs[2 * chunks * chips :]
        outs, (keys, values) = rest[: len(distances)], rest[len(distances) :]
        gather_keys(chips, chunks, meta_ref, pieces, keys, values)
        backs = [(chips - distance) % chips for distance in distances]
        sources = [[pieces[chunk * chips + back] for chunk in range(chunks)] for back in backs]
    else:
        taken = chunks * len(distances)
        pieces, (keys, values), outs = refs[:taken], refs[taken : taken + 2], refs[taken + 2 :]
        sources = [pieces[index * chunks : (index + 1) * chunks] for index in range(len(distances))]
    chip, core = meta_ref[4], meta_ref[5]
    count = keys.shape[2]

    def scores_of(side, place, queries):
        return lax.dot_general(
            keys[side, place], queries, (((1,), (1,)), ((), ())), preferred_element_type=F32
        )

    def update(state, mine, others, place):
        top, total, acc = state
        new_top = jnp.maximum(jnp.max(mine, axis=0, keepdims=True), jnp.max(others, axis=0, keepdims=True))
        if top is not None:
            new_top = jnp.maximum(new_top, top)
        mine = jnp.exp2(mine - new_top)
        others = jnp.exp2(others - new_top)
        gained = jnp.sum(mine, axis=0, keepdims=True) + jnp.sum(others, axis=0, keepdims=True)
        added = jnp.dot(values[0, place], mine.astype(BF16), preferred_element_type=F32)
        added = added + jnp.dot(values[1, place], others.astype(BF16), preferred_element_type=F32)
        if top is None:
            return new_top, gained, added
        shrink = jnp.exp2(top - new_top)
        return new_top, total * shrink + gained, acc * shrink + added

    key_row = lax.broadcasted_iota(jnp.int32, (count, count), 0)
    query_column = lax.broadcasted_iota(jnp.int32, (count, count), 1)
    for distance, source, out in zip(distances, sources, outs):
        place = lax.rem(chip + distance, chips)
        queries = jnp.concatenate([piece[0] for piece in source], axis=0)
        mine = jnp.where(key_row <= query_column, scores_of(0, place, queries), -1e30)
        others = jnp.where(core == 1, scores_of(1, place, queries), -1e30)
        state = update((None, None, None), mine, others, place)

        def earlier(index, state):
            return update(state, scores_of(0, index, queries), scores_of(1, index, queries), index)

        state = lax.fori_loop(0, place, earlier, state)
        out[...] = (state[2] / state[1]).T.astype(BF16)


def attend(meta, own, other, groups, chips, chunks):
    count = own[0].shape[1] * chunks
    laid = [((2, chips, count, HEAD), BF16), ((2, chips, HEAD, count), BF16)]
    given = [((count, HEAD), BF16)]
    first, second = groups
    body = functools.partial(attention_kernel, chips, chunks, first, True)
    *early, keys, values = vmem_call(body, "attention", meta, own + other, given * len(first) + laid)
    pieces = [own[chunk * chips + (chips - distance) % chips] for distance in second for chunk in range(chunks)]
    body = functools.partial(attention_kernel, chips, chunks, second, False)
    late = vmem_call(body, "attention", meta, pieces + [keys, values], given * len(second))
    return early, late


def mix_kernel(chips, distances, streams, meta_ref, *refs):
    heads, refs = refs[:4], refs[4:]
    before, (own_w, *others_w), (out, ordered) = refs[:streams], refs[streams:-2], refs[-2:]
    near_w, far_w = others_w[:3], others_w[3:]
    chip, core = meta_ref[4], meta_ref[5]
    parity = lax.rem(chip + distances[0], 2)
    for index, distance in enumerate(distances):
        head = lax.rem(chip - distance + chips, chips)
        column = pl.ds(pl.multiple_of(head // 2 * HEAD, HEAD), HEAD)
        for source in range(4):
            ordered[source, :, column] = heads[source][index]
    mine = jnp.concatenate(
        [own_w[pl.ds(pl.multiple_of((2 * j + parity) * HEAD, HEAD), HEAD), :] for j in range(chips // 2)], axis=0
    )

    def finish(weights):
        total = jnp.dot(ordered[0], mine, preferred_element_type=F32)
        for source in range(3):
            total = total + jnp.dot(ordered[source + 1], weights[source][...], preferred_element_type=F32)
        total = total + jnp.concatenate([part[...].astype(F32) for part in before], axis=0)
        out[...] = total.astype(out.dtype)

    @pl.when(core == parity)
    def _():
        finish(near_w)

    @pl.when(core != parity)
    def _():
        finish(far_w)


def mix(meta, heads, distances, before, own_w, near_w, far_w, kind, chips):
    rows, channels = heads[0].shape[1], own_w.shape[1]
    body = functools.partial(mix_kernel, chips, distances, len(before))
    operands = [*heads, *before, own_w, *near_w, *far_w]
    scratch = [pltpu.VMEM((4, rows, chips // 2 * HEAD), BF16)]
    return vmem_call(body, "attention_mix", meta, operands, [((rows, channels), kind)], scratch)[0]


def rotate_rows(block, positions):
    half_size = block.shape[-1] // 2
    frequency = 10000.0 ** (-jnp.arange(half_size, dtype=jnp.float32) * 2.0 / block.shape[-1])
    angles = positions.astype(jnp.float32)[:, None] * frequency[None, :]
    cosine = jnp.cos(angles)[:, None, :]
    sine_part = jnp.sin(angles)[:, None, :]
    first_half = block[..., :half_size]
    second_half = block[..., half_size:]
    return jnp.concatenate(
        [
            first_half * cosine - second_half * sine_part,
            second_half * cosine + first_half * sine_part,
        ],
        axis=-1,
    )


def run_attention(queries, query_pos, key_rows, value_rows, position_of):
    head_count = queries.shape[1]
    row_count = queries.shape[0]
    head_size = queries.shape[2]
    scale_factor = 1.0 / head_size**0.5
    last_query = jnp.max(query_pos)
    initial = (
        jnp.zeros((head_count, row_count, head_size), jnp.float32),
        jnp.full((head_count, row_count), -1e30, jnp.float32),
        jnp.zeros((head_count, row_count), jnp.float32),
    )
    piece_keys = lax.all_gather(key_rows, "ctx", axis=0, tiled=True)
    piece_values = lax.all_gather(value_rows, "ctx", axis=0, tiled=True)
    piece_rows = piece_keys.shape[0]
    block_rows = 512

    def one_block(state_in, block_index):
        first_block = block_index * block_rows
        key_block = lax.dynamic_slice_in_dim(piece_keys, first_block, block_rows, 0)
        value_block = lax.dynamic_slice_in_dim(piece_values, first_block, block_rows, 0)
        key_pos = position_of(first_block + jnp.arange(block_rows))

        def update(state_old):
            acc_sum, run_max, run_total = state_old
            scores = (
                jnp.einsum("thd,khd->htk", queries, key_block, preferred_element_type=jnp.float32)
                * scale_factor
            )
            causal = (key_pos[None, :] <= query_pos[:, None])[None]
            block_max = jnp.max(jnp.where(causal, scores, -1e30), axis=-1)
            new_max = jnp.maximum(run_max, block_max)
            weights = jnp.where(causal, jnp.exp(scores - new_max[..., None]), 0.0)
            correction = jnp.exp(run_max - new_max)
            new_total = run_total * correction + jnp.sum(weights, axis=-1)
            update_sum = jnp.einsum(
                "htk,khd->htd",
                weights.astype(jnp.bfloat16),
                value_block,
                preferred_element_type=jnp.float32,
            )
            return (acc_sum * correction[..., None] + update_sum, new_max, new_total)

        def unchanged(state_old):
            return state_old

        state_out = lax.cond(jnp.min(key_pos) > last_query, unchanged, update, state_in)
        return (state_out, None)

    state_end, unused = lax.scan(one_block, initial, jnp.arange(piece_rows // block_rows))
    acc_sum, run_max, run_total = state_end
    output = acc_sum / run_total[..., None]
    return jnp.transpose(output, (1, 0, 2)).astype(jnp.bfloat16)


def after_gating(gated, residual_in, out_weight, norm_gain, attn_weight, attn_out):
    tok_rows, chan_count = gated.shape
    hyena_terms = jnp.dot(gated, out_weight, preferred_element_type=jnp.float32)
    hyena_out = lax.psum_scatter(
        hyena_terms.astype(jnp.bfloat16), "ch", scatter_dimension=1, tiled=True
    ).astype(jnp.float32)
    stream = (residual_in.astype(jnp.float32) + hyena_out).astype(jnp.bfloat16)
    stream_wide = stream.astype(jnp.float32)
    full_width = chan_count * lax.axis_size("ch")
    head_cols = attn_weight.shape[1]
    square_total = lax.psum(jnp.sum(stream_wide * stream_wide, axis=1), "ch")
    inverse = lax.rsqrt(square_total / full_width + norm_eps)
    gain_part = lax.dynamic_slice_in_dim(norm_gain, lax.axis_index("ch") * chan_count, chan_count)
    normed = (stream_wide * inverse[:, None] * gain_part[None, :]).astype(jnp.bfloat16)
    projected = jnp.dot(
        lax.all_gather(normed, "ch", axis=1, tiled=True),
        attn_weight,
        preferred_element_type=jnp.float32,
    )
    head_count = head_cols // (3 * HEAD)
    projected = projected.reshape(tok_rows, head_count, 3, HEAD)
    ctx_index = lax.axis_index("ctx")
    positions = ctx_index * tok_rows + jnp.arange(tok_rows, dtype=jnp.int32)
    queries = rotate_rows(projected[:, :, 0, :], positions).astype(jnp.bfloat16)
    key_rows = rotate_rows(projected[:, :, 1, :], positions).astype(jnp.bfloat16)
    value_rows = projected[:, :, 2, :].astype(jnp.bfloat16)

    def position_of(global_row):
        return global_row

    attended = run_attention(queries, positions, key_rows, value_rows, position_of)
    head_terms = jnp.dot(
        attended.reshape(tok_rows, head_count * HEAD), attn_out, preferred_element_type=jnp.float32
    )
    attn_mix = lax.psum_scatter(
        head_terms.astype(jnp.bfloat16), "ch", scatter_dimension=1, tiled=True
    ).astype(jnp.float32)
    return (stream_wide + attn_mix).astype(jnp.bfloat16)


def rotation_tables(positions):
    half_size = HEAD // 2
    frequency = 10000.0 ** (-jnp.arange(half_size, dtype=F32) * 2.0 / HEAD)
    angles = positions.astype(F32)[:, None] * frequency[None, :]
    cosine, sine = jnp.cos(angles), jnp.sin(angles)
    return jnp.concatenate([cosine, cosine], axis=1), jnp.concatenate([-sine, sine], axis=1)


def shards(
    features,
    residual_in,
    short_filter,
    medium_filter,
    skip_gain,
    out_weight,
    norm_gain,
    attn_weight,
    attn_out,
):
    rows, _, channels = features.shape
    chips = lax.axis_size("ctx") // 2
    length = medium_filter.shape[0]
    chunk = rows // 2
    ctx, ch = lax.axis_index("ctx"), lax.axis_index("ch")
    meta = jnp.stack([ch, ch ^ 1, ch ^ 2, ch ^ 3, ctx // 2, ctx % 2]).astype(jnp.int32)

    by_kind = jnp.transpose(features, (1, 0, 2))
    count = lax.axis_size("ctx")
    halo = lax.ppermute(by_kind[:, rows - length - LEAD :], "ctx", [(i, i + 1) for i in range(count - 1)])
    medium_rows = medium_filter.T
    skip = skip_gain.reshape(1, channels)

    starts = [rows - chunk, 0]
    if lax.axis_size("ch") != 4 or attn_weight.shape[1] != 3 * HEAD * chips or chips % 2:
        gated = [gated_chunk(by_kind, halo, start, chunk, short_filter, medium_rows, skip) for start in starts]
        return after_gating(
            jnp.concatenate(gated[::-1], axis=0), residual_in, out_weight, norm_gain, attn_weight, attn_out
        )

    gain = norm_gain.reshape(4, channels)
    cosine, sine = rotation_tables(ctx * rows + jnp.arange(rows, dtype=jnp.int32))
    near_x, near_y, across = ch ^ 1, ch ^ 2, ch ^ 3
    order = [2 * across, 2 * across + 1, 2 * near_x, 2 * near_y + 1, 2 * near_x + 1, 2 * near_y, 2 * ch, 2 * ch + 1]
    order = jnp.stack(order).astype(jnp.int32)

    lower, out_held = gated_chunk(by_kind, halo, chunk, chunk, short_filter, medium_rows, skip, out_weight)
    upper, qkv_held = gated_chunk(by_kind, halo, 0, chunk, short_filter, medium_rows, skip, attn_weight)
    across_x, across_y = column_terms(order, upper, lower, out_held, 0, ((0, 0), (1, 0)))
    across_x, across_y = swap_ch(across_x, 1), swap_ch(across_y, 2)
    direct_x, direct_y, along_x, along_y, kept = column_terms(
        order, upper, lower, out_held, 2, ((0, 0), (1, 0), (2, 0), (3, 0), (4, 0), (4, 1))
    )
    direct_x, direct_y = swap_ch(direct_x, 1), swap_ch(direct_y, 2)
    late_x = swap_ch((along_x.astype(F32) + across_y.astype(F32)).astype(BF16), 1)
    late_y = swap_ch((along_y.astype(F32) + across_x.astype(F32)).astype(BF16), 2)
    quarters = vmem_call(
        stream_kernel,
        "add_stream",
        order,
        [kept, direct_x, direct_y, late_x, late_y, residual_in],
        [((rows // 4, channels), BF16)] * 4,
    )

    own, other = [], []
    for start in starts:
        top, bottom = quarters[start // (rows // 4) : start // (rows // 4) + 2]
        x_top, y_bottom, x_bottom, y_top = swap_ch(top, 1), swap_ch(bottom, 2), swap_ch(bottom, 1), swap_ch(top, 2)
        diag_a, diag_b = swap_ch(x_top, 2), swap_ch(y_bottom, 1)
        width = attn_weight.shape[1]
        near, square = vmem_call(
            near_kernel,
            "qkv_near",
            meta,
            [top, bottom, x_top, x_bottom, y_top, y_bottom, gain, qkv_held],
            [((chunk, width), F32), ((chunk, LANES), F32)],
        )
        turn = slice(start, start + chunk)
        outs = vmem_call(
            functools.partial(far_kernel, chips),
            "qkv_far",
            meta,
            [diag_a, diag_b, near, square, gain, cosine[turn], sine[turn], qkv_held],
            [((3, chunk, HEAD), BF16)] * chips,
            [pltpu.VMEM((chunk, width), F32)],
        )
        pieces = [outs[0]] + [rotate_chips(outs[d], d) for d in range(1, chips)]
        own = pieces + own
        other = [swap_core(piece) for piece in pieces] + other

    later, _ = lax.optimization_barrier((attn_out, own[0]))
    by_parity = later.reshape(chips // 2, 2, HEAD, later.shape[1])
    mine = lax.dynamic_slice_in_dim(by_parity, ctx % 2, 1, 1).reshape(chips // 2 * HEAD, later.shape[1])
    near_w = [
        swap_ch(lax.dynamic_slice_in_dim(mine, (ch ^ mask) * channels, channels, 1), mask) for mask in (1, 2, 3)
    ]
    own_w = lax.dynamic_slice_in_dim(later, ch * channels, channels, 1)

    groups = [tuple(range(0, chips, 2)), tuple(range(1, chips, 2))]
    attended = attend(meta, own, other, groups, chips, 2)
    near_w, _ = lax.optimization_barrier((near_w, attended[1]))
    far_w = [swap_core(weight) for weight in near_w]
    before = quarters
    for group, (distances, kind) in enumerate(zip(groups, [F32, BF16])):
        backs = [rotate_chips(piece, d) if d else piece for d, piece in zip(distances, attended[group])]
        backs = jnp.stack(backs)
        by_x, by_y = swap_ch(backs, 1), swap_ch(backs, 2)
        by_both = swap_ch(by_x, 2) if group == 0 else swap_ch(by_y, 1)
        heads = [backs, by_x, by_y, by_both]
        before = [mix(meta, heads, distances, before, own_w, near_w, far_w, kind, chips)]
    return before[0]


def solution(mesh):
    in_specs = (
        P("ctx", None, "ch"),
        P("ctx", "ch"),
        P(None, None, "ch"),
        P(None, "ch"),
        P("ch"),
        P("ch", None),
        P(),
        P(None, "ch"),
        P("ch", None),
    )
    out_specs = P("ctx", "ch")
    return jax.shard_map(shards, mesh=mesh, in_specs=in_specs, out_specs=out_specs, check_vma=False)
```

```python
import functools

import jax
import jax.numpy as jnp
from jax import lax
from jax.experimental import pallas as pl
from jax.experimental.pallas import tpu as pltpu
from jax.sharding import PartitionSpec as P

HEAD = 128
GROUP_SIZE = 16
LANES = 128
LEAD = 16
norm_eps = 1e-05
SCORE_SCALE = 1.4426950408889634 / HEAD**0.5
MIB = 1024 * 1024
F32 = jnp.float32
BF16 = jnp.bfloat16


def swap_ch(value, mask):
    count = lax.axis_size("ch")
    return lax.ppermute(value, "ch", [(i, i ^ mask) for i in range(count)])


def swap_core(value):
    count = lax.axis_size("ctx")
    return lax.ppermute(value, "ctx", [(i, i ^ 1) for i in range(count)])


def rotate_chips(value, distance):
    count = lax.axis_size("ctx")
    return lax.ppermute(value, "ctx", [(i, (i + 2 * distance) % count) for i in range(count)])


def filter_tile(first_row, tile, short_ref, medium_ref, skip_ref, halo_ref, rows_ref, wide, product, table, store):
    taps, groups_all = short_ref.shape[1:]
    groups, length = medium_ref.shape
    span = wide.shape[1]
    halo_rows = length + LEAD
    count = span - halo_rows

    for kind in range(3):
        if first_row == 0:
            wide[kind, :halo_rows] = halo_ref[kind].astype(F32)
            wide[kind, halo_rows:] = rows_ref[kind].astype(F32)
        else:
            wide[kind] = rows_ref[kind, first_row - halo_rows : first_row + count].astype(F32)

    group_row = lax.broadcasted_iota(jnp.int32, (groups_all, LANES), 0)
    group_col = lax.broadcasted_iota(jnp.int32, (groups_all, LANES), 1) // GROUP_SIZE + tile * groups
    chosen = jnp.where(group_row == group_col, 1.0, 0.0).astype(F32)
    weights = [
        jnp.dot(short_ref[kind], chosen, precision=lax.Precision.HIGHEST, preferred_element_type=F32)
        for kind in range(3)
    ]

    tap_row = lax.broadcasted_iota(jnp.int32, (length, 2 * length), 0)
    place = lax.broadcasted_iota(jnp.int32, (length, 2 * length), 1)
    turned = jnp.where(tap_row + place == length, 1.0, 0.0).astype(BF16)
    base = jnp.dot(medium_ref[...].astype(BF16), turned, preferred_element_type=F32)
    for group in range(groups):
        spread = jnp.broadcast_to(base[group : group + 1, :], (length, 2 * length))
        rolled = pltpu.roll(spread, 0, 1, stride=1, stride_axis=0)
        table[group * length : (group + 1) * length, :] = rolled.astype(BF16)

    def featured(kind, start):
        total = weights[kind][0:1, :] * wide[kind, start : start + length, :]
        for tap in range(1, taps):
            total = total + weights[kind][tap : tap + 1, :] * wide[kind, start - tap : start - tap + length, :]
        return total

    for block in range(count // length + 1):
        start = LEAD + block * length
        product[block * length : (block + 1) * length, :] = (
            featured(1, start) * featured(2, start)
        ).astype(BF16)

    group_of = lax.broadcasted_iota(jnp.int32, (length, 2 * LANES), 1) % LANES // GROUP_SIZE
    for pair in range(count // (2 * length)):
        begin = pair * 2 * length
        window = jnp.concatenate(
            [
                product[begin : begin + 2 * length, :],
                product[begin + length : begin + 3 * length, :],
            ],
            axis=1,
        )
        spread = jnp.dot(table[...], window, preferred_element_type=F32)
        mixed = spread[:length]
        for group in range(1, groups):
            mixed = jnp.where(group_of == group, spread[group * length : (group + 1) * length], mixed)
        for part in range(2):
            row = begin + part * length
            direct = skip_ref[...] * product[row + length : row + 2 * length, :].astype(F32)
            gate = featured(0, halo_rows + row)
            store(row, (gate * (mixed[:, part * LANES : (part + 1) * LANES] + direct)).astype(BF16))


def gated_kernel(first_row, loads, *refs):
    head, rest = refs[1:4], refs[4:]
    halo_ref, rest = (rest[0], rest[1:]) if first_row == 0 else (None, rest)
    rows_ref, rest = rest[0], rest[1:]
    if loads:
        weight, out_ref, held, wide, product, table, sem = rest
        copy = pltpu.make_async_copy(weight, held, sem)
        pl.when(pl.program_id(0) == 0)(copy.start)
    else:
        out_ref, wide, product, table = rest

    def store(row, value):
        out_ref[row : row + value.shape[0], :] = value

    filter_tile(first_row, pl.program_id(0), *head, halo_ref, rows_ref, wide, product, table, store)
    if loads:
        pl.when(pl.program_id(0) == pl.num_programs(0) - 1)(copy.wait)


def gated_chunk(meta, features, halo, first_row, count, short_filter, medium_rows, skip, weight=None):
    kinds, rows, channels = features.shape
    length = medium_rows.shape[1]
    groups = LANES // GROUP_SIZE
    loads = weight is not None
    in_hbm = lambda x: pltpu.with_memory_space_constraint(x, pltpu.HBM)
    in_specs = [
        pl.BlockSpec(memory_space=pltpu.SMEM),
        pl.BlockSpec(short_filter.shape, lambda i: (0, 0, 0)),
        pl.BlockSpec((groups, length), lambda i: (i, 0)),
        pl.BlockSpec((1, LANES), lambda i: (0, i)),
    ]
    operands = [meta, in_hbm(short_filter), in_hbm(medium_rows), in_hbm(skip)]
    if first_row == 0:
        in_specs.append(pl.BlockSpec((kinds, length + LEAD, LANES), lambda i: (0, 0, i)))
        operands.append(halo)
        in_specs.append(pl.BlockSpec((kinds, count, LANES), lambda i: (0, 0, i)))
    else:
        in_specs.append(pl.BlockSpec((kinds, rows, LANES), lambda i: (0, 0, i)))
    operands.append(in_hbm(features))
    out_specs = [pl.BlockSpec((count, LANES), lambda i: (0, i))]
    out_shape = [jax.ShapeDtypeStruct((count, channels), BF16)]
    scratch = [
        pltpu.VMEM((kinds, length + LEAD + count, LANES), F32),
        pltpu.VMEM((length + count, LANES), BF16),
        pltpu.VMEM((groups * length, 2 * length), BF16),
    ]
    if loads:
        in_specs.append(pl.BlockSpec(memory_space=pltpu.HBM))
        operands.append(in_hbm(weight))
        out_specs.append(pl.BlockSpec(memory_space=pltpu.VMEM))
        out_shape.append(pltpu.VMEM(weight.shape, weight.dtype))
        scratch.append(pltpu.SemaphoreType.DMA)
    outs = pl.pallas_call(
        functools.partial(gated_kernel, first_row, loads),
        grid=(channels // LANES,),
        in_specs=in_specs,
        out_specs=out_specs,
        out_shape=out_shape,
        scratch_shapes=scratch,
        compiler_params=pltpu.CompilerParams(vmem_limit_bytes=16 * MIB),
        name="hyena_filters",
    )(*operands)
    return outs if loads else outs[0]


def vmem_call(body, name, scalars, operands, outs, scratch=()):
    return pl.pallas_call(
        body,
        in_specs=[pl.BlockSpec(memory_space=pltpu.SMEM)] + [pl.BlockSpec(memory_space=pltpu.VMEM)] * len(operands),
        out_specs=[pl.BlockSpec(memory_space=pltpu.VMEM)] * len(outs),
        out_shape=[jax.ShapeDtypeStruct(shape, kind) for shape, kind in outs],
        scratch_shapes=list(scratch),
        compiler_params=pltpu.CompilerParams(vmem_limit_bytes=20 * MIB),
        name=name,
    )(scalars, *operands)


def columns_kernel(pieces, meta_ref, upper, lower, weight, *outs):
    gated = jnp.concatenate([upper[...], lower[...]], axis=0)
    width = weight.shape[1] // 8
    for owner, half, out, part in pieces:
        columns = pl.ds(pl.multiple_of((2 * meta_ref[owner] + half) * width, width), width)
        term = jnp.dot(gated, weight[:, columns], preferred_element_type=F32)
        outs[out][:, part * width : (part + 1) * width] = term.astype(BF16)


def column_terms(meta, upper, lower, weight, pieces):
    rows, width = 2 * upper.shape[0], weight.shape[1] // 8
    outs = [((rows, width * sum(p[2] == out for p in pieces)), BF16) for out in range(pieces[-1][2] + 1)]
    return vmem_call(functools.partial(columns_kernel, pieces), "hyena_terms", meta, [upper, lower, weight], outs)


def load_kernel(source, _, held, sem):
    copy = pltpu.make_async_copy(source, held, sem)
    copy.start()
    copy.wait()


def load(weight, after):
    return pl.pallas_call(
        load_kernel,
        in_specs=[pl.BlockSpec(memory_space=pltpu.HBM), pl.BlockSpec(memory_space=pltpu.VMEM)],
        out_specs=pl.BlockSpec(memory_space=pltpu.VMEM),
        out_shape=pltpu.VMEM(weight.shape, weight.dtype),
        scratch_shapes=[pltpu.SemaphoreType.DMA],
        compiler_params=pltpu.CompilerParams(vmem_limit_bytes=4 * MIB),
        name="load_weight",
    )(pltpu.with_memory_space_constraint(weight, pltpu.HBM), after)


def stream_kernel(_, kept, direct_x, direct_y, late_x, late_y, residual, after, *parts):
    half = late_x.shape[1]
    rows = parts[0].shape[0]
    for index, out in enumerate(parts):
        span = slice(index * rows, (index + 1) * rows)
        wide = lambda ref: ref[span].astype(F32)
        left = wide(residual)[:, :half] + (wide(kept)[:, :half] + wide(direct_x) + wide(late_y))
        right = wide(residual)[:, half:] + (wide(kept)[:, half:] + wide(direct_y) + wide(late_x))
        out[...] = jnp.concatenate([left, right], axis=1).astype(BF16)


def near_kernel(meta_ref, *refs):
    halves, (gain, weight, total, square) = refs[:6], refs[6:]
    channels = halves[0].shape[1]
    squares = jnp.zeros(square.shape, F32)
    result = None
    for index in range(3):
        wide = jnp.concatenate([half[...] for half in halves[2 * index : 2 * index + 2]], axis=0).astype(F32)
        squares = squares + jnp.sum(wide * wide, axis=1, keepdims=True)
        span = pl.ds(pl.multiple_of(meta_ref[index] * channels, channels), channels)
        factor, block = gain[:, span], weight[span, :]
        term = jnp.dot((wide * factor).astype(BF16), block, preferred_element_type=F32)
        result = term if result is None else result + term
    total[...] = result
    square[...] = squares


def far_kernel(chips, meta_ref, diag_a, diag_b, near, square, gain, cosine, sine, weight, *rest):
    outs, total = rest[:chips], rest[chips]
    channels = diag_a.shape[1]
    wide = jnp.concatenate([diag_a[...], diag_b[...]], axis=0).astype(F32)
    squares = square[...] + jnp.sum(wide * wide, axis=1, keepdims=True)
    span = pl.ds(pl.multiple_of(meta_ref[3] * channels, channels), channels)
    factor, block = gain[:, span], weight[span, :]
    total[...] = near[...] + jnp.dot((wide * factor).astype(BF16), block, preferred_element_type=F32)
    inverse = lax.rsqrt(squares / (4 * channels) + norm_eps)
    for distance, out in enumerate(outs):
        head = lax.rem(meta_ref[4] + distance, chips)
        for kind in range(3):
            column = pl.multiple_of((head * 3 + kind) * HEAD, HEAD)
            part = total[:, pl.ds(column, HEAD)] * inverse
            if kind < 2:
                part = part * cosine[...] + pltpu.roll(part, HEAD // 2, 1) * sine[...]
            if kind == 0:
                part = part * SCORE_SCALE
            if kind == 2:
                tiles = [part[row : row + HEAD].T for row in range(0, part.shape[0], HEAD)]
                part = jnp.concatenate(tiles, axis=0)
            out[kind] = part.astype(BF16)


def gather_keys(chips, meta_ref, own, other, keys, values):
    rows = own[0].shape[1]
    for distance in range(chips):
        place = lax.rem(meta_ref[4] - distance + chips, chips)
        for chunk, stacked in enumerate(other):
            mine = own[chunk * chips + distance]
            span = slice(chunk * rows, (chunk + 1) * rows)
            keys[0, place, span, :] = mine[1]
            keys[1, place, span, :] = stacked[distance, 0]
            for tile in range(rows // HEAD):
                first = chunk * rows + tile * HEAD
                taken = slice(tile * HEAD, (tile + 1) * HEAD)
                values[0, place, :, first : first + HEAD] = mine[2, taken, :]
                values[1, place, :, first : first + HEAD] = stacked[distance, 1, taken, :]


def attention_kernel(chips, chunks, distances, leading, meta_ref, *refs):
    if leading:
        pieces, rest = refs[: chunks * chips], refs[chunks * chips :]
        other, outs, (keys, values) = rest[:chunks], rest[chunks:-2], rest[-2:]
        gather_keys(chips, meta_ref, pieces, other, keys, values)
        backs = [(chips - distance) % chips for distance in distances]
        sources = [[pieces[chunk * chips + back] for chunk in range(chunks)] for back in backs]
    else:
        taken = chunks * len(distances)
        pieces, (keys, values), outs = refs[:taken], refs[taken : taken + 2], refs[taken + 2 :]
        sources = [pieces[index * chunks : (index + 1) * chunks] for index in range(len(distances))]
    chip, core = meta_ref[4], meta_ref[5]
    count = keys.shape[2]

    def scores_of(side, place, queries):
        return lax.dot_general(
            keys[side, place], queries, (((1,), (1,)), ((), ())), preferred_element_type=F32
        )

    def update(state, mine, others, place):
        top, total, acc = state
        new_top = jnp.maximum(jnp.max(mine, axis=0, keepdims=True), jnp.max(others, axis=0, keepdims=True))
        if top is not None:
            new_top = jnp.maximum(new_top, top)
        mine = jnp.exp2(mine - new_top)
        others = jnp.exp2(others - new_top)
        gained = jnp.sum(mine, axis=0, keepdims=True) + jnp.sum(others, axis=0, keepdims=True)
        added = jnp.dot(values[0, place], mine.astype(BF16), preferred_element_type=F32)
        added = added + jnp.dot(values[1, place], others.astype(BF16), preferred_element_type=F32)
        if top is None:
            return new_top, gained, added
        shrink = jnp.exp2(top - new_top)
        return new_top, total * shrink + gained, acc * shrink + added

    key_row = lax.broadcasted_iota(jnp.int32, (count, count), 0)
    query_column = lax.broadcasted_iota(jnp.int32, (count, count), 1)
    for distance, source, out in zip(distances, sources, outs):
        place = lax.rem(chip + distance, chips)
        queries = jnp.concatenate([piece[0] for piece in source], axis=0)
        mine = jnp.where(key_row <= query_column, scores_of(0, place, queries), -1e30)
        others = jnp.where(core == 1, scores_of(1, place, queries), -1e30)
        state = update((None, None, None), mine, others, place)

        def earlier(index, state):
            return update(state, scores_of(0, index, queries), scores_of(1, index, queries), index)

        state = lax.fori_loop(0, place, earlier, state)
        out[...] = (state[2] / state[1]).T.astype(BF16)


def attend(meta, own, other, groups, chips, chunks):
    count = own[0].shape[1] * chunks
    laid = [((2, chips, count, HEAD), BF16), ((2, chips, HEAD, count), BF16)]
    given = [((count, HEAD), BF16)]
    first, second = groups
    body = functools.partial(attention_kernel, chips, chunks, first, True)
    *early, keys, values = vmem_call(body, "attention", meta, own + other, given * len(first) + laid)
    pieces = [own[chunk * chips + (chips - distance) % chips] for distance in second for chunk in range(chunks)]
    body = functools.partial(attention_kernel, chips, chunks, second, False)
    late = vmem_call(body, "attention", meta, pieces + [keys, values], given * len(second))
    return early, late


def pick_kernel(chips, meta_ref, weight, _, *refs):
    *near, own, sems = refs
    channels = own.shape[1]
    columns = [pl.ds(pl.multiple_of(meta_ref[index] * channels, channels), channels) for index in range(4)]
    copies = [pltpu.make_async_copy(weight.at[:, columns[0]], own, sems.at[0])]
    for index, out in enumerate(near):
        for head in range(chips // 2):
            rows = pl.ds(pl.multiple_of((2 * head + meta_ref[5]) * HEAD, HEAD), HEAD)
            target = out.at[head * HEAD : (head + 1) * HEAD]
            sem = sems.at[1 + index * (chips // 2) + head]
            copies.append(pltpu.make_async_copy(weight.at[rows, columns[index + 1]], target, sem))
    for copy in copies:
        copy.start()
    for copy in copies:
        copy.wait()


def pick_weights(meta, weight, after, chips, channels):
    rows = weight.shape[0]
    near = jax.ShapeDtypeStruct((rows // 2, channels), BF16)
    return pl.pallas_call(
        functools.partial(pick_kernel, chips),
        in_specs=[
            pl.BlockSpec(memory_space=pltpu.SMEM),
            pl.BlockSpec(memory_space=pltpu.HBM),
            pl.BlockSpec(memory_space=pltpu.VMEM),
        ],
        out_specs=[pl.BlockSpec(memory_space=pltpu.VMEM)] * 4,
        out_shape=[near, near, near, jax.ShapeDtypeStruct((rows, channels), BF16)],
        scratch_shapes=[pltpu.SemaphoreType.DMA((1 + 3 * (chips // 2),))],
        compiler_params=pltpu.CompilerParams(vmem_limit_bytes=4 * MIB),
        name="pick_weights",
    )(meta, pltpu.with_memory_space_constraint(weight, pltpu.HBM), after)


def mix_kernel(chips, distances, streams, meta_ref, *refs):
    heads, refs = refs[:4], refs[4:]
    before, (own_w, *others_w), (out, ordered) = refs[:streams], refs[streams:-2], refs[-2:]
    near_w, far_w = others_w[:3], others_w[3:]
    chip, core = meta_ref[4], meta_ref[5]
    parity = lax.rem(chip + distances[0], 2)
    for index, distance in enumerate(distances):
        head = lax.rem(chip - distance + chips, chips)
        column = pl.ds(pl.multiple_of(head // 2 * HEAD, HEAD), HEAD)
        for source in range(4):
            ordered[source, :, column] = heads[source][index]
    mine = jnp.concatenate(
        [own_w[pl.ds(pl.multiple_of((2 * j + parity) * HEAD, HEAD), HEAD), :] for j in range(chips // 2)], axis=0
    )

    def finish(weights):
        total = jnp.dot(ordered[0], mine, preferred_element_type=F32)
        for source in range(3):
            total = total + jnp.dot(ordered[source + 1], weights[source][...], preferred_element_type=F32)
        total = total + jnp.concatenate([part[...].astype(F32) for part in before], axis=0)
        out[...] = total.astype(out.dtype)

    @pl.when(core == parity)
    def _():
        finish(near_w)

    @pl.when(core != parity)
    def _():
        finish(far_w)


def mix(meta, heads, distances, before, own_w, near_w, far_w, kind, chips):
    rows, channels = heads[0].shape[1], own_w.shape[1]
    body = functools.partial(mix_kernel, chips, distances, len(before))
    operands = [*heads, *before, own_w, *near_w, *far_w]
    scratch = [pltpu.VMEM((4, rows, chips // 2 * HEAD), BF16)]
    return vmem_call(body, "attention_mix", meta, operands, [((rows, channels), kind)], scratch)[0]


def rotate_rows(block, positions):
    half_size = block.shape[-1] // 2
    frequency = 10000.0 ** (-jnp.arange(half_size, dtype=jnp.float32) * 2.0 / block.shape[-1])
    angles = positions.astype(jnp.float32)[:, None] * frequency[None, :]
    cosine = jnp.cos(angles)[:, None, :]
    sine_part = jnp.sin(angles)[:, None, :]
    first_half = block[..., :half_size]
    second_half = block[..., half_size:]
    return jnp.concatenate(
        [
            first_half * cosine - second_half * sine_part,
            second_half * cosine + first_half * sine_part,
        ],
        axis=-1,
    )


def run_attention(queries, query_pos, key_rows, value_rows, position_of):
    head_count = queries.shape[1]
    row_count = queries.shape[0]
    head_size = queries.shape[2]
    scale_factor = 1.0 / head_size**0.5
    last_query = jnp.max(query_pos)
    initial = (
        jnp.zeros((head_count, row_count, head_size), jnp.float32),
        jnp.full((head_count, row_count), -1e30, jnp.float32),
        jnp.zeros((head_count, row_count), jnp.float32),
    )
    piece_keys = lax.all_gather(key_rows, "ctx", axis=0, tiled=True)
    piece_values = lax.all_gather(value_rows, "ctx", axis=0, tiled=True)
    piece_rows = piece_keys.shape[0]
    block_rows = 512

    def one_block(state_in, block_index):
        first_block = block_index * block_rows
        key_block = lax.dynamic_slice_in_dim(piece_keys, first_block, block_rows, 0)
        value_block = lax.dynamic_slice_in_dim(piece_values, first_block, block_rows, 0)
        key_pos = position_of(first_block + jnp.arange(block_rows))

        def update(state_old):
            acc_sum, run_max, run_total = state_old
            scores = (
                jnp.einsum("thd,khd->htk", queries, key_block, preferred_element_type=jnp.float32)
                * scale_factor
            )
            causal = (key_pos[None, :] <= query_pos[:, None])[None]
            block_max = jnp.max(jnp.where(causal, scores, -1e30), axis=-1)
            new_max = jnp.maximum(run_max, block_max)
            weights = jnp.where(causal, jnp.exp(scores - new_max[..., None]), 0.0)
            correction = jnp.exp(run_max - new_max)
            new_total = run_total * correction + jnp.sum(weights, axis=-1)
            update_sum = jnp.einsum(
                "htk,khd->htd",
                weights.astype(jnp.bfloat16),
                value_block,
                preferred_element_type=jnp.float32,
            )
            return (acc_sum * correction[..., None] + update_sum, new_max, new_total)

        def unchanged(state_old):
            return state_old

        state_out = lax.cond(jnp.min(key_pos) > last_query, unchanged, update, state_in)
        return (state_out, None)

    state_end, unused = lax.scan(one_block, initial, jnp.arange(piece_rows // block_rows))
    acc_sum, run_max, run_total = state_end
    output = acc_sum / run_total[..., None]
    return jnp.transpose(output, (1, 0, 2)).astype(jnp.bfloat16)


def after_gating(gated, residual_in, out_weight, norm_gain, attn_weight, attn_out):
    tok_rows, chan_count = gated.shape
    hyena_terms = jnp.dot(gated, out_weight, preferred_element_type=jnp.float32)
    hyena_out = lax.psum_scatter(
        hyena_terms.astype(jnp.bfloat16), "ch", scatter_dimension=1, tiled=True
    ).astype(jnp.float32)
    stream = (residual_in.astype(jnp.float32) + hyena_out).astype(jnp.bfloat16)
    stream_wide = stream.astype(jnp.float32)
    full_width = chan_count * lax.axis_size("ch")
    head_cols = attn_weight.shape[1]
    square_total = lax.psum(jnp.sum(stream_wide * stream_wide, axis=1), "ch")
    inverse = lax.rsqrt(square_total / full_width + norm_eps)
    gain_part = lax.dynamic_slice_in_dim(norm_gain, lax.axis_index("ch") * chan_count, chan_count)
    normed = (stream_wide * inverse[:, None] * gain_part[None, :]).astype(jnp.bfloat16)
    projected = jnp.dot(
        lax.all_gather(normed, "ch", axis=1, tiled=True),
        attn_weight,
        preferred_element_type=jnp.float32,
    )
    head_count = head_cols // (3 * HEAD)
    projected = projected.reshape(tok_rows, head_count, 3, HEAD)
    ctx_index = lax.axis_index("ctx")
    positions = ctx_index * tok_rows + jnp.arange(tok_rows, dtype=jnp.int32)
    queries = rotate_rows(projected[:, :, 0, :], positions).astype(jnp.bfloat16)
    key_rows = rotate_rows(projected[:, :, 1, :], positions).astype(jnp.bfloat16)
    value_rows = projected[:, :, 2, :].astype(jnp.bfloat16)

    def position_of(global_row):
        return global_row

    attended = run_attention(queries, positions, key_rows, value_rows, position_of)
    head_terms = jnp.dot(
        attended.reshape(tok_rows, head_count * HEAD), attn_out, preferred_element_type=jnp.float32
    )
    attn_mix = lax.psum_scatter(
        head_terms.astype(jnp.bfloat16), "ch", scatter_dimension=1, tiled=True
    ).astype(jnp.float32)
    return (stream_wide + attn_mix).astype(jnp.bfloat16)


def rotation_tables(positions):
    half_size = HEAD // 2
    frequency = 10000.0 ** (-jnp.arange(half_size, dtype=F32) * 2.0 / HEAD)
    angles = positions.astype(F32)[:, None] * frequency[None, :]
    cosine, sine = jnp.cos(angles), jnp.sin(angles)
    return jnp.concatenate([cosine, cosine], axis=1), jnp.concatenate([-sine, sine], axis=1)


def shards(
    features,
    residual_in,
    short_filter,
    medium_filter,
    skip_gain,
    out_weight,
    norm_gain,
    attn_weight,
    attn_out,
):
    rows, _, channels = features.shape
    chips = lax.axis_size("ctx") // 2
    length = medium_filter.shape[0]
    chunk = rows // 2
    ctx, ch = lax.axis_index("ctx"), lax.axis_index("ch")
    scalars = [ch, ch ^ 1, ch ^ 2, ch ^ 3, ctx // 2, ctx % 2, ctx * rows, ctx]
    meta = jnp.stack(scalars).astype(jnp.int32)

    by_kind = jnp.transpose(features, (1, 0, 2))
    count = lax.axis_size("ctx")
    halo = lax.ppermute(by_kind[:, rows - length - LEAD :], "ctx", [(i, i + 1) for i in range(count - 1)])
    medium_rows = medium_filter.T
    skip = skip_gain.reshape(1, channels)

    starts = [rows - chunk, 0]
    if lax.axis_size("ch") != 4 or attn_weight.shape[1] != 3 * HEAD * chips or chips % 2:
        gated = [gated_chunk(meta, by_kind, halo, start, chunk, short_filter, medium_rows, skip) for start in starts]
        return after_gating(
            jnp.concatenate(gated[::-1], axis=0), residual_in, out_weight, norm_gain, attn_weight, attn_out
        )

    gain = norm_gain.reshape(1, -1)
    cosine, sine = rotation_tables(meta[6:7] + jnp.arange(rows, dtype=jnp.int32))

    lower, out_held = gated_chunk(meta, by_kind, halo, chunk, chunk, short_filter, medium_rows, skip, out_weight)
    upper = gated_chunk(meta, by_kind, halo, 0, chunk, short_filter, medium_rows, skip)
    across_x, across_y = column_terms(meta, upper, lower, out_held, ((3, 0, 0, 0), (3, 1, 1, 0)))
    across_x, across_y = swap_ch(across_x, 1), swap_ch(across_y, 2)
    pieces = ((1, 0, 0, 0), (2, 1, 1, 0), (1, 1, 2, 0), (2, 0, 3, 0), (0, 0, 4, 0), (0, 1, 4, 1))
    direct_x, direct_y, along_x, along_y, kept = column_terms(meta, upper, lower, out_held, pieces)
    direct_x, direct_y = swap_ch(direct_x, 1), swap_ch(direct_y, 2)
    along_x = (along_x.astype(F32) + across_y.astype(F32)).astype(BF16)
    along_y = (along_y.astype(F32) + across_x.astype(F32)).astype(BF16)
    late_x, late_y = swap_ch(along_x, 1), swap_ch(along_y, 2)
    qkv_held = load(attn_weight, along_y)
    quarters = vmem_call(
        stream_kernel,
        "add_stream",
        meta,
        [kept, direct_x, direct_y, late_x, late_y, residual_in, qkv_held],
        [((rows // 4, channels), BF16)] * 4,
    )

    own, other, after = [], [], None
    width = attn_weight.shape[1]
    for start in starts:
        top, bottom = quarters[start // (rows // 4) : start // (rows // 4) + 2]
        if after is not None:
            (top, bottom), _ = lax.optimization_barrier(((top, bottom), after))
        x_top, y_bottom, x_bottom, y_top = swap_ch(top, 1), swap_ch(bottom, 2), swap_ch(bottom, 1), swap_ch(top, 2)
        diag_a, diag_b = swap_ch(x_top, 2), swap_ch(y_bottom, 1)
        after = x_top, y_bottom
        near, square = vmem_call(
            near_kernel,
            "qkv_near",
            meta,
            [top, bottom, x_top, x_bottom, y_top, y_bottom, gain, qkv_held],
            [((chunk, width), F32), ((chunk, LANES), F32)],
        )
        turn = slice(start, start + chunk)
        outs = vmem_call(
            functools.partial(far_kernel, chips),
            "qkv_far",
            meta,
            [diag_a, diag_b, near, square, gain, cosine[turn], sine[turn], qkv_held],
            [((3, chunk, HEAD), BF16)] * chips,
            [pltpu.VMEM((chunk, width), F32)],
        )
        arrived = [outs[0]] + [rotate_chips(outs[d], d) for d in range(1, chips)]
        own = arrived + own
        other = [swap_core(jnp.stack([piece[1:] for piece in arrived]))] + other

    *near_w, own_w = pick_weights(meta, attn_out, square, chips, channels)
    near_w = [swap_ch(weight, mask) for mask, weight in zip((1, 2, 3), near_w)]

    groups = [tuple(range(0, chips, 2)), tuple(range(1, chips, 2))]
    attended = attend(meta, own, other, groups, chips, 2)
    near_w, _ = lax.optimization_barrier((near_w, attended[1]))
    far_w = [swap_core(weight) for weight in near_w]
    before = quarters
    for group, (distances, kind) in enumerate(zip(groups, [F32, BF16])):
        backs = [rotate_chips(piece, d) if d else piece for d, piece in zip(distances, attended[group])]
        backs = jnp.stack(backs)
        by_x, by_y = swap_ch(backs, 1), swap_ch(backs, 2)
        by_both = swap_ch(by_x, 2) if group == 0 else swap_ch(by_y, 1)
        heads = [backs, by_x, by_y, by_both]
        before = [mix(meta, heads, distances, before, own_w, near_w, far_w, kind, chips)]
    return before[0]


def solution(mesh):
    in_specs = (
        P("ctx", None, "ch"),
        P("ctx", "ch"),
        P(None, None, "ch"),
        P(None, "ch"),
        P("ch"),
        P("ch", None),
        P(),
        P(None, "ch"),
        P("ch", None),
    )
    out_specs = P("ctx", "ch")
    return jax.shard_map(shards, mesh=mesh, in_specs=in_specs, out_specs=out_specs, check_vma=False)
```

```python
import functools

import jax
import jax.numpy as jnp
from jax import lax
from jax.experimental import pallas as pl
from jax.experimental.pallas import tpu as pltpu
from jax.sharding import PartitionSpec as P

HEAD = 128
GROUP_SIZE = 16
LANES = 128
LEAD = 16
norm_eps = 1e-05
SCORE_SCALE = 1.4426950408889634 / HEAD**0.5
MIB = 1024 * 1024
F32 = jnp.float32
BF16 = jnp.bfloat16


def lasting(micros):
    return pl.CostEstimate(
        flops=int(micros * 1.1e9), transcendentals=0, bytes_accessed=int(micros * 3.6e6)
    )


def swap_ch(value, mask):
    count = lax.axis_size("ch")
    return lax.ppermute(value, "ch", [(i, i ^ mask) for i in range(count)])


def swap_core(value):
    count = lax.axis_size("ctx")
    return lax.ppermute(value, "ctx", [(i, i ^ 1) for i in range(count)])


def rotate_chips(value, distance):
    count = lax.axis_size("ctx")
    return lax.ppermute(value, "ctx", [(i, (i + 2 * distance) % count) for i in range(count)])


def filter_tile(first_row, tile, short_ref, medium_ref, skip_ref, halo_ref, rows_ref, wide, product, table, make_table, store):
    taps, groups_all = short_ref.shape[1:]
    groups, length = medium_ref.shape
    span = wide.shape[1]
    halo_rows = length + LEAD
    count = span - halo_rows

    for kind in range(3):
        if first_row == 0:
            wide[kind, :halo_rows] = halo_ref[kind].astype(F32)
            wide[kind, halo_rows:] = rows_ref[kind].astype(F32)
        else:
            wide[kind] = rows_ref[kind, first_row - halo_rows : first_row + count].astype(F32)

    group_row = lax.broadcasted_iota(jnp.int32, (groups_all, LANES), 0)
    group_col = lax.broadcasted_iota(jnp.int32, (groups_all, LANES), 1) // GROUP_SIZE + tile * groups
    chosen = jnp.where(group_row == group_col, 1.0, 0.0).astype(F32)
    weights = [
        jnp.dot(short_ref[kind], chosen, precision=lax.Precision.HIGHEST, preferred_element_type=F32)
        for kind in range(3)
    ]

    if make_table:
        tap_row = lax.broadcasted_iota(jnp.int32, (length, 2 * length), 0)
        place = lax.broadcasted_iota(jnp.int32, (length, 2 * length), 1)
        turned = jnp.where(tap_row + place == length, 1.0, 0.0).astype(BF16)
        base = jnp.dot(medium_ref[...].astype(BF16), turned, preferred_element_type=F32)
        for group in range(groups):
            spread = jnp.broadcast_to(base[group : group + 1, :], (length, 2 * length))
            rolled = pltpu.roll(spread, 0, 1, stride=1, stride_axis=0)
            table[group * length : (group + 1) * length, :] = rolled.astype(BF16)

    def featured(kind, start):
        total = weights[kind][0:1, :] * wide[kind, start : start + length, :]
        for tap in range(1, taps):
            total = total + weights[kind][tap : tap + 1, :] * wide[kind, start - tap : start - tap + length, :]
        return total

    for block in range(count // length + 1):
        start = LEAD + block * length
        product[block * length : (block + 1) * length, :] = (
            featured(1, start) * featured(2, start)
        ).astype(BF16)

    group_of = lax.broadcasted_iota(jnp.int32, (length, 2 * LANES), 1) % LANES // GROUP_SIZE
    for pair in range(count // (2 * length)):
        begin = pair * 2 * length
        window = jnp.concatenate(
            [
                product[begin : begin + 2 * length, :],
                product[begin + length : begin + 3 * length, :],
            ],
            axis=1,
        )
        spread = jnp.dot(table[...], window, preferred_element_type=F32)
        mixed = spread[:length]
        for group in range(1, groups):
            mixed = jnp.where(group_of == group, spread[group * length : (group + 1) * length], mixed)
        for part in range(2):
            row = begin + part * length
            direct = skip_ref[...] * product[row + length : row + 2 * length, :].astype(F32)
            gate = featured(0, halo_rows + row)
            store(row, (gate * (mixed[:, part * LANES : (part + 1) * LANES] + direct)).astype(BF16))


def gated_kernel(first_row, loads, *refs):
    head, rest = refs[1:4], refs[4:]
    halo_ref, rest = (rest[0], rest[1:]) if first_row == 0 else (None, rest)
    rows_ref, rest = rest[0], rest[1:]
    if loads:
        weight, outer, out_ref, held, picked, table, wide, product, sems, pick_sems = rest
        parts = sems.shape[0]
        height = weight.shape[0] // parts

        def copy_of(part):
            span = pl.ds(pl.multiple_of(part * height, height), height)
            return pltpu.make_async_copy(weight.at[span, :], held.at[span, :], sems.at[part])

        def pick_of(index):
            _, taken, width = picked.shape
            rows = pl.ds(pl.multiple_of(refs[0][7] * taken, taken), taken)
            columns = pl.ds(pl.multiple_of(refs[0][index + 1] * width, width), width)
            return pltpu.make_async_copy(outer.at[rows, columns], picked.at[index], pick_sems.at[index])

        copy_of(pl.program_id(0)).start()

        @pl.when(pl.program_id(0) == 0)
        def _():
            for index in range(3):
                pick_of(index).start()

    elif first_row == 0:
        table, out_ref, wide, product = rest
    else:
        out_ref, table, wide, product = rest

    def store(row, value):
        out_ref[row : row + value.shape[0], :] = value

    make_table = first_row > 0
    filter_tile(first_row, pl.program_id(0), *head, halo_ref, rows_ref, wide, product, table, make_table, store)
    if loads:

        @pl.when(pl.program_id(0) == pl.num_programs(0) - 1)
        def _():
            for part in range(parts):
                copy_of(part).wait()
            for index in range(3):
                pick_of(index).wait()


def gated_chunk(meta, features, halo, first_row, count, short_filter, medium_rows, skip, weights, tables):
    kinds, rows, channels = features.shape
    length = medium_rows.shape[1]
    groups = LANES // GROUP_SIZE
    loads = weights is not None
    in_hbm = lambda x: pltpu.with_memory_space_constraint(x, pltpu.HBM)
    table_spec = pl.BlockSpec((groups * length, 2 * length), lambda i: (i, 0))
    in_specs = [
        pl.BlockSpec(memory_space=pltpu.SMEM),
        pl.BlockSpec(short_filter.shape, lambda i: (0, 0, 0)),
        pl.BlockSpec((groups, length), lambda i: (i, 0)),
        pl.BlockSpec((1, LANES), lambda i: (0, i)),
    ]
    operands = [meta, in_hbm(short_filter), in_hbm(medium_rows), in_hbm(skip)]
    out_specs = [pl.BlockSpec((count, LANES), lambda i: (0, i))]
    out_shape = [jax.ShapeDtypeStruct((count, channels), BF16)]
    scratch = [
        pltpu.VMEM((kinds, length + LEAD + count, LANES), F32),
        pltpu.VMEM((length + count, LANES), BF16),
    ]
    if first_row == 0:
        in_specs.append(pl.BlockSpec((kinds, length + LEAD, LANES), lambda i: (0, 0, i)))
        in_specs.append(pl.BlockSpec((kinds, count, LANES), lambda i: (0, 0, i)))
        in_specs.append(table_spec)
        operands += [halo, in_hbm(features), tables]
    else:
        in_specs.append(pl.BlockSpec((kinds, rows, LANES), lambda i: (0, 0, i)))
        operands.append(in_hbm(features))
        if loads:
            weight, outer = weights
            in_specs += [pl.BlockSpec(memory_space=pltpu.HBM)] * 2
            operands += [in_hbm(weight), in_hbm(outer)]
            out_specs += [pl.BlockSpec(memory_space=pltpu.VMEM)] * 2
            out_shape.append(pltpu.VMEM(weight.shape, weight.dtype))
            out_shape.append(pltpu.VMEM((3, HEAD // 2, channels), outer.dtype))
            scratch += [pltpu.SemaphoreType.DMA((channels // LANES,)), pltpu.SemaphoreType.DMA((3,))]
        out_specs.append(table_spec)
        out_shape.append(jax.ShapeDtypeStruct((channels // GROUP_SIZE * length, 2 * length), BF16))
    return pl.pallas_call(
        functools.partial(gated_kernel, first_row, loads),
        grid=(channels // LANES,),
        in_specs=in_specs,
        out_specs=out_specs,
        out_shape=out_shape,
        scratch_shapes=scratch,
        compiler_params=pltpu.CompilerParams(vmem_limit_bytes=16 * MIB),
        cost_estimate=lasting(7),
        name="hyena_filters",
    )(*operands)


def vmem_call(body, name, micros, scalars, operands, outs, scratch=(), waits=()):
    run = lambda *refs: body(*refs[: 1 + len(operands)], *refs[1 + len(operands) + len(waits) :])
    return pl.pallas_call(
        run,
        in_specs=[pl.BlockSpec(memory_space=pltpu.SMEM)]
        + [pl.BlockSpec(memory_space=pltpu.VMEM)] * len(operands)
        + [pl.BlockSpec(memory_space=pltpu.HBM)] * len(waits),
        out_specs=[pl.BlockSpec(memory_space=pltpu.VMEM)] * len(outs),
        out_shape=[jax.ShapeDtypeStruct(shape, kind) for shape, kind in outs],
        scratch_shapes=list(scratch),
        compiler_params=pltpu.CompilerParams(vmem_limit_bytes=20 * MIB),
        cost_estimate=lasting(micros),
        name=name,
    )(scalars, *operands, *[pltpu.with_memory_space_constraint(x, pltpu.HBM) for x in waits])


def columns_kernel(pieces, meta_ref, upper, lower, weight, *outs):
    gated = jnp.concatenate([upper[...], lower[...]], axis=0)
    width = weight.shape[1] // 8
    for owner, half, out, part in pieces:
        columns = pl.ds(pl.multiple_of((2 * meta_ref[owner] + half) * width, width), width)
        term = jnp.dot(gated, weight[:, columns], preferred_element_type=F32)
        outs[out][:, part * width : (part + 1) * width] = term.astype(BF16)


def column_terms(meta, upper, lower, weight, pieces):
    rows, width = 2 * upper.shape[0], weight.shape[1] // 8
    outs = [((rows, width * sum(p[2] == out for p in pieces)), BF16) for out in range(pieces[-1][2] + 1)]
    return vmem_call(functools.partial(columns_kernel, pieces), "hyena_terms", 0.7 * len(pieces), meta, [upper, lower, weight], outs)


def load_kernel(meta_ref, source, outer, _, held, own, sems):
    channels = own.shape[1]
    columns = pl.ds(pl.multiple_of(meta_ref[0] * channels, channels), channels)
    copies = [
        pltpu.make_async_copy(source, held, sems.at[0]),
        pltpu.make_async_copy(outer.at[:, columns], own, sems.at[1]),
    ]
    for copy in copies:
        copy.start()
    for copy in copies:
        copy.wait()


def load(meta, weight, outer, after, channels):
    in_hbm = lambda x: pltpu.with_memory_space_constraint(x, pltpu.HBM)
    hbm, vmem = pl.BlockSpec(memory_space=pltpu.HBM), pl.BlockSpec(memory_space=pltpu.VMEM)
    return pl.pallas_call(
        load_kernel,
        in_specs=[pl.BlockSpec(memory_space=pltpu.SMEM), hbm, hbm, vmem],
        out_specs=[vmem, vmem],
        out_shape=[pltpu.VMEM(weight.shape, weight.dtype), pltpu.VMEM((outer.shape[0], channels), outer.dtype)],
        scratch_shapes=[pltpu.SemaphoreType.DMA((2,))],
        compiler_params=pltpu.CompilerParams(vmem_limit_bytes=4 * MIB),
        cost_estimate=lasting(5),
        name="load_weights",
    )(meta, in_hbm(weight), in_hbm(outer), after)


def stream_kernel(_, kept, direct_x, direct_y, late_x, late_y, residual, after, shares, *parts):
    half = late_x.shape[1]
    rows = parts[0].shape[0]
    for index, out in enumerate(parts):
        span = slice(index * rows, (index + 1) * rows)
        wide = lambda ref: ref[span].astype(F32)
        left = wide(residual)[:, :half] + (wide(kept)[:, :half] + wide(direct_x) + wide(late_y))
        right = wide(residual)[:, half:] + (wide(kept)[:, half:] + wide(direct_y) + wide(late_x))
        out[...] = jnp.concatenate([left, right], axis=1).astype(BF16)


def near_kernel(meta_ref, *refs):
    halves, (gain, weight, total, square) = refs[:6], refs[6:]
    channels = halves[0].shape[1]
    squares = jnp.zeros(square.shape, F32)
    result = None
    for index in range(3):
        wide = jnp.concatenate([half[...] for half in halves[2 * index : 2 * index + 2]], axis=0).astype(F32)
        squares = squares + jnp.sum(wide * wide, axis=1, keepdims=True)
        span = pl.ds(pl.multiple_of(meta_ref[index] * channels, channels), channels)
        factor, block = gain[:, span], weight[span, :]
        term = jnp.dot((wide * factor).astype(BF16), block, preferred_element_type=F32)
        result = term if result is None else result + term
    total[...] = result
    square[...] = squares


def far_kernel(chips, meta_ref, diag_a, diag_b, near, square, gain, cosine, sine, weight, *rest):
    outs, total = rest[:chips], rest[chips]
    channels = diag_a.shape[1]
    wide = jnp.concatenate([diag_a[...], diag_b[...]], axis=0).astype(F32)
    squares = square[...] + jnp.sum(wide * wide, axis=1, keepdims=True)
    span = pl.ds(pl.multiple_of(meta_ref[3] * channels, channels), channels)
    factor, block = gain[:, span], weight[span, :]
    total[...] = near[...] + jnp.dot((wide * factor).astype(BF16), block, preferred_element_type=F32)
    inverse = lax.rsqrt(squares / (4 * channels) + norm_eps)
    for distance, out in enumerate(outs):
        head = lax.rem(meta_ref[4] + distance, chips)
        for kind in range(3):
            column = pl.multiple_of((head * 3 + kind) * HEAD, HEAD)
            part = total[:, pl.ds(column, HEAD)] * inverse
            if kind < 2:
                part = part * cosine[...] + pltpu.roll(part, HEAD // 2, 1) * sine[...]
            if kind == 0:
                part = part * SCORE_SCALE
            if kind == 2:
                tiles = [part[row : row + HEAD].T for row in range(0, part.shape[0], HEAD)]
                part = jnp.concatenate(tiles, axis=0)
            out[kind] = part.astype(BF16)


def gather_keys(chips, meta_ref, own, other, keys, values):
    rows = own[0].shape[1]
    for distance in range(chips):
        place = lax.rem(meta_ref[4] - distance + chips, chips)
        for chunk, stacked in enumerate(other):
            mine = own[chunk * chips + distance]
            span = slice(chunk * rows, (chunk + 1) * rows)
            keys[0, place, span, :] = mine[1]
            keys[1, place, span, :] = stacked[distance, 0]
            for tile in range(rows // HEAD):
                first = chunk * rows + tile * HEAD
                taken = slice(tile * HEAD, (tile + 1) * HEAD)
                values[0, place, :, first : first + HEAD] = mine[2, taken, :]
                values[1, place, :, first : first + HEAD] = stacked[distance, 1, taken, :]


def attention_kernel(chips, chunks, distance, leading, meta_ref, *refs):
    if leading:
        pieces, other = refs[: chunks * chips], refs[chunks * chips : chunks * (chips + 1)]
        out, keys, values = refs[chunks * (chips + 1) :]
        gather_keys(chips, meta_ref, pieces, other, keys, values)
        source = pieces[(chips - distance) % chips :: chips]
    else:
        source, (keys, values), out = refs[:chunks], refs[chunks : chunks + 2], refs[-1]
    chip, core = meta_ref[4], meta_ref[5]
    count = keys.shape[2]

    def scores_of(side, place, queries):
        return lax.dot_general(
            keys[side, place], queries, (((1,), (1,)), ((), ())), preferred_element_type=F32
        )

    def update(state, mine, others, place):
        top, total, acc = state
        new_top = jnp.maximum(jnp.max(mine, axis=0, keepdims=True), jnp.max(others, axis=0, keepdims=True))
        if top is not None:
            new_top = jnp.maximum(new_top, top)
        mine = jnp.exp2(mine - new_top)
        others = jnp.exp2(others - new_top)
        gained = jnp.sum(mine, axis=0, keepdims=True) + jnp.sum(others, axis=0, keepdims=True)
        added = jnp.dot(values[0, place], mine.astype(BF16), preferred_element_type=F32)
        added = added + jnp.dot(values[1, place], others.astype(BF16), preferred_element_type=F32)
        if top is None:
            return new_top, gained, added
        shrink = jnp.exp2(top - new_top)
        return new_top, total * shrink + gained, acc * shrink + added

    key_row = lax.broadcasted_iota(jnp.int32, (count, count), 0)
    query_column = lax.broadcasted_iota(jnp.int32, (count, count), 1)
    place = lax.rem(chip + distance, chips)
    queries = jnp.concatenate([piece[0] for piece in source], axis=0)
    mine = jnp.where(key_row <= query_column, scores_of(0, place, queries), -1e30)
    others = jnp.where(core == 1, scores_of(1, place, queries), -1e30)
    state = update((None, None, None), mine, others, place)

    def earlier(index, state):
        return update(state, scores_of(0, index, queries), scores_of(1, index, queries), index)

    state = lax.fori_loop(0, place, earlier, state)
    out[...] = (state[2] / state[1]).T.astype(BF16)


def attend(meta, own, other, laid, distance, after, chips):
    chunks, leading = len(other), laid is None
    count = own[0].shape[1] * chunks
    outs = [((count, HEAD), BF16)]
    if leading:
        operands = own + other
        outs += [((2, chips, count, HEAD), BF16), ((2, chips, HEAD, count), BF16)]
    else:
        operands = [*own[(chips - distance) % chips :: chips], *laid, *after]
    body = functools.partial(attention_kernel, chips, chunks, distance, leading)
    out, *made = vmem_call(body, "attention", 3, meta, operands, outs)
    return out, laid or made


def mix_kernel(chips, distances, streams, meta_ref, *refs):
    heads, refs = refs[:4], refs[4:]
    before, (own_w, others_w, out, ordered) = refs[:streams], refs[streams:]
    chip = meta_ref[4]
    parity = lax.rem(chip + distances[0], 2)
    for index, distance in enumerate(distances):
        head = lax.rem(chip - distance + chips, chips)
        column = pl.ds(pl.multiple_of(head // 2 * HEAD, HEAD), HEAD)
        for source in range(4):
            ordered[source, :, column] = heads[source][index]
    numbers = [2 * j + parity for j in range(chips // 2)]
    weights = jnp.concatenate([own_w[pl.ds(pl.multiple_of(n * HEAD, HEAD), HEAD), :] for n in numbers], axis=0)
    total = jnp.dot(ordered[0], weights, preferred_element_type=F32)
    for source in range(3):
        weights = jnp.concatenate([others_w[2 * n + part, source] for n in numbers for part in range(2)], axis=0)
        total = total + jnp.dot(ordered[source + 1], weights, preferred_element_type=F32)
    total = total + jnp.concatenate([part[...].astype(F32) for part in before], axis=0)
    out[...] = total.astype(out.dtype)


def mix(meta, heads, distances, before, own_w, others_w, kind, chips):
    rows, channels = heads[0].shape[1], own_w.shape[1]
    body = functools.partial(mix_kernel, chips, distances, len(before))
    operands = [*heads, *before, own_w, others_w]
    scratch = [pltpu.VMEM((4, rows, chips // 2 * HEAD), BF16)]
    return vmem_call(body, "attention_mix", 2.5, meta, operands, [((rows, channels), kind)], scratch)[0]


def rotate_rows(block, positions):
    half_size = block.shape[-1] // 2
    frequency = 10000.0 ** (-jnp.arange(half_size, dtype=jnp.float32) * 2.0 / block.shape[-1])
    angles = positions.astype(jnp.float32)[:, None] * frequency[None, :]
    cosine = jnp.cos(angles)[:, None, :]
    sine_part = jnp.sin(angles)[:, None, :]
    first_half = block[..., :half_size]
    second_half = block[..., half_size:]
    return jnp.concatenate(
        [
            first_half * cosine - second_half * sine_part,
            second_half * cosine + first_half * sine_part,
        ],
        axis=-1,
    )


def run_attention(queries, query_pos, key_rows, value_rows, position_of):
    head_count = queries.shape[1]
    row_count = queries.shape[0]
    head_size = queries.shape[2]
    scale_factor = 1.0 / head_size**0.5
    last_query = jnp.max(query_pos)
    initial = (
        jnp.zeros((head_count, row_count, head_size), jnp.float32),
        jnp.full((head_count, row_count), -1e30, jnp.float32),
        jnp.zeros((head_count, row_count), jnp.float32),
    )
    piece_keys = lax.all_gather(key_rows, "ctx", axis=0, tiled=True)
    piece_values = lax.all_gather(value_rows, "ctx", axis=0, tiled=True)
    piece_rows = piece_keys.shape[0]
    block_rows = 512

    def one_block(state_in, block_index):
        first_block = block_index * block_rows
        key_block = lax.dynamic_slice_in_dim(piece_keys, first_block, block_rows, 0)
        value_block = lax.dynamic_slice_in_dim(piece_values, first_block, block_rows, 0)
        key_pos = position_of(first_block + jnp.arange(block_rows))

        def update(state_old):
            acc_sum, run_max, run_total = state_old
            scores = (
                jnp.einsum("thd,khd->htk", queries, key_block, preferred_element_type=jnp.float32)
                * scale_factor
            )
            causal = (key_pos[None, :] <= query_pos[:, None])[None]
            block_max = jnp.max(jnp.where(causal, scores, -1e30), axis=-1)
            new_max = jnp.maximum(run_max, block_max)
            weights = jnp.where(causal, jnp.exp(scores - new_max[..., None]), 0.0)
            correction = jnp.exp(run_max - new_max)
            new_total = run_total * correction + jnp.sum(weights, axis=-1)
            update_sum = jnp.einsum(
                "htk,khd->htd",
                weights.astype(jnp.bfloat16),
                value_block,
                preferred_element_type=jnp.float32,
            )
            return (acc_sum * correction[..., None] + update_sum, new_max, new_total)

        def unchanged(state_old):
            return state_old

        state_out = lax.cond(jnp.min(key_pos) > last_query, unchanged, update, state_in)
        return (state_out, None)

    state_end, unused = lax.scan(one_block, initial, jnp.arange(piece_rows // block_rows))
    acc_sum, run_max, run_total = state_end
    output = acc_sum / run_total[..., None]
    return jnp.transpose(output, (1, 0, 2)).astype(jnp.bfloat16)


def after_gating(gated, residual_in, out_weight, norm_gain, attn_weight, attn_out):
    tok_rows, chan_count = gated.shape
    hyena_terms = jnp.dot(gated, out_weight, preferred_element_type=jnp.float32)
    hyena_out = lax.psum_scatter(
        hyena_terms.astype(jnp.bfloat16), "ch", scatter_dimension=1, tiled=True
    ).astype(jnp.float32)
    stream = (residual_in.astype(jnp.float32) + hyena_out).astype(jnp.bfloat16)
    stream_wide = stream.astype(jnp.float32)
    full_width = chan_count * lax.axis_size("ch")
    head_cols = attn_weight.shape[1]
    square_total = lax.psum(jnp.sum(stream_wide * stream_wide, axis=1), "ch")
    inverse = lax.rsqrt(square_total / full_width + norm_eps)
    gain_part = lax.dynamic_slice_in_dim(norm_gain, lax.axis_index("ch") * chan_count, chan_count)
    normed = (stream_wide * inverse[:, None] * gain_part[None, :]).astype(jnp.bfloat16)
    projected = jnp.dot(
        lax.all_gather(normed, "ch", axis=1, tiled=True),
        attn_weight,
        preferred_element_type=jnp.float32,
    )
    head_count = head_cols // (3 * HEAD)
    projected = projected.reshape(tok_rows, head_count, 3, HEAD)
    ctx_index = lax.axis_index("ctx")
    positions = ctx_index * tok_rows + jnp.arange(tok_rows, dtype=jnp.int32)
    queries = rotate_rows(projected[:, :, 0, :], positions).astype(jnp.bfloat16)
    key_rows = rotate_rows(projected[:, :, 1, :], positions).astype(jnp.bfloat16)
    value_rows = projected[:, :, 2, :].astype(jnp.bfloat16)

    def position_of(global_row):
        return global_row

    attended = run_attention(queries, positions, key_rows, value_rows, position_of)
    head_terms = jnp.dot(
        attended.reshape(tok_rows, head_count * HEAD), attn_out, preferred_element_type=jnp.float32
    )
    attn_mix = lax.psum_scatter(
        head_terms.astype(jnp.bfloat16), "ch", scatter_dimension=1, tiled=True
    ).astype(jnp.float32)
    return (stream_wide + attn_mix).astype(jnp.bfloat16)


def rotation_tables(positions):
    half_size = HEAD // 2
    frequency = 10000.0 ** (-jnp.arange(half_size, dtype=F32) * 2.0 / HEAD)
    angles = positions.astype(F32)[:, None] * frequency[None, :]
    cosine, sine = jnp.cos(angles), jnp.sin(angles)
    return jnp.concatenate([cosine, cosine], axis=1), jnp.concatenate([-sine, sine], axis=1)


def shards(
    features,
    residual_in,
    short_filter,
    medium_filter,
    skip_gain,
    out_weight,
    norm_gain,
    attn_weight,
    attn_out,
):
    rows, _, channels = features.shape
    chips = lax.axis_size("ctx") // 2
    length = medium_filter.shape[0]
    chunk = rows // 2
    ctx, ch = lax.axis_index("ctx"), lax.axis_index("ch")
    scalars = [ch, ch ^ 1, ch ^ 2, ch ^ 3, ctx // 2, ctx % 2, ctx * rows, ctx]
    meta = jnp.stack(scalars).astype(jnp.int32)

    by_kind = jnp.transpose(features, (1, 0, 2))
    count = lax.axis_size("ctx")
    halo = lax.ppermute(by_kind[:, rows - length - LEAD :], "ctx", [(i, i + 1) for i in range(count - 1)])
    medium_rows = medium_filter.T
    skip = skip_gain.reshape(1, channels)

    starts = [rows - chunk, 0]
    if lax.axis_size("ch") != 4 or attn_weight.shape[1] != 3 * HEAD * chips or chips % 2:
        lower, tables = gated_chunk(meta, by_kind, halo, chunk, chunk, short_filter, medium_rows, skip, None, None)
        (upper,) = gated_chunk(meta, by_kind, halo, 0, chunk, short_filter, medium_rows, skip, None, tables)
        return after_gating(
            jnp.concatenate([upper, lower], axis=0), residual_in, out_weight, norm_gain, attn_weight, attn_out
        )

    gain = norm_gain.reshape(1, -1)
    cosine, sine = rotation_tables(meta[6:7] + jnp.arange(rows, dtype=jnp.int32))

    lower, out_held, picked, tables = gated_chunk(
        meta, by_kind, halo, chunk, chunk, short_filter, medium_rows, skip, (out_weight, attn_out), None
    )
    (upper,) = gated_chunk(meta, by_kind, halo, 0, chunk, short_filter, medium_rows, skip, None, tables)
    across_x, across_y = column_terms(meta, upper, lower, out_held, ((3, 0, 0, 0), (3, 1, 1, 0)))
    across_x, across_y = swap_ch(across_x, 1), swap_ch(across_y, 2)
    pieces = ((1, 0, 0, 0), (2, 1, 1, 0), (1, 1, 2, 0), (2, 0, 3, 0), (0, 0, 4, 0), (0, 1, 4, 1))
    direct_x, direct_y, along_x, along_y, kept = column_terms(meta, upper, lower, out_held, pieces)
    direct_x, direct_y = swap_ch(direct_x, 1), swap_ch(direct_y, 2)
    along_x = (along_x.astype(F32) + across_y.astype(F32)).astype(BF16)
    along_y = (along_y.astype(F32) + across_x.astype(F32)).astype(BF16)
    late_x, late_y = swap_ch(along_x, 1), swap_ch(along_y, 2)
    qkv_held, own_w = load(meta, attn_weight, attn_out, along_y, channels)

    shares = jnp.stack([swap_ch(picked[index], index + 1) for index in range(3)])
    others_w = lax.all_gather(shares, "ctx", axis=0)
    quarters = vmem_call(
        stream_kernel,
        "add_stream",
        1,
        meta,
        [kept, direct_x, direct_y, late_x, late_y, residual_in, qkv_held, shares],
        [((rows // 4, channels), BF16)] * 4,
    )

    own, other, after = [], [], None
    width = attn_weight.shape[1]
    for start in starts:
        top, bottom = quarters[start // (rows // 4) : start // (rows // 4) + 2]
        if after is not None:
            (top, bottom), _ = lax.optimization_barrier(((top, bottom), after))
        x_top, y_bottom, x_bottom, y_top = swap_ch(top, 1), swap_ch(bottom, 2), swap_ch(bottom, 1), swap_ch(top, 2)
        diag_a, diag_b = swap_ch(x_top, 2), swap_ch(y_bottom, 1)
        after = diag_a, diag_b
        near, square = vmem_call(
            near_kernel,
            "qkv_near",
            3,
            meta,
            [top, bottom, x_top, x_bottom, y_top, y_bottom, gain, qkv_held],
            [((chunk, width), F32), ((chunk, LANES), F32)],
        )
        turn = slice(start, start + chunk)
        outs = vmem_call(
            functools.partial(far_kernel, chips),
            "qkv_far",
            2,
            meta,
            [diag_a, diag_b, near, square, gain, cosine[turn], sine[turn], qkv_held],
            [((3, chunk, HEAD), BF16)] * chips,
            [pltpu.VMEM((chunk, width), F32)],
            waits=[others_w] if start == starts[-1] else [],
        )
        arrived = [outs[0]] + [rotate_chips(outs[d], d) for d in range(1, chips)]
        own.append(arrived)

    own, _ = lax.optimization_barrier((own, outs))
    other = [swap_core(jnp.stack([piece[1:] for piece in arrived])) for arrived in own]
    own, other = own[1] + own[0], other[::-1]

    laid, after, before, backs = None, [], quarters, []
    groups = [(*range(2, chips, 2), 0), tuple(range(1, chips, 2))]
    for distances in groups:
        back = []
        for distance in distances:
            piece, laid = attend(meta, own, other, laid, distance, after, chips)
            back.append(rotate_chips(piece, distance) if distance else piece)
        after = [back[0]]
        backs.append(jnp.stack(back))
    for group, (distances, kind) in enumerate(zip(groups, [F32, BF16])):
        by_x, by_y = swap_ch(backs[group], 1), swap_ch(backs[group], 2)
        by_both = swap_ch(by_x, 2) if group == 0 else swap_ch(by_y, 1)
        heads = [backs[group], by_x, by_y, by_both]
        before = [mix(meta, heads, distances, before, own_w, others_w, kind, chips)]
    return before[0]


def solution(mesh):
    in_specs = (
        P("ctx", None, "ch"),
        P("ctx", "ch"),
        P(None, None, "ch"),
        P(None, "ch"),
        P("ch"),
        P("ch", None),
        P(),
        P(None, "ch"),
        P("ch", None),
    )
    out_specs = P("ctx", "ch")
    return jax.shard_map(shards, mesh=mesh, in_specs=in_specs, out_specs=out_specs, check_vma=False)
```

```python
import functools

import jax
import jax.numpy as jnp
from jax import lax
from jax.experimental import pallas as pl
from jax.experimental.pallas import tpu as pltpu
from jax.sharding import PartitionSpec as P

HEAD = 128
GROUP_SIZE = 16
LANES = 128
LEAD = 16
norm_eps = 1e-05
SCORE_SCALE = 1.4426950408889634 / HEAD**0.5
MIB = 1024 * 1024
F32 = jnp.float32
BF16 = jnp.bfloat16


def lasting(micros):
    return pl.CostEstimate(
        flops=int(micros * 1.1e9), transcendentals=0, bytes_accessed=int(micros * 3.6e6)
    )


def swap_ch(value, mask):
    count = lax.axis_size("ch")
    return lax.ppermute(value, "ch", [(i, i ^ mask) for i in range(count)])


def swap_core(value):
    count = lax.axis_size("ctx")
    return lax.ppermute(value, "ctx", [(i, i ^ 1) for i in range(count)])


def rotate_chips(value, distance):
    count = lax.axis_size("ctx")
    return lax.ppermute(value, "ctx", [(i, (i + 2 * distance) % count) for i in range(count)])


def filter_tile(first_row, tile, short_ref, medium_ref, skip_ref, halo_ref, rows_ref, wide, product, table, make_table, store):
    taps, groups_all = short_ref.shape[1:]
    groups, length = medium_ref.shape
    span = wide.shape[1]
    halo_rows = length + LEAD
    count = span - halo_rows

    for kind in range(3):
        if first_row == 0:
            wide[kind, :halo_rows] = halo_ref[kind].astype(F32)
            wide[kind, halo_rows:] = rows_ref[kind].astype(F32)
        else:
            wide[kind] = rows_ref[kind, first_row - halo_rows : first_row + count].astype(F32)

    group_row = lax.broadcasted_iota(jnp.int32, (groups_all, LANES), 0)
    group_col = lax.broadcasted_iota(jnp.int32, (groups_all, LANES), 1) // GROUP_SIZE + tile * groups
    chosen = jnp.where(group_row == group_col, 1.0, 0.0).astype(F32)
    weights = [
        jnp.dot(short_ref[kind], chosen, precision=lax.Precision.HIGHEST, preferred_element_type=F32)
        for kind in range(3)
    ]

    if make_table:
        tap_row = lax.broadcasted_iota(jnp.int32, (length, 2 * length), 0)
        place = lax.broadcasted_iota(jnp.int32, (length, 2 * length), 1)
        turned = jnp.where(tap_row + place == length, 1.0, 0.0).astype(BF16)
        base = jnp.dot(medium_ref[...].astype(BF16), turned, preferred_element_type=F32)
        for group in range(groups):
            spread = jnp.broadcast_to(base[group : group + 1, :], (length, 2 * length))
            rolled = pltpu.roll(spread, 0, 1, stride=1, stride_axis=0)
            table[group * length : (group + 1) * length, :] = rolled.astype(BF16)

    def featured(kind, start):
        total = weights[kind][0:1, :] * wide[kind, start : start + length, :]
        for tap in range(1, taps):
            total = total + weights[kind][tap : tap + 1, :] * wide[kind, start - tap : start - tap + length, :]
        return total

    for block in range(count // length + 1):
        start = LEAD + block * length
        product[block * length : (block + 1) * length, :] = (
            featured(1, start) * featured(2, start)
        ).astype(BF16)

    group_of = lax.broadcasted_iota(jnp.int32, (length, 2 * LANES), 1) % LANES // GROUP_SIZE
    for pair in range(count // (2 * length)):
        begin = pair * 2 * length
        window = jnp.concatenate(
            [
                product[begin : begin + 2 * length, :],
                product[begin + length : begin + 3 * length, :],
            ],
            axis=1,
        )
        spread = jnp.dot(table[...], window, preferred_element_type=F32)
        mixed = spread[:length]
        for group in range(1, groups):
            mixed = jnp.where(group_of == group, spread[group * length : (group + 1) * length], mixed)
        for part in range(2):
            row = begin + part * length
            direct = skip_ref[...] * product[row + length : row + 2 * length, :].astype(F32)
            gate = featured(0, halo_rows + row)
            store(row, (gate * (mixed[:, part * LANES : (part + 1) * LANES] + direct)).astype(BF16))


def gated_kernel(first_row, loads, *refs):
    head, rest = refs[1:4], refs[4:]
    halo_ref, rest = (rest[0], rest[1:]) if first_row == 0 else (None, rest)
    rows_ref, rest = rest[0], rest[1:]
    if loads:
        weight, out_ref, held, table, wide, product, sems = rest
        parts = sems.shape[0]
        height = weight.shape[0] // parts

        def copy_of(part):
            span = pl.ds(pl.multiple_of(part * height, height), height)
            return pltpu.make_async_copy(weight.at[span, :], held.at[span, :], sems.at[part])

        copy_of(pl.program_id(0)).start()
    elif first_row == 0:
        table, out_ref, wide, product = rest
    else:
        out_ref, table, wide, product = rest

    def store(row, value):
        out_ref[row : row + value.shape[0], :] = value

    make_table = first_row > 0
    filter_tile(first_row, pl.program_id(0), *head, halo_ref, rows_ref, wide, product, table, make_table, store)
    if loads:

        @pl.when(pl.program_id(0) == pl.num_programs(0) - 1)
        def _():
            for part in range(parts):
                copy_of(part).wait()


def gated_chunk(meta, features, halo, first_row, count, short_filter, medium_rows, skip, weight, tables):
    kinds, rows, channels = features.shape
    length = medium_rows.shape[1]
    groups = LANES // GROUP_SIZE
    loads = weight is not None
    in_hbm = lambda x: pltpu.with_memory_space_constraint(x, pltpu.HBM)
    table_spec = pl.BlockSpec((groups * length, 2 * length), lambda i: (i, 0))
    in_specs = [
        pl.BlockSpec(memory_space=pltpu.SMEM),
        pl.BlockSpec(short_filter.shape, lambda i: (0, 0, 0)),
        pl.BlockSpec((groups, length), lambda i: (i, 0)),
        pl.BlockSpec((1, LANES), lambda i: (0, i)),
    ]
    operands = [meta, in_hbm(short_filter), in_hbm(medium_rows), in_hbm(skip)]
    out_specs = [pl.BlockSpec((count, LANES), lambda i: (0, i))]
    out_shape = [jax.ShapeDtypeStruct((count, channels), BF16)]
    scratch = [
        pltpu.VMEM((kinds, length + LEAD + count, LANES), F32),
        pltpu.VMEM((length + count, LANES), BF16),
    ]
    if first_row == 0:
        in_specs.append(pl.BlockSpec((kinds, length + LEAD, LANES), lambda i: (0, 0, i)))
        in_specs.append(pl.BlockSpec((kinds, count, LANES), lambda i: (0, 0, i)))
        in_specs.append(table_spec)
        operands += [halo, features, tables]
    else:
        in_specs.append(pl.BlockSpec((kinds, rows, LANES), lambda i: (0, 0, i)))
        operands.append(features)
        if loads:
            in_specs.append(pl.BlockSpec(memory_space=pltpu.HBM))
            operands.append(in_hbm(weight))
            out_specs.append(pl.BlockSpec(memory_space=pltpu.VMEM))
            out_shape.append(pltpu.VMEM(weight.shape, weight.dtype))
            scratch.append(pltpu.SemaphoreType.DMA((channels // LANES,)))
        out_specs.append(table_spec)
        out_shape.append(jax.ShapeDtypeStruct((channels // GROUP_SIZE * length, 2 * length), BF16))
    return pl.pallas_call(
        functools.partial(gated_kernel, first_row, loads),
        grid=(channels // LANES,),
        in_specs=in_specs,
        out_specs=out_specs,
        out_shape=out_shape,
        scratch_shapes=scratch,
        compiler_params=pltpu.CompilerParams(vmem_limit_bytes=16 * MIB),
        name="hyena_filters",
    )(*operands)


def vmem_call(body, name, micros, scalars, operands, outs, scratch=(), waits=()):
    given = 1 + len(operands)
    run = lambda *refs: body(*refs[:given], *refs[given + len(waits) :])
    return pl.pallas_call(
        run,
        in_specs=[pl.BlockSpec(memory_space=pltpu.SMEM)]
        + [pl.BlockSpec(memory_space=pltpu.VMEM)] * (len(operands) + len(waits)),
        out_specs=[pl.BlockSpec(memory_space=pltpu.VMEM)] * len(outs),
        out_shape=[jax.ShapeDtypeStruct(shape, kind) for shape, kind in outs],
        scratch_shapes=list(scratch),
        compiler_params=pltpu.CompilerParams(vmem_limit_bytes=20 * MIB),
        cost_estimate=lasting(micros) if micros else None,
        name=name,
    )(scalars, *operands, *waits)


def columns_kernel(pieces, meta_ref, upper, lower, weight, *outs):
    gated = jnp.concatenate([upper[...], lower[...]], axis=0)
    width = weight.shape[1] // 8
    for owner, half, out, part in pieces:
        columns = pl.ds(pl.multiple_of((2 * meta_ref[owner] + half) * width, width), width)
        term = jnp.dot(gated, weight[:, columns], preferred_element_type=F32)
        outs[out][:, part * width : (part + 1) * width] = term.astype(BF16)


def column_terms(meta, upper, lower, weight, pieces, waits=()):
    rows, width = 2 * upper.shape[0], weight.shape[1] // 8
    outs = [((rows, width * sum(p[2] == out for p in pieces)), BF16) for out in range(pieces[-1][2] + 1)]
    body = functools.partial(columns_kernel, pieces)
    return vmem_call(body, "hyena_terms", None, meta, [upper, lower, weight], outs, waits=waits)


def load_kernel(source, _, held, sem):
    copy = pltpu.make_async_copy(source, held, sem)
    copy.start()
    copy.wait()


def load(weight, after):
    return pl.pallas_call(
        load_kernel,
        in_specs=[pl.BlockSpec(memory_space=pltpu.HBM), pl.BlockSpec(memory_space=pltpu.VMEM)],
        out_specs=pl.BlockSpec(memory_space=pltpu.VMEM),
        out_shape=pltpu.VMEM(weight.shape, weight.dtype),
        scratch_shapes=[pltpu.SemaphoreType.DMA],
        compiler_params=pltpu.CompilerParams(vmem_limit_bytes=4 * MIB),
        name="load_weight",
    )(pltpu.with_memory_space_constraint(weight, pltpu.HBM), after)


def stream_kernel(_, kept, direct_x, direct_y, late_x, late_y, residual, *parts):
    half = late_x.shape[1]
    rows = parts[0].shape[0]
    for index, out in enumerate(parts):
        span = slice(index * rows, (index + 1) * rows)
        wide = lambda ref: ref[span].astype(F32)
        left = wide(residual)[:, :half] + (wide(kept)[:, :half] + wide(direct_x) + wide(late_y))
        right = wide(residual)[:, half:] + (wide(kept)[:, half:] + wide(direct_y) + wide(late_x))
        out[...] = jnp.concatenate([left, right], axis=1).astype(BF16)


def near_kernel(meta_ref, *refs):
    blocks, (gain, weight, total, square) = refs[:3], refs[3:]
    channels = blocks[0].shape[1]
    squares = jnp.zeros(square.shape, F32)
    result = None
    for index in range(3):
        wide = blocks[index][...].astype(F32)
        squares = squares + jnp.sum(wide * wide, axis=1, keepdims=True)
        span = pl.ds(pl.multiple_of(meta_ref[index] * channels, channels), channels)
        factor, block = gain[:, span], weight[span, :]
        term = jnp.dot((wide * factor).astype(BF16), block, preferred_element_type=F32)
        result = term if result is None else result + term
    total[...] = result
    square[...] = squares


def far_kernel(chips, meta_ref, diag_a, diag_b, near, square, gain, cosine, sine, weight, *rest):
    outs, total = rest[:chips], rest[chips]
    channels = diag_a.shape[1]
    wide = jnp.concatenate([diag_a[...], diag_b[...]], axis=0).astype(F32)
    squares = square[...] + jnp.sum(wide * wide, axis=1, keepdims=True)
    span = pl.ds(pl.multiple_of(meta_ref[3] * channels, channels), channels)
    factor, block = gain[:, span], weight[span, :]
    total[...] = near[...] + jnp.dot((wide * factor).astype(BF16), block, preferred_element_type=F32)
    inverse = lax.rsqrt(squares / (4 * channels) + norm_eps)
    for distance, out in enumerate(outs):
        head = lax.rem(meta_ref[4] + distance, chips)
        for kind in range(3):
            column = pl.multiple_of((head * 3 + kind) * HEAD, HEAD)
            part = total[:, pl.ds(column, HEAD)] * inverse
            if kind < 2:
                part = part * cosine[...] + pltpu.roll(part, HEAD // 2, 1) * sine[...]
            if kind == 0:
                part = part * SCORE_SCALE
            if kind == 2:
                tiles = [part[row : row + HEAD].T for row in range(0, part.shape[0], HEAD)]
                part = jnp.concatenate(tiles, axis=0)
            out[kind] = part.astype(BF16)


def gather_keys(chips, meta_ref, own, other, keys, values):
    rows = own[0].shape[1]
    for distance in range(chips):
        place = lax.rem(meta_ref[4] - distance + chips, chips)
        for chunk, stacked in enumerate(other):
            mine = own[chunk * chips + distance]
            span = slice(chunk * rows, (chunk + 1) * rows)
            keys[0, place, span, :] = mine[1]
            keys[1, place, span, :] = stacked[distance, 0]
            for tile in range(rows // HEAD):
                first = chunk * rows + tile * HEAD
                taken = slice(tile * HEAD, (tile + 1) * HEAD)
                values[0, place, :, first : first + HEAD] = mine[2, taken, :]
                values[1, place, :, first : first + HEAD] = stacked[distance, 1, taken, :]


def attention_kernel(chips, chunks, distance, leading, meta_ref, *refs):
    if leading:
        pieces, other = refs[: chunks * chips], refs[chunks * chips : chunks * (chips + 1)]
        out, keys, values = refs[chunks * (chips + 1) :]
        gather_keys(chips, meta_ref, pieces, other, keys, values)
        source = pieces[(chips - distance) % chips :: chips]
    else:
        source, (keys, values), out = refs[:chunks], refs[chunks : chunks + 2], refs[-1]
    chip, core = meta_ref[4], meta_ref[5]
    count = keys.shape[2]

    def scores_of(side, place, queries):
        return lax.dot_general(
            keys[side, place], queries, (((1,), (1,)), ((), ())), preferred_element_type=F32
        )

    def update(state, mine, others, place):
        top, total, acc = state
        new_top = jnp.maximum(jnp.max(mine, axis=0, keepdims=True), jnp.max(others, axis=0, keepdims=True))
        if top is not None:
            new_top = jnp.maximum(new_top, top)
        mine = jnp.exp2(mine - new_top)
        others = jnp.exp2(others - new_top)
        gained = jnp.sum(mine, axis=0, keepdims=True) + jnp.sum(others, axis=0, keepdims=True)
        added = jnp.dot(values[0, place], mine.astype(BF16), preferred_element_type=F32)
        added = added + jnp.dot(values[1, place], others.astype(BF16), preferred_element_type=F32)
        if top is None:
            return new_top, gained, added
        shrink = jnp.exp2(top - new_top)
        return new_top, total * shrink + gained, acc * shrink + added

    key_row = lax.broadcasted_iota(jnp.int32, (count, count), 0)
    query_column = lax.broadcasted_iota(jnp.int32, (count, count), 1)
    place = lax.rem(chip + distance, chips)
    queries = jnp.concatenate([piece[0] for piece in source], axis=0)
    mine = jnp.where(key_row <= query_column, scores_of(0, place, queries), -1e30)
    others = jnp.where(core == 1, scores_of(1, place, queries), -1e30)
    state = update((None, None, None), mine, others, place)

    def earlier(index, state):
        return update(state, scores_of(0, index, queries), scores_of(1, index, queries), index)

    state = lax.fori_loop(0, place, earlier, state)
    out[...] = (state[2] / state[1]).T.astype(BF16)


def attend(meta, own, other, laid, distance, after, chips):
    chunks, leading = len(other), laid is None
    count = own[0].shape[1] * chunks
    outs = [((count, HEAD), BF16)]
    if leading:
        operands = own + other
        outs += [((2, chips, count, HEAD), BF16), ((2, chips, HEAD, count), BF16)]
    else:
        operands = [*own[(chips - distance) % chips :: chips], *laid, *after]
    body = functools.partial(attention_kernel, chips, chunks, distance, leading)
    out, *made = vmem_call(body, "attention", 3, meta, operands, outs)
    return out, laid or made


def pick_kernel(chips, meta_ref, weight, *refs):
    *near, own, sems = refs
    channels = own.shape[1]
    columns = [pl.ds(pl.multiple_of(meta_ref[index] * channels, channels), channels) for index in range(4)]
    copies = [pltpu.make_async_copy(weight.at[:, columns[0]], own, sems.at[0])]
    for index, out in enumerate(near):
        for head in range(chips // 2):
            rows = pl.ds(pl.multiple_of((2 * head + meta_ref[5]) * HEAD, HEAD), HEAD)
            target = out.at[head * HEAD : (head + 1) * HEAD]
            sem = sems.at[1 + index * (chips // 2) + head]
            copies.append(pltpu.make_async_copy(weight.at[rows, columns[index + 1]], target, sem))
    for copy in copies:
        copy.start()
    for copy in copies:
        copy.wait()


def pick_weights(meta, weight, chips, channels):
    rows = weight.shape[0]
    near = jax.ShapeDtypeStruct((rows // 2, channels), BF16)
    return pl.pallas_call(
        functools.partial(pick_kernel, chips),
        in_specs=[
            pl.BlockSpec(memory_space=pltpu.SMEM),
            pl.BlockSpec(memory_space=pltpu.HBM),
        ],
        out_specs=[pl.BlockSpec(memory_space=pltpu.VMEM)] * 4,
        out_shape=[near, near, near, jax.ShapeDtypeStruct((rows, channels), BF16)],
        scratch_shapes=[pltpu.SemaphoreType.DMA((1 + 3 * (chips // 2),))],
        compiler_params=pltpu.CompilerParams(vmem_limit_bytes=4 * MIB),
        name="pick_weights",
    )(meta, pltpu.with_memory_space_constraint(weight, pltpu.HBM))


def mix_kernel(chips, distances, streams, meta_ref, *refs):
    heads, refs = refs[:4], refs[4:]
    before, (own_w, *others_w), (out, ordered) = refs[:streams], refs[streams:-2], refs[-2:]
    near_w, far_w = others_w[:3], others_w[3:]
    chip, core = meta_ref[4], meta_ref[5]
    parity = lax.rem(chip + distances[0], 2)
    for index, distance in enumerate(distances):
        head = lax.rem(chip - distance + chips, chips)
        column = pl.ds(pl.multiple_of(head // 2 * HEAD, HEAD), HEAD)
        for source in range(4):
            ordered[source, :, column] = heads[source][index]
    mine = jnp.concatenate(
        [own_w[pl.ds(pl.multiple_of((2 * j + parity) * HEAD, HEAD), HEAD), :] for j in range(chips // 2)], axis=0
    )

    def finish(weights):
        total = jnp.dot(ordered[0], mine, preferred_element_type=F32)
        for source in range(3):
            total = total + jnp.dot(ordered[source + 1], weights[source][...], preferred_element_type=F32)
        total = total + jnp.concatenate([part[...].astype(F32) for part in before], axis=0)
        out[...] = total.astype(out.dtype)

    @pl.when(core == parity)
    def _():
        finish(near_w)

    @pl.when(core != parity)
    def _():
        finish(far_w)


def mix(meta, heads, distances, before, own_w, near_w, far_w, kind, chips):
    rows, channels = heads[0].shape[1], own_w.shape[1]
    body = functools.partial(mix_kernel, chips, distances, len(before))
    operands = [*heads, *before, own_w, *near_w, *far_w]
    scratch = [pltpu.VMEM((4, rows, chips // 2 * HEAD), BF16)]
    return vmem_call(body, "attention_mix", 2.5, meta, operands, [((rows, channels), kind)], scratch)[0]


def rotate_rows(block, positions):
    half_size = block.shape[-1] // 2
    frequency = 10000.0 ** (-jnp.arange(half_size, dtype=jnp.float32) * 2.0 / block.shape[-1])
    angles = positions.astype(jnp.float32)[:, None] * frequency[None, :]
    cosine = jnp.cos(angles)[:, None, :]
    sine_part = jnp.sin(angles)[:, None, :]
    first_half = block[..., :half_size]
    second_half = block[..., half_size:]
    return jnp.concatenate(
        [
            first_half * cosine - second_half * sine_part,
            second_half * cosine + first_half * sine_part,
        ],
        axis=-1,
    )


def run_attention(queries, query_pos, key_rows, value_rows, position_of):
    head_count = queries.shape[1]
    row_count = queries.shape[0]
    head_size = queries.shape[2]
    scale_factor = 1.0 / head_size**0.5
    last_query = jnp.max(query_pos)
    initial = (
        jnp.zeros((head_count, row_count, head_size), jnp.float32),
        jnp.full((head_count, row_count), -1e30, jnp.float32),
        jnp.zeros((head_count, row_count), jnp.float32),
    )
    piece_keys = lax.all_gather(key_rows, "ctx", axis=0, tiled=True)
    piece_values = lax.all_gather(value_rows, "ctx", axis=0, tiled=True)
    piece_rows = piece_keys.shape[0]
    block_rows = 512

    def one_block(state_in, block_index):
        first_block = block_index * block_rows
        key_block = lax.dynamic_slice_in_dim(piece_keys, first_block, block_rows, 0)
        value_block = lax.dynamic_slice_in_dim(piece_values, first_block, block_rows, 0)
        key_pos = position_of(first_block + jnp.arange(block_rows))

        def update(state_old):
            acc_sum, run_max, run_total = state_old
            scores = (
                jnp.einsum("thd,khd->htk", queries, key_block, preferred_element_type=jnp.float32)
                * scale_factor
            )
            causal = (key_pos[None, :] <= query_pos[:, None])[None]
            block_max = jnp.max(jnp.where(causal, scores, -1e30), axis=-1)
            new_max = jnp.maximum(run_max, block_max)
            weights = jnp.where(causal, jnp.exp(scores - new_max[..., None]), 0.0)
            correction = jnp.exp(run_max - new_max)
            new_total = run_total * correction + jnp.sum(weights, axis=-1)
            update_sum = jnp.einsum(
                "htk,khd->htd",
                weights.astype(jnp.bfloat16),
                value_block,
                preferred_element_type=jnp.float32,
            )
            return (acc_sum * correction[..., None] + update_sum, new_max, new_total)

        def unchanged(state_old):
            return state_old

        state_out = lax.cond(jnp.min(key_pos) > last_query, unchanged, update, state_in)
        return (state_out, None)

    state_end, unused = lax.scan(one_block, initial, jnp.arange(piece_rows // block_rows))
    acc_sum, run_max, run_total = state_end
    output = acc_sum / run_total[..., None]
    return jnp.transpose(output, (1, 0, 2)).astype(jnp.bfloat16)


def after_gating(gated, residual_in, out_weight, norm_gain, attn_weight, attn_out):
    tok_rows, chan_count = gated.shape
    hyena_terms = jnp.dot(gated, out_weight, preferred_element_type=jnp.float32)
    hyena_out = lax.psum_scatter(
        hyena_terms.astype(jnp.bfloat16), "ch", scatter_dimension=1, tiled=True
    ).astype(jnp.float32)
    stream = (residual_in.astype(jnp.float32) + hyena_out).astype(jnp.bfloat16)
    stream_wide = stream.astype(jnp.float32)
    full_width = chan_count * lax.axis_size("ch")
    head_cols = attn_weight.shape[1]
    square_total = lax.psum(jnp.sum(stream_wide * stream_wide, axis=1), "ch")
    inverse = lax.rsqrt(square_total / full_width + norm_eps)
    gain_part = lax.dynamic_slice_in_dim(norm_gain, lax.axis_index("ch") * chan_count, chan_count)
    normed = (stream_wide * inverse[:, None] * gain_part[None, :]).astype(jnp.bfloat16)
    projected = jnp.dot(
        lax.all_gather(normed, "ch", axis=1, tiled=True),
        attn_weight,
        preferred_element_type=jnp.float32,
    )
    head_count = head_cols // (3 * HEAD)
    projected = projected.reshape(tok_rows, head_count, 3, HEAD)
    ctx_index = lax.axis_index("ctx")
    positions = ctx_index * tok_rows + jnp.arange(tok_rows, dtype=jnp.int32)
    queries = rotate_rows(projected[:, :, 0, :], positions).astype(jnp.bfloat16)
    key_rows = rotate_rows(projected[:, :, 1, :], positions).astype(jnp.bfloat16)
    value_rows = projected[:, :, 2, :].astype(jnp.bfloat16)

    def position_of(global_row):
        return global_row

    attended = run_attention(queries, positions, key_rows, value_rows, position_of)
    head_terms = jnp.dot(
        attended.reshape(tok_rows, head_count * HEAD), attn_out, preferred_element_type=jnp.float32
    )
    attn_mix = lax.psum_scatter(
        head_terms.astype(jnp.bfloat16), "ch", scatter_dimension=1, tiled=True
    ).astype(jnp.float32)
    return (stream_wide + attn_mix).astype(jnp.bfloat16)


def rotation_tables(positions):
    half_size = HEAD // 2
    frequency = 10000.0 ** (-jnp.arange(half_size, dtype=F32) * 2.0 / HEAD)
    angles = positions.astype(F32)[:, None] * frequency[None, :]
    cosine, sine = jnp.cos(angles), jnp.sin(angles)
    return jnp.concatenate([cosine, cosine], axis=1), jnp.concatenate([-sine, sine], axis=1)


def shards(
    features,
    residual_in,
    short_filter,
    medium_filter,
    skip_gain,
    out_weight,
    norm_gain,
    attn_weight,
    attn_out,
):
    rows, _, channels = features.shape
    chips = lax.axis_size("ctx") // 2
    length = medium_filter.shape[0]
    chunk = rows // 2
    ctx, ch = lax.axis_index("ctx"), lax.axis_index("ch")
    scalars = [ch, ch ^ 1, ch ^ 2, ch ^ 3, ctx // 2, ctx % 2, ctx * rows, ctx]
    meta = jnp.stack(scalars).astype(jnp.int32)

    by_kind = jnp.transpose(features, (1, 0, 2))
    count = lax.axis_size("ctx")
    halo = lax.ppermute(by_kind[:, rows - length - LEAD :], "ctx", [(i, i + 1) for i in range(count - 1)])
    medium_rows = medium_filter.T
    skip = skip_gain.reshape(1, channels)

    starts = [rows - chunk, 0]
    if lax.axis_size("ch") != 4 or attn_weight.shape[1] != 3 * HEAD * chips or chips % 2:
        lower, tables = gated_chunk(meta, by_kind, halo, chunk, chunk, short_filter, medium_rows, skip, None, None)
        (upper,) = gated_chunk(meta, by_kind, halo, 0, chunk, short_filter, medium_rows, skip, None, tables)
        return after_gating(
            jnp.concatenate([upper, lower], axis=0), residual_in, out_weight, norm_gain, attn_weight, attn_out
        )

    gain = norm_gain.reshape(1, -1)
    cosine, sine = rotation_tables(meta[6:7] + jnp.arange(rows, dtype=jnp.int32))

    *near_w, own_w = pick_weights(meta, attn_out, chips, channels)
    near_w = [swap_ch(weight, mask) for mask, weight in zip((1, 2, 3), near_w)]
    far_w = [swap_core(weight) for weight in near_w]

    lower, out_held, tables = gated_chunk(
        meta, by_kind, halo, chunk, chunk, short_filter, medium_rows, skip, out_weight, None
    )
    (upper,) = gated_chunk(meta, by_kind, halo, 0, chunk, short_filter, medium_rows, skip, None, tables)
    across_x, across_y = column_terms(meta, upper, lower, out_held, ((3, 0, 0, 0), (3, 1, 1, 0)))
    across_x, across_y = swap_ch(across_x, 1), swap_ch(across_y, 2)
    pieces = ((1, 0, 0, 0), (2, 1, 1, 0), (1, 1, 2, 0), (2, 0, 3, 0), (0, 0, 4, 0), (0, 1, 4, 1))
    direct_x, direct_y, along_x, along_y, kept = column_terms(meta, upper, lower, out_held, pieces, near_w)
    direct_x, direct_y = swap_ch(direct_x, 1), swap_ch(direct_y, 2)
    along_x = (along_x.astype(F32) + across_y.astype(F32)).astype(BF16)
    along_y = (along_y.astype(F32) + across_x.astype(F32)).astype(BF16)
    late_x, late_y = swap_ch(along_x, 1), swap_ch(along_y, 2)
    qkv_held = load(attn_weight, along_y)
    parts = vmem_call(
        stream_kernel,
        "add_stream",
        1,
        meta,
        [kept, direct_x, direct_y, late_x, late_y, residual_in],
        [((chunk, channels), BF16)] * 2,
        waits=[qkv_held, *far_w],
    )

    own, other, after = [], [], None
    width = attn_weight.shape[1]
    for start in starts:
        part = parts[start // chunk]
        if after is not None:
            part, _ = lax.optimization_barrier((part, after))
        by_x, by_y = swap_ch(part, 1), swap_ch(part, 2)
        after = by_x[: chunk // 2], by_y[chunk // 2 :]
        diag_a, diag_b = swap_ch(after[0], 2), swap_ch(after[1], 1)
        near, square = vmem_call(
            near_kernel,
            "qkv_near",
            3,
            meta,
            [part, by_x, by_y, gain, qkv_held],
            [((chunk, width), F32), ((chunk, LANES), F32)],
        )
        turn = slice(start, start + chunk)
        outs = vmem_call(
            functools.partial(far_kernel, chips),
            "qkv_far",
            2,
            meta,
            [diag_a, diag_b, near, square, gain, cosine[turn], sine[turn], qkv_held],
            [((3, chunk, HEAD), BF16)] * chips,
            [pltpu.VMEM((chunk, width), F32)],
        )
        arrived = [outs[0]] + [rotate_chips(outs[d], d) for d in range(1, chips)]
        own.append(arrived)

    own, _ = lax.optimization_barrier((own, outs))
    other = [swap_core(jnp.stack([piece[1:] for piece in arrived])) for arrived in own]
    own, other = own[1] + own[0], other[::-1]

    laid, before, backs = None, parts, []
    groups = [(*range(2, chips, 2), 0), tuple(range(1, chips, 2))]
    for distances in groups:
        back = []
        for distance in distances:
            after = backs if distance == chips - 1 else []
            piece, laid = attend(meta, own, other, laid, distance, after, chips)
            back.append(rotate_chips(piece, distance) if distance else piece)
        backs.append(jnp.stack(back))
    for group, (distances, kind) in enumerate(zip(groups, [F32, BF16])):
        by_x, by_y = swap_ch(backs[group], 1), swap_ch(backs[group], 2)
        by_both = swap_ch(by_x, 2) if group == 0 else swap_ch(by_y, 1)
        heads = [backs[group], by_x, by_y, by_both]
        before = [mix(meta, heads, distances, before, own_w, near_w, far_w, kind, chips)]
    return before[0]


def solution(mesh):
    in_specs = (
        P("ctx", None, "ch"),
        P("ctx", "ch"),
        P(None, None, "ch"),
        P(None, "ch"),
        P("ch"),
        P("ch", None),
        P(),
        P(None, "ch"),
        P("ch", None),
    )
    out_specs = P("ctx", "ch")
    return jax.shard_map(shards, mesh=mesh, in_specs=in_specs, out_specs=out_specs, check_vma=False)
```

```python
import functools

import jax
import jax.numpy as jnp
from jax import lax
from jax.experimental import pallas as pl
from jax.experimental.pallas import tpu as pltpu
from jax.sharding import PartitionSpec as P

HEAD = 128
GROUP_SIZE = 16
LANES = 128
LEAD = 16
norm_eps = 1e-05
SCORE_SCALE = 1.4426950408889634 / HEAD**0.5
MIB = 1024 * 1024
F32 = jnp.float32
BF16 = jnp.bfloat16


def lasting(micros):
    return pl.CostEstimate(
        flops=int(micros * 1.1e9), transcendentals=0, bytes_accessed=int(micros * 3.6e6)
    )


def swap_ch(value, mask):
    count = lax.axis_size("ch")
    return lax.ppermute(value, "ch", [(i, i ^ mask) for i in range(count)])


def swap_core(value):
    count = lax.axis_size("ctx")
    return lax.ppermute(value, "ctx", [(i, i ^ 1) for i in range(count)])


def shift_rows(value):
    count = lax.axis_size("ctx")
    return lax.ppermute(value, "ctx", [(i, i + 1) for i in range(count - 1)])


def rotate_chips(value, distance):
    count = lax.axis_size("ctx")
    return lax.ppermute(value, "ctx", [(i, (i + 2 * distance) % count) for i in range(count)])


def filter_tile(first_row, tile, short_ref, medium_ref, skip_ref, halo_ref, rows_ref, wide, product, table, store):
    taps, groups_all = short_ref.shape[1:]
    groups, length = medium_ref.shape
    span = wide.shape[1]
    halo_rows = length + LEAD
    count = span - halo_rows

    for kind in range(3):
        if first_row == 0:
            wide[kind, :halo_rows] = halo_ref[kind].astype(F32)
            wide[kind, halo_rows:] = rows_ref[kind].astype(F32)
        else:
            wide[kind] = rows_ref[kind, first_row - halo_rows : first_row + count].astype(F32)

    group_row = lax.broadcasted_iota(jnp.int32, (groups_all, LANES), 0)
    group_col = lax.broadcasted_iota(jnp.int32, (groups_all, LANES), 1) // GROUP_SIZE + tile * groups
    chosen = jnp.where(group_row == group_col, 1.0, 0.0).astype(F32)
    weights = [
        jnp.dot(short_ref[kind], chosen, precision=lax.Precision.HIGHEST, preferred_element_type=F32)
        for kind in range(3)
    ]

    tap_row = lax.broadcasted_iota(jnp.int32, (length, 2 * length), 0)
    place = lax.broadcasted_iota(jnp.int32, (length, 2 * length), 1)
    turned = jnp.where(tap_row + place == length, 1.0, 0.0).astype(BF16)
    base = jnp.dot(medium_ref[...].astype(BF16), turned, preferred_element_type=F32)
    for group in range(groups):
        spread = jnp.broadcast_to(base[group : group + 1, :], (length, 2 * length))
        rolled = pltpu.roll(spread, 0, 1, stride=1, stride_axis=0)
        table[group * length : (group + 1) * length, :] = rolled.astype(BF16)

    def featured(kind, start):
        total = weights[kind][0:1, :] * wide[kind, start : start + length, :]
        for tap in range(1, taps):
            total = total + weights[kind][tap : tap + 1, :] * wide[kind, start - tap : start - tap + length, :]
        return total

    for block in range(count // length + 1):
        start = LEAD + block * length
        product[block * length : (block + 1) * length, :] = (
            featured(1, start) * featured(2, start)
        ).astype(BF16)

    group_of = lax.broadcasted_iota(jnp.int32, (length, 2 * LANES), 1) % LANES // GROUP_SIZE
    for pair in range(count // (2 * length)):
        begin = pair * 2 * length
        window = jnp.concatenate(
            [
                product[begin : begin + 2 * length, :],
                product[begin + length : begin + 3 * length, :],
            ],
            axis=1,
        )
        spread = jnp.dot(table[...], window, preferred_element_type=F32)
        mixed = spread[:length]
        for group in range(1, groups):
            mixed = jnp.where(group_of == group, spread[group * length : (group + 1) * length], mixed)
        for part in range(2):
            row = begin + part * length
            direct = skip_ref[...] * product[row + length : row + 2 * length, :].astype(F32)
            gate = featured(0, halo_rows + row)
            store(row, (gate * (mixed[:, part * LANES : (part + 1) * LANES] + direct)).astype(BF16))


def gated_kernel(first_row, loads, *refs):
    head, rest = refs[1:4], refs[4:]
    halo_ref, rest = (rest[0], rest[1:]) if first_row == 0 else (None, rest)
    rows_ref, rest = rest[0], rest[1:]
    if loads:
        weight, out_ref, held, wide, product, table, sems = rest
        parts = sems.shape[0]
        height = weight.shape[0] // parts

        def copy_of(part):
            span = pl.ds(pl.multiple_of(part * height, height), height)
            return pltpu.make_async_copy(weight.at[span, :], held.at[span, :], sems.at[part])

        copy_of(pl.program_id(0)).start()
    else:
        out_ref, wide, product, table = rest

    def store(row, value):
        out_ref[row : row + value.shape[0], :] = value

    filter_tile(first_row, pl.program_id(0), *head, halo_ref, rows_ref, wide, product, table, store)
    if loads:

        @pl.when(pl.program_id(0) == pl.num_programs(0) - 1)
        def _():
            for part in range(parts):
                copy_of(part).wait()


def gated_chunk(meta, features, halo, first_row, count, short_filter, medium_rows, skip, weight=None):
    kinds, rows, channels = features.shape
    length = medium_rows.shape[1]
    groups = LANES // GROUP_SIZE
    loads = weight is not None
    in_hbm = lambda x: pltpu.with_memory_space_constraint(x, pltpu.HBM)
    in_specs = [
        pl.BlockSpec(memory_space=pltpu.SMEM),
        pl.BlockSpec(short_filter.shape, lambda i: (0, 0, 0)),
        pl.BlockSpec((groups, length), lambda i: (i, 0)),
        pl.BlockSpec((1, LANES), lambda i: (0, i)),
    ]
    operands = [meta, in_hbm(short_filter), in_hbm(medium_rows), in_hbm(skip)]
    out_specs = [pl.BlockSpec((count, LANES), lambda i: (0, i))]
    out_shape = [jax.ShapeDtypeStruct((count, channels), BF16)]
    scratch = [
        pltpu.VMEM((kinds, length + LEAD + count, LANES), F32),
        pltpu.VMEM((length + count, LANES), BF16),
        pltpu.VMEM((groups * length, 2 * length), BF16),
    ]
    if first_row == 0:
        in_specs.append(pl.BlockSpec((kinds, length + LEAD, LANES), lambda i: (0, 0, i)))
        in_specs.append(pl.BlockSpec((kinds, count, LANES), lambda i: (0, 0, i)))
        operands += [halo, features]
    else:
        in_specs.append(pl.BlockSpec((kinds, rows, LANES), lambda i: (0, 0, i)))
        operands.append(features)
    if loads:
        in_specs.append(pl.BlockSpec(memory_space=pltpu.HBM))
        operands.append(in_hbm(weight))
        out_specs.append(pl.BlockSpec(memory_space=pltpu.VMEM))
        out_shape.append(pltpu.VMEM(weight.shape, weight.dtype))
        scratch.append(pltpu.SemaphoreType.DMA((channels // LANES,)))
    return pl.pallas_call(
        functools.partial(gated_kernel, first_row, loads),
        grid=(channels // LANES,),
        in_specs=in_specs,
        out_specs=out_specs,
        out_shape=out_shape,
        scratch_shapes=scratch,
        compiler_params=pltpu.CompilerParams(vmem_limit_bytes=16 * MIB),
        name="hyena_filters",
    )(*operands)


def vmem_call(body, name, micros, scalars, operands, outs, scratch=(), waits=()):
    given = 1 + len(operands)
    run = lambda *refs: body(*refs[:given], *refs[given + len(waits) :])
    return pl.pallas_call(
        run,
        in_specs=[pl.BlockSpec(memory_space=pltpu.SMEM)]
        + [pl.BlockSpec(memory_space=pltpu.VMEM)] * (len(operands) + len(waits)),
        out_specs=[pl.BlockSpec(memory_space=pltpu.VMEM)] * len(outs),
        out_shape=[jax.ShapeDtypeStruct(shape, kind) for shape, kind in outs],
        scratch_shapes=list(scratch),
        compiler_params=pltpu.CompilerParams(vmem_limit_bytes=20 * MIB),
        cost_estimate=lasting(micros) if micros else None,
        name=name,
    )(scalars, *operands, *waits)


def columns_kernel(pieces, meta_ref, upper, lower, weight, *outs):
    gated = jnp.concatenate([upper[...], lower[...]], axis=0)
    width = weight.shape[1] // 8
    for owner, half, out, part in pieces:
        columns = pl.ds(pl.multiple_of((2 * meta_ref[owner] + half) * width, width), width)
        term = jnp.dot(gated, weight[:, columns], preferred_element_type=F32)
        outs[out][:, part * width : (part + 1) * width] = term.astype(BF16)


def column_terms(meta, upper, lower, weight, pieces, waits=()):
    rows, width = 2 * upper.shape[0], weight.shape[1] // 8
    outs = [((rows, width * sum(p[2] == out for p in pieces)), BF16) for out in range(pieces[-1][2] + 1)]
    body = functools.partial(columns_kernel, pieces)
    return vmem_call(body, "hyena_terms", None, meta, [upper, lower, weight], outs, waits=waits)


def load_kernel(meta_ref, source, outer, _, held, own, sems):
    channels = own.shape[1]
    columns = pl.ds(pl.multiple_of(meta_ref[0] * channels, channels), channels)
    copies = [
        pltpu.make_async_copy(source, held, sems.at[0]),
        pltpu.make_async_copy(outer.at[:, columns], own, sems.at[1]),
    ]
    for copy in copies:
        copy.start()
    for copy in copies:
        copy.wait()


def load(meta, weight, outer, after, channels):
    in_hbm = lambda x: pltpu.with_memory_space_constraint(x, pltpu.HBM)
    hbm, vmem = pl.BlockSpec(memory_space=pltpu.HBM), pl.BlockSpec(memory_space=pltpu.VMEM)
    return pl.pallas_call(
        load_kernel,
        in_specs=[pl.BlockSpec(memory_space=pltpu.SMEM), hbm, hbm, vmem],
        out_specs=[vmem, vmem],
        out_shape=[pltpu.VMEM(weight.shape, weight.dtype), pltpu.VMEM((outer.shape[0], channels), outer.dtype)],
        scratch_shapes=[pltpu.SemaphoreType.DMA((2,))],
        compiler_params=pltpu.CompilerParams(vmem_limit_bytes=4 * MIB),
        name="load_weights",
    )(meta, in_hbm(weight), in_hbm(outer), after)


def stream_kernel(_, kept, direct_x, direct_y, late_x, late_y, residual, *parts):
    half = late_x.shape[1]
    rows = parts[0].shape[0]
    for index, out in enumerate(parts):
        span = slice(index * rows, (index + 1) * rows)
        wide = lambda ref: ref[span].astype(F32)
        left = wide(residual)[:, :half] + (wide(kept)[:, :half] + wide(direct_x) + wide(late_y))
        right = wide(residual)[:, half:] + (wide(kept)[:, half:] + wide(direct_y) + wide(late_x))
        out[...] = jnp.concatenate([left, right], axis=1).astype(BF16)


def near_kernel(meta_ref, *refs):
    blocks, (gain, weight, total, square) = refs[:3], refs[3:]
    channels = blocks[0].shape[1]
    squares = jnp.zeros(square.shape, F32)
    result = None
    for index in range(3):
        wide = blocks[index][...].astype(F32)
        squares = squares + jnp.sum(wide * wide, axis=1, keepdims=True)
        span = pl.ds(pl.multiple_of(meta_ref[index] * channels, channels), channels)
        factor, block = gain[:, span], weight[span, :]
        term = jnp.dot((wide * factor).astype(BF16), block, preferred_element_type=F32)
        result = term if result is None else result + term
    total[...] = result
    square[...] = squares


def far_kernel(chips, meta_ref, diag_a, diag_b, near, square, gain, cosine, sine, weight, *rest):
    outs, total = rest[:chips], rest[chips]
    channels = diag_a.shape[1]
    wide = jnp.concatenate([diag_a[...], diag_b[...]], axis=0).astype(F32)
    squares = square[...] + jnp.sum(wide * wide, axis=1, keepdims=True)
    span = pl.ds(pl.multiple_of(meta_ref[3] * channels, channels), channels)
    factor, block = gain[:, span], weight[span, :]
    total[...] = near[...] + jnp.dot((wide * factor).astype(BF16), block, preferred_element_type=F32)
    inverse = lax.rsqrt(squares / (4 * channels) + norm_eps)
    for distance, out in enumerate(outs):
        head = lax.rem(meta_ref[4] + distance, chips)
        for kind in range(3):
            column = pl.multiple_of((head * 3 + kind) * HEAD, HEAD)
            part = total[:, pl.ds(column, HEAD)] * inverse
            if kind < 2:
                part = part * cosine[...] + pltpu.roll(part, HEAD // 2, 1) * sine[...]
            if kind == 0:
                part = part * SCORE_SCALE
            if kind == 2:
                tiles = [part[row : row + HEAD].T for row in range(0, part.shape[0], HEAD)]
                part = jnp.concatenate(tiles, axis=0)
            out[kind] = part.astype(BF16)


def gather_keys(chips, meta_ref, own, other, keys, values):
    rows = own[0].shape[1]
    for distance in range(chips):
        place = lax.rem(meta_ref[4] - distance + chips, chips)
        for chunk, stacked in enumerate(other):
            mine = own[chunk * chips + distance]
            span = slice(chunk * rows, (chunk + 1) * rows)
            keys[0, place, span, :] = mine[1]
            keys[1, place, span, :] = stacked[distance, 0]
            for tile in range(rows // HEAD):
                first = chunk * rows + tile * HEAD
                taken = slice(tile * HEAD, (tile + 1) * HEAD)
                values[0, place, :, first : first + HEAD] = mine[2, taken, :]
                values[1, place, :, first : first + HEAD] = stacked[distance, 1, taken, :]


def attention_kernel(chips, chunks, distances, leading, meta_ref, *refs):
    if leading:
        pieces, other = refs[: chunks * chips], refs[chunks * chips : chunks * (chips + 1)]
        *outs, keys, values = refs[chunks * (chips + 1) :]
        gather_keys(chips, meta_ref, pieces, other, keys, values)
        sources = [pieces[(chips - distance) % chips :: chips] for distance in distances]
    else:
        taken = chunks * len(distances)
        pieces, (keys, values), outs = refs[:taken], refs[taken : taken + 2], refs[taken + 2 :]
        sources = [pieces[index * chunks : (index + 1) * chunks] for index in range(len(distances))]
    chip, core = meta_ref[4], meta_ref[5]
    count = keys.shape[2]

    def scores_of(side, place, queries):
        return lax.dot_general(
            keys[side, place], queries, (((1,), (1,)), ((), ())), preferred_element_type=F32
        )

    def update(state, mine, others, place):
        top, total, acc = state
        new_top = jnp.maximum(jnp.max(mine, axis=0, keepdims=True), jnp.max(others, axis=0, keepdims=True))
        if top is not None:
            new_top = jnp.maximum(new_top, top)
        mine = jnp.exp2(mine - new_top)
        others = jnp.exp2(others - new_top)
        gained = jnp.sum(mine, axis=0, keepdims=True) + jnp.sum(others, axis=0, keepdims=True)
        added = jnp.dot(values[0, place], mine.astype(BF16), preferred_element_type=F32)
        added = added + jnp.dot(values[1, place], others.astype(BF16), preferred_element_type=F32)
        if top is None:
            return new_top, gained, added
        shrink = jnp.exp2(top - new_top)
        return new_top, total * shrink + gained, acc * shrink + added

    key_row = lax.broadcasted_iota(jnp.int32, (count, count), 0)
    query_column = lax.broadcasted_iota(jnp.int32, (count, count), 1)
    for distance, source, out in zip(distances, sources, outs):
        place = lax.rem(chip + distance, chips)
        queries = jnp.concatenate([piece[0] for piece in source], axis=0)
        mine = jnp.where(key_row <= query_column, scores_of(0, place, queries), -1e30)
        others = jnp.where(core == 1, scores_of(1, place, queries), -1e30)
        state = update((None, None, None), mine, others, place)

        def earlier(index, state):
            return update(state, scores_of(0, index, queries), scores_of(1, index, queries), index)

        state = lax.fori_loop(0, place, earlier, state)
        out[...] = (state[2] / state[1]).T.astype(BF16)


def attend(meta, own, other, laid, distances, chips):
    chunks, leading = len(other), laid is None
    count = own[0].shape[1] * chunks
    outs = [((count, HEAD), BF16)] * len(distances)
    if leading:
        operands = own + other
        outs = outs + [((2, chips, count, HEAD), BF16), ((2, chips, HEAD, count), BF16)]
    else:
        operands = [piece for distance in distances for piece in own[(chips - distance) % chips :: chips]]
        operands = [*operands, *laid]
    body = functools.partial(attention_kernel, chips, chunks, distances, leading)
    made = list(vmem_call(body, "attention", 6, meta, operands, outs))
    return made[: len(distances)], laid or made[len(distances) :]


def pick_kernel(chips, meta_ref, weight, features, *refs):
    *near, edge, sems = refs
    channels = near[0].shape[1]
    kinds, count, _ = edge.shape
    last = features.shape[1] - count
    copies = []
    for kind in range(kinds):
        copies.append(
            pltpu.make_async_copy(features.at[kind, last : last + count], edge.at[kind], sems.at[kind])
        )
    for index, out in enumerate(near):
        columns = pl.ds(pl.multiple_of(meta_ref[index + 1] * channels, channels), channels)
        for head in range(chips // 2):
            rows = pl.ds(pl.multiple_of((2 * head + meta_ref[5]) * HEAD, HEAD), HEAD)
            target = out.at[head * HEAD : (head + 1) * HEAD]
            sem = sems.at[kinds + index * (chips // 2) + head]
            copies.append(pltpu.make_async_copy(weight.at[rows, columns], target, sem))
    for copy in copies:
        copy.start()
    for copy in copies:
        copy.wait()


def pick(meta, weight, features, count, chips):
    kinds, _, channels = features.shape
    near = jax.ShapeDtypeStruct((weight.shape[0] // 2, channels), BF16)
    in_hbm = lambda x: pltpu.with_memory_space_constraint(x, pltpu.HBM)
    hbm, vmem = pl.BlockSpec(memory_space=pltpu.HBM), pl.BlockSpec(memory_space=pltpu.VMEM)
    return pl.pallas_call(
        functools.partial(pick_kernel, chips),
        in_specs=[pl.BlockSpec(memory_space=pltpu.SMEM), hbm, hbm],
        out_specs=[vmem] * 4,
        out_shape=[near, near, near, jax.ShapeDtypeStruct((kinds, count, channels), BF16)],
        scratch_shapes=[pltpu.SemaphoreType.DMA((kinds + 3 * (chips // 2),))],
        compiler_params=pltpu.CompilerParams(vmem_limit_bytes=4 * MIB),
        name="pick",
    )(meta, in_hbm(weight), in_hbm(features))


def mix_kernel(chips, groups, items, streams, meta_ref, *refs):
    heads, refs = refs[: len(items)], refs[len(items) :]
    before, (own_w, *others_w), (out, ordered) = refs[:streams], refs[streams:-2], refs[-2:]
    near_w, far_w = others_w[:3], others_w[3:]
    chip, core = meta_ref[4], meta_ref[5]
    parities = [lax.rem(chip + distances[0], 2) for distances in groups]
    for place, (group, _) in enumerate(items):
        for index, distance in enumerate(groups[group]):
            head = lax.rem(chip - distance + chips, chips)
            column = pl.ds(pl.multiple_of(head // 2 * HEAD, HEAD), HEAD)
            ordered[place, :, column] = heads[place][index]

    def own_rows(parity):
        rows = [pl.ds(pl.multiple_of((2 * j + parity) * HEAD, HEAD), HEAD) for j in range(chips // 2)]
        return jnp.concatenate([own_w[span, :] for span in rows], axis=0)

    def finish(by_group):
        total = jnp.concatenate([part[...].astype(F32) for part in before], axis=0)
        for place, (group, source) in enumerate(items):
            weights = by_group[group][source - 1][...] if source else own_rows(parities[group])
            total = total + jnp.dot(ordered[place], weights, preferred_element_type=F32)
        out[...] = total.astype(out.dtype)

    @pl.when(core == parities[0])
    def _():
        finish([near_w, far_w])

    @pl.when(core != parities[0])
    def _():
        finish([far_w, near_w])


def mix(meta, heads, groups, items, before, own_w, near_w, far_w, kind, chips):
    rows, channels = heads[0].shape[1], own_w.shape[1]
    body = functools.partial(mix_kernel, chips, groups, items, len(before))
    operands = [*heads, *before, own_w, *near_w, *far_w]
    scratch = [pltpu.VMEM((len(items), rows, chips // 2 * HEAD), BF16)]
    micros = 0.6 * len(items)
    return vmem_call(body, "attention_mix", micros, meta, operands, [((rows, channels), kind)], scratch)[0]


def rotate_rows(block, positions):
    half_size = block.shape[-1] // 2
    frequency = 10000.0 ** (-jnp.arange(half_size, dtype=jnp.float32) * 2.0 / block.shape[-1])
    angles = positions.astype(jnp.float32)[:, None] * frequency[None, :]
    cosine = jnp.cos(angles)[:, None, :]
    sine_part = jnp.sin(angles)[:, None, :]
    first_half = block[..., :half_size]
    second_half = block[..., half_size:]
    return jnp.concatenate(
        [
            first_half * cosine - second_half * sine_part,
            second_half * cosine + first_half * sine_part,
        ],
        axis=-1,
    )


def run_attention(queries, query_pos, key_rows, value_rows, position_of):
    head_count = queries.shape[1]
    row_count = queries.shape[0]
    head_size = queries.shape[2]
    scale_factor = 1.0 / head_size**0.5
    last_query = jnp.max(query_pos)
    initial = (
        jnp.zeros((head_count, row_count, head_size), jnp.float32),
        jnp.full((head_count, row_count), -1e30, jnp.float32),
        jnp.zeros((head_count, row_count), jnp.float32),
    )
    piece_keys = lax.all_gather(key_rows, "ctx", axis=0, tiled=True)
    piece_values = lax.all_gather(value_rows, "ctx", axis=0, tiled=True)
    piece_rows = piece_keys.shape[0]
    block_rows = 512

    def one_block(state_in, block_index):
        first_block = block_index * block_rows
        key_block = lax.dynamic_slice_in_dim(piece_keys, first_block, block_rows, 0)
        value_block = lax.dynamic_slice_in_dim(piece_values, first_block, block_rows, 0)
        key_pos = position_of(first_block + jnp.arange(block_rows))

        def update(state_old):
            acc_sum, run_max, run_total = state_old
            scores = (
                jnp.einsum("thd,khd->htk", queries, key_block, preferred_element_type=jnp.float32)
                * scale_factor
            )
            causal = (key_pos[None, :] <= query_pos[:, None])[None]
            block_max = jnp.max(jnp.where(causal, scores, -1e30), axis=-1)
            new_max = jnp.maximum(run_max, block_max)
            weights = jnp.where(causal, jnp.exp(scores - new_max[..., None]), 0.0)
            correction = jnp.exp(run_max - new_max)
            new_total = run_total * correction + jnp.sum(weights, axis=-1)
            update_sum = jnp.einsum(
                "htk,khd->htd",
                weights.astype(jnp.bfloat16),
                value_block,
                preferred_element_type=jnp.float32,
            )
            return (acc_sum * correction[..., None] + update_sum, new_max, new_total)

        def unchanged(state_old):
            return state_old

        state_out = lax.cond(jnp.min(key_pos) > last_query, unchanged, update, state_in)
        return (state_out, None)

    state_end, unused = lax.scan(one_block, initial, jnp.arange(piece_rows // block_rows))
    acc_sum, run_max, run_total = state_end
    output = acc_sum / run_total[..., None]
    return jnp.transpose(output, (1, 0, 2)).astype(jnp.bfloat16)


def after_gating(gated, residual_in, out_weight, norm_gain, attn_weight, attn_out):
    tok_rows, chan_count = gated.shape
    hyena_terms = jnp.dot(gated, out_weight, preferred_element_type=jnp.float32)
    hyena_out = lax.psum_scatter(
        hyena_terms.astype(jnp.bfloat16), "ch", scatter_dimension=1, tiled=True
    ).astype(jnp.float32)
    stream = (residual_in.astype(jnp.float32) + hyena_out).astype(jnp.bfloat16)
    stream_wide = stream.astype(jnp.float32)
    full_width = chan_count * lax.axis_size("ch")
    head_cols = attn_weight.shape[1]
    square_total = lax.psum(jnp.sum(stream_wide * stream_wide, axis=1), "ch")
    inverse = lax.rsqrt(square_total / full_width + norm_eps)
    gain_part = lax.dynamic_slice_in_dim(norm_gain, lax.axis_index("ch") * chan_count, chan_count)
    normed = (stream_wide * inverse[:, None] * gain_part[None, :]).astype(jnp.bfloat16)
    projected = jnp.dot(
        lax.all_gather(normed, "ch", axis=1, tiled=True),
        attn_weight,
        preferred_element_type=jnp.float32,
    )
    head_count = head_cols // (3 * HEAD)
    projected = projected.reshape(tok_rows, head_count, 3, HEAD)
    ctx_index = lax.axis_index("ctx")
    positions = ctx_index * tok_rows + jnp.arange(tok_rows, dtype=jnp.int32)
    queries = rotate_rows(projected[:, :, 0, :], positions).astype(jnp.bfloat16)
    key_rows = rotate_rows(projected[:, :, 1, :], positions).astype(jnp.bfloat16)
    value_rows = projected[:, :, 2, :].astype(jnp.bfloat16)

    def position_of(global_row):
        return global_row

    attended = run_attention(queries, positions, key_rows, value_rows, position_of)
    head_terms = jnp.dot(
        attended.reshape(tok_rows, head_count * HEAD), attn_out, preferred_element_type=jnp.float32
    )
    attn_mix = lax.psum_scatter(
        head_terms.astype(jnp.bfloat16), "ch", scatter_dimension=1, tiled=True
    ).astype(jnp.float32)
    return (stream_wide + attn_mix).astype(jnp.bfloat16)


def rotation_tables(positions):
    half_size = HEAD // 2
    frequency = 10000.0 ** (-jnp.arange(half_size, dtype=F32) * 2.0 / HEAD)
    angles = positions.astype(F32)[:, None] * frequency[None, :]
    cosine, sine = jnp.cos(angles), jnp.sin(angles)
    return jnp.concatenate([cosine, cosine], axis=1), jnp.concatenate([-sine, sine], axis=1)


def shards(
    features,
    residual_in,
    short_filter,
    medium_filter,
    skip_gain,
    out_weight,
    norm_gain,
    attn_weight,
    attn_out,
):
    rows, _, channels = features.shape
    chips = lax.axis_size("ctx") // 2
    length = medium_filter.shape[0]
    chunk = rows // 2
    ctx, ch = lax.axis_index("ctx"), lax.axis_index("ch")
    scalars = [ch, ch ^ 1, ch ^ 2, ch ^ 3, ctx // 2, ctx % 2, ctx * rows, ctx]
    meta = jnp.stack(scalars).astype(jnp.int32)

    by_kind = jnp.transpose(features, (1, 0, 2))
    medium_rows = medium_filter.T
    skip = skip_gain.reshape(1, channels)

    starts = [rows - chunk, 0]
    if lax.axis_size("ch") != 4 or attn_weight.shape[1] != 3 * HEAD * chips or chips % 2:
        halo = shift_rows(by_kind[:, rows - length - LEAD :])
        (lower,) = gated_chunk(meta, by_kind, halo, chunk, chunk, short_filter, medium_rows, skip)
        (upper,) = gated_chunk(meta, by_kind, halo, 0, chunk, short_filter, medium_rows, skip)
        return after_gating(
            jnp.concatenate([upper, lower], axis=0), residual_in, out_weight, norm_gain, attn_weight, attn_out
        )

    gain = norm_gain.reshape(1, -1)
    cosine, sine = rotation_tables(meta[6:7] + jnp.arange(rows, dtype=jnp.int32))

    *near_w, edge = pick(meta, attn_out, by_kind, length + LEAD, chips)
    halo = shift_rows(edge)
    near_w = [swap_ch(weight, mask) for mask, weight in zip((1, 2, 3), near_w)]
    far_w = [swap_core(weight) for weight in near_w]

    lower, out_held = gated_chunk(meta, by_kind, halo, chunk, chunk, short_filter, medium_rows, skip, out_weight)
    (upper,) = gated_chunk(meta, by_kind, halo, 0, chunk, short_filter, medium_rows, skip)
    across_x, across_y = column_terms(meta, upper, lower, out_held, ((3, 0, 0, 0), (3, 1, 1, 0)))
    across_x, across_y = swap_ch(across_x, 1), swap_ch(across_y, 2)
    pieces = ((1, 0, 0, 0), (2, 1, 1, 0), (1, 1, 2, 0), (2, 0, 3, 0), (0, 0, 4, 0), (0, 1, 4, 1))
    direct_x, direct_y, along_x, along_y, kept = column_terms(meta, upper, lower, out_held, pieces, near_w)
    direct_x, direct_y = swap_ch(direct_x, 1), swap_ch(direct_y, 2)
    along_x = (along_x.astype(F32) + across_y.astype(F32)).astype(BF16)
    along_y = (along_y.astype(F32) + across_x.astype(F32)).astype(BF16)
    late_x, late_y = swap_ch(along_x, 1), swap_ch(along_y, 2)
    qkv_held, own_w = load(meta, attn_weight, attn_out, along_y, channels)
    parts = vmem_call(
        stream_kernel,
        "add_stream",
        1,
        meta,
        [kept, direct_x, direct_y, late_x, late_y, residual_in],
        [((chunk, channels), BF16)] * 2,
        waits=[qkv_held, *far_w],
    )

    own, other, after = [], [], None
    width = attn_weight.shape[1]
    for start in starts:
        part = parts[start // chunk]
        if after is not None:
            part, _ = lax.optimization_barrier((part, after))
        by_x, by_y = swap_ch(part, 1), swap_ch(part, 2)
        diag_a, diag_b = swap_ch(by_x[: chunk // 2], 2), swap_ch(by_y[chunk // 2 :], 1)
        near, square = vmem_call(
            near_kernel,
            "qkv_near",
            3,
            meta,
            [part, by_x, by_y, gain, qkv_held],
            [((chunk, width), F32), ((chunk, LANES), F32)],
        )
        after = diag_a, diag_b
        turn = slice(start, start + chunk)
        outs = vmem_call(
            functools.partial(far_kernel, chips),
            "qkv_far",
            2,
            meta,
            [diag_a, diag_b, near, square, gain, cosine[turn], sine[turn], qkv_held],
            [((3, chunk, HEAD), BF16)] * chips,
            [pltpu.VMEM((chunk, width), F32)],
        )
        arrived = [outs[0]] + [rotate_chips(outs[d], d) for d in range(1, chips)]
        own.append(arrived)

    own, _ = lax.optimization_barrier((own, outs))
    other = [swap_core(jnp.stack([piece[1:] for piece in arrived])) for arrived in own]
    own, other = own[1] + own[0], other[::-1]

    groups = [(*range(2, chips, 2), 0), tuple(range(1, chips, 2))]
    given, laid = attend(meta, own, other, None, groups[0], chips)
    first = [rotate_chips(piece, d) if d else piece for d, piece in zip(groups[0], given)]
    given, _ = attend(meta, own, other, laid, groups[1], chips)
    first, given = lax.optimization_barrier((first, given))
    second = [rotate_chips(piece, d) for d, piece in zip(groups[1], given)]
    heads, places = [], []
    for group, back in enumerate([first, second]):
        back = jnp.stack(back)
        by_x, by_y = swap_ch(back, 1), swap_ch(back, 2)
        by_both = swap_ch(by_x, 2) if group == 0 else swap_ch(by_y, 1)
        heads += [back, by_x, by_y, by_both]
        places += [(group, source) for source in range(4)]
    weights = own_w, near_w, far_w
    early = mix(meta, heads[:-1], groups, places[:-1], parts, *weights, F32, chips)
    return mix(meta, heads[-1:], groups, places[-1:], [early], *weights, BF16, chips)


def solution(mesh):
    in_specs = (
        P("ctx", None, "ch"),
        P("ctx", "ch"),
        P(None, None, "ch"),
        P(None, "ch"),
        P("ch"),
        P("ch", None),
        P(),
        P(None, "ch"),
        P("ch", None),
    )
    out_specs = P("ctx", "ch")
    return jax.shard_map(shards, mesh=mesh, in_specs=in_specs, out_specs=out_specs, check_vma=False)
```

```python
import functools

import jax
import jax.numpy as jnp
from jax import lax
from jax.experimental import pallas as pl
from jax.experimental.pallas import tpu as pltpu
from jax.sharding import PartitionSpec as P

HEAD = 128
GROUP_SIZE = 16
LANES = 128
LEAD = 16
norm_eps = 1e-05
SCORE_SCALE = 1.4426950408889634 / HEAD**0.5
MIB = 1024 * 1024
F32 = jnp.float32
BF16 = jnp.bfloat16


def lasting(micros):
    return pl.CostEstimate(
        flops=int(micros * 1.1e9), transcendentals=0, bytes_accessed=int(micros * 3.6e6)
    )


def swap_ch(value, mask):
    count = lax.axis_size("ch")
    return lax.ppermute(value, "ch", [(i, i ^ mask) for i in range(count)])


def swap_ctx(value, mask):
    count = lax.axis_size("ctx")
    return lax.ppermute(value, "ctx", [(i, i ^ mask) for i in range(count)])


def shift_rows(value):
    count = lax.axis_size("ctx")
    return lax.ppermute(value, "ctx", [(i, i + 1) for i in range(count - 1)])


def rotate_chips(value, distance):
    count = lax.axis_size("ctx")
    return lax.ppermute(value, "ctx", [(i, (i + 2 * distance) % count) for i in range(count)])


def filter_tile(first_row, tile, short_ref, medium_ref, skip_ref, halo_ref, rows_ref, wide, product, table, store):
    taps, groups_all = short_ref.shape[1:]
    length = medium_ref.shape[1]
    groups = LANES // GROUP_SIZE
    medium = medium_ref[pl.ds(pl.multiple_of(tile * groups, groups), groups), :]
    gain = skip_ref[:, pl.ds(pl.multiple_of(tile * LANES, LANES), LANES)]
    span = wide.shape[1]
    halo_rows = length + LEAD
    count = span - halo_rows

    for kind in range(3):
        if first_row == 0:
            wide[kind, :halo_rows] = halo_ref[kind].astype(F32)
            wide[kind, halo_rows:] = rows_ref[kind].astype(F32)
        else:
            wide[kind] = rows_ref[kind, first_row - halo_rows : first_row + count].astype(F32)

    group_row = lax.broadcasted_iota(jnp.int32, (groups_all, LANES), 0)
    group_col = lax.broadcasted_iota(jnp.int32, (groups_all, LANES), 1) // GROUP_SIZE + tile * groups
    chosen = jnp.where(group_row == group_col, 1.0, 0.0).astype(F32)
    weights = [
        jnp.dot(short_ref[kind], chosen, precision=lax.Precision.HIGHEST, preferred_element_type=F32)
        for kind in range(3)
    ]

    tap_row = lax.broadcasted_iota(jnp.int32, (length, 2 * length), 0)
    place = lax.broadcasted_iota(jnp.int32, (length, 2 * length), 1)
    turned = jnp.where(tap_row + place == length, 1.0, 0.0).astype(BF16)
    base = jnp.dot(medium.astype(BF16), turned, preferred_element_type=F32)
    for group in range(groups):
        spread = jnp.broadcast_to(base[group : group + 1, :], (length, 2 * length))
        rolled = pltpu.roll(spread, 0, 1, stride=1, stride_axis=0)
        table[group * length : (group + 1) * length, :] = rolled.astype(BF16)

    def featured(kind, start):
        total = weights[kind][0:1, :] * wide[kind, start : start + length, :]
        for tap in range(1, taps):
            total = total + weights[kind][tap : tap + 1, :] * wide[kind, start - tap : start - tap + length, :]
        return total

    for block in range(count // length + 1):
        start = LEAD + block * length
        product[block * length : (block + 1) * length, :] = (
            featured(1, start) * featured(2, start)
        ).astype(BF16)

    group_of = lax.broadcasted_iota(jnp.int32, (length, 2 * LANES), 1) % LANES // GROUP_SIZE
    for pair in range(count // (2 * length)):
        begin = pair * 2 * length
        window = jnp.concatenate(
            [
                product[begin : begin + 2 * length, :],
                product[begin + length : begin + 3 * length, :],
            ],
            axis=1,
        )
        spread = jnp.dot(table[...], window, preferred_element_type=F32)
        mixed = spread[:length]
        for group in range(1, groups):
            mixed = jnp.where(group_of == group, spread[group * length : (group + 1) * length], mixed)
        for part in range(2):
            row = begin + part * length
            direct = gain * product[row + length : row + 2 * length, :].astype(F32)
            gate = featured(0, halo_rows + row)
            store(row, (gate * (mixed[:, part * LANES : (part + 1) * LANES] + direct)).astype(BF16))


def gated_kernel(first_row, loads, *refs):
    head, rest = refs[1:4], refs[4:]
    halo_ref, rest = (rest[0], rest[1:]) if first_row == 0 else (None, rest)
    rows_ref, rest = rest[0], rest[1:]
    if loads:
        weight, out_ref, held, wide, product, table, sems = rest
        parts = sems.shape[0]
        height = weight.shape[0] // parts

        def copy_of(part):
            span = pl.ds(pl.multiple_of(part * height, height), height)
            return pltpu.make_async_copy(weight.at[span, :], held.at[span, :], sems.at[part])

        copy_of(pl.program_id(0)).start()
    else:
        out_ref, wide, product, table = rest

    def store(row, value):
        out_ref[row : row + value.shape[0], :] = value

    filter_tile(first_row, pl.program_id(0), *head, halo_ref, rows_ref, wide, product, table, store)
    if loads:

        @pl.when(pl.program_id(0) == pl.num_programs(0) - 1)
        def _():
            for part in range(parts):
                copy_of(part).wait()


def gated_chunk(meta, features, halo, first_row, count, short_filter, medium_rows, skip, weight=None):
    kinds, rows, channels = features.shape
    length = medium_rows.shape[1]
    groups = LANES // GROUP_SIZE
    loads = weight is not None
    in_hbm = lambda x: pltpu.with_memory_space_constraint(x, pltpu.HBM)
    in_specs = [
        pl.BlockSpec(memory_space=pltpu.SMEM),
        pl.BlockSpec(short_filter.shape, lambda i: (0, 0, 0)),
        pl.BlockSpec(medium_rows.shape, lambda i: (0, 0)),
        pl.BlockSpec(skip.shape, lambda i: (0, 0)),
    ]
    operands = [meta, in_hbm(short_filter), in_hbm(medium_rows), in_hbm(skip)]
    out_specs = [pl.BlockSpec((count, LANES), lambda i: (0, i))]
    out_shape = [jax.ShapeDtypeStruct((count, channels), BF16)]
    scratch = [
        pltpu.VMEM((kinds, length + LEAD + count, LANES), F32),
        pltpu.VMEM((length + count, LANES), BF16),
        pltpu.VMEM((groups * length, 2 * length), BF16),
    ]
    if first_row == 0:
        in_specs.append(pl.BlockSpec((kinds, length + LEAD, LANES), lambda i: (0, 0, i)))
        in_specs.append(pl.BlockSpec((kinds, count, LANES), lambda i: (0, 0, i)))
        operands += [halo, features]
    else:
        in_specs.append(pl.BlockSpec((kinds, rows, LANES), lambda i: (0, 0, i)))
        operands.append(features)
    if loads:
        in_specs.append(pl.BlockSpec(memory_space=pltpu.HBM))
        operands.append(in_hbm(weight))
        out_specs.append(pl.BlockSpec(memory_space=pltpu.VMEM))
        out_shape.append(pltpu.VMEM(weight.shape, weight.dtype))
        scratch.append(pltpu.SemaphoreType.DMA((channels // LANES,)))
    return pl.pallas_call(
        functools.partial(gated_kernel, first_row, loads),
        grid=(channels // LANES,),
        in_specs=in_specs,
        out_specs=out_specs,
        out_shape=out_shape,
        scratch_shapes=scratch,
        compiler_params=pltpu.CompilerParams(vmem_limit_bytes=16 * MIB),
        name="hyena_filters",
    )(*operands)


def vmem_call(body, name, micros, scalars, operands, outs, scratch=(), waits=()):
    given = 1 + len(operands)
    run = lambda *refs: body(*refs[:given], *refs[given + len(waits) :])
    return pl.pallas_call(
        run,
        in_specs=[pl.BlockSpec(memory_space=pltpu.SMEM)]
        + [pl.BlockSpec(memory_space=pltpu.VMEM)] * (len(operands) + len(waits)),
        out_specs=[pl.BlockSpec(memory_space=pltpu.VMEM)] * len(outs),
        out_shape=[jax.ShapeDtypeStruct(shape, kind) for shape, kind in outs],
        scratch_shapes=list(scratch),
        compiler_params=pltpu.CompilerParams(vmem_limit_bytes=20 * MIB),
        cost_estimate=lasting(micros) if micros else None,
        name=name,
    )(scalars, *operands, *waits)


def columns_kernel(pieces, meta_ref, upper, lower, weight, *outs):
    gated = jnp.concatenate([upper[...], lower[...]], axis=0)
    width = weight.shape[1] // 8
    for owner, half, out, part in pieces:
        columns = pl.ds(pl.multiple_of((2 * meta_ref[owner] + half) * width, width), width)
        term = jnp.dot(gated, weight[:, columns], preferred_element_type=F32)
        outs[out][:, part * width : (part + 1) * width] = term.astype(BF16)


def column_terms(meta, upper, lower, weight, pieces, waits=()):
    rows, width = 2 * upper.shape[0], weight.shape[1] // 8
    outs = [((rows, width * sum(p[2] == out for p in pieces)), BF16) for out in range(pieces[-1][2] + 1)]
    body = functools.partial(columns_kernel, pieces)
    return vmem_call(body, "hyena_terms", None, meta, [upper, lower, weight], outs, waits=waits)


def load_kernel(meta_ref, source, outer, _, held, own, sems):
    channels = own.shape[1]
    columns = pl.ds(pl.multiple_of(meta_ref[0] * channels, channels), channels)
    copies = [
        pltpu.make_async_copy(source, held, sems.at[0]),
        pltpu.make_async_copy(outer.at[:, columns], own, sems.at[1]),
    ]
    for copy in copies:
        copy.start()
    for copy in copies:
        copy.wait()


def load(meta, weight, outer, after, channels):
    in_hbm = lambda x: pltpu.with_memory_space_constraint(x, pltpu.HBM)
    hbm, vmem = pl.BlockSpec(memory_space=pltpu.HBM), pl.BlockSpec(memory_space=pltpu.VMEM)
    return pl.pallas_call(
        load_kernel,
        in_specs=[pl.BlockSpec(memory_space=pltpu.SMEM), hbm, hbm, vmem],
        out_specs=[vmem, vmem],
        out_shape=[pltpu.VMEM(weight.shape, weight.dtype), pltpu.VMEM((outer.shape[0], channels), outer.dtype)],
        scratch_shapes=[pltpu.SemaphoreType.DMA((2,))],
        compiler_params=pltpu.CompilerParams(vmem_limit_bytes=4 * MIB),
        name="load_weights",
    )(meta, in_hbm(weight), in_hbm(outer), after)


def stream_kernel(_, kept, direct_x, direct_y, late_x, late_y, residual, *parts):
    half = late_x.shape[1]
    rows = parts[0].shape[0]
    for index, out in enumerate(parts):
        span = slice(index * rows, (index + 1) * rows)
        wide = lambda ref: ref[span].astype(F32)
        left = wide(residual)[:, :half] + (wide(kept)[:, :half] + wide(direct_x) + wide(late_y))
        right = wide(residual)[:, half:] + (wide(kept)[:, half:] + wide(direct_y) + wide(late_x))
        out[...] = jnp.concatenate([left, right], axis=1).astype(BF16)


def near_kernel(meta_ref, *refs):
    blocks, (gain, weight, total, square) = refs[:3], refs[3:]
    channels = blocks[0].shape[1]
    squares = jnp.zeros(square.shape, F32)
    result = None
    for index in range(3):
        wide = blocks[index][...].astype(F32)
        squares = squares + jnp.sum(wide * wide, axis=1, keepdims=True)
        span = pl.ds(pl.multiple_of(meta_ref[index] * channels, channels), channels)
        factor, block = gain[:, span], weight[span, :]
        term = jnp.dot((wide * factor).astype(BF16), block, preferred_element_type=F32)
        result = term if result is None else result + term
    total[...] = result
    square[...] = squares


def far_kernel(chips, meta_ref, diag_a, diag_b, near, square, gain, cosine, sine, weight, *rest):
    outs, total = rest[:chips], rest[chips]
    channels = diag_a.shape[1]
    wide = jnp.concatenate([diag_a[...], diag_b[...]], axis=0).astype(F32)
    squares = square[...] + jnp.sum(wide * wide, axis=1, keepdims=True)
    span = pl.ds(pl.multiple_of(meta_ref[3] * channels, channels), channels)
    factor, block = gain[:, span], weight[span, :]
    total[...] = near[...] + jnp.dot((wide * factor).astype(BF16), block, preferred_element_type=F32)
    inverse = lax.rsqrt(squares / (4 * channels) + norm_eps)
    for distance, out in enumerate(outs):
        head = lax.rem(meta_ref[4] + distance, chips)
        for kind in range(3):
            column = pl.multiple_of((head * 3 + kind) * HEAD, HEAD)
            part = total[:, pl.ds(column, HEAD)] * inverse
            if kind < 2:
                part = part * cosine[...] + pltpu.roll(part, HEAD // 2, 1) * sine[...]
            if kind == 0:
                part = part * SCORE_SCALE
            if kind == 2:
                tiles = [part[row : row + HEAD].T for row in range(0, part.shape[0], HEAD)]
                part = jnp.concatenate(tiles, axis=0)
            out[kind] = part.astype(BF16)


def gather_keys(chips, meta_ref, own, other, keys, values):
    rows = own[0].shape[1]
    for distance in range(chips):
        place = lax.rem(meta_ref[4] - distance + chips, chips)
        for chunk, stacked in enumerate(other):
            mine = own[chunk * chips + distance]
            span = slice(chunk * rows, (chunk + 1) * rows)
            keys[0, place, span, :] = mine[1]
            keys[1, place, span, :] = stacked[distance, 0]
            for tile in range(rows // HEAD):
                first = chunk * rows + tile * HEAD
                taken = slice(tile * HEAD, (tile + 1) * HEAD)
                values[0, place, :, first : first + HEAD] = mine[2, taken, :]
                values[1, place, :, first : first + HEAD] = stacked[distance, 1, taken, :]


def attention_kernel(chips, chunks, distances, leading, meta_ref, *refs):
    if leading:
        pieces, other = refs[: chunks * chips], refs[chunks * chips : chunks * (chips + 1)]
        *outs, keys, values = refs[chunks * (chips + 1) :]
        gather_keys(chips, meta_ref, pieces, other, keys, values)
        sources = [pieces[(chips - distance) % chips :: chips] for distance in distances]
    else:
        taken = chunks * len(distances)
        pieces, (keys, values), outs = refs[:taken], refs[taken : taken + 2], refs[taken + 2 :]
        sources = [pieces[index * chunks : (index + 1) * chunks] for index in range(len(distances))]
    chip, core = meta_ref[4], meta_ref[5]
    count = keys.shape[2]

    def scores_of(side, place, queries):
        return lax.dot_general(
            keys[side, place], queries, (((1,), (1,)), ((), ())), preferred_element_type=F32
        )

    def update(state, mine, others, place):
        top, total, acc = state
        new_top = jnp.maximum(jnp.max(mine, axis=0, keepdims=True), jnp.max(others, axis=0, keepdims=True))
        if top is not None:
            new_top = jnp.maximum(new_top, top)
        mine = jnp.exp2(mine - new_top)
        others = jnp.exp2(others - new_top)
        gained = jnp.sum(mine, axis=0, keepdims=True) + jnp.sum(others, axis=0, keepdims=True)
        added = jnp.dot(values[0, place], mine.astype(BF16), preferred_element_type=F32)
        added = added + jnp.dot(values[1, place], others.astype(BF16), preferred_element_type=F32)
        if top is None:
            return new_top, gained, added
        shrink = jnp.exp2(top - new_top)
        return new_top, total * shrink + gained, acc * shrink + added

    key_row = lax.broadcasted_iota(jnp.int32, (count, count), 0)
    query_column = lax.broadcasted_iota(jnp.int32, (count, count), 1)
    for distance, source, out in zip(distances, sources, outs):
        place = lax.rem(chip + distance, chips)
        queries = jnp.concatenate([piece[0] for piece in source], axis=0)
        mine = jnp.where(key_row <= query_column, scores_of(0, place, queries), -1e30)
        others = jnp.where(core == 1, scores_of(1, place, queries), -1e30)
        state = update((None, None, None), mine, others, place)

        def earlier(index, state):
            return update(state, scores_of(0, index, queries), scores_of(1, index, queries), index)

        state = lax.fori_loop(0, place, earlier, state)
        out[...] = (state[2] / state[1]).T.astype(BF16)


def attend(meta, own, other, laid, distances, chips):
    chunks, leading = len(other), laid is None
    count = own[0].shape[1] * chunks
    outs = [((count, HEAD), BF16)] * len(distances)
    if leading:
        operands = own + other
        outs = outs + [((2, chips, count, HEAD), BF16), ((2, chips, HEAD, count), BF16)]
    else:
        operands = [piece for distance in distances for piece in own[(chips - distance) % chips :: chips]]
        operands = [*operands, *laid]
    body = functools.partial(attention_kernel, chips, chunks, distances, leading)
    made = list(vmem_call(body, "attention", 6, meta, operands, outs))
    return made[: len(distances)], laid or made[len(distances) :]


def pick_kernel(meta_ref, weight, features, *refs):
    *near, edge, sems = refs
    channels = near[0].shape[1]
    kinds, count, _ = edge.shape
    last = features.shape[1] - count
    copies = []
    for kind in range(kinds):
        copies.append(
            pltpu.make_async_copy(features.at[kind, last : last + count], edge.at[kind], sems.at[kind])
        )
    rows = pl.ds(pl.multiple_of((2 * lax.rem(meta_ref[4], 2) + meta_ref[5]) * HEAD, HEAD), HEAD)
    for index, out in enumerate(near):
        columns = pl.ds(pl.multiple_of(meta_ref[index + 1] * channels, channels), channels)
        copies.append(pltpu.make_async_copy(weight.at[rows, columns], out, sems.at[kinds + index]))
    for copy in copies:
        copy.start()
    for copy in copies:
        copy.wait()


def pick(meta, weight, features, count):
    kinds, _, channels = features.shape
    near = jax.ShapeDtypeStruct((HEAD, channels), BF16)
    in_hbm = lambda x: pltpu.with_memory_space_constraint(x, pltpu.HBM)
    hbm, vmem = pl.BlockSpec(memory_space=pltpu.HBM), pl.BlockSpec(memory_space=pltpu.VMEM)
    return pl.pallas_call(
        pick_kernel,
        in_specs=[pl.BlockSpec(memory_space=pltpu.SMEM), hbm, hbm],
        out_specs=[vmem] * 4,
        out_shape=[near, near, near, jax.ShapeDtypeStruct((kinds, count, channels), BF16)],
        scratch_shapes=[pltpu.SemaphoreType.DMA((kinds + 3,))],
        compiler_params=pltpu.CompilerParams(vmem_limit_bytes=4 * MIB),
        name="pick",
    )(meta, in_hbm(weight), in_hbm(features))


def mix_kernel(chips, groups, items, streams, meta_ref, *refs):
    heads, refs = refs[: len(items)], refs[len(items) :]
    before, (own_w, near_w, far_w, out, ordered) = refs[:streams], refs[streams:]
    chip, core = meta_ref[4], meta_ref[5]
    swapped = lax.rem(chip, 2)
    parities = [lax.rem(chip + distances[0], 2) for distances in groups]
    for place, (group, _) in enumerate(items):
        for index, distance in enumerate(groups[group]):
            head = lax.rem(chip - distance + chips, chips)
            column = pl.ds(pl.multiple_of(head // 2 * HEAD, HEAD), HEAD)
            ordered[place, :, column] = heads[place][index]

    def own_rows(parity):
        rows = [pl.ds(pl.multiple_of((2 * j + parity) * HEAD, HEAD), HEAD) for j in range(chips // 2)]
        return jnp.concatenate([own_w[span, :] for span in rows], axis=0)

    def finish(by_group):
        total = jnp.concatenate([part[...].astype(F32) for part in before], axis=0)
        for place, (group, source) in enumerate(items):
            if source:
                held = by_group[group]
                weights = jnp.concatenate([held[swapped, source - 1], held[1 - swapped, source - 1]], axis=0)
            else:
                weights = own_rows(parities[group])
            total = total + jnp.dot(ordered[place], weights, preferred_element_type=F32)
        out[...] = total.astype(out.dtype)

    @pl.when(core == parities[0])
    def _():
        finish([near_w, far_w])

    @pl.when(core != parities[0])
    def _():
        finish([far_w, near_w])


def mix(meta, heads, groups, items, before, own_w, near_w, far_w, kind, chips):
    rows, channels = heads[0].shape[1], own_w.shape[1]
    body = functools.partial(mix_kernel, chips, groups, items, len(before))
    operands = [*heads, *before, own_w, near_w, far_w]
    scratch = [pltpu.VMEM((len(items), rows, chips // 2 * HEAD), BF16)]
    micros = 0.6 * len(items)
    return vmem_call(body, "attention_mix", micros, meta, operands, [((rows, channels), kind)], scratch)[0]


def rotate_rows(block, positions):
    half_size = block.shape[-1] // 2
    frequency = 10000.0 ** (-jnp.arange(half_size, dtype=jnp.float32) * 2.0 / block.shape[-1])
    angles = positions.astype(jnp.float32)[:, None] * frequency[None, :]
    cosine = jnp.cos(angles)[:, None, :]
    sine_part = jnp.sin(angles)[:, None, :]
    first_half = block[..., :half_size]
    second_half = block[..., half_size:]
    return jnp.concatenate(
        [
            first_half * cosine - second_half * sine_part,
            second_half * cosine + first_half * sine_part,
        ],
        axis=-1,
    )


def run_attention(queries, query_pos, key_rows, value_rows, position_of):
    head_count = queries.shape[1]
    row_count = queries.shape[0]
    head_size = queries.shape[2]
    scale_factor = 1.0 / head_size**0.5
    last_query = jnp.max(query_pos)
    initial = (
        jnp.zeros((head_count, row_count, head_size), jnp.float32),
        jnp.full((head_count, row_count), -1e30, jnp.float32),
        jnp.zeros((head_count, row_count), jnp.float32),
    )
    piece_keys = lax.all_gather(key_rows, "ctx", axis=0, tiled=True)
    piece_values = lax.all_gather(value_rows, "ctx", axis=0, tiled=True)
    piece_rows = piece_keys.shape[0]
    block_rows = 512

    def one_block(state_in, block_index):
        first_block = block_index * block_rows
        key_block = lax.dynamic_slice_in_dim(piece_keys, first_block, block_rows, 0)
        value_block = lax.dynamic_slice_in_dim(piece_values, first_block, block_rows, 0)
        key_pos = position_of(first_block + jnp.arange(block_rows))

        def update(state_old):
            acc_sum, run_max, run_total = state_old
            scores = (
                jnp.einsum("thd,khd->htk", queries, key_block, preferred_element_type=jnp.float32)
                * scale_factor
            )
            causal = (key_pos[None, :] <= query_pos[:, None])[None]
            block_max = jnp.max(jnp.where(causal, scores, -1e30), axis=-1)
            new_max = jnp.maximum(run_max, block_max)
            weights = jnp.where(causal, jnp.exp(scores - new_max[..., None]), 0.0)
            correction = jnp.exp(run_max - new_max)
            new_total = run_total * correction + jnp.sum(weights, axis=-1)
            update_sum = jnp.einsum(
                "htk,khd->htd",
                weights.astype(jnp.bfloat16),
                value_block,
                preferred_element_type=jnp.float32,
            )
            return (acc_sum * correction[..., None] + update_sum, new_max, new_total)

        def unchanged(state_old):
            return state_old

        state_out = lax.cond(jnp.min(key_pos) > last_query, unchanged, update, state_in)
        return (state_out, None)

    state_end, unused = lax.scan(one_block, initial, jnp.arange(piece_rows // block_rows))
    acc_sum, run_max, run_total = state_end
    output = acc_sum / run_total[..., None]
    return jnp.transpose(output, (1, 0, 2)).astype(jnp.bfloat16)


def after_gating(gated, residual_in, out_weight, norm_gain, attn_weight, attn_out):
    tok_rows, chan_count = gated.shape
    hyena_terms = jnp.dot(gated, out_weight, preferred_element_type=jnp.float32)
    hyena_out = lax.psum_scatter(
        hyena_terms.astype(jnp.bfloat16), "ch", scatter_dimension=1, tiled=True
    ).astype(jnp.float32)
    stream = (residual_in.astype(jnp.float32) + hyena_out).astype(jnp.bfloat16)
    stream_wide = stream.astype(jnp.float32)
    full_width = chan_count * lax.axis_size("ch")
    head_cols = attn_weight.shape[1]
    square_total = lax.psum(jnp.sum(stream_wide * stream_wide, axis=1), "ch")
    inverse = lax.rsqrt(square_total / full_width + norm_eps)
    gain_part = lax.dynamic_slice_in_dim(norm_gain, lax.axis_index("ch") * chan_count, chan_count)
    normed = (stream_wide * inverse[:, None] * gain_part[None, :]).astype(jnp.bfloat16)
    projected = jnp.dot(
        lax.all_gather(normed, "ch", axis=1, tiled=True),
        attn_weight,
        preferred_element_type=jnp.float32,
    )
    head_count = head_cols // (3 * HEAD)
    projected = projected.reshape(tok_rows, head_count, 3, HEAD)
    ctx_index = lax.axis_index("ctx")
    positions = ctx_index * tok_rows + jnp.arange(tok_rows, dtype=jnp.int32)
    queries = rotate_rows(projected[:, :, 0, :], positions).astype(jnp.bfloat16)
    key_rows = rotate_rows(projected[:, :, 1, :], positions).astype(jnp.bfloat16)
    value_rows = projected[:, :, 2, :].astype(jnp.bfloat16)

    def position_of(global_row):
        return global_row

    attended = run_attention(queries, positions, key_rows, value_rows, position_of)
    head_terms = jnp.dot(
        attended.reshape(tok_rows, head_count * HEAD), attn_out, preferred_element_type=jnp.float32
    )
    attn_mix = lax.psum_scatter(
        head_terms.astype(jnp.bfloat16), "ch", scatter_dimension=1, tiled=True
    ).astype(jnp.float32)
    return (stream_wide + attn_mix).astype(jnp.bfloat16)


def rotation_tables(positions):
    half_size = HEAD // 2
    frequency = 10000.0 ** (-jnp.arange(half_size, dtype=F32) * 2.0 / HEAD)
    angles = positions.astype(F32)[:, None] * frequency[None, :]
    cosine, sine = jnp.cos(angles), jnp.sin(angles)
    return jnp.concatenate([cosine, cosine], axis=1), jnp.concatenate([-sine, sine], axis=1)


def shards(
    features,
    residual_in,
    short_filter,
    medium_filter,
    skip_gain,
    out_weight,
    norm_gain,
    attn_weight,
    attn_out,
):
    rows, _, channels = features.shape
    chips = lax.axis_size("ctx") // 2
    length = medium_filter.shape[0]
    chunk = rows // 2
    ctx, ch = lax.axis_index("ctx"), lax.axis_index("ch")
    scalars = [ch, ch ^ 1, ch ^ 2, ch ^ 3, ctx // 2, ctx % 2, ctx * rows, ctx]
    meta = jnp.stack(scalars).astype(jnp.int32)

    by_kind = jnp.transpose(features, (1, 0, 2))
    medium_rows = medium_filter.T
    skip = skip_gain.reshape(1, channels)

    starts = [rows - chunk, 0]
    if lax.axis_size("ch") != 4 or attn_weight.shape[1] != 3 * HEAD * chips or chips != 4:
        halo = shift_rows(by_kind[:, rows - length - LEAD :])
        (lower,) = gated_chunk(meta, by_kind, halo, chunk, chunk, short_filter, medium_rows, skip)
        (upper,) = gated_chunk(meta, by_kind, halo, 0, chunk, short_filter, medium_rows, skip)
        return after_gating(
            jnp.concatenate([upper, lower], axis=0), residual_in, out_weight, norm_gain, attn_weight, attn_out
        )

    gain = norm_gain.reshape(1, -1)
    cosine, sine = rotation_tables(meta[6:7] + jnp.arange(rows, dtype=jnp.int32))

    *near_w, edge = pick(meta, attn_out, by_kind, length + LEAD)
    halo = shift_rows(edge)
    picked = [swap_ch(weight, mask) for mask, weight in zip((1, 2, 3), near_w)]

    lower, out_held = gated_chunk(meta, by_kind, halo, chunk, chunk, short_filter, medium_rows, skip, out_weight)
    (upper,) = gated_chunk(meta, by_kind, halo, 0, chunk, short_filter, medium_rows, skip)
    picked, _ = lax.optimization_barrier((picked, upper))
    picked = jnp.stack(picked)
    swapped = swap_ctx(picked, 2)
    across_x, across_y = column_terms(meta, upper, lower, out_held, ((3, 0, 0, 0), (3, 1, 1, 0)))
    across_x, across_y = swap_ch(across_x, 1), swap_ch(across_y, 2)
    pieces = ((1, 0, 0, 0), (2, 1, 1, 0), (1, 1, 2, 0), (2, 0, 3, 0), (0, 0, 4, 0), (0, 1, 4, 1))
    direct_x, direct_y, along_x, along_y, kept = column_terms(meta, upper, lower, out_held, pieces, [picked])
    direct_x, direct_y = swap_ch(direct_x, 1), swap_ch(direct_y, 2)
    along_x = (along_x.astype(F32) + across_y.astype(F32)).astype(BF16)
    along_y = (along_y.astype(F32) + across_x.astype(F32)).astype(BF16)
    late_x, late_y = swap_ch(along_x, 1), swap_ch(along_y, 2)
    swapped, _ = lax.optimization_barrier((swapped, along_y))
    near_w = jnp.stack([picked, swapped])
    far_w = swap_ctx(near_w, 1)
    qkv_held, own_w = load(meta, attn_weight, attn_out, along_y, channels)
    parts = vmem_call(
        stream_kernel,
        "add_stream",
        1,
        meta,
        [kept, direct_x, direct_y, late_x, late_y, residual_in],
        [((chunk, channels), BF16)] * 2,
        waits=[qkv_held, far_w],
    )

    own, other, after = [], [], None
    width = attn_weight.shape[1]
    for start in starts:
        part = parts[start // chunk]
        if after is not None:
            part, _ = lax.optimization_barrier((part, after))
        by_x, by_y = swap_ch(part, 1), swap_ch(part, 2)
        diag_a, diag_b = swap_ch(by_x[: chunk // 2], 2), swap_ch(by_y[chunk // 2 :], 1)
        near, square = vmem_call(
            near_kernel,
            "qkv_near",
            3,
            meta,
            [part, by_x, by_y, gain, qkv_held],
            [((chunk, width), F32), ((chunk, LANES), F32)],
        )
        after = diag_a, diag_b, square
        turn = slice(start, start + chunk)
        outs = vmem_call(
            functools.partial(far_kernel, chips),
            "qkv_far",
            2,
            meta,
            [diag_a, diag_b, near, square, gain, cosine[turn], sine[turn], qkv_held],
            [((3, chunk, HEAD), BF16)] * chips,
            [pltpu.VMEM((chunk, width), F32)],
        )
        arrived = [outs[0]] + [rotate_chips(outs[d], d) for d in range(1, chips)]
        own.append(arrived)

    own, _ = lax.optimization_barrier((own, outs))
    other = [swap_ctx(jnp.stack([piece[1:] for piece in arrived]), 1) for arrived in own]
    own, other = own[1] + own[0], other[::-1]

    groups = [(*range(2, chips, 2), 0), tuple(range(1, chips, 2))]
    given, laid = attend(meta, own, other, None, groups[0], chips)
    first = [rotate_chips(piece, d) if d else piece for d, piece in zip(groups[0], given)]
    given, _ = attend(meta, own, other, laid, groups[1], chips)
    first, given = lax.optimization_barrier((first, given))
    second = [rotate_chips(piece, d) for d, piece in zip(groups[1], given)]
    back = jnp.stack(first)
    by_x, by_y = swap_ch(back, 1), swap_ch(back, 2)
    second, by_x, by_y = lax.optimization_barrier((second, by_x, by_y))
    heads = [back, by_x, by_y, swap_ch(by_x, 2)]
    back = jnp.stack(second)
    by_x, by_y = swap_ch(back, 1), swap_ch(back, 2)
    heads += [back, by_x, by_y, swap_ch(by_y, 1)]
    places = [(group, source) for group in range(2) for source in range(4)]
    weights = own_w, near_w, far_w
    early = mix(meta, heads[:-1], groups, places[:-1], parts, *weights, F32, chips)
    return mix(meta, heads[-1:], groups, places[-1:], [early], *weights, BF16, chips)


def solution(mesh):
    in_specs = (
        P("ctx", None, "ch"),
        P("ctx", "ch"),
        P(None, None, "ch"),
        P(None, "ch"),
        P("ch"),
        P("ch", None),
        P(),
        P(None, "ch"),
        P("ch", None),
    )
    out_specs = P("ctx", "ch")
    return jax.shard_map(shards, mesh=mesh, in_specs=in_specs, out_specs=out_specs, check_vma=False)
```

```python
import functools

import jax
import jax.numpy as jnp
from jax import lax
from jax.experimental import pallas as pl
from jax.experimental.pallas import tpu as pltpu
from jax.sharding import PartitionSpec as P

HEAD = 128
GROUP_SIZE = 16
LANES = 128
LEAD = 16
norm_eps = 1e-05
SCORE_SCALE = 1.4426950408889634 / HEAD**0.5
MIB = 1024 * 1024
F32 = jnp.float32
BF16 = jnp.bfloat16


def lasting(micros):
    return pl.CostEstimate(
        flops=int(micros * 1.1e9), transcendentals=0, bytes_accessed=int(micros * 3.6e6)
    )


def swap_ch(value, mask):
    count = lax.axis_size("ch")
    return lax.ppermute(value, "ch", [(i, i ^ mask) for i in range(count)])


def swap_ctx(value, mask):
    count = lax.axis_size("ctx")
    return lax.ppermute(value, "ctx", [(i, i ^ mask) for i in range(count)])


def shift_rows(value):
    count = lax.axis_size("ctx")
    return lax.ppermute(value, "ctx", [(i, i + 1) for i in range(count - 1)])


def rotate_chips(value, distance):
    count = lax.axis_size("ctx")
    return lax.ppermute(value, "ctx", [(i, (i + 2 * distance) % count) for i in range(count)])


def filter_tile(first_row, tile, short_ref, medium_ref, skip_ref, halo_ref, rows_ref, wide, product, table, store):
    taps, groups_all = short_ref.shape[1:]
    length = medium_ref.shape[1]
    groups = LANES // GROUP_SIZE
    medium = medium_ref[pl.ds(pl.multiple_of(tile * groups, groups), groups), :]
    gain = skip_ref[:, pl.ds(pl.multiple_of(tile * LANES, LANES), LANES)]
    span = wide.shape[1]
    halo_rows = length + LEAD
    count = span - halo_rows

    for kind in range(3):
        if first_row == 0:
            wide[kind, :halo_rows] = halo_ref[kind].astype(F32)
            wide[kind, halo_rows:] = rows_ref[kind].astype(F32)
        else:
            wide[kind] = rows_ref[kind, first_row - halo_rows : first_row + count].astype(F32)

    group_row = lax.broadcasted_iota(jnp.int32, (groups_all, LANES), 0)
    group_col = lax.broadcasted_iota(jnp.int32, (groups_all, LANES), 1) // GROUP_SIZE + tile * groups
    chosen = jnp.where(group_row == group_col, 1.0, 0.0).astype(F32)
    weights = [
        jnp.dot(short_ref[kind], chosen, precision=lax.Precision.HIGHEST, preferred_element_type=F32)
        for kind in range(3)
    ]

    tap_row = lax.broadcasted_iota(jnp.int32, (length, 2 * length), 0)
    place = lax.broadcasted_iota(jnp.int32, (length, 2 * length), 1)
    turned = jnp.where(tap_row + place == length, 1.0, 0.0).astype(BF16)
    base = jnp.dot(medium.astype(BF16), turned, preferred_element_type=F32)
    for group in range(groups):
        spread = jnp.broadcast_to(base[group : group + 1, :], (length, 2 * length))
        rolled = pltpu.roll(spread, 0, 1, stride=1, stride_axis=0)
        table[group * length : (group + 1) * length, :] = rolled.astype(BF16)

    def featured(kind, start):
        total = weights[kind][0:1, :] * wide[kind, start : start + length, :]
        for tap in range(1, taps):
            total = total + weights[kind][tap : tap + 1, :] * wide[kind, start - tap : start - tap + length, :]
        return total

    for block in range(count // length + 1):
        start = LEAD + block * length
        product[block * length : (block + 1) * length, :] = (
            featured(1, start) * featured(2, start)
        ).astype(BF16)

    group_of = lax.broadcasted_iota(jnp.int32, (length, 2 * LANES), 1) % LANES // GROUP_SIZE
    for pair in range(count // (2 * length)):
        begin = pair * 2 * length
        window = jnp.concatenate(
            [
                product[begin : begin + 2 * length, :],
                product[begin + length : begin + 3 * length, :],
            ],
            axis=1,
        )
        spread = jnp.dot(table[...], window, preferred_element_type=F32)
        mixed = spread[:length]
        for group in range(1, groups):
            mixed = jnp.where(group_of == group, spread[group * length : (group + 1) * length], mixed)
        for part in range(2):
            row = begin + part * length
            direct = gain * product[row + length : row + 2 * length, :].astype(F32)
            gate = featured(0, halo_rows + row)
            store(row, (gate * (mixed[:, part * LANES : (part + 1) * LANES] + direct)).astype(BF16))


def gated_kernel(first_row, loads, *refs):
    head, rest = refs[1:4], refs[4:]
    halo_ref, rest = (rest[0], rest[1:]) if first_row == 0 else (None, rest)
    rows_ref, rest = rest[0], rest[1:]
    if loads:
        weight, out_ref, held, wide, product, table, sem = rest
        copy = pltpu.make_async_copy(weight, held, sem)
        pl.when(pl.program_id(0) == 0)(copy.start)
    else:
        out_ref, wide, product, table = rest

    def store(row, value):
        out_ref[row : row + value.shape[0], :] = value

    filter_tile(first_row, pl.program_id(0), *head, halo_ref, rows_ref, wide, product, table, store)
    if loads:
        pl.when(pl.program_id(0) == pl.num_programs(0) - 1)(copy.wait)


def gated_chunk(meta, features, halo, first_row, count, short_filter, medium_rows, skip, weight=None):
    kinds, rows, channels = features.shape
    length = medium_rows.shape[1]
    groups = LANES // GROUP_SIZE
    loads = weight is not None
    in_hbm = lambda x: pltpu.with_memory_space_constraint(x, pltpu.HBM)
    in_specs = [
        pl.BlockSpec(memory_space=pltpu.SMEM),
        pl.BlockSpec(short_filter.shape, lambda i: (0, 0, 0)),
        pl.BlockSpec(medium_rows.shape, lambda i: (0, 0)),
        pl.BlockSpec(skip.shape, lambda i: (0, 0)),
    ]
    operands = [meta, in_hbm(short_filter), in_hbm(medium_rows), in_hbm(skip)]
    out_specs = [pl.BlockSpec((count, LANES), lambda i: (0, i))]
    out_shape = [jax.ShapeDtypeStruct((count, channels), BF16)]
    scratch = [
        pltpu.VMEM((kinds, length + LEAD + count, LANES), F32),
        pltpu.VMEM((length + count, LANES), BF16),
        pltpu.VMEM((groups * length, 2 * length), BF16),
    ]
    if first_row == 0:
        in_specs.append(pl.BlockSpec((kinds, length + LEAD, LANES), lambda i: (0, 0, i)))
        in_specs.append(pl.BlockSpec((kinds, count, LANES), lambda i: (0, 0, i)))
        operands += [halo, features]
    else:
        in_specs.append(pl.BlockSpec((kinds, rows, LANES), lambda i: (0, 0, i)))
        operands.append(features)
    if loads:
        in_specs.append(pl.BlockSpec(memory_space=pltpu.HBM))
        operands.append(in_hbm(weight))
        out_specs.append(pl.BlockSpec(memory_space=pltpu.VMEM))
        out_shape.append(pltpu.VMEM(weight.shape, weight.dtype))
        scratch.append(pltpu.SemaphoreType.DMA)
    return pl.pallas_call(
        functools.partial(gated_kernel, first_row, loads),
        grid=(channels // LANES,),
        in_specs=in_specs,
        out_specs=out_specs,
        out_shape=out_shape,
        scratch_shapes=scratch,
        compiler_params=pltpu.CompilerParams(vmem_limit_bytes=16 * MIB),
        name="hyena_filters",
    )(*operands)


def vmem_call(body, name, micros, scalars, operands, outs, scratch=(), waits=()):
    given = 1 + len(operands)
    run = lambda *refs: body(*refs[:given], *refs[given + len(waits) :])
    return pl.pallas_call(
        run,
        in_specs=[pl.BlockSpec(memory_space=pltpu.SMEM)]
        + [pl.BlockSpec(memory_space=pltpu.VMEM)] * (len(operands) + len(waits)),
        out_specs=[pl.BlockSpec(memory_space=pltpu.VMEM)] * len(outs),
        out_shape=[jax.ShapeDtypeStruct(shape, kind) for shape, kind in outs],
        scratch_shapes=list(scratch),
        compiler_params=pltpu.CompilerParams(vmem_limit_bytes=20 * MIB),
        cost_estimate=lasting(micros) if micros else None,
        name=name,
    )(scalars, *operands, *waits)


def columns_kernel(pieces, meta_ref, upper, lower, weight, *outs):
    gated = jnp.concatenate([upper[...], lower[...]], axis=0)
    width = weight.shape[1] // 8
    for owner, half, out, part in pieces:
        columns = pl.ds(pl.multiple_of((2 * meta_ref[owner] + half) * width, width), width)
        term = jnp.dot(gated, weight[:, columns], preferred_element_type=F32)
        outs[out][:, part * width : (part + 1) * width] = term.astype(BF16)


def column_terms(meta, upper, lower, weight, pieces, waits=()):
    rows, width = 2 * upper.shape[0], weight.shape[1] // 8
    outs = [((rows, width * sum(p[2] == out for p in pieces)), BF16) for out in range(pieces[-1][2] + 1)]
    body = functools.partial(columns_kernel, pieces)
    return vmem_call(body, "hyena_terms", None, meta, [upper, lower, weight], outs, waits=waits)


def load_kernel(meta_ref, source, outer, along, swapped, held, own, sems):
    channels = own.shape[1]
    columns = pl.ds(pl.multiple_of(meta_ref[0] * channels, channels), channels)
    copies = [
        pltpu.make_async_copy(source, held, sems.at[0]),
        pltpu.make_async_copy(outer.at[:, columns], own, sems.at[1]),
    ]
    for copy in copies:
        copy.start()
    for copy in copies:
        copy.wait()


def load(meta, weight, outer, after, channels):
    in_hbm = lambda x: pltpu.with_memory_space_constraint(x, pltpu.HBM)
    hbm, vmem = pl.BlockSpec(memory_space=pltpu.HBM), pl.BlockSpec(memory_space=pltpu.VMEM)
    return pl.pallas_call(
        load_kernel,
        in_specs=[pl.BlockSpec(memory_space=pltpu.SMEM), hbm, hbm, vmem, vmem],
        out_specs=[vmem, vmem],
        out_shape=[pltpu.VMEM(weight.shape, weight.dtype), pltpu.VMEM((outer.shape[0], channels), outer.dtype)],
        scratch_shapes=[pltpu.SemaphoreType.DMA((2,))],
        compiler_params=pltpu.CompilerParams(vmem_limit_bytes=4 * MIB),
        name="load_weights",
    )(meta, in_hbm(weight), in_hbm(outer), *after)


def stream_kernel(_, kept, direct_x, direct_y, late_x, late_y, residual, *parts):
    half = late_x.shape[1]
    rows = parts[0].shape[0]
    for index, out in enumerate(parts):
        span = slice(index * rows, (index + 1) * rows)
        wide = lambda ref: ref[span].astype(F32)
        left = wide(residual)[:, :half] + (wide(kept)[:, :half] + wide(direct_x) + wide(late_y))
        right = wide(residual)[:, half:] + (wide(kept)[:, half:] + wide(direct_y) + wide(late_x))
        out[...] = jnp.concatenate([left, right], axis=1).astype(BF16)


def near_kernel(meta_ref, *refs):
    blocks, (gain, weight, total, square) = refs[:3], refs[3:]
    channels = blocks[0].shape[1]
    squares = jnp.zeros(square.shape, F32)
    result = None
    for index in range(3):
        wide = blocks[index][...].astype(F32)
        squares = squares + jnp.sum(wide * wide, axis=1, keepdims=True)
        span = pl.ds(pl.multiple_of(meta_ref[index] * channels, channels), channels)
        factor, block = gain[:, span], weight[span, :]
        term = jnp.dot((wide * factor).astype(BF16), block, preferred_element_type=F32)
        result = term if result is None else result + term
    total[...] = result
    square[...] = squares


def far_kernel(chips, meta_ref, diag_a, diag_b, near, square, gain, cosine, sine, weight, *rest):
    outs, total = rest[:chips], rest[chips]
    channels = diag_a.shape[1]
    wide = jnp.concatenate([diag_a[...], diag_b[...]], axis=0).astype(F32)
    squares = square[...] + jnp.sum(wide * wide, axis=1, keepdims=True)
    span = pl.ds(pl.multiple_of(meta_ref[3] * channels, channels), channels)
    factor, block = gain[:, span], weight[span, :]
    total[...] = near[...] + jnp.dot((wide * factor).astype(BF16), block, preferred_element_type=F32)
    inverse = lax.rsqrt(squares / (4 * channels) + norm_eps)
    for distance, out in enumerate(outs):
        head = lax.rem(meta_ref[4] + distance, chips)
        for kind in range(3):
            column = pl.multiple_of((head * 3 + kind) * HEAD, HEAD)
            part = total[:, pl.ds(column, HEAD)] * inverse
            if kind < 2:
                part = part * cosine[...] + pltpu.roll(part, HEAD // 2, 1) * sine[...]
            if kind == 0:
                part = part * SCORE_SCALE
            if kind == 2:
                tiles = [part[row : row + HEAD].T for row in range(0, part.shape[0], HEAD)]
                part = jnp.concatenate(tiles, axis=0)
            out[kind] = part.astype(BF16)


def gather_keys(chips, meta_ref, own, other, keys, values):
    rows = own[0].shape[1]
    for distance in range(chips):
        place = lax.rem(meta_ref[4] - distance + chips, chips)
        for chunk, stacked in enumerate(other):
            mine = own[chunk * chips + distance]
            span = slice(chunk * rows, (chunk + 1) * rows)
            keys[0, place, span, :] = mine[1]
            keys[1, place, span, :] = stacked[distance, 0]
            for tile in range(rows // HEAD):
                first = chunk * rows + tile * HEAD
                taken = slice(tile * HEAD, (tile + 1) * HEAD)
                values[0, place, :, first : first + HEAD] = mine[2, taken, :]
                values[1, place, :, first : first + HEAD] = stacked[distance, 1, taken, :]


def attention_kernel(chips, chunks, distances, leading, meta_ref, *refs):
    if leading:
        pieces, other = refs[: chunks * chips], refs[chunks * chips : chunks * (chips + 1)]
        *outs, keys, values = refs[chunks * (chips + 1) :]
        gather_keys(chips, meta_ref, pieces, other, keys, values)
        sources = [pieces[(chips - distance) % chips :: chips] for distance in distances]
    else:
        taken = chunks * len(distances)
        pieces, (keys, values), outs = refs[:taken], refs[taken : taken + 2], refs[taken + 2 :]
        sources = [pieces[index * chunks : (index + 1) * chunks] for index in range(len(distances))]
    chip, core = meta_ref[4], meta_ref[5]
    count = keys.shape[2]

    def scores_of(side, place, queries):
        return lax.dot_general(
            keys[side, place], queries, (((1,), (1,)), ((), ())), preferred_element_type=F32
        )

    def update(state, mine, others, place):
        top, total, acc = state
        new_top = jnp.maximum(jnp.max(mine, axis=0, keepdims=True), jnp.max(others, axis=0, keepdims=True))
        if top is not None:
            new_top = jnp.maximum(new_top, top)
        mine = jnp.exp2(mine - new_top)
        others = jnp.exp2(others - new_top)
        gained = jnp.sum(mine, axis=0, keepdims=True) + jnp.sum(others, axis=0, keepdims=True)
        added = jnp.dot(values[0, place], mine.astype(BF16), preferred_element_type=F32)
        added = added + jnp.dot(values[1, place], others.astype(BF16), preferred_element_type=F32)
        if top is None:
            return new_top, gained, added
        shrink = jnp.exp2(top - new_top)
        return new_top, total * shrink + gained, acc * shrink + added

    key_row = lax.broadcasted_iota(jnp.int32, (count, count), 0)
    query_column = lax.broadcasted_iota(jnp.int32, (count, count), 1)
    for distance, source, out in zip(distances, sources, outs):
        place = lax.rem(chip + distance, chips)
        queries = jnp.concatenate([piece[0] for piece in source], axis=0)
        mine = jnp.where(key_row <= query_column, scores_of(0, place, queries), -1e30)
        others = jnp.where(core == 1, scores_of(1, place, queries), -1e30)
        state = update((None, None, None), mine, others, place)

        def earlier(index, state):
            return update(state, scores_of(0, index, queries), scores_of(1, index, queries), index)

        state = lax.fori_loop(0, place, earlier, state)
        out[...] = (state[2] / state[1]).T.astype(BF16)


def attend(meta, own, other, laid, distances, waits, chips):
    chunks, leading = len(other), laid is None
    count = own[0].shape[1] * chunks
    outs = [((count, HEAD), BF16)] * len(distances)
    if leading:
        operands = own + other
        outs = outs + [((2, chips, count, HEAD), BF16), ((2, chips, HEAD, count), BF16)]
    else:
        operands = [piece for distance in distances for piece in own[(chips - distance) % chips :: chips]]
        operands = [*operands, *laid]
    body = functools.partial(attention_kernel, chips, chunks, distances, leading)
    made = list(vmem_call(body, "attention", 6, meta, operands, outs, waits=waits))
    return made[: len(distances)], laid or made[len(distances) :]


def pick_kernel(meta_ref, weight, features, *refs):
    *near, edge, sems = refs
    channels = near[0].shape[1]
    kinds, count, _ = edge.shape
    last = features.shape[1] - count
    copies = []
    for kind in range(kinds):
        copies.append(
            pltpu.make_async_copy(features.at[kind, last : last + count], edge.at[kind], sems.at[kind])
        )
    rows = pl.ds(pl.multiple_of((2 * lax.rem(meta_ref[4], 2) + meta_ref[5]) * HEAD, HEAD), HEAD)
    for index, out in enumerate(near):
        columns = pl.ds(pl.multiple_of(meta_ref[index + 1] * channels, channels), channels)
        copies.append(pltpu.make_async_copy(weight.at[rows, columns], out, sems.at[kinds + index]))
    for copy in copies:
        copy.start()
    for copy in copies:
        copy.wait()


def pick(meta, weight, features, count):
    kinds, _, channels = features.shape
    near = jax.ShapeDtypeStruct((HEAD, channels), BF16)
    in_hbm = lambda x: pltpu.with_memory_space_constraint(x, pltpu.HBM)
    hbm, vmem = pl.BlockSpec(memory_space=pltpu.HBM), pl.BlockSpec(memory_space=pltpu.VMEM)
    return pl.pallas_call(
        pick_kernel,
        in_specs=[pl.BlockSpec(memory_space=pltpu.SMEM), hbm, hbm],
        out_specs=[vmem] * 4,
        out_shape=[near, near, near, jax.ShapeDtypeStruct((kinds, count, channels), BF16)],
        scratch_shapes=[pltpu.SemaphoreType.DMA((kinds + 3,))],
        compiler_params=pltpu.CompilerParams(vmem_limit_bytes=4 * MIB),
        name="pick",
    )(meta, in_hbm(weight), in_hbm(features))


def mix_kernel(chips, groups, items, streams, meta_ref, *refs):
    heads, refs = refs[: len(items)], refs[len(items) :]
    before, (own_w, near_w, far_w, out, ordered) = refs[:streams], refs[streams:]
    chip, core = meta_ref[4], meta_ref[5]
    swapped = lax.rem(chip, 2)
    parities = [lax.rem(chip + distances[0], 2) for distances in groups]
    for place, (group, _) in enumerate(items):
        for index, distance in enumerate(groups[group]):
            head = lax.rem(chip - distance + chips, chips)
            column = pl.ds(pl.multiple_of(head // 2 * HEAD, HEAD), HEAD)
            ordered[place, :, column] = heads[place][index]

    def own_rows(parity):
        rows = [pl.ds(pl.multiple_of((2 * j + parity) * HEAD, HEAD), HEAD) for j in range(chips // 2)]
        return jnp.concatenate([own_w[span, :] for span in rows], axis=0)

    def finish(by_group):
        total = jnp.concatenate([part[...].astype(F32) for part in before], axis=0)
        for place, (group, source) in enumerate(items):
            if source:
                held = by_group[group]
                weights = jnp.concatenate([held[swapped, source - 1], held[1 - swapped, source - 1]], axis=0)
            else:
                weights = own_rows(parities[group])
            total = total + jnp.dot(ordered[place], weights, preferred_element_type=F32)
        out[...] = total.astype(out.dtype)

    @pl.when(core == parities[0])
    def _():
        finish([near_w, far_w])

    @pl.when(core != parities[0])
    def _():
        finish([far_w, near_w])


def mix(meta, heads, groups, items, before, own_w, near_w, far_w, kind, chips):
    rows, channels = heads[0].shape[1], own_w.shape[1]
    body = functools.partial(mix_kernel, chips, groups, items, len(before))
    operands = [*heads, *before, own_w, near_w, far_w]
    scratch = [pltpu.VMEM((len(items), rows, chips // 2 * HEAD), BF16)]
    micros = 0.6 * len(items)
    return vmem_call(body, "attention_mix", micros, meta, operands, [((rows, channels), kind)], scratch)[0]


def rotate_rows(block, positions):
    half_size = block.shape[-1] // 2
    frequency = 10000.0 ** (-jnp.arange(half_size, dtype=jnp.float32) * 2.0 / block.shape[-1])
    angles = positions.astype(jnp.float32)[:, None] * frequency[None, :]
    cosine = jnp.cos(angles)[:, None, :]
    sine_part = jnp.sin(angles)[:, None, :]
    first_half = block[..., :half_size]
    second_half = block[..., half_size:]
    return jnp.concatenate(
        [
            first_half * cosine - second_half * sine_part,
            second_half * cosine + first_half * sine_part,
        ],
        axis=-1,
    )


def run_attention(queries, query_pos, key_rows, value_rows, position_of):
    head_count = queries.shape[1]
    row_count = queries.shape[0]
    head_size = queries.shape[2]
    scale_factor = 1.0 / head_size**0.5
    last_query = jnp.max(query_pos)
    initial = (
        jnp.zeros((head_count, row_count, head_size), jnp.float32),
        jnp.full((head_count, row_count), -1e30, jnp.float32),
        jnp.zeros((head_count, row_count), jnp.float32),
    )
    piece_keys = lax.all_gather(key_rows, "ctx", axis=0, tiled=True)
    piece_values = lax.all_gather(value_rows, "ctx", axis=0, tiled=True)
    piece_rows = piece_keys.shape[0]
    block_rows = 512

    def one_block(state_in, block_index):
        first_block = block_index * block_rows
        key_block = lax.dynamic_slice_in_dim(piece_keys, first_block, block_rows, 0)
        value_block = lax.dynamic_slice_in_dim(piece_values, first_block, block_rows, 0)
        key_pos = position_of(first_block + jnp.arange(block_rows))

        def update(state_old):
            acc_sum, run_max, run_total = state_old
            scores = (
                jnp.einsum("thd,khd->htk", queries, key_block, preferred_element_type=jnp.float32)
                * scale_factor
            )
            causal = (key_pos[None, :] <= query_pos[:, None])[None]
            block_max = jnp.max(jnp.where(causal, scores, -1e30), axis=-1)
            new_max = jnp.maximum(run_max, block_max)
            weights = jnp.where(causal, jnp.exp(scores - new_max[..., None]), 0.0)
            correction = jnp.exp(run_max - new_max)
            new_total = run_total * correction + jnp.sum(weights, axis=-1)
            update_sum = jnp.einsum(
                "htk,khd->htd",
                weights.astype(jnp.bfloat16),
                value_block,
                preferred_element_type=jnp.float32,
            )
            return (acc_sum * correction[..., None] + update_sum, new_max, new_total)

        def unchanged(state_old):
            return state_old

        state_out = lax.cond(jnp.min(key_pos) > last_query, unchanged, update, state_in)
        return (state_out, None)

    state_end, unused = lax.scan(one_block, initial, jnp.arange(piece_rows // block_rows))
    acc_sum, run_max, run_total = state_end
    output = acc_sum / run_total[..., None]
    return jnp.transpose(output, (1, 0, 2)).astype(jnp.bfloat16)


def after_gating(gated, residual_in, out_weight, norm_gain, attn_weight, attn_out):
    tok_rows, chan_count = gated.shape
    hyena_terms = jnp.dot(gated, out_weight, preferred_element_type=jnp.float32)
    hyena_out = lax.psum_scatter(
        hyena_terms.astype(jnp.bfloat16), "ch", scatter_dimension=1, tiled=True
    ).astype(jnp.float32)
    stream = (residual_in.astype(jnp.float32) + hyena_out).astype(jnp.bfloat16)
    stream_wide = stream.astype(jnp.float32)
    full_width = chan_count * lax.axis_size("ch")
    head_cols = attn_weight.shape[1]
    square_total = lax.psum(jnp.sum(stream_wide * stream_wide, axis=1), "ch")
    inverse = lax.rsqrt(square_total / full_width + norm_eps)
    gain_part = lax.dynamic_slice_in_dim(norm_gain, lax.axis_index("ch") * chan_count, chan_count)
    normed = (stream_wide * inverse[:, None] * gain_part[None, :]).astype(jnp.bfloat16)
    projected = jnp.dot(
        lax.all_gather(normed, "ch", axis=1, tiled=True),
        attn_weight,
        preferred_element_type=jnp.float32,
    )
    head_count = head_cols // (3 * HEAD)
    projected = projected.reshape(tok_rows, head_count, 3, HEAD)
    ctx_index = lax.axis_index("ctx")
    positions = ctx_index * tok_rows + jnp.arange(tok_rows, dtype=jnp.int32)
    queries = rotate_rows(projected[:, :, 0, :], positions).astype(jnp.bfloat16)
    key_rows = rotate_rows(projected[:, :, 1, :], positions).astype(jnp.bfloat16)
    value_rows = projected[:, :, 2, :].astype(jnp.bfloat16)

    def position_of(global_row):
        return global_row

    attended = run_attention(queries, positions, key_rows, value_rows, position_of)
    head_terms = jnp.dot(
        attended.reshape(tok_rows, head_count * HEAD), attn_out, preferred_element_type=jnp.float32
    )
    attn_mix = lax.psum_scatter(
        head_terms.astype(jnp.bfloat16), "ch", scatter_dimension=1, tiled=True
    ).astype(jnp.float32)
    return (stream_wide + attn_mix).astype(jnp.bfloat16)


def rotation_tables(positions):
    half_size = HEAD // 2
    frequency = 10000.0 ** (-jnp.arange(half_size, dtype=F32) * 2.0 / HEAD)
    angles = positions.astype(F32)[:, None] * frequency[None, :]
    cosine, sine = jnp.cos(angles), jnp.sin(angles)
    return jnp.concatenate([cosine, cosine], axis=1), jnp.concatenate([-sine, sine], axis=1)


def shards(
    features,
    residual_in,
    short_filter,
    medium_filter,
    skip_gain,
    out_weight,
    norm_gain,
    attn_weight,
    attn_out,
):
    rows, _, channels = features.shape
    chips = lax.axis_size("ctx") // 2
    length = medium_filter.shape[0]
    chunk = rows // 2
    ctx, ch = lax.axis_index("ctx"), lax.axis_index("ch")
    scalars = [ch, ch ^ 1, ch ^ 2, ch ^ 3, ctx // 2, ctx % 2, ctx * rows, ctx]
    meta = jnp.stack(scalars).astype(jnp.int32)

    by_kind = jnp.transpose(features, (1, 0, 2))
    medium_rows = medium_filter.T
    skip = skip_gain.reshape(1, channels)

    starts = [rows - chunk, 0]
    if lax.axis_size("ch") != 4 or attn_weight.shape[1] != 3 * HEAD * chips or chips != 4:
        halo = shift_rows(by_kind[:, rows - length - LEAD :])
        (lower,) = gated_chunk(meta, by_kind, halo, chunk, chunk, short_filter, medium_rows, skip)
        (upper,) = gated_chunk(meta, by_kind, halo, 0, chunk, short_filter, medium_rows, skip)
        return after_gating(
            jnp.concatenate([upper, lower], axis=0), residual_in, out_weight, norm_gain, attn_weight, attn_out
        )

    gain = norm_gain.reshape(1, -1)
    cosine, sine = rotation_tables(meta[6:7] + jnp.arange(rows, dtype=jnp.int32))

    *near_w, edge = pick(meta, attn_out, by_kind, length + LEAD)
    halo = shift_rows(edge)
    picked = [swap_ch(weight, mask) for mask, weight in zip((1, 2, 3), near_w)]

    lower, out_held = gated_chunk(meta, by_kind, halo, chunk, chunk, short_filter, medium_rows, skip, out_weight)
    (upper,) = gated_chunk(meta, by_kind, halo, 0, chunk, short_filter, medium_rows, skip)
    across_x, across_y = column_terms(meta, upper, lower, out_held, ((3, 0, 0, 0), (3, 1, 1, 0)), picked)
    picked = jnp.stack(picked)
    swapped = swap_ctx(picked, 2)
    across_x, across_y = swap_ch(across_x, 1), swap_ch(across_y, 2)
    pieces = ((1, 0, 0, 0), (2, 1, 1, 0), (1, 1, 2, 0), (2, 0, 3, 0), (0, 0, 4, 0), (0, 1, 4, 1))
    direct_x, direct_y, along_x, along_y, kept = column_terms(meta, upper, lower, out_held, pieces, [picked])
    direct_x, direct_y = swap_ch(direct_x, 1), swap_ch(direct_y, 2)
    along_x = (along_x.astype(F32) + across_y.astype(F32)).astype(BF16)
    along_y = (along_y.astype(F32) + across_x.astype(F32)).astype(BF16)
    late_x, late_y = swap_ch(along_x, 1), swap_ch(along_y, 2)
    qkv_held, own_w = load(meta, attn_weight, attn_out, (along_y, swapped), channels)
    parts = vmem_call(
        stream_kernel,
        "add_stream",
        1,
        meta,
        [kept, direct_x, direct_y, late_x, late_y, residual_in],
        [((chunk, channels), BF16)] * 2,
        waits=[qkv_held],
    )

    own, other, after = [], [], None
    width = attn_weight.shape[1]
    for start in starts:
        part = parts[start // chunk]
        if after is not None:
            part, _ = lax.optimization_barrier((part, after))
        by_x, by_y = swap_ch(part, 1), swap_ch(part, 2)
        diag_a, diag_b = swap_ch(by_x[: chunk // 2], 2), swap_ch(by_y[chunk // 2 :], 1)
        near, square = vmem_call(
            near_kernel,
            "qkv_near",
            3,
            meta,
            [part, by_x, by_y, gain, qkv_held],
            [((chunk, width), F32), ((chunk, LANES), F32)],
        )
        after = diag_a, diag_b, square
        turn = slice(start, start + chunk)
        outs = vmem_call(
            functools.partial(far_kernel, chips),
            "qkv_far",
            2,
            meta,
            [diag_a, diag_b, near, square, gain, cosine[turn], sine[turn], qkv_held],
            [((3, chunk, HEAD), BF16)] * chips,
            [pltpu.VMEM((chunk, width), F32)],
        )
        arrived = [outs[0]] + [rotate_chips(outs[d], d) for d in range(1, chips)]
        own.append(arrived)

    swapped, _ = lax.optimization_barrier((swapped, outs))
    near_w = jnp.stack([picked, swapped])
    far_w = swap_ctx(near_w, 1)
    own, _ = lax.optimization_barrier((own, outs))
    other = [swap_ctx(jnp.stack([piece[1:] for piece in arrived]), 1) for arrived in own]
    own, other = own[1] + own[0], other[::-1]

    groups = [(*range(2, chips, 2), 0), tuple(range(1, chips, 2))]
    given, laid = attend(meta, own, other, None, groups[0], [far_w], chips)
    first = [rotate_chips(piece, d) if d else piece for d, piece in zip(groups[0], given)]
    given, _ = attend(meta, own, other, laid, groups[1], [], chips)
    first, given = lax.optimization_barrier((first, given))
    second = [rotate_chips(piece, d) for d, piece in zip(groups[1], given)]
    back = jnp.stack(first)
    by_x, by_y = swap_ch(back, 1), swap_ch(back, 2)
    second, by_x, by_y = lax.optimization_barrier((second, by_x, by_y))
    heads = [back, by_x, by_y, swap_ch(by_x, 2)]
    back = jnp.stack(second)
    by_x, by_y = swap_ch(back, 1), swap_ch(back, 2)
    heads += [back, by_x, by_y, swap_ch(by_y, 1)]
    places = [(group, source) for group in range(2) for source in range(4)]
    weights = own_w, near_w, far_w
    early = mix(meta, heads[:-1], groups, places[:-1], parts, *weights, F32, chips)
    return mix(meta, heads[-1:], groups, places[-1:], [early], *weights, BF16, chips)


def solution(mesh):
    in_specs = (
        P("ctx", None, "ch"),
        P("ctx", "ch"),
        P(None, None, "ch"),
        P(None, "ch"),
        P("ch"),
        P("ch", None),
        P(),
        P(None, "ch"),
        P("ch", None),
    )
    out_specs = P("ctx", "ch")
    return jax.shard_map(shards, mesh=mesh, in_specs=in_specs, out_specs=out_specs, check_vma=False)
```

```python
import functools

import jax
import jax.numpy as jnp
from jax import lax
from jax.experimental import pallas as pl
from jax.experimental.pallas import tpu as pltpu
from jax.sharding import PartitionSpec as P

HEAD = 128
GROUP_SIZE = 16
LANES = 128
TILES = 2
LEAD = 16
norm_eps = 1e-05
SCORE_SCALE = 1.4426950408889634 / HEAD**0.5
MIB = 1024 * 1024
F32 = jnp.float32
BF16 = jnp.bfloat16


def lasting(micros):
    return pl.CostEstimate(
        flops=int(micros * 1.1e9), transcendentals=0, bytes_accessed=int(micros * 3.6e6)
    )


def swap_ch(value, mask):
    count = lax.axis_size("ch")
    return lax.ppermute(value, "ch", [(i, i ^ mask) for i in range(count)])


def swap_ctx(value, mask):
    count = lax.axis_size("ctx")
    return lax.ppermute(value, "ctx", [(i, i ^ mask) for i in range(count)])


def shift_rows(value):
    count = lax.axis_size("ctx")
    return lax.ppermute(value, "ctx", [(i, i + 1) for i in range(count - 1)])


def rotate_chips(value, distance):
    count = lax.axis_size("ctx")
    return lax.ppermute(value, "ctx", [(i, (i + 2 * distance) % count) for i in range(count)])


def filter_tile(first_row, tile, lanes, short_ref, medium_ref, skip_ref, halo_ref, rows_ref, wide, product, table, store):
    taps, groups_all = short_ref.shape[1:]
    length = medium_ref.shape[1]
    groups = LANES // GROUP_SIZE
    medium = medium_ref[pl.ds(pl.multiple_of(tile * groups, groups), groups), :]
    gain = skip_ref[:, pl.ds(pl.multiple_of(tile * LANES, LANES), LANES)]
    span = wide.shape[1]
    halo_rows = length + LEAD
    count = span - halo_rows

    for kind in range(3):
        if first_row == 0:
            wide[kind, :halo_rows] = halo_ref[kind, :, lanes].astype(F32)
            wide[kind, halo_rows:] = rows_ref[kind, :, lanes].astype(F32)
        else:
            wide[kind] = rows_ref[kind, first_row - halo_rows : first_row + count, lanes].astype(F32)

    group_row = lax.broadcasted_iota(jnp.int32, (groups_all, LANES), 0)
    group_col = lax.broadcasted_iota(jnp.int32, (groups_all, LANES), 1) // GROUP_SIZE + tile * groups
    chosen = jnp.where(group_row == group_col, 1.0, 0.0).astype(F32)
    weights = [
        jnp.dot(short_ref[kind], chosen, precision=lax.Precision.HIGHEST, preferred_element_type=F32)
        for kind in range(3)
    ]

    tap_row = lax.broadcasted_iota(jnp.int32, (length, 2 * length), 0)
    place = lax.broadcasted_iota(jnp.int32, (length, 2 * length), 1)
    turned = jnp.where(tap_row + place == length, 1.0, 0.0).astype(BF16)
    base = jnp.dot(medium.astype(BF16), turned, preferred_element_type=F32)
    for group in range(groups):
        spread = jnp.broadcast_to(base[group : group + 1, :], (length, 2 * length))
        rolled = pltpu.roll(spread, 0, 1, stride=1, stride_axis=0)
        table[group * length : (group + 1) * length, :] = rolled.astype(BF16)

    def featured(kind, start):
        total = weights[kind][0:1, :] * wide[kind, start : start + length, :]
        for tap in range(1, taps):
            total = total + weights[kind][tap : tap + 1, :] * wide[kind, start - tap : start - tap + length, :]
        return total

    for block in range(count // length + 1):
        start = LEAD + block * length
        product[block * length : (block + 1) * length, :] = (
            featured(1, start) * featured(2, start)
        ).astype(BF16)

    group_of = lax.broadcasted_iota(jnp.int32, (length, 2 * LANES), 1) % LANES // GROUP_SIZE
    for pair in range(count // (2 * length)):
        begin = pair * 2 * length
        window = jnp.concatenate(
            [
                product[begin : begin + 2 * length, :],
                product[begin + length : begin + 3 * length, :],
            ],
            axis=1,
        )
        spread = jnp.dot(table[...], window, preferred_element_type=F32)
        mixed = spread[:length]
        for group in range(1, groups):
            mixed = jnp.where(group_of == group, spread[group * length : (group + 1) * length], mixed)
        for part in range(2):
            row = begin + part * length
            direct = gain * product[row + length : row + 2 * length, :].astype(F32)
            gate = featured(0, halo_rows + row)
            store(row, (gate * (mixed[:, part * LANES : (part + 1) * LANES] + direct)).astype(BF16))


def gated_kernel(first_row, loads, *refs):
    head, rest = refs[1:4], refs[4:]
    halo_ref, rest = (rest[0], rest[1:]) if first_row == 0 else (None, rest)
    rows_ref, rest = rest[0], rest[1:]
    if loads:
        weight, out_ref, held, wide, product, table, sem = rest
        copy = pltpu.make_async_copy(weight, held, sem)
        pl.when(pl.program_id(0) == 0)(copy.start)
    else:
        out_ref, wide, product, table = rest

    for part in range(TILES):
        lanes = slice(part * LANES, (part + 1) * LANES)

        def store(row, value):
            out_ref[row : row + value.shape[0], lanes] = value

        scratch = wide.at[part], product.at[part], table.at[part]
        tile = pl.program_id(0) * TILES + part
        filter_tile(first_row, tile, lanes, *head, halo_ref, rows_ref, *scratch, store)
    if loads:
        pl.when(pl.program_id(0) == pl.num_programs(0) - 1)(copy.wait)


def gated_chunk(meta, features, halo, first_row, count, short_filter, medium_rows, skip, weight=None):
    kinds, rows, channels = features.shape
    length = medium_rows.shape[1]
    groups = LANES // GROUP_SIZE
    step = TILES * LANES
    loads = weight is not None
    in_hbm = lambda x: pltpu.with_memory_space_constraint(x, pltpu.HBM)
    in_specs = [
        pl.BlockSpec(memory_space=pltpu.SMEM),
        pl.BlockSpec(short_filter.shape, lambda i: (0, 0, 0)),
        pl.BlockSpec(medium_rows.shape, lambda i: (0, 0)),
        pl.BlockSpec(skip.shape, lambda i: (0, 0)),
    ]
    operands = [meta, in_hbm(short_filter), in_hbm(medium_rows), in_hbm(skip)]
    out_specs = [pl.BlockSpec((count, step), lambda i: (0, i))]
    out_shape = [jax.ShapeDtypeStruct((count, channels), BF16)]
    scratch = [
        pltpu.VMEM((TILES, kinds, length + LEAD + count, LANES), F32),
        pltpu.VMEM((TILES, length + count, LANES), BF16),
        pltpu.VMEM((TILES, groups * length, 2 * length), BF16),
    ]
    if first_row == 0:
        in_specs.append(pl.BlockSpec((kinds, length + LEAD, step), lambda i: (0, 0, i)))
        in_specs.append(pl.BlockSpec((kinds, count, step), lambda i: (0, 0, i)))
        operands += [halo, features]
    else:
        in_specs.append(pl.BlockSpec((kinds, rows, step), lambda i: (0, 0, i)))
        operands.append(features)
    if loads:
        in_specs.append(pl.BlockSpec(memory_space=pltpu.HBM))
        operands.append(in_hbm(weight))
        out_specs.append(pl.BlockSpec(memory_space=pltpu.VMEM))
        out_shape.append(pltpu.VMEM(weight.shape, weight.dtype))
        scratch.append(pltpu.SemaphoreType.DMA)
    return pl.pallas_call(
        functools.partial(gated_kernel, first_row, loads),
        grid=(channels // step,),
        in_specs=in_specs,
        out_specs=out_specs,
        out_shape=out_shape,
        scratch_shapes=scratch,
        compiler_params=pltpu.CompilerParams(vmem_limit_bytes=16 * MIB),
        name="hyena_filters",
    )(*operands)


def vmem_call(body, name, micros, scalars, operands, outs, scratch=(), waits=()):
    given = 1 + len(operands)
    run = lambda *refs: body(*refs[:given], *refs[given + len(waits) :])
    return pl.pallas_call(
        run,
        in_specs=[pl.BlockSpec(memory_space=pltpu.SMEM)]
        + [pl.BlockSpec(memory_space=pltpu.VMEM)] * (len(operands) + len(waits)),
        out_specs=[pl.BlockSpec(memory_space=pltpu.VMEM)] * len(outs),
        out_shape=[jax.ShapeDtypeStruct(shape, kind) for shape, kind in outs],
        scratch_shapes=list(scratch),
        compiler_params=pltpu.CompilerParams(vmem_limit_bytes=20 * MIB),
        cost_estimate=lasting(micros) if micros else None,
        name=name,
    )(scalars, *operands, *waits)


def columns_kernel(pieces, meta_ref, upper, lower, weight, *outs):
    gated = jnp.concatenate([upper[...], lower[...]], axis=0)
    width = weight.shape[1] // 8
    for owner, half, out, part in pieces:
        columns = pl.ds(pl.multiple_of((2 * meta_ref[owner] + half) * width, width), width)
        term = jnp.dot(gated, weight[:, columns], preferred_element_type=F32)
        outs[out][:, part * width : (part + 1) * width] = term.astype(BF16)


def column_terms(meta, upper, lower, weight, pieces, waits=()):
    rows, width = 2 * upper.shape[0], weight.shape[1] // 8
    outs = [((rows, width * sum(p[2] == out for p in pieces)), BF16) for out in range(pieces[-1][2] + 1)]
    body = functools.partial(columns_kernel, pieces)
    return vmem_call(body, "hyena_terms", None, meta, [upper, lower, weight], outs, waits=waits)


def load_kernel(meta_ref, source, outer, along, swapped, held, own, sems):
    channels = own.shape[1]
    columns = pl.ds(pl.multiple_of(meta_ref[0] * channels, channels), channels)
    copies = [
        pltpu.make_async_copy(source, held, sems.at[0]),
        pltpu.make_async_copy(outer.at[:, columns], own, sems.at[1]),
    ]
    for copy in copies:
        copy.start()
    for copy in copies:
        copy.wait()


def load(meta, weight, outer, after, channels):
    in_hbm = lambda x: pltpu.with_memory_space_constraint(x, pltpu.HBM)
    hbm, vmem = pl.BlockSpec(memory_space=pltpu.HBM), pl.BlockSpec(memory_space=pltpu.VMEM)
    return pl.pallas_call(
        load_kernel,
        in_specs=[pl.BlockSpec(memory_space=pltpu.SMEM), hbm, hbm, vmem, vmem],
        out_specs=[vmem, vmem],
        out_shape=[pltpu.VMEM(weight.shape, weight.dtype), pltpu.VMEM((outer.shape[0], channels), outer.dtype)],
        scratch_shapes=[pltpu.SemaphoreType.DMA((2,))],
        compiler_params=pltpu.CompilerParams(vmem_limit_bytes=4 * MIB),
        name="load_weights",
    )(meta, in_hbm(weight), in_hbm(outer), *after)


def stream_kernel(_, kept, direct_x, direct_y, late_x, late_y, residual, *parts):
    half = late_x.shape[1]
    rows = parts[0].shape[0]
    for index, out in enumerate(parts):
        span = slice(index * rows, (index + 1) * rows)
        wide = lambda ref: ref[span].astype(F32)
        left = wide(residual)[:, :half] + (wide(kept)[:, :half] + wide(direct_x) + wide(late_y))
        right = wide(residual)[:, half:] + (wide(kept)[:, half:] + wide(direct_y) + wide(late_x))
        out[...] = jnp.concatenate([left, right], axis=1).astype(BF16)


def near_kernel(meta_ref, *refs):
    blocks, (gain, weight, total, square) = refs[:3], refs[3:]
    channels = blocks[0].shape[1]
    squares = jnp.zeros(square.shape, F32)
    result = None
    for index in range(3):
        wide = blocks[index][...].astype(F32)
        squares = squares + jnp.sum(wide * wide, axis=1, keepdims=True)
        span = pl.ds(pl.multiple_of(meta_ref[index] * channels, channels), channels)
        factor, block = gain[:, span], weight[span, :]
        term = jnp.dot((wide * factor).astype(BF16), block, preferred_element_type=F32)
        result = term if result is None else result + term
    total[...] = result
    square[...] = squares


def far_kernel(chips, meta_ref, diag_a, diag_b, near, square, gain, cosine, sine, weight, *rest):
    outs, total = rest[:chips], rest[chips]
    channels = diag_a.shape[1]
    wide = jnp.concatenate([diag_a[...], diag_b[...]], axis=0).astype(F32)
    squares = square[...] + jnp.sum(wide * wide, axis=1, keepdims=True)
    span = pl.ds(pl.multiple_of(meta_ref[3] * channels, channels), channels)
    factor, block = gain[:, span], weight[span, :]
    total[...] = near[...] + jnp.dot((wide * factor).astype(BF16), block, preferred_element_type=F32)
    inverse = lax.rsqrt(squares / (4 * channels) + norm_eps)
    for distance, out in enumerate(outs):
        head = lax.rem(meta_ref[4] + distance, chips)
        for kind in range(3):
            column = pl.multiple_of((head * 3 + kind) * HEAD, HEAD)
            part = total[:, pl.ds(column, HEAD)] * inverse
            if kind < 2:
                part = part * cosine[...] + pltpu.roll(part, HEAD // 2, 1) * sine[...]
            if kind == 0:
                part = part * SCORE_SCALE
            if kind == 2:
                tiles = [part[row : row + HEAD].T for row in range(0, part.shape[0], HEAD)]
                part = jnp.concatenate(tiles, axis=0)
            out[kind] = part.astype(BF16)


def gather_keys(chips, meta_ref, own, other, keys, values):
    rows = own[0].shape[1]
    for distance in range(chips):
        place = lax.rem(meta_ref[4] - distance + chips, chips)
        for chunk, stacked in enumerate(other):
            mine = own[chunk * chips + distance]
            span = slice(chunk * rows, (chunk + 1) * rows)
            keys[0, place, span, :] = mine[1]
            keys[1, place, span, :] = stacked[distance, 0]
            for tile in range(rows // HEAD):
                first = chunk * rows + tile * HEAD
                taken = slice(tile * HEAD, (tile + 1) * HEAD)
                values[0, place, :, first : first + HEAD] = mine[2, taken, :]
                values[1, place, :, first : first + HEAD] = stacked[distance, 1, taken, :]


def attention_kernel(chips, chunks, distances, leading, meta_ref, *refs):
    if leading:
        pieces, other = refs[: chunks * chips], refs[chunks * chips : chunks * (chips + 1)]
        *outs, keys, values = refs[chunks * (chips + 1) :]
        gather_keys(chips, meta_ref, pieces, other, keys, values)
        sources = [pieces[(chips - distance) % chips :: chips] for distance in distances]
    else:
        taken = chunks * len(distances)
        pieces, (keys, values), outs = refs[:taken], refs[taken : taken + 2], refs[taken + 2 :]
        sources = [pieces[index * chunks : (index + 1) * chunks] for index in range(len(distances))]
    chip, core = meta_ref[4], meta_ref[5]
    count = keys.shape[2]

    def scores_of(side, place, queries):
        return lax.dot_general(
            keys[side, place], queries, (((1,), (1,)), ((), ())), preferred_element_type=F32
        )

    def update(state, mine, others, place):
        top, total, acc = state
        new_top = jnp.maximum(jnp.max(mine, axis=0, keepdims=True), jnp.max(others, axis=0, keepdims=True))
        if top is not None:
            new_top = jnp.maximum(new_top, top)
        mine = jnp.exp2(mine - new_top)
        others = jnp.exp2(others - new_top)
        gained = jnp.sum(mine, axis=0, keepdims=True) + jnp.sum(others, axis=0, keepdims=True)
        added = jnp.dot(values[0, place], mine.astype(BF16), preferred_element_type=F32)
        added = added + jnp.dot(values[1, place], others.astype(BF16), preferred_element_type=F32)
        if top is None:
            return new_top, gained, added
        shrink = jnp.exp2(top - new_top)
        return new_top, total * shrink + gained, acc * shrink + added

    key_row = lax.broadcasted_iota(jnp.int32, (count, count), 0)
    query_column = lax.broadcasted_iota(jnp.int32, (count, count), 1)
    for distance, source, out in zip(distances, sources, outs):
        place = lax.rem(chip + distance, chips)
        queries = jnp.concatenate([piece[0] for piece in source], axis=0)
        mine = jnp.where(key_row <= query_column, scores_of(0, place, queries), -1e30)
        others = jnp.where(core == 1, scores_of(1, place, queries), -1e30)
        state = update((None, None, None), mine, others, place)

        def earlier(index, state):
            return update(state, scores_of(0, index, queries), scores_of(1, index, queries), index)

        state = lax.fori_loop(0, place, earlier, state)
        out[...] = (state[2] / state[1]).T.astype(BF16)


def attend(meta, own, other, laid, distances, waits, chips):
    chunks, leading = len(other), laid is None
    count = own[0].shape[1] * chunks
    outs = [((count, HEAD), BF16)] * len(distances)
    if leading:
        operands = own + other
        outs = outs + [((2, chips, count, HEAD), BF16), ((2, chips, HEAD, count), BF16)]
    else:
        operands = [piece for distance in distances for piece in own[(chips - distance) % chips :: chips]]
        operands = [*operands, *laid]
    body = functools.partial(attention_kernel, chips, chunks, distances, leading)
    made = list(vmem_call(body, "attention", 6, meta, operands, outs, waits=waits))
    return made[: len(distances)], laid or made[len(distances) :]


def pick_kernel(meta_ref, weight, features, *refs):
    *near, edge, sems = refs
    channels = near[0].shape[1]
    kinds, count, _ = edge.shape
    last = features.shape[1] - count
    copies = []
    for kind in range(kinds):
        copies.append(
            pltpu.make_async_copy(features.at[kind, last : last + count], edge.at[kind], sems.at[kind])
        )
    rows = pl.ds(pl.multiple_of((2 * lax.rem(meta_ref[4], 2) + meta_ref[5]) * HEAD, HEAD), HEAD)
    for index, out in enumerate(near):
        columns = pl.ds(pl.multiple_of(meta_ref[index + 1] * channels, channels), channels)
        copies.append(pltpu.make_async_copy(weight.at[rows, columns], out, sems.at[kinds + index]))
    for copy in copies:
        copy.start()
    for copy in copies:
        copy.wait()


def pick(meta, weight, features, count):
    kinds, _, channels = features.shape
    near = jax.ShapeDtypeStruct((HEAD, channels), BF16)
    in_hbm = lambda x: pltpu.with_memory_space_constraint(x, pltpu.HBM)
    hbm, vmem = pl.BlockSpec(memory_space=pltpu.HBM), pl.BlockSpec(memory_space=pltpu.VMEM)
    return pl.pallas_call(
        pick_kernel,
        in_specs=[pl.BlockSpec(memory_space=pltpu.SMEM), hbm, hbm],
        out_specs=[vmem] * 4,
        out_shape=[near, near, near, jax.ShapeDtypeStruct((kinds, count, channels), BF16)],
        scratch_shapes=[pltpu.SemaphoreType.DMA((kinds + 3,))],
        compiler_params=pltpu.CompilerParams(vmem_limit_bytes=4 * MIB),
        name="pick",
    )(meta, in_hbm(weight), in_hbm(features))


def mix_kernel(chips, groups, items, streams, meta_ref, *refs):
    heads, refs = refs[: len(items)], refs[len(items) :]
    before, (own_w, near_w, far_w, out, ordered) = refs[:streams], refs[streams:]
    chip, core = meta_ref[4], meta_ref[5]
    swapped = lax.rem(chip, 2)
    parities = [lax.rem(chip + distances[0], 2) for distances in groups]
    for place, (group, _) in enumerate(items):
        for index, distance in enumerate(groups[group]):
            head = lax.rem(chip - distance + chips, chips)
            column = pl.ds(pl.multiple_of(head // 2 * HEAD, HEAD), HEAD)
            ordered[place, :, column] = heads[place][index]

    def own_rows(parity):
        rows = [pl.ds(pl.multiple_of((2 * j + parity) * HEAD, HEAD), HEAD) for j in range(chips // 2)]
        return jnp.concatenate([own_w[span, :] for span in rows], axis=0)

    def finish(by_group):
        total = jnp.concatenate([part[...].astype(F32) for part in before], axis=0)
        for place, (group, source) in enumerate(items):
            if source:
                held = by_group[group]
                weights = jnp.concatenate([held[swapped, source - 1], held[1 - swapped, source - 1]], axis=0)
            else:
                weights = own_rows(parities[group])
            total = total + jnp.dot(ordered[place], weights, preferred_element_type=F32)
        out[...] = total.astype(out.dtype)

    @pl.when(core == parities[0])
    def _():
        finish([near_w, far_w])

    @pl.when(core != parities[0])
    def _():
        finish([far_w, near_w])


def mix(meta, heads, *, groups, items, before, own_w, near_w, far_w, kind, chips):
    rows, channels = heads[0].shape[1], own_w.shape[1]
    body = functools.partial(mix_kernel, chips, groups, items, len(before))
    operands = [*heads, *before, own_w, near_w, far_w]
    scratch = [pltpu.VMEM((len(items), rows, chips // 2 * HEAD), BF16)]
    micros = 0.6 * len(items)
    return vmem_call(body, "attention_mix", micros, meta, operands, [((rows, channels), kind)], scratch)[0]


def rotate_rows(block, positions):
    half_size = block.shape[-1] // 2
    frequency = 10000.0 ** (-jnp.arange(half_size, dtype=jnp.float32) * 2.0 / block.shape[-1])
    angles = positions.astype(jnp.float32)[:, None] * frequency[None, :]
    cosine = jnp.cos(angles)[:, None, :]
    sine_part = jnp.sin(angles)[:, None, :]
    first_half = block[..., :half_size]
    second_half = block[..., half_size:]
    return jnp.concatenate(
        [
            first_half * cosine - second_half * sine_part,
            second_half * cosine + first_half * sine_part,
        ],
        axis=-1,
    )


def run_attention(queries, query_pos, key_rows, value_rows, position_of):
    head_count = queries.shape[1]
    row_count = queries.shape[0]
    head_size = queries.shape[2]
    scale_factor = 1.0 / head_size**0.5
    last_query = jnp.max(query_pos)
    initial = (
        jnp.zeros((head_count, row_count, head_size), jnp.float32),
        jnp.full((head_count, row_count), -1e30, jnp.float32),
        jnp.zeros((head_count, row_count), jnp.float32),
    )
    piece_keys = lax.all_gather(key_rows, "ctx", axis=0, tiled=True)
    piece_values = lax.all_gather(value_rows, "ctx", axis=0, tiled=True)
    piece_rows = piece_keys.shape[0]
    block_rows = 512

    def one_block(state_in, block_index):
        first_block = block_index * block_rows
        key_block = lax.dynamic_slice_in_dim(piece_keys, first_block, block_rows, 0)
        value_block = lax.dynamic_slice_in_dim(piece_values, first_block, block_rows, 0)
        key_pos = position_of(first_block + jnp.arange(block_rows))

        def update(state_old):
            acc_sum, run_max, run_total = state_old
            scores = (
                jnp.einsum("thd,khd->htk", queries, key_block, preferred_element_type=jnp.float32)
                * scale_factor
            )
            causal = (key_pos[None, :] <= query_pos[:, None])[None]
            block_max = jnp.max(jnp.where(causal, scores, -1e30), axis=-1)
            new_max = jnp.maximum(run_max, block_max)
            weights = jnp.where(causal, jnp.exp(scores - new_max[..., None]), 0.0)
            correction = jnp.exp(run_max - new_max)
            new_total = run_total * correction + jnp.sum(weights, axis=-1)
            update_sum = jnp.einsum(
                "htk,khd->htd",
                weights.astype(jnp.bfloat16),
                value_block,
                preferred_element_type=jnp.float32,
            )
            return (acc_sum * correction[..., None] + update_sum, new_max, new_total)

        def unchanged(state_old):
            return state_old

        state_out = lax.cond(jnp.min(key_pos) > last_query, unchanged, update, state_in)
        return (state_out, None)

    state_end, unused = lax.scan(one_block, initial, jnp.arange(piece_rows // block_rows))
    acc_sum, run_max, run_total = state_end
    output = acc_sum / run_total[..., None]
    return jnp.transpose(output, (1, 0, 2)).astype(jnp.bfloat16)


def after_gating(gated, residual_in, out_weight, norm_gain, attn_weight, attn_out):
    tok_rows, chan_count = gated.shape
    hyena_terms = jnp.dot(gated, out_weight, preferred_element_type=jnp.float32)
    hyena_out = lax.psum_scatter(
        hyena_terms.astype(jnp.bfloat16), "ch", scatter_dimension=1, tiled=True
    ).astype(jnp.float32)
    stream = (residual_in.astype(jnp.float32) + hyena_out).astype(jnp.bfloat16)
    stream_wide = stream.astype(jnp.float32)
    full_width = chan_count * lax.axis_size("ch")
    head_cols = attn_weight.shape[1]
    square_total = lax.psum(jnp.sum(stream_wide * stream_wide, axis=1), "ch")
    inverse = lax.rsqrt(square_total / full_width + norm_eps)
    gain_part = lax.dynamic_slice_in_dim(norm_gain, lax.axis_index("ch") * chan_count, chan_count)
    normed = (stream_wide * inverse[:, None] * gain_part[None, :]).astype(jnp.bfloat16)
    projected = jnp.dot(
        lax.all_gather(normed, "ch", axis=1, tiled=True),
        attn_weight,
        preferred_element_type=jnp.float32,
    )
    head_count = head_cols // (3 * HEAD)
    projected = projected.reshape(tok_rows, head_count, 3, HEAD)
    ctx_index = lax.axis_index("ctx")
    positions = ctx_index * tok_rows + jnp.arange(tok_rows, dtype=jnp.int32)
    queries = rotate_rows(projected[:, :, 0, :], positions).astype(jnp.bfloat16)
    key_rows = rotate_rows(projected[:, :, 1, :], positions).astype(jnp.bfloat16)
    value_rows = projected[:, :, 2, :].astype(jnp.bfloat16)

    def position_of(global_row):
        return global_row

    attended = run_attention(queries, positions, key_rows, value_rows, position_of)
    head_terms = jnp.dot(
        attended.reshape(tok_rows, head_count * HEAD), attn_out, preferred_element_type=jnp.float32
    )
    attn_mix = lax.psum_scatter(
        head_terms.astype(jnp.bfloat16), "ch", scatter_dimension=1, tiled=True
    ).astype(jnp.float32)
    return (stream_wide + attn_mix).astype(jnp.bfloat16)


def rotation_tables(positions):
    half_size = HEAD // 2
    frequency = 10000.0 ** (-jnp.arange(half_size, dtype=F32) * 2.0 / HEAD)
    angles = positions.astype(F32)[:, None] * frequency[None, :]
    cosine, sine = jnp.cos(angles), jnp.sin(angles)
    return jnp.concatenate([cosine, cosine], axis=1), jnp.concatenate([-sine, sine], axis=1)


def shards(
    features,
    residual_in,
    short_filter,
    medium_filter,
    skip_gain,
    out_weight,
    norm_gain,
    attn_weight,
    attn_out,
):
    rows, _, channels = features.shape
    chips = lax.axis_size("ctx") // 2
    length = medium_filter.shape[0]
    chunk = rows // 2
    ctx, ch = lax.axis_index("ctx"), lax.axis_index("ch")
    scalars = [ch, ch ^ 1, ch ^ 2, ch ^ 3, ctx // 2, ctx % 2, ctx * rows, ctx]
    meta = jnp.stack(scalars).astype(jnp.int32)

    by_kind = jnp.transpose(features, (1, 0, 2))
    medium_rows = medium_filter.T
    skip = skip_gain.reshape(1, channels)

    starts = [rows - chunk, 0]
    if lax.axis_size("ch") != 4 or attn_weight.shape[1] != 3 * HEAD * chips or chips != 4:
        halo = shift_rows(by_kind[:, rows - length - LEAD :])
        (lower,) = gated_chunk(meta, by_kind, halo, chunk, chunk, short_filter, medium_rows, skip)
        (upper,) = gated_chunk(meta, by_kind, halo, 0, chunk, short_filter, medium_rows, skip)
        return after_gating(
            jnp.concatenate([upper, lower], axis=0), residual_in, out_weight, norm_gain, attn_weight, attn_out
        )

    gain = norm_gain.reshape(1, -1)
    cosine, sine = rotation_tables(meta[6:7] + jnp.arange(rows, dtype=jnp.int32))

    *near_w, edge = pick(meta, attn_out, by_kind, length + LEAD)
    halo = shift_rows(edge)
    picked = [swap_ch(weight, mask) for mask, weight in zip((1, 2, 3), near_w)]

    lower, out_held = gated_chunk(meta, by_kind, halo, chunk, chunk, short_filter, medium_rows, skip, out_weight)
    (upper,) = gated_chunk(meta, by_kind, halo, 0, chunk, short_filter, medium_rows, skip)
    across_x, across_y = column_terms(meta, upper, lower, out_held, ((3, 0, 0, 0), (3, 1, 1, 0)), picked)
    picked = jnp.stack(picked)
    swapped = swap_ctx(picked, 2)
    across_x, across_y = swap_ch(across_x, 1), swap_ch(across_y, 2)
    pieces = ((1, 0, 0, 0), (2, 1, 1, 0), (1, 1, 2, 0), (2, 0, 3, 0), (0, 0, 4, 0), (0, 1, 4, 1))
    direct_x, direct_y, along_x, along_y, kept = column_terms(meta, upper, lower, out_held, pieces, [picked])
    direct_x, direct_y = swap_ch(direct_x, 1), swap_ch(direct_y, 2)
    along_x = (along_x.astype(F32) + across_y.astype(F32)).astype(BF16)
    along_y = (along_y.astype(F32) + across_x.astype(F32)).astype(BF16)
    late_x, late_y = swap_ch(along_x, 1), swap_ch(along_y, 2)
    qkv_held, own_w = load(meta, attn_weight, attn_out, (along_y, swapped), channels)
    parts = vmem_call(
        stream_kernel,
        "add_stream",
        1,
        meta,
        [kept, direct_x, direct_y, late_x, late_y, residual_in],
        [((chunk, channels), BF16)] * 2,
        waits=[qkv_held, cosine, sine],
    )

    own, other, after = [], [], None
    width = attn_weight.shape[1]
    for start in starts:
        part = parts[start // chunk]
        if after is not None:
            part, _ = lax.optimization_barrier((part, after))
        by_x, by_y = swap_ch(part, 1), swap_ch(part, 2)
        diag_a, diag_b = swap_ch(by_x[: chunk // 2], 2), swap_ch(by_y[chunk // 2 :], 1)
        near, square = vmem_call(
            near_kernel,
            "qkv_near",
            3,
            meta,
            [part, by_x, by_y, gain, qkv_held],
            [((chunk, width), F32), ((chunk, LANES), F32)],
        )
        after = diag_a, diag_b, square
        turn = slice(start, start + chunk)
        outs = vmem_call(
            functools.partial(far_kernel, chips),
            "qkv_far",
            2,
            meta,
            [diag_a, diag_b, near, square, gain, cosine[turn], sine[turn], qkv_held],
            [((3, chunk, HEAD), BF16)] * chips,
            [pltpu.VMEM((chunk, width), F32)],
        )
        arrived = [outs[0]] + [rotate_chips(outs[d], d) for d in range(1, chips)]
        own.append(arrived)

    swapped, _ = lax.optimization_barrier((swapped, outs))
    near_w = jnp.stack([picked, swapped])
    far_w = swap_ctx(near_w, 1)
    own, _ = lax.optimization_barrier((own, outs))
    other = [swap_ctx(jnp.stack([piece[1:] for piece in arrived]), 1) for arrived in own]
    own, other = own[1] + own[0], other[::-1]

    groups = [(*range(2, chips, 2), 0), tuple(range(1, chips, 2))]
    given, laid = attend(meta, own, other, None, groups[0], [far_w], chips)
    first = [rotate_chips(piece, d) if d else piece for d, piece in zip(groups[0], given)]
    given, _ = attend(meta, own, other, laid, groups[1], [], chips)
    first, given = lax.optimization_barrier((first, given))
    second = [rotate_chips(piece, d) for d, piece in zip(groups[1], given)]
    back = jnp.stack(first)
    by_x, by_y = swap_ch(back, 1), swap_ch(back, 2)
    add = functools.partial(mix, meta, groups=groups, own_w=own_w, near_w=near_w, far_w=far_w, chips=chips)
    total = add([back, by_x, by_y], items=((0, 0), (0, 1), (0, 2)), before=parts, kind=F32)
    second, by_x, total = lax.optimization_barrier((second, by_x, total))
    across = swap_ch(by_x, 2)
    back = jnp.stack(second)
    by_x, by_y = swap_ch(back, 1), swap_ch(back, 2)
    total = add([across, back, by_y], items=((0, 3), (1, 0), (1, 2)), before=[total], kind=F32)
    return add([by_x, swap_ch(by_y, 1)], items=((1, 1), (1, 3)), before=[total], kind=BF16)


def solution(mesh):
    in_specs = (
        P("ctx", None, "ch"),
        P("ctx", "ch"),
        P(None, None, "ch"),
        P(None, "ch"),
        P("ch"),
        P("ch", None),
        P(),
        P(None, "ch"),
        P("ch", None),
    )
    out_specs = P("ctx", "ch")
    return jax.shard_map(shards, mesh=mesh, in_specs=in_specs, out_specs=out_specs, check_vma=False)
```

```python
import functools

import jax
import jax.numpy as jnp
from jax import lax
from jax.experimental import pallas as pl
from jax.experimental.pallas import tpu as pltpu
from jax.sharding import PartitionSpec as P

HEAD = 128
GROUP_SIZE = 16
LANES = 128
TILES = 4
LEAD = 16
norm_eps = 1e-05
SCORE_SCALE = 1.4426950408889634 / HEAD**0.5
MIB = 1024 * 1024
F32 = jnp.float32
BF16 = jnp.bfloat16


def lasting(micros):
    return pl.CostEstimate(
        flops=int(micros * 1.1e9), transcendentals=0, bytes_accessed=int(micros * 3.6e6)
    )


def swap_ch(value, mask):
    count = lax.axis_size("ch")
    return lax.ppermute(value, "ch", [(i, i ^ mask) for i in range(count)])


def swap_ctx(value, mask):
    count = lax.axis_size("ctx")
    return lax.ppermute(value, "ctx", [(i, i ^ mask) for i in range(count)])


def shift_rows(value):
    count = lax.axis_size("ctx")
    return lax.ppermute(value, "ctx", [(i, i + 1) for i in range(count - 1)])


def rotate_chips(value, distance):
    count = lax.axis_size("ctx")
    return lax.ppermute(value, "ctx", [(i, (i + 2 * distance) % count) for i in range(count)])


def filter_tile(first_row, tile, lanes, short_ref, medium_ref, skip_ref, halo_ref, rows_ref, wide, product, table, store):
    taps, groups_all = short_ref.shape[1:]
    length = medium_ref.shape[1]
    groups = LANES // GROUP_SIZE
    medium = medium_ref[pl.ds(pl.multiple_of(tile * groups, groups), groups), :]
    gain = skip_ref[:, pl.ds(pl.multiple_of(tile * LANES, LANES), LANES)]
    span = wide.shape[1]
    halo_rows = length + LEAD
    count = span - halo_rows

    for kind in range(3):
        if first_row == 0:
            wide[kind, :halo_rows] = halo_ref[kind, :, lanes].astype(F32)
            wide[kind, halo_rows:] = rows_ref[kind, :, lanes].astype(F32)
        else:
            wide[kind] = rows_ref[kind, first_row - halo_rows : first_row + count, lanes].astype(F32)

    group_row = lax.broadcasted_iota(jnp.int32, (groups_all, LANES), 0)
    group_col = lax.broadcasted_iota(jnp.int32, (groups_all, LANES), 1) // GROUP_SIZE + tile * groups
    chosen = jnp.where(group_row == group_col, 1.0, 0.0).astype(F32)
    weights = [
        jnp.dot(short_ref[kind], chosen, precision=lax.Precision.HIGHEST, preferred_element_type=F32)
        for kind in range(3)
    ]

    tap_row = lax.broadcasted_iota(jnp.int32, (length, 2 * length), 0)
    place = lax.broadcasted_iota(jnp.int32, (length, 2 * length), 1)
    turned = jnp.where(tap_row + place == length, 1.0, 0.0).astype(BF16)
    base = jnp.dot(medium.astype(BF16), turned, preferred_element_type=F32)
    for group in range(groups):
        spread = jnp.broadcast_to(base[group : group + 1, :], (length, 2 * length))
        rolled = pltpu.roll(spread, 0, 1, stride=1, stride_axis=0)
        table[group * length : (group + 1) * length, :] = rolled.astype(BF16)

    def featured(kind, start):
        total = weights[kind][0:1, :] * wide[kind, start : start + length, :]
        for tap in range(1, taps):
            total = total + weights[kind][tap : tap + 1, :] * wide[kind, start - tap : start - tap + length, :]
        return total

    for block in range(count // length + 1):
        start = LEAD + block * length
        product[block * length : (block + 1) * length, :] = (
            featured(1, start) * featured(2, start)
        ).astype(BF16)

    group_of = lax.broadcasted_iota(jnp.int32, (length, 2 * LANES), 1) % LANES // GROUP_SIZE
    for pair in range(count // (2 * length)):
        begin = pair * 2 * length
        window = jnp.concatenate(
            [
                product[begin : begin + 2 * length, :],
                product[begin + length : begin + 3 * length, :],
            ],
            axis=1,
        )
        spread = jnp.dot(table[...], window, preferred_element_type=F32)
        mixed = spread[:length]
        for group in range(1, groups):
            mixed = jnp.where(group_of == group, spread[group * length : (group + 1) * length], mixed)
        for part in range(2):
            row = begin + part * length
            direct = gain * product[row + length : row + 2 * length, :].astype(F32)
            gate = featured(0, halo_rows + row)
            store(row, (gate * (mixed[:, part * LANES : (part + 1) * LANES] + direct)).astype(BF16))


def gated_kernel(first_row, loads, *refs):
    head, rest = refs[1:4], refs[4:]
    halo_ref, rest = (rest[0], rest[1:]) if first_row == 0 else (None, rest)
    rows_ref, rest = rest[0], rest[1:]
    if loads:
        weight, out_ref, held, wide, product, table, sem = rest
        copy = pltpu.make_async_copy(weight, held, sem)
        pl.when(pl.program_id(0) == 0)(copy.start)
    else:
        out_ref, wide, product, table = rest

    for part in range(TILES):
        lanes = slice(part * LANES, (part + 1) * LANES)

        def store(row, value):
            out_ref[row : row + value.shape[0], lanes] = value

        scratch = wide.at[part], product.at[part], table.at[part]
        tile = pl.program_id(0) * TILES + part
        filter_tile(first_row, tile, lanes, *head, halo_ref, rows_ref, *scratch, store)
    if loads:
        pl.when(pl.program_id(0) == pl.num_programs(0) - 1)(copy.wait)


def gated_chunk(meta, features, halo, first_row, count, short_filter, medium_rows, skip, weight=None):
    kinds, rows, channels = features.shape
    length = medium_rows.shape[1]
    groups = LANES // GROUP_SIZE
    step = TILES * LANES
    loads = weight is not None
    in_hbm = lambda x: pltpu.with_memory_space_constraint(x, pltpu.HBM)
    in_specs = [
        pl.BlockSpec(memory_space=pltpu.SMEM),
        pl.BlockSpec(short_filter.shape, lambda i: (0, 0, 0)),
        pl.BlockSpec(medium_rows.shape, lambda i: (0, 0)),
        pl.BlockSpec(skip.shape, lambda i: (0, 0)),
    ]
    operands = [meta, in_hbm(short_filter), in_hbm(medium_rows), in_hbm(skip)]
    out_specs = [pl.BlockSpec((count, step), lambda i: (0, i))]
    out_shape = [jax.ShapeDtypeStruct((count, channels), BF16)]
    scratch = [
        pltpu.VMEM((TILES, kinds, length + LEAD + count, LANES), F32),
        pltpu.VMEM((TILES, length + count, LANES), BF16),
        pltpu.VMEM((TILES, groups * length, 2 * length), BF16),
    ]
    if first_row == 0:
        in_specs.append(pl.BlockSpec((kinds, length + LEAD, step), lambda i: (0, 0, i)))
        in_specs.append(pl.BlockSpec((kinds, count, step), lambda i: (0, 0, i)))
        operands += [halo, features]
    else:
        in_specs.append(pl.BlockSpec((kinds, rows, step), lambda i: (0, 0, i)))
        operands.append(features)
    if loads:
        in_specs.append(pl.BlockSpec(memory_space=pltpu.HBM))
        operands.append(in_hbm(weight))
        out_specs.append(pl.BlockSpec(memory_space=pltpu.VMEM))
        out_shape.append(pltpu.VMEM(weight.shape, weight.dtype))
        scratch.append(pltpu.SemaphoreType.DMA)
    return pl.pallas_call(
        functools.partial(gated_kernel, first_row, loads),
        grid=(channels // step,),
        in_specs=in_specs,
        out_specs=out_specs,
        out_shape=out_shape,
        scratch_shapes=scratch,
        compiler_params=pltpu.CompilerParams(vmem_limit_bytes=16 * MIB),
        name="hyena_filters",
    )(*operands)


def vmem_call(body, name, micros, scalars, operands, outs, scratch=(), waits=()):
    given = 1 + len(operands)
    run = lambda *refs: body(*refs[:given], *refs[given + len(waits) :])
    return pl.pallas_call(
        run,
        in_specs=[pl.BlockSpec(memory_space=pltpu.SMEM)]
        + [pl.BlockSpec(memory_space=pltpu.VMEM)] * (len(operands) + len(waits)),
        out_specs=[pl.BlockSpec(memory_space=pltpu.VMEM)] * len(outs),
        out_shape=[jax.ShapeDtypeStruct(shape, kind) for shape, kind in outs],
        scratch_shapes=list(scratch),
        compiler_params=pltpu.CompilerParams(vmem_limit_bytes=20 * MIB),
        cost_estimate=lasting(micros) if micros else None,
        name=name,
    )(scalars, *operands, *waits)


def columns_kernel(pieces, meta_ref, upper, lower, weight, *outs):
    gated = jnp.concatenate([upper[...], lower[...]], axis=0)
    width = weight.shape[1] // 8
    for owner, half, out, part in pieces:
        columns = pl.ds(pl.multiple_of((2 * meta_ref[owner] + half) * width, width), width)
        term = jnp.dot(gated, weight[:, columns], preferred_element_type=F32)
        outs[out][:, part * width : (part + 1) * width] = term.astype(BF16)


def column_terms(meta, upper, lower, weight, pieces, waits=()):
    rows, width = 2 * upper.shape[0], weight.shape[1] // 8
    outs = [((rows, width * sum(p[2] == out for p in pieces)), BF16) for out in range(pieces[-1][2] + 1)]
    body = functools.partial(columns_kernel, pieces)
    return vmem_call(body, "hyena_terms", None, meta, [upper, lower, weight], outs, waits=waits)


def load_kernel(meta_ref, source, outer, along, swapped, held, own, sems):
    channels = own.shape[1]
    columns = pl.ds(pl.multiple_of(meta_ref[0] * channels, channels), channels)
    copies = [
        pltpu.make_async_copy(source, held, sems.at[0]),
        pltpu.make_async_copy(outer.at[:, columns], own, sems.at[1]),
    ]
    for copy in copies:
        copy.start()
    for copy in copies:
        copy.wait()


def load(meta, weight, outer, after, channels):
    in_hbm = lambda x: pltpu.with_memory_space_constraint(x, pltpu.HBM)
    hbm, vmem = pl.BlockSpec(memory_space=pltpu.HBM), pl.BlockSpec(memory_space=pltpu.VMEM)
    return pl.pallas_call(
        load_kernel,
        in_specs=[pl.BlockSpec(memory_space=pltpu.SMEM), hbm, hbm, vmem, vmem],
        out_specs=[vmem, vmem],
        out_shape=[pltpu.VMEM(weight.shape, weight.dtype), pltpu.VMEM((outer.shape[0], channels), outer.dtype)],
        scratch_shapes=[pltpu.SemaphoreType.DMA((2,))],
        compiler_params=pltpu.CompilerParams(vmem_limit_bytes=4 * MIB),
        name="load_weights",
    )(meta, in_hbm(weight), in_hbm(outer), *after)


def stream_kernel(_, kept, direct_x, direct_y, late_x, late_y, residual, *parts):
    half = late_x.shape[1]
    rows = parts[0].shape[0]
    for index, out in enumerate(parts):
        span = slice(index * rows, (index + 1) * rows)
        wide = lambda ref: ref[span].astype(F32)
        left = wide(residual)[:, :half] + (wide(kept)[:, :half] + wide(direct_x) + wide(late_y))
        right = wide(residual)[:, half:] + (wide(kept)[:, half:] + wide(direct_y) + wide(late_x))
        out[...] = jnp.concatenate([left, right], axis=1).astype(BF16)


def near_kernel(meta_ref, *refs):
    blocks, (gain, weight, total, square) = refs[:3], refs[3:]
    channels = blocks[0].shape[1]
    squares = jnp.zeros(square.shape, F32)
    result = None
    for index in range(3):
        wide = blocks[index][...].astype(F32)
        squares = squares + jnp.sum(wide * wide, axis=1, keepdims=True)
        span = pl.ds(pl.multiple_of(meta_ref[index] * channels, channels), channels)
        factor, block = gain[:, span], weight[span, :]
        term = jnp.dot((wide * factor).astype(BF16), block, preferred_element_type=F32)
        result = term if result is None else result + term
    total[...] = result
    square[...] = squares


def far_kernel(chips, meta_ref, diag_a, diag_b, near, square, gain, cosine, sine, weight, *rest):
    outs, total = rest[:chips], rest[chips]
    channels = diag_a.shape[1]
    wide = jnp.concatenate([diag_a[...], diag_b[...]], axis=0).astype(F32)
    squares = square[...] + jnp.sum(wide * wide, axis=1, keepdims=True)
    span = pl.ds(pl.multiple_of(meta_ref[3] * channels, channels), channels)
    factor, block = gain[:, span], weight[span, :]
    total[...] = near[...] + jnp.dot((wide * factor).astype(BF16), block, preferred_element_type=F32)
    inverse = lax.rsqrt(squares / (4 * channels) + norm_eps)
    for distance, out in enumerate(outs):
        head = lax.rem(meta_ref[4] + distance, chips)
        for kind in range(3):
            column = pl.multiple_of((head * 3 + kind) * HEAD, HEAD)
            part = total[:, pl.ds(column, HEAD)] * inverse
            if kind < 2:
                part = part * cosine[...] + pltpu.roll(part, HEAD // 2, 1) * sine[...]
            if kind == 0:
                part = part * SCORE_SCALE
            if kind == 2:
                tiles = [part[row : row + HEAD].T for row in range(0, part.shape[0], HEAD)]
                part = jnp.concatenate(tiles, axis=0)
            out[kind] = part.astype(BF16)


def gather_keys(chips, meta_ref, own, other, keys, values):
    rows = own[0].shape[1]
    for distance in range(chips):
        place = lax.rem(meta_ref[4] - distance + chips, chips)
        for chunk, stacked in enumerate(other):
            mine = own[chunk * chips + distance]
            span = slice(chunk * rows, (chunk + 1) * rows)
            keys[0, place, span, :] = mine[1]
            keys[1, place, span, :] = stacked[distance, 0]
            for tile in range(rows // HEAD):
                first = chunk * rows + tile * HEAD
                taken = slice(tile * HEAD, (tile + 1) * HEAD)
                values[0, place, :, first : first + HEAD] = mine[2, taken, :]
                values[1, place, :, first : first + HEAD] = stacked[distance, 1, taken, :]


def attention_kernel(chips, chunks, meta_ref, *refs):
    pieces, other = refs[: chunks * chips], refs[chunks * chips : chunks * (chips + 1)]
    *outs, keys, values = refs[chunks * (chips + 1) :]
    gather_keys(chips, meta_ref, pieces, other, keys, values)
    chip, core = meta_ref[4], meta_ref[5]
    count = keys.shape[2]

    def scores_of(side, place, queries):
        return lax.dot_general(
            keys[side, place], queries, (((1,), (1,)), ((), ())), preferred_element_type=F32
        )

    def update(state, mine, others, place):
        top, total, acc = state
        new_top = jnp.maximum(jnp.max(mine, axis=0, keepdims=True), jnp.max(others, axis=0, keepdims=True))
        if top is not None:
            new_top = jnp.maximum(new_top, top)
        mine = jnp.exp2(mine - new_top)
        others = jnp.exp2(others - new_top)
        gained = jnp.sum(mine, axis=0, keepdims=True) + jnp.sum(others, axis=0, keepdims=True)
        added = jnp.dot(values[0, place], mine.astype(BF16), preferred_element_type=F32)
        added = added + jnp.dot(values[1, place], others.astype(BF16), preferred_element_type=F32)
        if top is None:
            return new_top, gained, added
        shrink = jnp.exp2(top - new_top)
        return new_top, total * shrink + gained, acc * shrink + added

    key_row = lax.broadcasted_iota(jnp.int32, (count, count), 0)
    query_column = lax.broadcasted_iota(jnp.int32, (count, count), 1)
    for distance, out in enumerate(outs):
        source = pieces[(chips - distance) % chips :: chips]
        place = lax.rem(chip + distance, chips)
        queries = jnp.concatenate([piece[0] for piece in source], axis=0)
        mine = jnp.where(key_row <= query_column, scores_of(0, place, queries), -1e30)
        others = jnp.where(core == 1, scores_of(1, place, queries), -1e30)
        state = update((None, None, None), mine, others, place)

        def earlier(index, state):
            return update(state, scores_of(0, index, queries), scores_of(1, index, queries), index)

        state = lax.fori_loop(0, place, earlier, state)
        out[...] = (state[2] / state[1]).T.astype(BF16)


def attend(meta, own, other, waits, chips):
    chunks = len(other)
    count = own[0].shape[1] * chunks
    body = functools.partial(attention_kernel, chips, chunks)
    outs = [((count, HEAD), BF16)] * chips
    scratch = [pltpu.VMEM((2, chips, count, HEAD), BF16), pltpu.VMEM((2, chips, HEAD, count), BF16)]
    return vmem_call(body, "attention", 12, meta, own + other, outs, scratch, waits)


def pick_kernel(meta_ref, weight, features, *refs):
    *near, edge, sems = refs
    channels = near[0].shape[1]
    kinds, count, _ = edge.shape
    last = features.shape[1] - count
    copies = []
    for kind in range(kinds):
        copies.append(
            pltpu.make_async_copy(features.at[kind, last : last + count], edge.at[kind], sems.at[kind])
        )
    rows = pl.ds(pl.multiple_of((2 * lax.rem(meta_ref[4], 2) + meta_ref[5]) * HEAD, HEAD), HEAD)
    for index, out in enumerate(near):
        columns = pl.ds(pl.multiple_of(meta_ref[index + 1] * channels, channels), channels)
        copies.append(pltpu.make_async_copy(weight.at[rows, columns], out, sems.at[kinds + index]))
    for copy in copies:
        copy.start()
    for copy in copies:
        copy.wait()


def pick(meta, weight, features, count):
    kinds, _, channels = features.shape
    near = jax.ShapeDtypeStruct((HEAD, channels), BF16)
    in_hbm = lambda x: pltpu.with_memory_space_constraint(x, pltpu.HBM)
    hbm, vmem = pl.BlockSpec(memory_space=pltpu.HBM), pl.BlockSpec(memory_space=pltpu.VMEM)
    return pl.pallas_call(
        pick_kernel,
        in_specs=[pl.BlockSpec(memory_space=pltpu.SMEM), hbm, hbm],
        out_specs=[vmem] * 4,
        out_shape=[near, near, near, jax.ShapeDtypeStruct((kinds, count, channels), BF16)],
        scratch_shapes=[pltpu.SemaphoreType.DMA((kinds + 3,))],
        compiler_params=pltpu.CompilerParams(vmem_limit_bytes=4 * MIB),
        name="pick",
    )(meta, in_hbm(weight), in_hbm(features))


def mix_kernel(chips, groups, items, streams, meta_ref, *refs):
    heads, refs = refs[: len(items)], refs[len(items) :]
    before, (own_w, near_w, far_w, out, ordered) = refs[:streams], refs[streams:]
    chip, core = meta_ref[4], meta_ref[5]
    swapped = lax.rem(chip, 2)
    parities = [lax.rem(chip + distances[0], 2) for distances in groups]
    for place, (group, _) in enumerate(items):
        for index, distance in enumerate(groups[group]):
            head = lax.rem(chip - distance + chips, chips)
            column = pl.ds(pl.multiple_of(head // 2 * HEAD, HEAD), HEAD)
            ordered[place, :, column] = heads[place][index]

    def own_rows(parity):
        rows = [pl.ds(pl.multiple_of((2 * j + parity) * HEAD, HEAD), HEAD) for j in range(chips // 2)]
        return jnp.concatenate([own_w[span, :] for span in rows], axis=0)

    def finish(by_group):
        total = jnp.concatenate([part[...].astype(F32) for part in before], axis=0)
        for place, (group, source) in enumerate(items):
            if source:
                held = by_group[group]
                weights = jnp.concatenate([held[swapped, source - 1], held[1 - swapped, source - 1]], axis=0)
            else:
                weights = own_rows(parities[group])
            total = total + jnp.dot(ordered[place], weights, preferred_element_type=F32)
        out[...] = total.astype(out.dtype)

    @pl.when(core == parities[0])
    def _():
        finish([near_w, far_w])

    @pl.when(core != parities[0])
    def _():
        finish([far_w, near_w])


def mix(meta, heads, *, groups, items, before, own_w, near_w, far_w, kind, chips):
    rows, channels = heads[0].shape[1], own_w.shape[1]
    body = functools.partial(mix_kernel, chips, groups, items, len(before))
    operands = [*heads, *before, own_w, near_w, far_w]
    scratch = [pltpu.VMEM((len(items), rows, chips // 2 * HEAD), BF16)]
    micros = 0.6 * len(items)
    return vmem_call(body, "attention_mix", micros, meta, operands, [((rows, channels), kind)], scratch)[0]


def rotate_rows(block, positions):
    half_size = block.shape[-1] // 2
    frequency = 10000.0 ** (-jnp.arange(half_size, dtype=jnp.float32) * 2.0 / block.shape[-1])
    angles = positions.astype(jnp.float32)[:, None] * frequency[None, :]
    cosine = jnp.cos(angles)[:, None, :]
    sine_part = jnp.sin(angles)[:, None, :]
    first_half = block[..., :half_size]
    second_half = block[..., half_size:]
    return jnp.concatenate(
        [
            first_half * cosine - second_half * sine_part,
            second_half * cosine + first_half * sine_part,
        ],
        axis=-1,
    )


def run_attention(queries, query_pos, key_rows, value_rows, position_of):
    head_count = queries.shape[1]
    row_count = queries.shape[0]
    head_size = queries.shape[2]
    scale_factor = 1.0 / head_size**0.5
    last_query = jnp.max(query_pos)
    initial = (
        jnp.zeros((head_count, row_count, head_size), jnp.float32),
        jnp.full((head_count, row_count), -1e30, jnp.float32),
        jnp.zeros((head_count, row_count), jnp.float32),
    )
    piece_keys = lax.all_gather(key_rows, "ctx", axis=0, tiled=True)
    piece_values = lax.all_gather(value_rows, "ctx", axis=0, tiled=True)
    piece_rows = piece_keys.shape[0]
    block_rows = 512

    def one_block(state_in, block_index):
        first_block = block_index * block_rows
        key_block = lax.dynamic_slice_in_dim(piece_keys, first_block, block_rows, 0)
        value_block = lax.dynamic_slice_in_dim(piece_values, first_block, block_rows, 0)
        key_pos = position_of(first_block + jnp.arange(block_rows))

        def update(state_old):
            acc_sum, run_max, run_total = state_old
            scores = (
                jnp.einsum("thd,khd->htk", queries, key_block, preferred_element_type=jnp.float32)
                * scale_factor
            )
            causal = (key_pos[None, :] <= query_pos[:, None])[None]
            block_max = jnp.max(jnp.where(causal, scores, -1e30), axis=-1)
            new_max = jnp.maximum(run_max, block_max)
            weights = jnp.where(causal, jnp.exp(scores - new_max[..., None]), 0.0)
            correction = jnp.exp(run_max - new_max)
            new_total = run_total * correction + jnp.sum(weights, axis=-1)
            update_sum = jnp.einsum(
                "htk,khd->htd",
                weights.astype(jnp.bfloat16),
                value_block,
                preferred_element_type=jnp.float32,
            )
            return (acc_sum * correction[..., None] + update_sum, new_max, new_total)

        def unchanged(state_old):
            return state_old

        state_out = lax.cond(jnp.min(key_pos) > last_query, unchanged, update, state_in)
        return (state_out, None)

    state_end, unused = lax.scan(one_block, initial, jnp.arange(piece_rows // block_rows))
    acc_sum, run_max, run_total = state_end
    output = acc_sum / run_total[..., None]
    return jnp.transpose(output, (1, 0, 2)).astype(jnp.bfloat16)


def after_gating(gated, residual_in, out_weight, norm_gain, attn_weight, attn_out):
    tok_rows, chan_count = gated.shape
    hyena_terms = jnp.dot(gated, out_weight, preferred_element_type=jnp.float32)
    hyena_out = lax.psum_scatter(
        hyena_terms.astype(jnp.bfloat16), "ch", scatter_dimension=1, tiled=True
    ).astype(jnp.float32)
    stream = (residual_in.astype(jnp.float32) + hyena_out).astype(jnp.bfloat16)
    stream_wide = stream.astype(jnp.float32)
    full_width = chan_count * lax.axis_size("ch")
    head_cols = attn_weight.shape[1]
    square_total = lax.psum(jnp.sum(stream_wide * stream_wide, axis=1), "ch")
    inverse = lax.rsqrt(square_total / full_width + norm_eps)
    gain_part = lax.dynamic_slice_in_dim(norm_gain, lax.axis_index("ch") * chan_count, chan_count)
    normed = (stream_wide * inverse[:, None] * gain_part[None, :]).astype(jnp.bfloat16)
    projected = jnp.dot(
        lax.all_gather(normed, "ch", axis=1, tiled=True),
        attn_weight,
        preferred_element_type=jnp.float32,
    )
    head_count = head_cols // (3 * HEAD)
    projected = projected.reshape(tok_rows, head_count, 3, HEAD)
    ctx_index = lax.axis_index("ctx")
    positions = ctx_index * tok_rows + jnp.arange(tok_rows, dtype=jnp.int32)
    queries = rotate_rows(projected[:, :, 0, :], positions).astype(jnp.bfloat16)
    key_rows = rotate_rows(projected[:, :, 1, :], positions).astype(jnp.bfloat16)
    value_rows = projected[:, :, 2, :].astype(jnp.bfloat16)

    def position_of(global_row):
        return global_row

    attended = run_attention(queries, positions, key_rows, value_rows, position_of)
    head_terms = jnp.dot(
        attended.reshape(tok_rows, head_count * HEAD), attn_out, preferred_element_type=jnp.float32
    )
    attn_mix = lax.psum_scatter(
        head_terms.astype(jnp.bfloat16), "ch", scatter_dimension=1, tiled=True
    ).astype(jnp.float32)
    return (stream_wide + attn_mix).astype(jnp.bfloat16)


def rotation_tables(positions):
    half_size = HEAD // 2
    frequency = 10000.0 ** (-jnp.arange(half_size, dtype=F32) * 2.0 / HEAD)
    angles = positions.astype(F32)[:, None] * frequency[None, :]
    cosine, sine = jnp.cos(angles), jnp.sin(angles)
    return jnp.concatenate([cosine, cosine], axis=1), jnp.concatenate([-sine, sine], axis=1)


def shards(
    features,
    residual_in,
    short_filter,
    medium_filter,
    skip_gain,
    out_weight,
    norm_gain,
    attn_weight,
    attn_out,
):
    rows, _, channels = features.shape
    chips = lax.axis_size("ctx") // 2
    length = medium_filter.shape[0]
    chunk = rows // 2
    ctx, ch = lax.axis_index("ctx"), lax.axis_index("ch")
    scalars = [ch, ch ^ 1, ch ^ 2, ch ^ 3, ctx // 2, ctx % 2, ctx * rows, ctx]
    meta = jnp.stack(scalars).astype(jnp.int32)

    by_kind = jnp.transpose(features, (1, 0, 2))
    medium_rows = medium_filter.T
    skip = skip_gain.reshape(1, channels)

    starts = [rows - chunk, 0]
    if lax.axis_size("ch") != 4 or attn_weight.shape[1] != 3 * HEAD * chips or chips != 4:
        halo = shift_rows(by_kind[:, rows - length - LEAD :])
        (lower,) = gated_chunk(meta, by_kind, halo, chunk, chunk, short_filter, medium_rows, skip)
        (upper,) = gated_chunk(meta, by_kind, halo, 0, chunk, short_filter, medium_rows, skip)
        return after_gating(
            jnp.concatenate([upper, lower], axis=0), residual_in, out_weight, norm_gain, attn_weight, attn_out
        )

    gain = norm_gain.reshape(1, -1)
    cosine, sine = rotation_tables(meta[6:7] + jnp.arange(rows, dtype=jnp.int32))

    *near_w, edge = pick(meta, attn_out, by_kind, length + LEAD)
    halo = shift_rows(edge)
    picked = [swap_ch(weight, mask) for mask, weight in zip((1, 2, 3), near_w)]

    lower, out_held = gated_chunk(meta, by_kind, halo, chunk, chunk, short_filter, medium_rows, skip, out_weight)
    (upper,) = gated_chunk(meta, by_kind, halo, 0, chunk, short_filter, medium_rows, skip)
    across_x, across_y = column_terms(meta, upper, lower, out_held, ((3, 0, 0, 0), (3, 1, 1, 0)), picked)
    picked = jnp.stack(picked)
    swapped = swap_ctx(picked, 2)
    across_x, across_y = swap_ch(across_x, 1), swap_ch(across_y, 2)
    pieces = ((1, 0, 0, 0), (2, 1, 1, 0), (1, 1, 2, 0), (2, 0, 3, 0), (0, 0, 4, 0), (0, 1, 4, 1))
    direct_x, direct_y, along_x, along_y, kept = column_terms(meta, upper, lower, out_held, pieces, [picked])
    direct_x, direct_y = swap_ch(direct_x, 1), swap_ch(direct_y, 2)
    along_x = (along_x.astype(F32) + across_y.astype(F32)).astype(BF16)
    along_y = (along_y.astype(F32) + across_x.astype(F32)).astype(BF16)
    late_x, late_y = swap_ch(along_x, 1), swap_ch(along_y, 2)
    qkv_held, own_w = load(meta, attn_weight, attn_out, (along_y, swapped), channels)
    parts = vmem_call(
        stream_kernel,
        "add_stream",
        1,
        meta,
        [kept, direct_x, direct_y, late_x, late_y, residual_in],
        [((chunk, channels), BF16)] * 2,
        waits=[qkv_held, cosine, sine],
    )

    own, other, after = [], [], None
    width = attn_weight.shape[1]
    for start in starts:
        part = parts[start // chunk]
        if after is not None:
            part, _ = lax.optimization_barrier((part, after))
        by_x, by_y = swap_ch(part, 1), swap_ch(part, 2)
        diag_a, diag_b = swap_ch(by_x[: chunk // 2], 2), swap_ch(by_y[chunk // 2 :], 1)
        near, square = vmem_call(
            near_kernel,
            "qkv_near",
            3,
            meta,
            [part, by_x, by_y, gain, qkv_held],
            [((chunk, width), F32), ((chunk, LANES), F32)],
        )
        after = diag_a, diag_b, square
        turn = slice(start, start + chunk)
        outs = vmem_call(
            functools.partial(far_kernel, chips),
            "qkv_far",
            2,
            meta,
            [diag_a, diag_b, near, square, gain, cosine[turn], sine[turn], qkv_held],
            [((3, chunk, HEAD), BF16)] * chips,
            [pltpu.VMEM((chunk, width), F32)],
        )
        arrived = [outs[0]] + [rotate_chips(outs[d], d) for d in range(1, chips)]
        own.append(arrived)

    swapped, _ = lax.optimization_barrier((swapped, outs))
    near_w = jnp.stack([picked, swapped])
    far_w = swap_ctx(near_w, 1)
    own, _ = lax.optimization_barrier((own, outs))
    other = [swap_ctx(jnp.stack([piece[1:] for piece in arrived]), 1) for arrived in own]
    own, other = own[1] + own[0], other[::-1]

    groups = [(*range(2, chips, 2), 0), tuple(range(1, chips, 2))]
    given = attend(meta, own, other, [far_w], chips)
    first, second = [[rotate_chips(given[d], d) if d else given[d] for d in group] for group in groups]
    first, second = lax.optimization_barrier((first, second[:1]))[0], second
    back = jnp.stack(first)
    by_x, by_y = swap_ch(back, 1), swap_ch(back, 2)
    add = functools.partial(mix, meta, groups=groups, own_w=own_w, near_w=near_w, far_w=far_w, chips=chips)
    total = add([back, by_x, by_y], items=((0, 0), (0, 1), (0, 2)), before=parts, kind=F32)
    second, by_x, total = lax.optimization_barrier((second, by_x, total))
    across = swap_ch(by_x, 2)
    back = jnp.stack(second)
    by_x, by_y = swap_ch(back, 1), swap_ch(back, 2)
    total = add([across, back, by_y], items=((0, 3), (1, 0), (1, 2)), before=[total], kind=F32)
    return add([by_x, swap_ch(by_y, 1)], items=((1, 1), (1, 3)), before=[total], kind=BF16)


def solution(mesh):
    in_specs = (
        P("ctx", None, "ch"),
        P("ctx", "ch"),
        P(None, None, "ch"),
        P(None, "ch"),
        P("ch"),
        P("ch", None),
        P(),
        P(None, "ch"),
        P("ch", None),
    )
    out_specs = P("ctx", "ch")
    return jax.shard_map(shards, mesh=mesh, in_specs=in_specs, out_specs=out_specs, check_vma=False)
```

```python
import functools

import jax
import jax.numpy as jnp
from jax import lax
from jax.experimental import pallas as pl
from jax.experimental.pallas import tpu as pltpu
from jax.sharding import PartitionSpec as P

HEAD = 128
GROUP_SIZE = 16
LANES = 128
TILES = 4
LEAD = 16
norm_eps = 1e-05
SCORE_SCALE = 1.4426950408889634 / HEAD**0.5
MIB = 1024 * 1024
F32 = jnp.float32
BF16 = jnp.bfloat16


def lasting(micros):
    return pl.CostEstimate(
        flops=int(micros * 1.1e9), transcendentals=0, bytes_accessed=int(micros * 3.6e6)
    )


def swap_ch(value, mask):
    count = lax.axis_size("ch")
    return lax.ppermute(value, "ch", [(i, i ^ mask) for i in range(count)])


def swap_ctx(value, mask):
    count = lax.axis_size("ctx")
    return lax.ppermute(value, "ctx", [(i, i ^ mask) for i in range(count)])


def shift_rows(value):
    count = lax.axis_size("ctx")
    return lax.ppermute(value, "ctx", [(i, i + 1) for i in range(count - 1)])


def rotate_chips(value, distance):
    count = lax.axis_size("ctx")
    return lax.ppermute(value, "ctx", [(i, (i + 2 * distance) % count) for i in range(count)])


def filter_tile(first_row, tile, lanes, short_ref, medium_ref, skip_ref, halo_ref, rows_ref, wide, product, table, store):
    taps, groups_all = short_ref.shape[1:]
    length = medium_ref.shape[1]
    groups = LANES // GROUP_SIZE
    medium = medium_ref[pl.ds(pl.multiple_of(tile * groups, groups), groups), :]
    gain = skip_ref[:, pl.ds(pl.multiple_of(tile * LANES, LANES), LANES)]
    span = wide.shape[1]
    halo_rows = length + LEAD
    count = span - halo_rows

    for kind in range(3):
        if first_row == 0:
            wide[kind, :halo_rows] = halo_ref[kind, :, lanes].astype(F32)
            wide[kind, halo_rows:] = rows_ref[kind, :, lanes].astype(F32)
        else:
            wide[kind] = rows_ref[kind, first_row - halo_rows : first_row + count, lanes].astype(F32)

    group_row = lax.broadcasted_iota(jnp.int32, (groups_all, LANES), 0)
    group_col = lax.broadcasted_iota(jnp.int32, (groups_all, LANES), 1) // GROUP_SIZE + tile * groups
    chosen = jnp.where(group_row == group_col, 1.0, 0.0).astype(F32)
    weights = [
        jnp.dot(short_ref[kind], chosen, precision=lax.Precision.HIGHEST, preferred_element_type=F32)
        for kind in range(3)
    ]

    tap_row = lax.broadcasted_iota(jnp.int32, (length, 2 * length), 0)
    place = lax.broadcasted_iota(jnp.int32, (length, 2 * length), 1)
    turned = jnp.where(tap_row + place == length, 1.0, 0.0).astype(BF16)
    base = jnp.dot(medium.astype(BF16), turned, preferred_element_type=F32)
    for group in range(groups):
        spread = jnp.broadcast_to(base[group : group + 1, :], (length, 2 * length))
        rolled = pltpu.roll(spread, 0, 1, stride=1, stride_axis=0)
        table[group * length : (group + 1) * length, :] = rolled.astype(BF16)

    def featured(kind, start):
        total = weights[kind][0:1, :] * wide[kind, start : start + length, :]
        for tap in range(1, taps):
            total = total + weights[kind][tap : tap + 1, :] * wide[kind, start - tap : start - tap + length, :]
        return total

    for block in range(count // length + 1):
        start = LEAD + block * length
        product[block * length : (block + 1) * length, :] = (
            featured(1, start) * featured(2, start)
        ).astype(BF16)

    group_of = lax.broadcasted_iota(jnp.int32, (length, 2 * LANES), 1) % LANES // GROUP_SIZE
    for pair in range(count // (2 * length)):
        begin = pair * 2 * length
        window = jnp.concatenate(
            [
                product[begin : begin + 2 * length, :],
                product[begin + length : begin + 3 * length, :],
            ],
            axis=1,
        )
        spread = jnp.dot(table[...], window, preferred_element_type=F32)
        mixed = spread[:length]
        for group in range(1, groups):
            mixed = jnp.where(group_of == group, spread[group * length : (group + 1) * length], mixed)
        for part in range(2):
            row = begin + part * length
            direct = gain * product[row + length : row + 2 * length, :].astype(F32)
            gate = featured(0, halo_rows + row)
            store(row, (gate * (mixed[:, part * LANES : (part + 1) * LANES] + direct)).astype(BF16))


def gated_kernel(first_row, loads, *refs):
    head, rest = refs[1:4], refs[4:]
    halo_ref, rest = (rest[0], rest[1:]) if first_row == 0 else (None, rest)
    rows_ref, rest = rest[0], rest[1:]
    if loads:
        weight, out_ref, held, wide, product, table, sem = rest
        copy = pltpu.make_async_copy(weight, held, sem)
        pl.when(pl.program_id(0) == 0)(copy.start)
    else:
        out_ref, wide, product, table = rest

    for part in range(TILES):
        lanes = slice(part * LANES, (part + 1) * LANES)

        def store(row, value):
            out_ref[row : row + value.shape[0], lanes] = value

        scratch = wide.at[part], product.at[part], table.at[part]
        tile = pl.program_id(0) * TILES + part
        filter_tile(first_row, tile, lanes, *head, halo_ref, rows_ref, *scratch, store)
    if loads:
        pl.when(pl.program_id(0) == pl.num_programs(0) - 1)(copy.wait)


def gated_chunk(meta, features, halo, first_row, count, short_filter, medium_rows, skip, weight=None):
    kinds, rows, channels = features.shape
    length = medium_rows.shape[1]
    groups = LANES // GROUP_SIZE
    step = TILES * LANES
    loads = weight is not None
    in_hbm = lambda x: pltpu.with_memory_space_constraint(x, pltpu.HBM)
    in_specs = [
        pl.BlockSpec(memory_space=pltpu.SMEM),
        pl.BlockSpec(short_filter.shape, lambda i: (0, 0, 0)),
        pl.BlockSpec(medium_rows.shape, lambda i: (0, 0)),
        pl.BlockSpec(skip.shape, lambda i: (0, 0)),
    ]
    operands = [meta, in_hbm(short_filter), in_hbm(medium_rows), in_hbm(skip)]
    out_specs = [pl.BlockSpec((count, step), lambda i: (0, i))]
    out_shape = [jax.ShapeDtypeStruct((count, channels), BF16)]
    scratch = [
        pltpu.VMEM((TILES, kinds, length + LEAD + count, LANES), F32),
        pltpu.VMEM((TILES, length + count, LANES), BF16),
        pltpu.VMEM((TILES, groups * length, 2 * length), BF16),
    ]
    if first_row == 0:
        in_specs.append(pl.BlockSpec((kinds, length + LEAD, step), lambda i: (0, 0, i)))
        in_specs.append(pl.BlockSpec((kinds, count, step), lambda i: (0, 0, i)))
        operands += [halo, features]
    else:
        in_specs.append(pl.BlockSpec((kinds, rows, step), lambda i: (0, 0, i)))
        operands.append(features)
    if loads:
        in_specs.append(pl.BlockSpec(memory_space=pltpu.HBM))
        operands.append(in_hbm(weight))
        out_specs.append(pl.BlockSpec(memory_space=pltpu.VMEM))
        out_shape.append(pltpu.VMEM(weight.shape, weight.dtype))
        scratch.append(pltpu.SemaphoreType.DMA)
    return pl.pallas_call(
        functools.partial(gated_kernel, first_row, loads),
        grid=(channels // step,),
        in_specs=in_specs,
        out_specs=out_specs,
        out_shape=out_shape,
        scratch_shapes=scratch,
        compiler_params=pltpu.CompilerParams(vmem_limit_bytes=16 * MIB),
        name="hyena_filters",
    )(*operands)


def vmem_call(body, name, micros, scalars, operands, outs, scratch=(), waits=()):
    given = 1 + len(operands)
    run = lambda *refs: body(*refs[:given], *refs[given + len(waits) :])
    return pl.pallas_call(
        run,
        in_specs=[pl.BlockSpec(memory_space=pltpu.SMEM)]
        + [pl.BlockSpec(memory_space=pltpu.VMEM)] * (len(operands) + len(waits)),
        out_specs=[pl.BlockSpec(memory_space=pltpu.VMEM)] * len(outs),
        out_shape=[jax.ShapeDtypeStruct(shape, kind) for shape, kind in outs],
        scratch_shapes=list(scratch),
        compiler_params=pltpu.CompilerParams(vmem_limit_bytes=20 * MIB),
        cost_estimate=lasting(micros) if micros else None,
        name=name,
    )(scalars, *operands, *waits)


def columns_kernel(pieces, meta_ref, upper, lower, weight, *outs):
    gated = jnp.concatenate([upper[...], lower[...]], axis=0)
    width = weight.shape[1] // 8
    for owner, half, out, part in pieces:
        columns = pl.ds(pl.multiple_of((2 * meta_ref[owner] + half) * width, width), width)
        term = jnp.dot(gated, weight[:, columns], preferred_element_type=F32)
        outs[out][:, part * width : (part + 1) * width] = term.astype(BF16)


def column_terms(meta, upper, lower, weight, pieces, waits=()):
    rows, width = 2 * upper.shape[0], weight.shape[1] // 8
    outs = [((rows, width * sum(p[2] == out for p in pieces)), BF16) for out in range(pieces[-1][2] + 1)]
    body = functools.partial(columns_kernel, pieces)
    return vmem_call(body, "hyena_terms", None, meta, [upper, lower, weight], outs, waits=waits)


def load_kernel(meta_ref, source, outer, along, swapped, held, own, sems):
    channels = own.shape[1]
    columns = pl.ds(pl.multiple_of(meta_ref[0] * channels, channels), channels)
    copies = [
        pltpu.make_async_copy(source, held, sems.at[0]),
        pltpu.make_async_copy(outer.at[:, columns], own, sems.at[1]),
    ]
    for copy in copies:
        copy.start()
    for copy in copies:
        copy.wait()


def load(meta, weight, outer, after, channels):
    in_hbm = lambda x: pltpu.with_memory_space_constraint(x, pltpu.HBM)
    hbm, vmem = pl.BlockSpec(memory_space=pltpu.HBM), pl.BlockSpec(memory_space=pltpu.VMEM)
    return pl.pallas_call(
        load_kernel,
        in_specs=[pl.BlockSpec(memory_space=pltpu.SMEM), hbm, hbm, vmem, vmem],
        out_specs=[vmem, vmem],
        out_shape=[pltpu.VMEM(weight.shape, weight.dtype), pltpu.VMEM((outer.shape[0], channels), outer.dtype)],
        scratch_shapes=[pltpu.SemaphoreType.DMA((2,))],
        compiler_params=pltpu.CompilerParams(vmem_limit_bytes=4 * MIB),
        name="load_weights",
    )(meta, in_hbm(weight), in_hbm(outer), *after)


def stream_kernel(_, kept, direct_x, direct_y, late_x, late_y, residual, *parts):
    half = late_x.shape[1]
    rows = parts[0].shape[0]
    for index, out in enumerate(parts):
        span = slice(index * rows, (index + 1) * rows)
        wide = lambda ref: ref[span].astype(F32)
        left = wide(residual)[:, :half] + (wide(kept)[:, :half] + wide(direct_x) + wide(late_y))
        right = wide(residual)[:, half:] + (wide(kept)[:, half:] + wide(direct_y) + wide(late_x))
        out[...] = jnp.concatenate([left, right], axis=1).astype(BF16)


def near_kernel(meta_ref, *refs):
    blocks, (gain, weight, total, square) = refs[:3], refs[3:]
    channels = blocks[0].shape[1]
    squares = jnp.zeros(square.shape, F32)
    result = None
    for index in range(3):
        wide = blocks[index][...].astype(F32)
        squares = squares + jnp.sum(wide * wide, axis=1, keepdims=True)
        span = pl.ds(pl.multiple_of(meta_ref[index] * channels, channels), channels)
        factor, block = gain[:, span], weight[span, :]
        term = jnp.dot((wide * factor).astype(BF16), block, preferred_element_type=F32)
        result = term if result is None else result + term
    total[...] = result
    square[...] = squares


def far_kernel(chips, meta_ref, diag_a, diag_b, near, square, gain, cosine, sine, weight, *rest):
    outs, total = rest[:chips], rest[chips]
    channels = diag_a.shape[1]
    wide = jnp.concatenate([diag_a[...], diag_b[...]], axis=0).astype(F32)
    squares = square[...] + jnp.sum(wide * wide, axis=1, keepdims=True)
    span = pl.ds(pl.multiple_of(meta_ref[3] * channels, channels), channels)
    factor, block = gain[:, span], weight[span, :]
    total[...] = near[...] + jnp.dot((wide * factor).astype(BF16), block, preferred_element_type=F32)
    inverse = lax.rsqrt(squares / (4 * channels) + norm_eps)
    for distance, out in enumerate(outs):
        head = lax.rem(meta_ref[4] + distance, chips)
        for kind in range(3):
            column = pl.multiple_of((head * 3 + kind) * HEAD, HEAD)
            part = total[:, pl.ds(column, HEAD)] * inverse
            if kind < 2:
                part = part * cosine[...] + pltpu.roll(part, HEAD // 2, 1) * sine[...]
            if kind == 0:
                part = part * SCORE_SCALE
            if kind == 2:
                tiles = [part[row : row + HEAD].T for row in range(0, part.shape[0], HEAD)]
                part = jnp.concatenate(tiles, axis=0)
            out[kind] = part.astype(BF16)


def gather_keys(chips, meta_ref, own, other, keys, values):
    rows = own[0].shape[1]
    for distance in range(chips):
        place = lax.rem(meta_ref[4] - distance + chips, chips)
        for chunk, stacked in enumerate(other):
            mine = own[chunk * chips + distance]
            span = slice(chunk * rows, (chunk + 1) * rows)
            keys[0, place, span, :] = mine[1]
            keys[1, place, span, :] = stacked[distance, 0]
            for tile in range(rows // HEAD):
                first = chunk * rows + tile * HEAD
                taken = slice(tile * HEAD, (tile + 1) * HEAD)
                values[0, place, :, first : first + HEAD] = mine[2, taken, :]
                values[1, place, :, first : first + HEAD] = stacked[distance, 1, taken, :]


def attention_kernel(chips, chunks, distances, leading, meta_ref, *refs):
    if leading:
        pieces, other = refs[: chunks * chips], refs[chunks * chips : chunks * (chips + 1)]
        *outs, keys, values = refs[chunks * (chips + 1) :]
        gather_keys(chips, meta_ref, pieces, other, keys, values)
        sources = [pieces[(chips - distance) % chips :: chips] for distance in distances]
    else:
        taken = chunks * len(distances)
        pieces, (keys, values), outs = refs[:taken], refs[taken : taken + 2], refs[taken + 2 :]
        sources = [pieces[index * chunks : (index + 1) * chunks] for index in range(len(distances))]
    chip, core = meta_ref[4], meta_ref[5]
    count = keys.shape[2]

    def scores_of(side, place, queries):
        return lax.dot_general(
            keys[side, place], queries, (((1,), (1,)), ((), ())), preferred_element_type=F32
        )

    def update(state, mine, others, place):
        top, total, acc = state
        new_top = jnp.maximum(jnp.max(mine, axis=0, keepdims=True), jnp.max(others, axis=0, keepdims=True))
        if top is not None:
            new_top = jnp.maximum(new_top, top)
        mine = jnp.exp2(mine - new_top)
        others = jnp.exp2(others - new_top)
        gained = jnp.sum(mine, axis=0, keepdims=True) + jnp.sum(others, axis=0, keepdims=True)
        added = jnp.dot(values[0, place], mine.astype(BF16), preferred_element_type=F32)
        added = added + jnp.dot(values[1, place], others.astype(BF16), preferred_element_type=F32)
        if top is None:
            return new_top, gained, added
        shrink = jnp.exp2(top - new_top)
        return new_top, total * shrink + gained, acc * shrink + added

    key_row = lax.broadcasted_iota(jnp.int32, (count, count), 0)
    query_column = lax.broadcasted_iota(jnp.int32, (count, count), 1)
    for distance, source, out in zip(distances, sources, outs):
        place = lax.rem(chip + distance, chips)
        queries = jnp.concatenate([piece[0] for piece in source], axis=0)
        mine = jnp.where(key_row <= query_column, scores_of(0, place, queries), -1e30)
        others = jnp.where(core == 1, scores_of(1, place, queries), -1e30)
        state = update((None, None, None), mine, others, place)

        def earlier(index, state):
            return update(state, scores_of(0, index, queries), scores_of(1, index, queries), index)

        state = lax.fori_loop(0, place, earlier, state)
        out[...] = (state[2] / state[1]).T.astype(BF16)


def attend(meta, own, other, laid, distances, waits, chips):
    chunks, leading = len(other), laid is None
    count = own[0].shape[1] * chunks
    outs = [((count, HEAD), BF16)] * len(distances)
    if leading:
        operands = own + other
        outs = outs + [((2, chips, count, HEAD), BF16), ((2, chips, HEAD, count), BF16)]
    else:
        operands = [piece for distance in distances for piece in own[(chips - distance) % chips :: chips]]
        operands = [*operands, *laid]
    body = functools.partial(attention_kernel, chips, chunks, distances, leading)
    made = list(vmem_call(body, "attention", 6, meta, operands, outs, waits=waits))
    return made[: len(distances)], laid or made[len(distances) :]


def pick_kernel(meta_ref, weight, features, *refs):
    *near, edge, sems = refs
    channels = near[0].shape[1]
    kinds, count, _ = edge.shape
    last = features.shape[1] - count
    copies = []
    for kind in range(kinds):
        copies.append(
            pltpu.make_async_copy(features.at[kind, last : last + count], edge.at[kind], sems.at[kind])
        )
    rows = pl.ds(pl.multiple_of((2 * lax.rem(meta_ref[4], 2) + meta_ref[5]) * HEAD, HEAD), HEAD)
    for index, out in enumerate(near):
        columns = pl.ds(pl.multiple_of(meta_ref[index + 1] * channels, channels), channels)
        copies.append(pltpu.make_async_copy(weight.at[rows, columns], out, sems.at[kinds + index]))
    for copy in copies:
        copy.start()
    for copy in copies:
        copy.wait()


def pick(meta, weight, features, count):
    kinds, _, channels = features.shape
    near = jax.ShapeDtypeStruct((HEAD, channels), BF16)
    in_hbm = lambda x: pltpu.with_memory_space_constraint(x, pltpu.HBM)
    hbm, vmem = pl.BlockSpec(memory_space=pltpu.HBM), pl.BlockSpec(memory_space=pltpu.VMEM)
    return pl.pallas_call(
        pick_kernel,
        in_specs=[pl.BlockSpec(memory_space=pltpu.SMEM), hbm, hbm],
        out_specs=[vmem] * 4,
        out_shape=[near, near, near, jax.ShapeDtypeStruct((kinds, count, channels), BF16)],
        scratch_shapes=[pltpu.SemaphoreType.DMA((kinds + 3,))],
        compiler_params=pltpu.CompilerParams(vmem_limit_bytes=4 * MIB),
        name="pick",
    )(meta, in_hbm(weight), in_hbm(features))


def mix_kernel(chips, groups, items, streams, meta_ref, *refs):
    heads, refs = refs[: len(items)], refs[len(items) :]
    before, (own_w, near_w, far_w, out, ordered) = refs[:streams], refs[streams:]
    chip, core = meta_ref[4], meta_ref[5]
    swapped = lax.rem(chip, 2)
    parities = [lax.rem(chip + distances[0], 2) for distances in groups]
    for place, (group, _) in enumerate(items):
        for index, distance in enumerate(groups[group]):
            head = lax.rem(chip - distance + chips, chips)
            column = pl.ds(pl.multiple_of(head // 2 * HEAD, HEAD), HEAD)
            ordered[place, :, column] = heads[place][index]

    def own_rows(parity):
        rows = [pl.ds(pl.multiple_of((2 * j + parity) * HEAD, HEAD), HEAD) for j in range(chips // 2)]
        return jnp.concatenate([own_w[span, :] for span in rows], axis=0)

    def finish(by_group):
        total = jnp.concatenate([part[...].astype(F32) for part in before], axis=0)
        for place, (group, source) in enumerate(items):
            if source:
                held = by_group[group]
                weights = jnp.concatenate([held[swapped, source - 1], held[1 - swapped, source - 1]], axis=0)
            else:
                weights = own_rows(parities[group])
            total = total + jnp.dot(ordered[place], weights, preferred_element_type=F32)
        out[...] = total.astype(out.dtype)

    @pl.when(core == parities[0])
    def _():
        finish([near_w, far_w])

    @pl.when(core != parities[0])
    def _():
        finish([far_w, near_w])


def mix(meta, heads, *, groups, items, before, own_w, near_w, far_w, kind, chips):
    rows, channels = heads[0].shape[1], own_w.shape[1]
    body = functools.partial(mix_kernel, chips, groups, items, len(before))
    operands = [*heads, *before, own_w, near_w, far_w]
    scratch = [pltpu.VMEM((len(items), rows, chips // 2 * HEAD), BF16)]
    micros = 0.6 * len(items)
    return vmem_call(body, "attention_mix", micros, meta, operands, [((rows, channels), kind)], scratch)[0]


def rotate_rows(block, positions):
    half_size = block.shape[-1] // 2
    frequency = 10000.0 ** (-jnp.arange(half_size, dtype=jnp.float32) * 2.0 / block.shape[-1])
    angles = positions.astype(jnp.float32)[:, None] * frequency[None, :]
    cosine = jnp.cos(angles)[:, None, :]
    sine_part = jnp.sin(angles)[:, None, :]
    first_half = block[..., :half_size]
    second_half = block[..., half_size:]
    return jnp.concatenate(
        [
            first_half * cosine - second_half * sine_part,
            second_half * cosine + first_half * sine_part,
        ],
        axis=-1,
    )


def run_attention(queries, query_pos, key_rows, value_rows, position_of):
    head_count = queries.shape[1]
    row_count = queries.shape[0]
    head_size = queries.shape[2]
    scale_factor = 1.0 / head_size**0.5
    last_query = jnp.max(query_pos)
    initial = (
        jnp.zeros((head_count, row_count, head_size), jnp.float32),
        jnp.full((head_count, row_count), -1e30, jnp.float32),
        jnp.zeros((head_count, row_count), jnp.float32),
    )
    piece_keys = lax.all_gather(key_rows, "ctx", axis=0, tiled=True)
    piece_values = lax.all_gather(value_rows, "ctx", axis=0, tiled=True)
    piece_rows = piece_keys.shape[0]
    block_rows = 512

    def one_block(state_in, block_index):
        first_block = block_index * block_rows
        key_block = lax.dynamic_slice_in_dim(piece_keys, first_block, block_rows, 0)
        value_block = lax.dynamic_slice_in_dim(piece_values, first_block, block_rows, 0)
        key_pos = position_of(first_block + jnp.arange(block_rows))

        def update(state_old):
            acc_sum, run_max, run_total = state_old
            scores = (
                jnp.einsum("thd,khd->htk", queries, key_block, preferred_element_type=jnp.float32)
                * scale_factor
            )
            causal = (key_pos[None, :] <= query_pos[:, None])[None]
            block_max = jnp.max(jnp.where(causal, scores, -1e30), axis=-1)
            new_max = jnp.maximum(run_max, block_max)
            weights = jnp.where(causal, jnp.exp(scores - new_max[..., None]), 0.0)
            correction = jnp.exp(run_max - new_max)
            new_total = run_total * correction + jnp.sum(weights, axis=-1)
            update_sum = jnp.einsum(
                "htk,khd->htd",
                weights.astype(jnp.bfloat16),
                value_block,
                preferred_element_type=jnp.float32,
            )
            return (acc_sum * correction[..., None] + update_sum, new_max, new_total)

        def unchanged(state_old):
            return state_old

        state_out = lax.cond(jnp.min(key_pos) > last_query, unchanged, update, state_in)
        return (state_out, None)

    state_end, unused = lax.scan(one_block, initial, jnp.arange(piece_rows // block_rows))
    acc_sum, run_max, run_total = state_end
    output = acc_sum / run_total[..., None]
    return jnp.transpose(output, (1, 0, 2)).astype(jnp.bfloat16)


def after_gating(gated, residual_in, out_weight, norm_gain, attn_weight, attn_out):
    tok_rows, chan_count = gated.shape
    hyena_terms = jnp.dot(gated, out_weight, preferred_element_type=jnp.float32)
    hyena_out = lax.psum_scatter(
        hyena_terms.astype(jnp.bfloat16), "ch", scatter_dimension=1, tiled=True
    ).astype(jnp.float32)
    stream = (residual_in.astype(jnp.float32) + hyena_out).astype(jnp.bfloat16)
    stream_wide = stream.astype(jnp.float32)
    full_width = chan_count * lax.axis_size("ch")
    head_cols = attn_weight.shape[1]
    square_total = lax.psum(jnp.sum(stream_wide * stream_wide, axis=1), "ch")
    inverse = lax.rsqrt(square_total / full_width + norm_eps)
    gain_part = lax.dynamic_slice_in_dim(norm_gain, lax.axis_index("ch") * chan_count, chan_count)
    normed = (stream_wide * inverse[:, None] * gain_part[None, :]).astype(jnp.bfloat16)
    projected = jnp.dot(
        lax.all_gather(normed, "ch", axis=1, tiled=True),
        attn_weight,
        preferred_element_type=jnp.float32,
    )
    head_count = head_cols // (3 * HEAD)
    projected = projected.reshape(tok_rows, head_count, 3, HEAD)
    ctx_index = lax.axis_index("ctx")
    positions = ctx_index * tok_rows + jnp.arange(tok_rows, dtype=jnp.int32)
    queries = rotate_rows(projected[:, :, 0, :], positions).astype(jnp.bfloat16)
    key_rows = rotate_rows(projected[:, :, 1, :], positions).astype(jnp.bfloat16)
    value_rows = projected[:, :, 2, :].astype(jnp.bfloat16)

    def position_of(global_row):
        return global_row

    attended = run_attention(queries, positions, key_rows, value_rows, position_of)
    head_terms = jnp.dot(
        attended.reshape(tok_rows, head_count * HEAD), attn_out, preferred_element_type=jnp.float32
    )
    attn_mix = lax.psum_scatter(
        head_terms.astype(jnp.bfloat16), "ch", scatter_dimension=1, tiled=True
    ).astype(jnp.float32)
    return (stream_wide + attn_mix).astype(jnp.bfloat16)


def rotation_tables(positions):
    half_size = HEAD // 2
    frequency = 10000.0 ** (-jnp.arange(half_size, dtype=F32) * 2.0 / HEAD)
    angles = positions.astype(F32)[:, None] * frequency[None, :]
    cosine, sine = jnp.cos(angles), jnp.sin(angles)
    return jnp.concatenate([cosine, cosine], axis=1), jnp.concatenate([-sine, sine], axis=1)


def shards(
    features,
    residual_in,
    short_filter,
    medium_filter,
    skip_gain,
    out_weight,
    norm_gain,
    attn_weight,
    attn_out,
):
    rows, _, channels = features.shape
    chips = lax.axis_size("ctx") // 2
    length = medium_filter.shape[0]
    chunk = rows // 2
    ctx, ch = lax.axis_index("ctx"), lax.axis_index("ch")
    scalars = [ch, ch ^ 1, ch ^ 2, ch ^ 3, ctx // 2, ctx % 2, ctx * rows, ctx]
    meta = jnp.stack(scalars).astype(jnp.int32)

    by_kind = jnp.transpose(features, (1, 0, 2))
    medium_rows = medium_filter.T
    skip = skip_gain.reshape(1, channels)

    starts = [rows - chunk, 0]
    if lax.axis_size("ch") != 4 or attn_weight.shape[1] != 3 * HEAD * chips or chips != 4:
        halo = shift_rows(by_kind[:, rows - length - LEAD :])
        (lower,) = gated_chunk(meta, by_kind, halo, chunk, chunk, short_filter, medium_rows, skip)
        (upper,) = gated_chunk(meta, by_kind, halo, 0, chunk, short_filter, medium_rows, skip)
        return after_gating(
            jnp.concatenate([upper, lower], axis=0), residual_in, out_weight, norm_gain, attn_weight, attn_out
        )

    gain = norm_gain.reshape(1, -1)
    cosine, sine = rotation_tables(meta[6:7] + jnp.arange(rows, dtype=jnp.int32))

    *near_w, edge = pick(meta, attn_out, by_kind, length + LEAD)
    halo = shift_rows(edge)
    picked = [swap_ch(weight, mask) for mask, weight in zip((1, 2, 3), near_w)]

    lower, out_held = gated_chunk(meta, by_kind, halo, chunk, chunk, short_filter, medium_rows, skip, out_weight)
    (upper,) = gated_chunk(meta, by_kind, halo, 0, chunk, short_filter, medium_rows, skip)
    across_x, across_y = column_terms(meta, upper, lower, out_held, ((3, 0, 0, 0), (3, 1, 1, 0)), picked)
    picked = jnp.stack(picked)
    swapped = swap_ctx(picked, 2)
    across_x, across_y = swap_ch(across_x, 1), swap_ch(across_y, 2)
    pieces = ((1, 0, 0, 0), (2, 1, 1, 0), (1, 1, 2, 0), (2, 0, 3, 0), (0, 0, 4, 0), (0, 1, 4, 1))
    direct_x, direct_y, along_x, along_y, kept = column_terms(meta, upper, lower, out_held, pieces, [picked])
    direct_x, direct_y = swap_ch(direct_x, 1), swap_ch(direct_y, 2)
    along_x = (along_x.astype(F32) + across_y.astype(F32)).astype(BF16)
    along_y = (along_y.astype(F32) + across_x.astype(F32)).astype(BF16)
    late_x, late_y = swap_ch(along_x, 1), swap_ch(along_y, 2)
    qkv_held, own_w = load(meta, attn_weight, attn_out, (along_y, swapped), channels)
    parts = vmem_call(
        stream_kernel,
        "add_stream",
        1,
        meta,
        [kept, direct_x, direct_y, late_x, late_y, residual_in],
        [((chunk, channels), BF16)] * 2,
        waits=[qkv_held, cosine, sine],
    )

    own, other, after = [], [], None
    width = attn_weight.shape[1]
    for start in starts:
        part = parts[start // chunk]
        if after is not None:
            part, _ = lax.optimization_barrier((part, after))
        by_x, by_y = swap_ch(part, 1), swap_ch(part, 2)
        diag_a, diag_b = swap_ch(by_x[: chunk // 2], 2), swap_ch(by_y[chunk // 2 :], 1)
        near, square = vmem_call(
            near_kernel,
            "qkv_near",
            3,
            meta,
            [part, by_x, by_y, gain, qkv_held],
            [((chunk, width), F32), ((chunk, LANES), F32)],
        )
        after = diag_a, diag_b, square
        turn = slice(start, start + chunk)
        outs = vmem_call(
            functools.partial(far_kernel, chips),
            "qkv_far",
            2,
            meta,
            [diag_a, diag_b, near, square, gain, cosine[turn], sine[turn], qkv_held],
            [((3, chunk, HEAD), BF16)] * chips,
            [pltpu.VMEM((chunk, width), F32)],
        )
        arrived = [outs[0]] + [rotate_chips(outs[d], d) for d in range(1, chips)]
        own.append(arrived)

    swapped, _ = lax.optimization_barrier((swapped, outs))
    near_w = jnp.stack([picked, swapped])
    far_w = swap_ctx(near_w, 1)
    own, _ = lax.optimization_barrier((own, outs))
    other = [swap_ctx(jnp.stack([piece[1:] for piece in arrived]), 1) for arrived in own]
    own, other = own[1] + own[0], other[::-1]

    groups = [tuple(range(1, chips, 2)), (*range(2, chips, 2), 0)]
    given, laid = attend(meta, own, other, None, groups[0], [far_w], chips)
    first = [rotate_chips(piece, d) for d, piece in zip(groups[0], given)]
    given, _ = attend(meta, own, other, laid, groups[1], [], chips)
    first, given = lax.optimization_barrier((first, given))
    second = [rotate_chips(piece, d) if d else piece for d, piece in zip(groups[1], given)]
    back = jnp.stack(first)
    by_x, by_y = swap_ch(back, 1), swap_ch(back, 2)
    add = functools.partial(mix, meta, groups=groups, own_w=own_w, near_w=near_w, far_w=far_w, chips=chips)
    total = add([back, by_x, by_y], items=((0, 0), (0, 1), (0, 2)), before=parts, kind=F32)
    second, by_x, total = lax.optimization_barrier((second, by_x, total))
    across = swap_ch(by_x, 2)
    back = jnp.stack(second)
    by_x, by_y = swap_ch(back, 1), swap_ch(back, 2)
    total = add([across, back, by_y], items=((0, 3), (1, 0), (1, 2)), before=[total], kind=F32)
    return add([by_x, swap_ch(by_y, 1)], items=((1, 1), (1, 3)), before=[total], kind=BF16)


def solution(mesh):
    in_specs = (
        P("ctx", None, "ch"),
        P("ctx", "ch"),
        P(None, None, "ch"),
        P(None, "ch"),
        P("ch"),
        P("ch", None),
        P(),
        P(None, "ch"),
        P("ch", None),
    )
    out_specs = P("ctx", "ch")
    return jax.shard_map(shards, mesh=mesh, in_specs=in_specs, out_specs=out_specs, check_vma=False)
```

```python
import functools

import jax
import jax.numpy as jnp
from jax import lax
from jax.experimental import pallas as pl
from jax.experimental.pallas import tpu as pltpu
from jax.sharding import PartitionSpec as P

HEAD = 128
GROUP_SIZE = 16
LANES = 128
TILES = 4
LEAD = 16
norm_eps = 1e-05
SCORE_SCALE = 1.4426950408889634 / HEAD**0.5
MIB = 1024 * 1024
F32 = jnp.float32
BF16 = jnp.bfloat16


def lasting(micros):
    return pl.CostEstimate(
        flops=int(micros * 1.1e9), transcendentals=0, bytes_accessed=int(micros * 3.6e6)
    )


def swap_ch(value, mask):
    count = lax.axis_size("ch")
    return lax.ppermute(value, "ch", [(i, i ^ mask) for i in range(count)])


def swap_ctx(value, mask):
    count = lax.axis_size("ctx")
    return lax.ppermute(value, "ctx", [(i, i ^ mask) for i in range(count)])


def shift_rows(value):
    count = lax.axis_size("ctx")
    return lax.ppermute(value, "ctx", [(i, i + 1) for i in range(count - 1)])


def rotate_chips(value, distance):
    count = lax.axis_size("ctx")
    return lax.ppermute(value, "ctx", [(i, (i + 2 * distance) % count) for i in range(count)])


def filter_tile(first_row, tile, lanes, short_ref, medium_ref, skip_ref, halo_ref, rows_ref, wide, product, table, store):
    taps, groups_all = short_ref.shape[1:]
    length = medium_ref.shape[1]
    groups = LANES // GROUP_SIZE
    medium = medium_ref[pl.ds(pl.multiple_of(tile * groups, groups), groups), :]
    gain = skip_ref[:, pl.ds(pl.multiple_of(tile * LANES, LANES), LANES)]
    span = wide.shape[1]
    halo_rows = length + LEAD
    count = span - halo_rows

    for kind in range(3):
        if first_row == 0:
            wide[kind, :halo_rows] = halo_ref[kind, :, lanes].astype(F32)
            wide[kind, halo_rows:] = rows_ref[kind, :, lanes].astype(F32)
        else:
            wide[kind] = rows_ref[kind, first_row - halo_rows : first_row + count, lanes].astype(F32)

    group_row = lax.broadcasted_iota(jnp.int32, (groups_all, LANES), 0)
    group_col = lax.broadcasted_iota(jnp.int32, (groups_all, LANES), 1) // GROUP_SIZE + tile * groups
    chosen = jnp.where(group_row == group_col, 1.0, 0.0).astype(F32)
    weights = [
        jnp.dot(short_ref[kind], chosen, precision=lax.Precision.HIGHEST, preferred_element_type=F32)
        for kind in range(3)
    ]

    tap_row = lax.broadcasted_iota(jnp.int32, (length, 2 * length), 0)
    place = lax.broadcasted_iota(jnp.int32, (length, 2 * length), 1)
    turned = jnp.where(tap_row + place == length, 1.0, 0.0).astype(BF16)
    base = jnp.dot(medium.astype(BF16), turned, preferred_element_type=F32)
    for group in range(groups):
        spread = jnp.broadcast_to(base[group : group + 1, :], (length, 2 * length))
        rolled = pltpu.roll(spread, 0, 1, stride=1, stride_axis=0)
        table[group * length : (group + 1) * length, :] = rolled.astype(BF16)

    def featured(kind, start):
        total = weights[kind][0:1, :] * wide[kind, start : start + length, :]
        for tap in range(1, taps):
            total = total + weights[kind][tap : tap + 1, :] * wide[kind, start - tap : start - tap + length, :]
        return total

    for block in range(count // length + 1):
        start = LEAD + block * length
        product[block * length : (block + 1) * length, :] = (
            featured(1, start) * featured(2, start)
        ).astype(BF16)

    group_of = lax.broadcasted_iota(jnp.int32, (length, 2 * LANES), 1) % LANES // GROUP_SIZE
    for pair in range(count // (2 * length)):
        begin = pair * 2 * length
        window = jnp.concatenate(
            [
                product[begin : begin + 2 * length, :],
                product[begin + length : begin + 3 * length, :],
            ],
            axis=1,
        )
        spread = jnp.dot(table[...], window, preferred_element_type=F32)
        mixed = spread[:length]
        for group in range(1, groups):
            mixed = jnp.where(group_of == group, spread[group * length : (group + 1) * length], mixed)
        for part in range(2):
            row = begin + part * length
            direct = gain * product[row + length : row + 2 * length, :].astype(F32)
            gate = featured(0, halo_rows + row)
            store(row, (gate * (mixed[:, part * LANES : (part + 1) * LANES] + direct)).astype(BF16))


def gated_kernel(first_row, loads, *refs):
    head, rest = refs[1:4], refs[4:]
    halo_ref, rest = (rest[0], rest[1:]) if first_row == 0 else (None, rest)
    rows_ref, rest = rest[0], rest[1:]
    if loads:
        weight, out_ref, held, wide, product, table, sem = rest
        copy = pltpu.make_async_copy(weight, held, sem)
        pl.when(pl.program_id(0) == 0)(copy.start)
    else:
        out_ref, wide, product, table = rest

    for part in range(TILES):
        lanes = slice(part * LANES, (part + 1) * LANES)

        def store(row, value):
            out_ref[row : row + value.shape[0], lanes] = value

        scratch = wide.at[part], product.at[part], table.at[part]
        tile = pl.program_id(0) * TILES + part
        filter_tile(first_row, tile, lanes, *head, halo_ref, rows_ref, *scratch, store)
    if loads:
        pl.when(pl.program_id(0) == pl.num_programs(0) - 1)(copy.wait)


def gated_chunk(meta, features, halo, first_row, count, short_filter, medium_rows, skip, weight=None):
    kinds, rows, channels = features.shape
    length = medium_rows.shape[1]
    groups = LANES // GROUP_SIZE
    step = TILES * LANES
    loads = weight is not None
    in_hbm = lambda x: pltpu.with_memory_space_constraint(x, pltpu.HBM)
    in_specs = [
        pl.BlockSpec(memory_space=pltpu.SMEM),
        pl.BlockSpec(short_filter.shape, lambda i: (0, 0, 0)),
        pl.BlockSpec(medium_rows.shape, lambda i: (0, 0)),
        pl.BlockSpec(skip.shape, lambda i: (0, 0)),
    ]
    operands = [meta, in_hbm(short_filter), in_hbm(medium_rows), in_hbm(skip)]
    out_specs = [pl.BlockSpec((count, step), lambda i: (0, i))]
    out_shape = [jax.ShapeDtypeStruct((count, channels), BF16)]
    scratch = [
        pltpu.VMEM((TILES, kinds, length + LEAD + count, LANES), F32),
        pltpu.VMEM((TILES, length + count, LANES), BF16),
        pltpu.VMEM((TILES, groups * length, 2 * length), BF16),
    ]
    if first_row == 0:
        in_specs.append(pl.BlockSpec((kinds, length + LEAD, step), lambda i: (0, 0, i)))
        in_specs.append(pl.BlockSpec((kinds, count, step), lambda i: (0, 0, i)))
        operands += [halo, features]
    else:
        in_specs.append(pl.BlockSpec((kinds, rows, step), lambda i: (0, 0, i)))
        operands.append(features)
    if loads:
        in_specs.append(pl.BlockSpec(memory_space=pltpu.HBM))
        operands.append(in_hbm(weight))
        out_specs.append(pl.BlockSpec(memory_space=pltpu.VMEM))
        out_shape.append(pltpu.VMEM(weight.shape, weight.dtype))
        scratch.append(pltpu.SemaphoreType.DMA)
    return pl.pallas_call(
        functools.partial(gated_kernel, first_row, loads),
        grid=(channels // step,),
        in_specs=in_specs,
        out_specs=out_specs,
        out_shape=out_shape,
        scratch_shapes=scratch,
        compiler_params=pltpu.CompilerParams(vmem_limit_bytes=16 * MIB),
        name="hyena_filters",
    )(*operands)


def vmem_call(body, name, micros, scalars, operands, outs, scratch=(), waits=()):
    given = 1 + len(operands)
    run = lambda *refs: body(*refs[:given], *refs[given + len(waits) :])
    return pl.pallas_call(
        run,
        in_specs=[pl.BlockSpec(memory_space=pltpu.SMEM)]
        + [pl.BlockSpec(memory_space=pltpu.VMEM)] * (len(operands) + len(waits)),
        out_specs=[pl.BlockSpec(memory_space=pltpu.VMEM)] * len(outs),
        out_shape=[jax.ShapeDtypeStruct(shape, kind) for shape, kind in outs],
        scratch_shapes=list(scratch),
        compiler_params=pltpu.CompilerParams(vmem_limit_bytes=20 * MIB),
        cost_estimate=lasting(micros) if micros else None,
        name=name,
    )(scalars, *operands, *waits)


def columns_kernel(pieces, meta_ref, upper, lower, weight, *outs):
    gated = jnp.concatenate([upper[...], lower[...]], axis=0)
    width = weight.shape[1] // 8
    for owner, half, out, part in pieces:
        columns = pl.ds(pl.multiple_of((2 * meta_ref[owner] + half) * width, width), width)
        term = jnp.dot(gated, weight[:, columns], preferred_element_type=F32)
        outs[out][:, part * width : (part + 1) * width] = term.astype(BF16)


def column_terms(meta, upper, lower, weight, pieces, waits=()):
    rows, width = 2 * upper.shape[0], weight.shape[1] // 8
    outs = [((rows, width * sum(p[2] == out for p in pieces)), BF16) for out in range(pieces[-1][2] + 1)]
    body = functools.partial(columns_kernel, pieces)
    return vmem_call(body, "hyena_terms", None, meta, [upper, lower, weight], outs, waits=waits)


def load_kernel(meta_ref, source, outer, along, swapped, held, own, sems):
    channels = own.shape[1]
    columns = pl.ds(pl.multiple_of(meta_ref[0] * channels, channels), channels)
    copies = [
        pltpu.make_async_copy(source, held, sems.at[0]),
        pltpu.make_async_copy(outer.at[:, columns], own, sems.at[1]),
    ]
    for copy in copies:
        copy.start()
    for copy in copies:
        copy.wait()


def load(meta, weight, outer, after, channels):
    in_hbm = lambda x: pltpu.with_memory_space_constraint(x, pltpu.HBM)
    hbm, vmem = pl.BlockSpec(memory_space=pltpu.HBM), pl.BlockSpec(memory_space=pltpu.VMEM)
    return pl.pallas_call(
        load_kernel,
        in_specs=[pl.BlockSpec(memory_space=pltpu.SMEM), hbm, hbm, vmem, vmem],
        out_specs=[vmem, vmem],
        out_shape=[pltpu.VMEM(weight.shape, weight.dtype), pltpu.VMEM((outer.shape[0], channels), outer.dtype)],
        scratch_shapes=[pltpu.SemaphoreType.DMA((2,))],
        compiler_params=pltpu.CompilerParams(vmem_limit_bytes=4 * MIB),
        name="load_weights",
    )(meta, in_hbm(weight), in_hbm(outer), *after)


def stream_kernel(_, kept, direct_x, direct_y, late_x, late_y, residual, *parts):
    half = late_x.shape[1]
    rows = parts[0].shape[0]
    for index, out in enumerate(parts):
        span = slice(index * rows, (index + 1) * rows)
        wide = lambda ref: ref[span].astype(F32)
        left = wide(residual)[:, :half] + (wide(kept)[:, :half] + wide(direct_x) + wide(late_y))
        right = wide(residual)[:, half:] + (wide(kept)[:, half:] + wide(direct_y) + wide(late_x))
        out[...] = jnp.concatenate([left, right], axis=1).astype(BF16)


def near_kernel(meta_ref, *refs):
    blocks, (gain, weight, total, square) = refs[:3], refs[3:]
    channels = blocks[0].shape[1]
    squares = jnp.zeros(square.shape, F32)
    result = None
    for index in range(3):
        wide = blocks[index][...].astype(F32)
        squares = squares + jnp.sum(wide * wide, axis=1, keepdims=True)
        span = pl.ds(pl.multiple_of(meta_ref[index] * channels, channels), channels)
        factor, block = gain[:, span], weight[span, :]
        term = jnp.dot((wide * factor).astype(BF16), block, preferred_element_type=F32)
        result = term if result is None else result + term
    total[...] = result
    square[...] = squares


def far_kernel(chips, meta_ref, diag_a, diag_b, near, square, gain, cosine, sine, weight, *rest):
    outs, total = rest[:chips], rest[chips]
    channels = diag_a.shape[1]
    wide = jnp.concatenate([diag_a[...], diag_b[...]], axis=0).astype(F32)
    squares = square[...] + jnp.sum(wide * wide, axis=1, keepdims=True)
    span = pl.ds(pl.multiple_of(meta_ref[3] * channels, channels), channels)
    factor, block = gain[:, span], weight[span, :]
    total[...] = near[...] + jnp.dot((wide * factor).astype(BF16), block, preferred_element_type=F32)
    inverse = lax.rsqrt(squares / (4 * channels) + norm_eps)
    for distance, out in enumerate(outs):
        head = lax.rem(meta_ref[4] + distance, chips)
        for kind in range(3):
            column = pl.multiple_of((head * 3 + kind) * HEAD, HEAD)
            part = total[:, pl.ds(column, HEAD)] * inverse
            if kind < 2:
                part = part * cosine[...] + pltpu.roll(part, HEAD // 2, 1) * sine[...]
            if kind == 0:
                part = part * SCORE_SCALE
            if kind == 2:
                tiles = [part[row : row + HEAD].T for row in range(0, part.shape[0], HEAD)]
                part = jnp.concatenate(tiles, axis=0)
            out[kind] = part.astype(BF16)


def gather_keys(chips, meta_ref, own, other, keys, values):
    rows = own[0].shape[1]
    for distance in range(chips):
        place = lax.rem(meta_ref[4] - distance + chips, chips)
        for chunk, stacked in enumerate(other):
            mine = own[chunk * chips + distance]
            span = slice(chunk * rows, (chunk + 1) * rows)
            keys[0, place, span, :] = mine[1]
            keys[1, place, span, :] = stacked[distance, 0]
            for tile in range(rows // HEAD):
                first = chunk * rows + tile * HEAD
                taken = slice(tile * HEAD, (tile + 1) * HEAD)
                values[0, place, :, first : first + HEAD] = mine[2, taken, :]
                values[1, place, :, first : first + HEAD] = stacked[distance, 1, taken, :]


def attention_kernel(chips, chunks, distances, leading, meta_ref, *refs):
    if leading:
        pieces, other = refs[: chunks * chips], refs[chunks * chips : chunks * (chips + 1)]
        *outs, keys, values = refs[chunks * (chips + 1) :]
        gather_keys(chips, meta_ref, pieces, other, keys, values)
        sources = [pieces[(chips - distance) % chips :: chips] for distance in distances]
    else:
        taken = chunks * len(distances)
        pieces, (keys, values), outs = refs[:taken], refs[taken : taken + 2], refs[taken + 2 :]
        sources = [pieces[index * chunks : (index + 1) * chunks] for index in range(len(distances))]
    chip, core = meta_ref[4], meta_ref[5]
    count = keys.shape[2]

    def scores_of(side, place, queries):
        return lax.dot_general(
            keys[side, place], queries, (((1,), (1,)), ((), ())), preferred_element_type=F32
        )

    def update(state, mine, others, place):
        top, total, acc = state
        new_top = jnp.maximum(jnp.max(mine, axis=0, keepdims=True), jnp.max(others, axis=0, keepdims=True))
        if top is not None:
            new_top = jnp.maximum(new_top, top)
        mine = jnp.exp2(mine - new_top)
        others = jnp.exp2(others - new_top)
        gained = jnp.sum(mine, axis=0, keepdims=True) + jnp.sum(others, axis=0, keepdims=True)
        added = jnp.dot(values[0, place], mine.astype(BF16), preferred_element_type=F32)
        added = added + jnp.dot(values[1, place], others.astype(BF16), preferred_element_type=F32)
        if top is None:
            return new_top, gained, added
        shrink = jnp.exp2(top - new_top)
        return new_top, total * shrink + gained, acc * shrink + added

    key_row = lax.broadcasted_iota(jnp.int32, (count, count), 0)
    query_column = lax.broadcasted_iota(jnp.int32, (count, count), 1)
    for distance, source, out in zip(distances, sources, outs):
        place = lax.rem(chip + distance, chips)
        queries = jnp.concatenate([piece[0] for piece in source], axis=0)
        mine = jnp.where(key_row <= query_column, scores_of(0, place, queries), -1e30)
        others = jnp.where(core == 1, scores_of(1, place, queries), -1e30)
        state = update((None, None, None), mine, others, place)

        def earlier(index, state):
            return update(state, scores_of(0, index, queries), scores_of(1, index, queries), index)

        state = lax.fori_loop(0, place, earlier, state)
        out[...] = (state[2] / state[1]).T.astype(BF16)


def attend(meta, own, other, laid, distances, waits, chips):
    chunks, leading = len(other), laid is None
    count = own[0].shape[1] * chunks
    outs = [((count, HEAD), BF16)] * len(distances)
    if leading:
        operands = own + other
        outs = outs + [((2, chips, count, HEAD), BF16), ((2, chips, HEAD, count), BF16)]
    else:
        operands = [piece for distance in distances for piece in own[(chips - distance) % chips :: chips]]
        operands = [*operands, *laid]
    body = functools.partial(attention_kernel, chips, chunks, distances, leading)
    made = list(vmem_call(body, "attention", 6, meta, operands, outs, waits=waits))
    return made[: len(distances)], laid or made[len(distances) :]


def pick_kernel(meta_ref, weight, features, *refs):
    *near, edge, sems = refs
    channels = near[0].shape[1]
    kinds, count, _ = edge.shape
    last = features.shape[1] - count
    copies = []
    for kind in range(kinds):
        copies.append(
            pltpu.make_async_copy(features.at[kind, last : last + count], edge.at[kind], sems.at[kind])
        )
    rows = pl.ds(pl.multiple_of((2 * lax.rem(meta_ref[4], 2) + meta_ref[5]) * HEAD, HEAD), HEAD)
    for index, out in enumerate(near):
        columns = pl.ds(pl.multiple_of(meta_ref[index + 1] * channels, channels), channels)
        copies.append(pltpu.make_async_copy(weight.at[rows, columns], out, sems.at[kinds + index]))
    for copy in copies:
        copy.start()
    for copy in copies:
        copy.wait()


def pick(meta, weight, features, count):
    kinds, _, channels = features.shape
    near = jax.ShapeDtypeStruct((HEAD, channels), BF16)
    in_hbm = lambda x: pltpu.with_memory_space_constraint(x, pltpu.HBM)
    hbm, vmem = pl.BlockSpec(memory_space=pltpu.HBM), pl.BlockSpec(memory_space=pltpu.VMEM)
    return pl.pallas_call(
        pick_kernel,
        in_specs=[pl.BlockSpec(memory_space=pltpu.SMEM), hbm, hbm],
        out_specs=[vmem] * 4,
        out_shape=[near, near, near, jax.ShapeDtypeStruct((kinds, count, channels), BF16)],
        scratch_shapes=[pltpu.SemaphoreType.DMA((kinds + 3,))],
        compiler_params=pltpu.CompilerParams(vmem_limit_bytes=4 * MIB),
        name="pick",
    )(meta, in_hbm(weight), in_hbm(features))


def mix_kernel(chips, groups, items, streams, meta_ref, *refs):
    heads, refs = refs[: len(items)], refs[len(items) :]
    before, (own_w, near_w, far_w, out, ordered) = refs[:streams], refs[streams:]
    chip, core = meta_ref[4], meta_ref[5]
    swapped = lax.rem(chip, 2)
    parities = [lax.rem(chip + distances[0], 2) for distances in groups]
    for place, (group, _) in enumerate(items):
        for index, distance in enumerate(groups[group]):
            head = lax.rem(chip - distance + chips, chips)
            column = pl.ds(pl.multiple_of(head // 2 * HEAD, HEAD), HEAD)
            ordered[place, :, column] = heads[place][index]

    def own_rows(parity):
        rows = [pl.ds(pl.multiple_of((2 * j + parity) * HEAD, HEAD), HEAD) for j in range(chips // 2)]
        return jnp.concatenate([own_w[span, :] for span in rows], axis=0)

    def finish(by_group):
        total = jnp.concatenate([part[...].astype(F32) for part in before], axis=0)
        for place, (group, source) in enumerate(items):
            if source:
                held = by_group[group]
                weights = jnp.concatenate([held[swapped, source - 1], held[1 - swapped, source - 1]], axis=0)
            else:
                weights = own_rows(parities[group])
            total = total + jnp.dot(ordered[place], weights, preferred_element_type=F32)
        out[...] = total.astype(out.dtype)

    @pl.when(core == parities[0])
    def _():
        finish([near_w, far_w])

    @pl.when(core != parities[0])
    def _():
        finish([far_w, near_w])


def mix(meta, heads, *, groups, items, before, own_w, near_w, far_w, kind, chips):
    rows, channels = heads[0].shape[1], own_w.shape[1]
    body = functools.partial(mix_kernel, chips, groups, items, len(before))
    operands = [*heads, *before, own_w, near_w, far_w]
    scratch = [pltpu.VMEM((len(items), rows, chips // 2 * HEAD), BF16)]
    micros = 0.6 * len(items)
    return vmem_call(body, "attention_mix", micros, meta, operands, [((rows, channels), kind)], scratch)[0]


def rotate_rows(block, positions):
    half_size = block.shape[-1] // 2
    frequency = 10000.0 ** (-jnp.arange(half_size, dtype=jnp.float32) * 2.0 / block.shape[-1])
    angles = positions.astype(jnp.float32)[:, None] * frequency[None, :]
    cosine = jnp.cos(angles)[:, None, :]
    sine_part = jnp.sin(angles)[:, None, :]
    first_half = block[..., :half_size]
    second_half = block[..., half_size:]
    return jnp.concatenate(
        [
            first_half * cosine - second_half * sine_part,
            second_half * cosine + first_half * sine_part,
        ],
        axis=-1,
    )


def run_attention(queries, query_pos, key_rows, value_rows, position_of):
    head_count = queries.shape[1]
    row_count = queries.shape[0]
    head_size = queries.shape[2]
    scale_factor = 1.0 / head_size**0.5
    last_query = jnp.max(query_pos)
    initial = (
        jnp.zeros((head_count, row_count, head_size), jnp.float32),
        jnp.full((head_count, row_count), -1e30, jnp.float32),
        jnp.zeros((head_count, row_count), jnp.float32),
    )
    piece_keys = lax.all_gather(key_rows, "ctx", axis=0, tiled=True)
    piece_values = lax.all_gather(value_rows, "ctx", axis=0, tiled=True)
    piece_rows = piece_keys.shape[0]
    block_rows = 512

    def one_block(state_in, block_index):
        first_block = block_index * block_rows
        key_block = lax.dynamic_slice_in_dim(piece_keys, first_block, block_rows, 0)
        value_block = lax.dynamic_slice_in_dim(piece_values, first_block, block_rows, 0)
        key_pos = position_of(first_block + jnp.arange(block_rows))

        def update(state_old):
            acc_sum, run_max, run_total = state_old
            scores = (
                jnp.einsum("thd,khd->htk", queries, key_block, preferred_element_type=jnp.float32)
                * scale_factor
            )
            causal = (key_pos[None, :] <= query_pos[:, None])[None]
            block_max = jnp.max(jnp.where(causal, scores, -1e30), axis=-1)
            new_max = jnp.maximum(run_max, block_max)
            weights = jnp.where(causal, jnp.exp(scores - new_max[..., None]), 0.0)
            correction = jnp.exp(run_max - new_max)
            new_total = run_total * correction + jnp.sum(weights, axis=-1)
            update_sum = jnp.einsum(
                "htk,khd->htd",
                weights.astype(jnp.bfloat16),
                value_block,
                preferred_element_type=jnp.float32,
            )
            return (acc_sum * correction[..., None] + update_sum, new_max, new_total)

        def unchanged(state_old):
            return state_old

        state_out = lax.cond(jnp.min(key_pos) > last_query, unchanged, update, state_in)
        return (state_out, None)

    state_end, unused = lax.scan(one_block, initial, jnp.arange(piece_rows // block_rows))
    acc_sum, run_max, run_total = state_end
    output = acc_sum / run_total[..., None]
    return jnp.transpose(output, (1, 0, 2)).astype(jnp.bfloat16)


def after_gating(gated, residual_in, out_weight, norm_gain, attn_weight, attn_out):
    tok_rows, chan_count = gated.shape
    hyena_terms = jnp.dot(gated, out_weight, preferred_element_type=jnp.float32)
    hyena_out = lax.psum_scatter(
        hyena_terms.astype(jnp.bfloat16), "ch", scatter_dimension=1, tiled=True
    ).astype(jnp.float32)
    stream = (residual_in.astype(jnp.float32) + hyena_out).astype(jnp.bfloat16)
    stream_wide = stream.astype(jnp.float32)
    full_width = chan_count * lax.axis_size("ch")
    head_cols = attn_weight.shape[1]
    square_total = lax.psum(jnp.sum(stream_wide * stream_wide, axis=1), "ch")
    inverse = lax.rsqrt(square_total / full_width + norm_eps)
    gain_part = lax.dynamic_slice_in_dim(norm_gain, lax.axis_index("ch") * chan_count, chan_count)
    normed = (stream_wide * inverse[:, None] * gain_part[None, :]).astype(jnp.bfloat16)
    projected = jnp.dot(
        lax.all_gather(normed, "ch", axis=1, tiled=True),
        attn_weight,
        preferred_element_type=jnp.float32,
    )
    head_count = head_cols // (3 * HEAD)
    projected = projected.reshape(tok_rows, head_count, 3, HEAD)
    ctx_index = lax.axis_index("ctx")
    positions = ctx_index * tok_rows + jnp.arange(tok_rows, dtype=jnp.int32)
    queries = rotate_rows(projected[:, :, 0, :], positions).astype(jnp.bfloat16)
    key_rows = rotate_rows(projected[:, :, 1, :], positions).astype(jnp.bfloat16)
    value_rows = projected[:, :, 2, :].astype(jnp.bfloat16)

    def position_of(global_row):
        return global_row

    attended = run_attention(queries, positions, key_rows, value_rows, position_of)
    head_terms = jnp.dot(
        attended.reshape(tok_rows, head_count * HEAD), attn_out, preferred_element_type=jnp.float32
    )
    attn_mix = lax.psum_scatter(
        head_terms.astype(jnp.bfloat16), "ch", scatter_dimension=1, tiled=True
    ).astype(jnp.float32)
    return (stream_wide + attn_mix).astype(jnp.bfloat16)


def rotation_tables(positions):
    half_size = HEAD // 2
    frequency = 10000.0 ** (-jnp.arange(half_size, dtype=F32) * 2.0 / HEAD)
    angles = positions.astype(F32)[:, None] * frequency[None, :]
    cosine, sine = jnp.cos(angles), jnp.sin(angles)
    return jnp.concatenate([cosine, cosine], axis=1), jnp.concatenate([-sine, sine], axis=1)


def shards(
    features,
    residual_in,
    short_filter,
    medium_filter,
    skip_gain,
    out_weight,
    norm_gain,
    attn_weight,
    attn_out,
):
    rows, _, channels = features.shape
    chips = lax.axis_size("ctx") // 2
    length = medium_filter.shape[0]
    chunk = rows // 2
    ctx, ch = lax.axis_index("ctx"), lax.axis_index("ch")
    scalars = [ch, ch ^ 1, ch ^ 2, ch ^ 3, ctx // 2, ctx % 2, ctx * rows, ctx]
    meta = jnp.stack(scalars).astype(jnp.int32)

    by_kind = jnp.transpose(features, (1, 0, 2))
    medium_rows = medium_filter.T
    skip = skip_gain.reshape(1, channels)

    starts = [rows - chunk, 0]
    if lax.axis_size("ch") != 4 or attn_weight.shape[1] != 3 * HEAD * chips or chips != 4:
        halo = shift_rows(by_kind[:, rows - length - LEAD :])
        (lower,) = gated_chunk(meta, by_kind, halo, chunk, chunk, short_filter, medium_rows, skip)
        (upper,) = gated_chunk(meta, by_kind, halo, 0, chunk, short_filter, medium_rows, skip)
        return after_gating(
            jnp.concatenate([upper, lower], axis=0), residual_in, out_weight, norm_gain, attn_weight, attn_out
        )

    gain = norm_gain.reshape(1, -1)
    cosine, sine = rotation_tables(meta[6:7] + jnp.arange(rows, dtype=jnp.int32))

    *near_w, edge = pick(meta, attn_out, by_kind, length + LEAD)
    halo = shift_rows(edge)
    picked = [swap_ch(weight, mask) for mask, weight in zip((1, 2, 3), near_w)]

    lower, out_held = gated_chunk(meta, by_kind, halo, chunk, chunk, short_filter, medium_rows, skip, out_weight)
    (upper,) = gated_chunk(meta, by_kind, halo, 0, chunk, short_filter, medium_rows, skip)
    across_x, across_y = column_terms(meta, upper, lower, out_held, ((3, 0, 0, 0), (3, 1, 1, 0)), picked)
    picked = jnp.stack(picked)
    swapped = swap_ctx(picked, 2)
    across_x, across_y = swap_ch(across_x, 1), swap_ch(across_y, 2)
    pieces = ((1, 0, 0, 0), (2, 1, 1, 0), (1, 1, 2, 0), (2, 0, 3, 0), (0, 0, 4, 0), (0, 1, 4, 1))
    direct_x, direct_y, along_x, along_y, kept = column_terms(meta, upper, lower, out_held, pieces, [picked])
    direct_x, direct_y = swap_ch(direct_x, 1), swap_ch(direct_y, 2)
    along_x = (along_x.astype(F32) + across_y.astype(F32)).astype(BF16)
    along_y = (along_y.astype(F32) + across_x.astype(F32)).astype(BF16)
    late_x, late_y = swap_ch(along_x, 1), swap_ch(along_y, 2)
    qkv_held, own_w = load(meta, attn_weight, attn_out, (along_y, swapped), channels)
    parts = vmem_call(
        stream_kernel,
        "add_stream",
        1,
        meta,
        [kept, direct_x, direct_y, late_x, late_y, residual_in],
        [((chunk, channels), BF16)] * 2,
        waits=[qkv_held, cosine, sine],
    )

    own, other, after = [], [], None
    width = attn_weight.shape[1]
    for start in starts:
        part = parts[start // chunk]
        if after is not None:
            part, _ = lax.optimization_barrier((part, after))
        by_x, by_y = swap_ch(part, 1), swap_ch(part, 2)
        diag_a, diag_b = swap_ch(by_x[: chunk // 2], 2), swap_ch(by_y[chunk // 2 :], 1)
        near, square = vmem_call(
            near_kernel,
            "qkv_near",
            3,
            meta,
            [part, by_x, by_y, gain, qkv_held],
            [((chunk, width), F32), ((chunk, LANES), F32)],
        )
        after = diag_a, diag_b, square
        turn = slice(start, start + chunk)
        outs = vmem_call(
            functools.partial(far_kernel, chips),
            "qkv_far",
            2,
            meta,
            [diag_a, diag_b, near, square, gain, cosine[turn], sine[turn], qkv_held],
            [((3, chunk, HEAD), BF16)] * chips,
            [pltpu.VMEM((chunk, width), F32)],
        )
        arrived = [outs[0]] + [rotate_chips(outs[d], d) for d in range(1, chips)]
        own.append(arrived)

    swapped, _ = lax.optimization_barrier((swapped, outs))
    near_w = jnp.stack([picked, swapped])
    far_w = swap_ctx(near_w, 1)
    own, _ = lax.optimization_barrier((own, outs))
    other = [swap_ctx(jnp.stack([piece[1:] for piece in arrived]), 1) for arrived in own]
    own, other = own[1] + own[0], other[::-1]

    groups = [(*range(2, chips, 2), 0), tuple(range(1, chips, 2))]
    given, laid = attend(meta, own, other, None, groups[0], [far_w], chips)
    first = [rotate_chips(piece, d) if d else piece for d, piece in zip(groups[0], given)]
    given, _ = attend(meta, own, other, laid, groups[1], [], chips)
    first, given = lax.optimization_barrier((first, given))
    second = [rotate_chips(piece, d) for d, piece in zip(groups[1], given)]
    back = jnp.stack(first)
    by_x, by_y = swap_ch(back, 1), swap_ch(back, 2)
    add = functools.partial(mix, meta, groups=groups, own_w=own_w, near_w=near_w, far_w=far_w, chips=chips)
    total = add([back, by_x, by_y], items=((0, 0), (0, 1), (0, 2)), before=parts, kind=F32)
    second, by_x, total = lax.optimization_barrier((second, by_x, total))
    across = swap_ch(by_x, 2)
    back = jnp.stack(second)
    by_x, by_y = swap_ch(back, 1), swap_ch(back, 2)
    total = add([across, back, by_x, by_y], items=((0, 3), (1, 0), (1, 1), (1, 2)), before=[total], kind=F32)
    return add([swap_ch(by_y, 1)], items=((1, 3),), before=[total], kind=BF16)


def solution(mesh):
    in_specs = (
        P("ctx", None, "ch"),
        P("ctx", "ch"),
        P(None, None, "ch"),
        P(None, "ch"),
        P("ch"),
        P("ch", None),
        P(),
        P(None, "ch"),
        P("ch", None),
    )
    out_specs = P("ctx", "ch")
    return jax.shard_map(shards, mesh=mesh, in_specs=in_specs, out_specs=out_specs, check_vma=False)
```
